32 devices in a mesh: dp: 32 (over z, y, x, core).
Axes of the slice: x: 2, y: 2, z: 4, core: 2. Of those that a mesh axis runs over, the one named last changes fastest.
Arguments:
- inputs: bfloat16 [64, 320, 1024], P('dp'), may hold values from -6 to 6
- lengths: int32 [64], replicated, may hold values from 192 to 320, as said below
- assignment: int32 [64], P('dp'), may hold values from 0 to 63, each once
- norm1_gain: bfloat16 [1024], P('dp'), may hold values from 0.099609375 to 1.8984375
- norm1_bias: bfloat16 [1024], P('dp'), may hold values from -3 to 3
- qkv_weight: bfloat16 [1024, 3072], P('dp'), may hold values from -0.1875 to 0.1875
- qv_bias: bfloat16 [2048], P('dp'), may hold values from -3 to 3
- out_weight: bfloat16 [1024, 1024], P('dp'), may hold values from -0.75 to 0.75
- out_bias: bfloat16 [1024], P('dp'), may hold values from -3 to 3
- norm2_gain: bfloat16 [1024], P('dp'), may hold values from 0.099609375 to 1.8984375
- norm2_bias: bfloat16 [1024], P('dp'), may hold values from -3 to 3
- up_weight: bfloat16 [1024, 4096], P('dp'), may hold values from -0.1875 to 0.1875
- up_bias: bfloat16 [4096], P('dp'), may hold values from -3 to 3
- down_weight: bfloat16 [4096, 1024], P('dp'), may hold values from -0.09375 to 0.09375
- down_bias: bfloat16 [1024], P('dp'), may hold values from -3 to 3
- cotangent: bfloat16 [64, 320, 1024], P('dp'), may hold values from -6 to 6
Outputs:
- result: bfloat16 [64, 320, 1024], P('dp')
- input_grad: bfloat16 [64, 320, 1024], P('dp')
- norm1_gain_grad: float32 [1024], P('dp')
- norm1_bias_grad: float32 [1024], P('dp')
- qkv_weight_grad: float32 [1024, 3072], P('dp')
- qv_bias_grad: float32 [2048], P('dp')
- out_weight_grad: float32 [1024, 1024], P('dp')
- out_bias_grad: float32 [1024], P('dp')
- norm2_gain_grad: float32 [1024], P('dp')
- norm2_bias_grad: float32 [1024], P('dp')
- up_weight_grad: float32 [1024, 4096], P('dp')
- up_bias_grad: float32 [4096], P('dp')
- down_weight_grad: float32 [4096, 1024], P('dp')
- down_bias_grad: float32 [1024], P('dp')
The draws below stay inside these ranges and needn't reach their ends.
Inputs may be any that keep to these rules, and one draw needn't show every extreme that they name: `lengths`: some sequence keeps all 320 tokens. `assignment`: every sequence stands in exactly one slot.
All inputs are finite; a program needn't handle non-finite values.
Results may differ from the reference program's by a relative error of at most 0.012.
Values may be sent and summed in bfloat16 or wider, within the bound.
A program may use at most 320 MiB of HBM per device.

```python
import jax
import jax.numpy as jnp
from jax import lax

D = 1024
HEADS = 16
HEAD = 64
FF = 4096
LEN = 320
SEQ_DEV = 2
SEQS = 64
N_DP = 32


def draw_lengths(key, part):
    key = jax.random.fold_in(key, 11)
    drawn = jax.random.randint(key, (SEQS,), LEN * 3 // 5, LEN + 1, dtype=jnp.int32)
    chosen = jax.random.randint(jax.random.fold_in(key, 5), (), 0, SEQS, dtype=jnp.int32)
    return jnp.where(jnp.arange(SEQS, dtype=jnp.int32) == chosen, LEN, drawn)


def strengthened(values, own_key, source, target, shards_of, factor):
    owner, partner = [(jnp.arange(values.shape[dim]) // (values.shape[dim] // shards_of)).reshape([-1 if axis == dim else 1 for axis in range(values.ndim)]) for dim in (source, target)]
    chosen = jax.random.permutation(own_key, shards_of)[partner]
    strong = (owner == chosen) | (owner == (partner + shards_of // 2) % shards_of)
    return jnp.where(strong, factor * values, values)


def block_scale(own_key, extent, cuts, smallest, largest):
    level = 1.0
    for dim, parts in cuts:
        steps = jax.random.uniform(jax.random.fold_in(jax.random.fold_in(own_key, 6), dim), (parts,), jnp.float32, smallest / len(cuts), largest / len(cuts))
        level = level * jnp.repeat(jnp.exp(steps), extent[dim] // parts).reshape((-1,) + (1,) * (len(extent) - 1 - dim))
    return level


def scatter_about(stream_key, dims, scale, reach, split=(), kind=jnp.bfloat16):
    entries = scale * jax.random.normal(stream_key, dims, jnp.float32)
    if split:
        entries = entries * block_scale(stream_key, dims, split, -0.22, 0.18)
    return jnp.clip(entries, -reach, reach).astype(kind)


def gaussian_with(own_key, shape, spread, reach, pieces, heavy, kind=jnp.bfloat16):
    entries = spread * jax.random.normal(own_key, shape, jnp.float32)
    if pieces:
        entries = entries * block_scale(own_key, shape, pieces, -0.22, 0.18)
    return jnp.clip(strengthened(entries, jax.random.fold_in(own_key, 3), *heavy), -reach, reach).astype(kind)


def setup_inputs(seed: int = 0) -> dict:
    key_list = jax.random.split(jax.random.key(seed), 17)
    inputs = scatter_about(key_list[0], (SEQS, LEN, D), 1.0, 6.0, ((0, 32),))
    lengths = draw_lengths(jax.random.fold_in(key_list[16], 71), 0)
    assignment = jax.random.permutation(key_list[2], SEQS).astype(jnp.int32)
    norm1_gain = jnp.clip(1.0 + 0.18 * jax.random.normal(key_list[3], (D,), jnp.float32), 0.099609375, 1.8984375).astype(jnp.bfloat16)
    norm1_bias = scatter_about(key_list[4], (D,), 0.5, 3.0, ((0, 32),))
    qkv_weight = scatter_about(key_list[5], (D, 3 * D), D ** -0.5, 0.1875, ((0, 32),))
    qv_bias = scatter_about(key_list[6], (2 * D,), 0.5, 3.0, ((0, 32),))
    out_weight = scatter_about(key_list[7], (D, D), (D // 16) ** -0.5, 0.75, ((0, 32),))
    out_bias = scatter_about(key_list[8], (D,), 0.5, 3.0, ((0, 32),))
    norm2_gain = jnp.clip(1.0 + 0.18 * jax.random.normal(key_list[9], (D,), jnp.float32), 0.099609375, 1.8984375).astype(jnp.bfloat16)
    norm2_bias = scatter_about(key_list[10], (D,), 0.5, 3.0, ((0, 32),))
    up_weight = scatter_about(key_list[11], (D, FF), D ** -0.5, 0.1875, ((0, 32),))
    up_bias = scatter_about(key_list[12], (FF,), 0.5, 3.0, ((0, 32),))
    down_weight = scatter_about(key_list[13], (FF, D), FF ** -0.5, 0.09375, ((0, 32),))
    down_bias = scatter_about(key_list[14], (D,), 0.5, 3.0, ((0, 32),))
    cotangent = gaussian_with(key_list[15], (SEQS, LEN, D), 1.0, 6.0, ((0, 32),), (0, 2, 32, 2.75))
    return {"inputs": inputs, "lengths": lengths, "assignment": assignment, "norm1_gain": norm1_gain, "norm1_bias": norm1_bias, "qkv_weight": qkv_weight, "qv_bias": qv_bias, "out_weight": out_weight, "out_bias": out_bias, "norm2_gain": norm2_gain, "norm2_bias": norm2_bias, "up_weight": up_weight, "up_bias": up_bias, "down_weight": down_weight, "down_bias": down_bias, "cotangent": cotangent}


@jax.custom_vjp
def low(v):
    return lax.optimization_barrier(v.astype(jnp.bfloat16)).astype(jnp.float32)

@jax.custom_vjp
def low_back(v):
    return v

def low_keep(v):
    return (low(v), None)

def low_pass(kept, grad):
    return (grad,)

def back_keep(v):
    return (v, None)

def back_low(kept, grad):
    return (low(grad),)
low.defvjp(low_keep, low_pass)
low_back.defvjp(back_keep, back_low)
eps = 1e-06
masked_score = -1000000000.0
highest = lax.Precision.HIGHEST

def layer_norm(values, norm_gain, norm_shift):
    average = lax.optimization_barrier(jnp.mean(values, axis=-1, keepdims=True))
    centered = values - average
    variance = lax.optimization_barrier(jnp.mean(centered * centered, axis=-1, keepdims=True))
    return centered * lax.rsqrt(variance + eps) * norm_gain + norm_shift

def forward(key_mask, inputs, norm1_gain, norm1_bias, qkv_weight, qv_bias, out_weight, out_bias, norm2_gain, norm2_bias, up_weight, up_bias, down_weight, down_bias):
    seq_count, tok_count, model_width = inputs.shape
    split_shape = (seq_count, tok_count, HEADS, HEAD)
    normed_first = low(layer_norm(inputs, norm1_gain, norm1_bias))
    full_bias = jnp.concatenate([qv_bias[:model_width], jnp.zeros((model_width,), jnp.float32), qv_bias[model_width:]])
    mixed_qkv = low(low_back(jnp.matmul(normed_first, qkv_weight, precision=highest) + full_bias))
    queries = mixed_qkv[..., :model_width].reshape(split_shape)
    keys_all = mixed_qkv[..., model_width:2 * model_width].reshape(split_shape)
    values_all = mixed_qkv[..., 2 * model_width:].reshape(split_shape)
    scores = low_back(jnp.einsum('bqhd,bkhd->bhqk', queries, keys_all, precision=highest) * HEAD ** (-0.5))
    scores = jnp.where(key_mask[:, None, None, :], scores, masked_score)
    row_max = lax.optimization_barrier(jnp.max(scores, axis=-1, keepdims=True))
    exponent = jnp.exp(scores - row_max)
    softmax_probs = exponent / lax.optimization_barrier(jnp.sum(exponent, axis=-1, keepdims=True))
    attended = jnp.einsum('bhqk,bkhd->bqhd', low(softmax_probs), values_all, precision=highest)
    attended = low(low_back(attended.reshape(seq_count, tok_count, model_width)))
    hidden = inputs + low_back(jnp.matmul(attended, out_weight, precision=highest) + out_bias)
    normed_second = low(layer_norm(hidden, norm2_gain, norm2_bias))
    pre_act = low_back(jnp.matmul(normed_second, up_weight, precision=highest) + up_bias)
    activation = low(jax.nn.gelu(pre_act, approximate=False))
    branch = low_back(jnp.matmul(activation, down_weight, precision=highest) + down_bias)
    return key_mask[:, :, None].astype(jnp.float32) * (hidden + branch)

def reference(inputs, lengths, assignment, norm1_gain, norm1_bias, qkv_weight, qv_bias, out_weight, out_bias, norm2_gain, norm2_bias, up_weight, up_bias, down_weight, down_bias, cotangent):
    kept_len = jnp.take(lengths, assignment)
    key_mask = jnp.arange(LEN, dtype=jnp.int32)[None, :] < kept_len[:, None]
    params = (norm1_gain.astype(jnp.float32), norm1_bias.astype(jnp.float32), qkv_weight.astype(jnp.float32), qv_bias.astype(jnp.float32), out_weight.astype(jnp.float32), out_bias.astype(jnp.float32), norm2_gain.astype(jnp.float32), norm2_bias.astype(jnp.float32), up_weight.astype(jnp.float32), up_bias.astype(jnp.float32), down_weight.astype(jnp.float32), down_bias.astype(jnp.float32))
    blocks = (inputs.reshape(N_DP, SEQ_DEV, LEN, D), key_mask.reshape(N_DP, SEQ_DEV, LEN), cotangent.reshape(N_DP, SEQ_DEV, LEN, D))

    def advance(running, block):
        rows_in, mask_in, tangent_in = block

        def local_layer(values, *weights_in):
            return forward(mask_in, values, *weights_in)
        output_rows, pullback = jax.vjp(local_layer, rows_in.astype(jnp.float32), *params)
        grad_list = pullback(tangent_in.astype(jnp.float32))
        running = tuple((summed + grad_part for summed, grad_part in zip(running, grad_list[1:])))
        return (running, (output_rows.astype(jnp.bfloat16), grad_list[0].astype(jnp.bfloat16)))
    start = tuple((jnp.zeros(member.shape, jnp.float32) for member in params))
    sums, (outputs, input_grads) = lax.scan(advance, start, blocks)
    return (outputs.reshape(SEQS, LEN, D), input_grads.reshape(SEQS, LEN, D), sums[0], sums[1], sums[2], sums[3], sums[4], sums[5], sums[6], sums[7], sums[8], sums[9], sums[10], sums[11])
```

```python
import jax
import jax.numpy as jnp
from jax import lax
from jax.experimental import pallas as pl
from jax.experimental.pallas import tpu as pltpu
from jax.sharding import PartitionSpec as P

HEADS = 16
HEAD = 64


eps = 1e-06
masked_score = -1000000000.0


def layer_norm(values, norm_gain, norm_shift):
    average = jnp.mean(values, axis=-1, keepdims=True)
    centered = values - average
    variance = jnp.mean(centered * centered, axis=-1, keepdims=True)
    return centered * lax.rsqrt(variance + eps) * norm_gain + norm_shift


def gelu_exact(values):
    return jax.nn.gelu(values, approximate=False)


def contract_rows(left, right):
    return lax.dot_general(
        left, right, (((0,), (0,)), ((), ())), preferred_element_type=jnp.float32
    )


def contract_cols(left, right):
    return lax.dot_general(
        left, right, (((1,), (1,)), ((), ())), preferred_element_type=jnp.float32
    )


BF16 = jnp.bfloat16
F32 = jnp.float32
MESH = pl.DeviceIdType.MESH
SIZES = {"z": 4, "y": 2, "x": 2}
STRIDE = {"z": 8, "y": 4, "x": 2}
ROWS = 32
WIDE = 1024
STREAMS = (("zyx", 0, 384), ("zxy", 384, 384), ("xzy", 768, 128), ("yzx", 896, 128))
CHUNKS = (
    tuple((0, 0, c) for c in (0, 1024, 2048))
    + ((1, 0, 0),)
    + tuple((2, 0, c) for c in (0, 1024, 2048, 3072))
    + tuple((3, r, 0) for r in (0, 32, 64, 96))
)


def coords():
    me = lax.axis_index("dp")
    at = {
        "z": lax.div(me, 8),
        "y": lax.rem(lax.div(me, 4), 2),
        "x": lax.rem(lax.div(me, 2), 2),
        "c": lax.rem(me, 2),
    }
    return me, at


def partners(me, at, dim):
    size = SIZES[dim]
    found = []
    for k in range(1, size):
        there = lax.rem(at[dim] + k, size)
        found.append((there, me + (there - at[dim]) * STRIDE[dim]))
    return found


def sibling(me, at):
    return me + 1 - 2 * at["c"]


def greet(me, at):
    barrier = pltpu.get_barrier_semaphore()
    devices = [sibling(me, at)]
    for dim in "zyx":
        devices += [device for _, device in partners(me, at, dim)]
    for device in devices:
        pl.semaphore_signal(barrier, inc=1, device_id=(device,), device_id_type=MESH)
    pl.semaphore_wait(barrier, len(devices))


def remote(src, dst, sems, slot, number, device):
    return pltpu.make_async_remote_copy(
        src_ref=src,
        dst_ref=dst,
        send_sem=sems[0].at[slot, number],
        recv_sem=sems[1].at[slot, number],
        device_id=(device,),
        device_id_type=MESH,
    )


def held(order, stage, at):
    return tuple(
        slice(None) if dim in order[:stage] else at[dim] for dim in "zyx"
    )


def gather_stage(k, stage, shards, wholes, me, at, sems):
    which, row, col = CHUNKS[k]
    rows = pl.ds(row, ROWS)
    whole, shard = wholes[which], shards[which]
    slot, number, copies = k % 4, 0, []
    if stage == 3:
        block = whole.at[:, :, :, at["c"], rows, pl.ds(col, WIDE)]
        return [remote(block, block, sems, slot, COPIES - 1, sibling(me, at))]
    for order, first, width in STREAMS:
        columns = pl.ds(col + first, width)
        for s in range(3):
            for _, device in partners(me, at, order[s]):
                if s == stage:
                    block = whole.at[held(order, stage, at) + (at["c"], rows, columns)]
                    src = shard.at[rows, columns] if stage == 0 else block
                    copies.append(remote(src, block, sems, slot, number, device))
                number += 1
    return copies


COPIES = 5 * len(STREAMS) + 1


def gather_kernel(*refs):
    shards, small, wholes, smalls = refs[:4], refs[4], refs[5:9], refs[9]
    send, recv, own = refs[10:]
    sems = (send, recv)
    me, at = coords()
    mine = (at["z"], at["y"], at["x"], at["c"])
    local = [
        pltpu.make_async_copy(shard, whole.at[mine], own.at[i])
        for i, (shard, whole) in enumerate(zip((*shards, small), (*wholes, smalls)))
    ]
    for copy in local:
        copy.start()
    greet(me, at)
    chunks = len(CHUNKS)
    for tick in range(chunks + 3):
        copies = []
        if tick < 4:
            copies += small_stage(tick, small, smalls, me, at, sems)
        for stage in (3, 2, 1, 0):
            if 0 <= tick - stage < chunks:
                copies += gather_stage(tick - stage, stage, shards, wholes, me, at, sems)
        for copy in copies:
            copy.start()
        if tick == 0:
            for copy in local:
                copy.wait()
        for copy in copies:
            copy.wait()


def small_stage(stage, small, smalls, me, at, sems):
    number = {0: 0, 1: 3, 2: 4, 3: 5}[stage]
    if stage == 3:
        block = smalls.at[:, :, :, at["c"]]
        return [remote(block, block, sems, 4, number, sibling(me, at))]
    copies = []
    for _, device in partners(me, at, "zyx"[stage]):
        block = smalls.at[held("zyx", stage, at) + (at["c"],)]
        copies.append(remote(small if stage == 0 else block, block, sems, 4, number, device))
        number += 1
    return copies


def gather(shards, small):
    shapes = [jax.ShapeDtypeStruct((4, 2, 2, 2) + a.shape, a.dtype) for a in (*shards, small)]
    anywhere = pl.BlockSpec(memory_space=pl.ANY)
    return pl.pallas_call(
        gather_kernel,
        out_shape=shapes,
        in_specs=[anywhere] * 5,
        out_specs=[anywhere] * 5,
        scratch_shapes=[
            pltpu.SemaphoreType.DMA((5, COPIES)),
            pltpu.SemaphoreType.DMA((5, COPIES)),
            pltpu.SemaphoreType.DMA((5,)),
        ],
        compiler_params=pltpu.CompilerParams(collective_id=0, has_side_effects=True),
        name="gather_weights",
    )(*shards, small)


def remaining(order, stage):
    return tuple(SIZES[dim] for dim in "zyx" if dim not in order[:stage])


def pick(order, stage, dim, index):
    return tuple(
        index if d == dim else slice(None) for d in "zyx" if d not in order[:stage]
    )


BACK = tuple((order[::-1], first, width) for order, first, width in STREAMS)


def add_up(dst, terms, lead):
    count = 1
    for n in lead:
        count *= n

    def at_index(i):
        index = []
        for n in lead[::-1]:
            index.append(lax.rem(i, n))
            i = lax.div(i, n)
        return tuple(index[::-1])

    def body(i, carry):
        index = at_index(i)
        total = terms[0][index + (slice(None),) * 2].astype(F32)
        for term in terms[1:]:
            total = total + term[index + (slice(None),) * 2].astype(F32)
        dst[index + (slice(None),) * 2] = total.astype(dst.dtype)
        return carry

    if count == 1:
        body(0, 0) if lead else None
        if not lead:
            total = terms[0][...].astype(F32)
            for term in terms[1:]:
                total = total + term[...].astype(F32)
            dst[...] = total.astype(dst.dtype)
    else:
        lax.fori_loop(0, count, body, 0)


class Sum:
    def __init__(self, grad, out, streams, dtype_bufs, slot, sems, me, at):
        self.grad, self.out, self.streams = grad, out, streams
        self.own, self.from_core, self.bufs = dtype_bufs
        self.slot, self.sems, self.me, self.at = slot, sems, me, at

    def start(self):
        there = 1 - self.at["c"]
        self.load = pltpu.make_async_copy(
            self.grad.at[:, :, :, self.at["c"]], self.own, self.sems[2].at[self.slot]
        )
        return [
            self.load,
            remote(
                self.grad.at[:, :, :, there],
                self.from_core,
                self.sems,
                self.slot,
                COPIES - 1,
                sibling(self.me, self.at),
            ),
        ]

    def step(self, stage):
        if stage == 1:
            add_up(self.own, [self.own, self.from_core], (4, 2, 2))
        copies, number = [], 0
        for (order, first, width), bufs in zip(self.streams, self.bufs):
            columns = pl.ds(first, width)
            everything = slice(None)
            for s in range(3):
                dim = order[s]
                if s + 1 == stage:
                    if stage == 1:
                        held_now = lambda index: self.own.at[index + (everything, columns)]
                    else:
                        prior = order[s - 1]
                        if stage == 2:
                            before = self.own.at[
                                pick(order, 0, prior, self.at[prior]) + (everything, columns)
                            ]
                        else:
                            before = bufs[s - 2][1].at[pick(order, s - 1, prior, self.at[prior])]
                        arrived, total = bufs[s - 1]
                        add_up(
                            total,
                            [before] + [arrived.at[i] for i in range(SIZES[prior] - 1)],
                            remaining(order, s),
                        )
                        held_now = lambda index, total=total: total.at[index]
                    for i, (there, device) in enumerate(partners(self.me, self.at, dim)):
                        copies.append(
                            remote(
                                held_now(pick(order, s, dim, there)),
                                bufs[s][0].at[i],
                                self.sems,
                                self.slot,
                                number + i,
                                device,
                            )
                        )
                number += SIZES[dim] - 1
            if stage == 4:
                prior = order[2]
                before = bufs[1][1].at[pick(order, 2, prior, self.at[prior])]
                arrived = bufs[2][0]
                add_up(
                    self.out.at[:, columns],
                    [before] + [arrived.at[i] for i in range(SIZES[prior] - 1)],
                    (),
                )
        return copies


def sum_buffers(streams, rows, width, dtype):
    shapes = [pltpu.VMEM((4, 2, 2, rows, width), dtype)] * 2
    for order, _, columns in streams:
        for s in range(3):
            left = remaining(order, s + 1)
            shapes.append(pltpu.VMEM((SIZES[order[s]] - 1,) + left + (rows, columns), dtype))
            if s < 2:
                shapes.append(pltpu.VMEM(left + (rows, columns), dtype))
    return shapes


def view_buffers(streams, refs, slot=None):
    refs = [r if slot is None else r.at[slot] for r in refs]
    own, from_core, rest = refs[0], refs[1], refs[2:]
    bufs = [(rest[5 * i : 5 * i + 2], rest[5 * i + 2 : 5 * i + 4], rest[5 * i + 4 : 5 * i + 5]) for i in range(len(streams))]
    return own, from_core, bufs


SMALL_STREAM = (("xyz", 0, 128),)


def sum_kernel(*refs):
    grads, small, outs, small_out, refs = refs[:4], refs[4], refs[5:9], refs[9], refs[10:]
    per = 2 + 5 * len(BACK)
    slots = [refs[:per], refs[per : 2 * per]]
    small_refs, refs = refs[2 * per : 2 * per + 7], refs[2 * per + 7 :]
    send, recv, own = refs
    sems = (send, recv, own)
    me, at = coords()
    greet(me, at)
    chunks = len(CHUNKS)
    flows = {}
    for tick in range(chunks + 4):
        copies = []
        if tick == 0:
            tiny = Sum(small, small_out, SMALL_STREAM, view_buffers(SMALL_STREAM, small_refs), 4, sems, me, at)
            copies += tiny.start()
        elif tick <= 4:
            copies += tiny.step(tick)
        for stage in (4, 3, 2, 1, 0):
            k = tick - stage
            if 0 <= k < chunks:
                which, row, col = CHUNKS[k]
                if stage == 0:
                    grad = grads[which].at[:, :, :, :, pl.ds(row, ROWS), pl.ds(col, WIDE)]
                    out = outs[which].at[pl.ds(row, ROWS), pl.ds(col, WIDE)]
                    flows[k] = Sum(grad, out, BACK, view_buffers(BACK, slots[k % 2]), k % 4, sems, me, at)
                    copies += flows[k].start()
                else:
                    copies += flows[k].step(stage)
        for copy in copies:
            copy.start()
        for copy in copies:
            copy.wait()


def sum_up(grads, small):
    anywhere = pl.BlockSpec(memory_space=pl.ANY)
    inside = pl.BlockSpec(memory_space=pltpu.VMEM)
    return pl.pallas_call(
        sum_kernel,
        out_shape=[jax.ShapeDtypeStruct(a.shape[4:], F32) for a in (*grads, small)],
        in_specs=[anywhere] * 5,
        out_specs=[inside] * 5,
        scratch_shapes=sum_buffers(BACK, ROWS, WIDE, BF16) * 2
        + sum_buffers(SMALL_STREAM, 8, 128, F32)
        + [
            pltpu.SemaphoreType.DMA((5, COPIES)),
            pltpu.SemaphoreType.DMA((5, COPIES)),
            pltpu.SemaphoreType.DMA((5,)),
        ],
        compiler_params=pltpu.CompilerParams(
            collective_id=1, has_side_effects=True, vmem_limit_bytes=48 << 20
        ),
        name="sum_gradients",
    )(*grads, small)

NARROW = (0, 1, 5, 6, 7, 11)
WEIGHTS = (2, 4, 8, 10)


def on_box():
    return lax.axis_size("dp") == 32


def gather_all(weights):
    if not on_box():
        return tuple(lax.all_gather(w, "dp", axis=0, tiled=True) for w in weights)
    me = lax.axis_index("dp")
    lane = jnp.arange(128, dtype=jnp.int32)[None, :]
    narrow = jnp.tile(jnp.stack([weights[i] for i in NARROW]), (1, 4))
    rows = [
        jnp.where(lane // 32 == me % 4, narrow, 0),
        jnp.where(lane // 64 == me % 2, jnp.tile(weights[3][None], (1, 2)), 0),
        weights[9][None],
    ]
    small = jnp.concatenate(rows, axis=0).astype(F32)
    *wholes, smalls = gather([weights[i] for i in WEIGHTS], small)
    smalls = smalls.reshape(32, 8, 128)
    fours = jnp.sum(smalls.reshape(8, 4, 8, 128), axis=1)
    gathered = [None] * 12
    for row, i in enumerate(NARROW):
        gathered[i] = fours[:, row].reshape(1024)
    gathered[3] = jnp.sum(smalls.reshape(16, 2, 8, 128)[:, :, 6], axis=1).reshape(2048)
    gathered[9] = smalls[:, 7].reshape(4096)
    for i, whole in zip(WEIGHTS, wholes):
        gathered[i] = whole.reshape(32 * whole.shape[4], whole.shape[5])
    return gathered


def scatter_all(grads):
    if not on_box():
        return tuple(
            lax.psum_scatter(g, "dp", scatter_dimension=0, tiled=True) for g in grads
        )
    me = lax.axis_index("dp")
    rows = [jnp.repeat(grads[i].reshape(8, 128), 4, axis=0) for i in NARROW]
    rows += [jnp.repeat(grads[3].reshape(16, 128), 2, axis=0), grads[9].reshape(32, 128)]
    small = jnp.stack(rows, axis=1).reshape(4, 2, 2, 2, 8, 128)
    wide = []
    for i in WEIGHTS:
        g = grads[i].astype(BF16)
        wide.append(g.reshape(4, 2, 2, 2, g.shape[0] // 32, g.shape[1]))
    *sums, total = sum_up(wide, small)
    found = [None] * 12
    for row, i in enumerate(NARROW):
        found[i] = lax.dynamic_slice(total[row], (me % 4 * 32,), (32,))
    found[3] = lax.dynamic_slice(total[6], (me % 2 * 64,), (64,))
    found[9] = total[7]
    for i, s in zip(WEIGHTS, sums):
        found[i] = s
    return found


def local(
    inputs,
    lengths,
    assignment,
    norm1_gain,
    norm1_bias,
    qkv_weight,
    qv_bias,
    out_weight,
    out_bias,
    norm2_gain,
    norm2_bias,
    up_weight,
    up_bias,
    down_weight,
    down_bias,
    cotangent,
):
    weights = (norm1_gain, norm1_bias, qkv_weight, qv_bias, out_weight, out_bias)
    weights += (norm2_gain, norm2_bias, up_weight, up_bias, down_weight, down_bias)
    gathered = gather_all(weights)
    seq_count, tok_count, model_width = inputs.shape
    rows_all = seq_count * tok_count
    split_shape = (seq_count, tok_count, HEADS, HEAD)
    head_scale = HEAD ** (-0.5)
    matches = assignment[:, None] == jnp.arange(lengths.shape[0], dtype=jnp.int32)[None, :]
    kept_len = jnp.sum(jnp.where(matches, lengths[None, :], 0), axis=1)
    key_mask = jnp.arange(tok_count, dtype=jnp.int32)[None, :] < kept_len[:, None]
    row_mask = key_mask.reshape(rows_all, 1).astype(jnp.float32)
    gain_first = gathered[0].astype(jnp.float32)
    shift_first = gathered[1].astype(jnp.float32)
    qv_full = gathered[3].astype(jnp.float32)
    proj_shift = gathered[5].astype(jnp.float32)
    gain_second = gathered[6].astype(jnp.float32)
    shift_second = gathered[7].astype(jnp.float32)
    up_shift = gathered[9].astype(jnp.float32)
    down_shift = gathered[11].astype(jnp.float32)
    inputs_flat = inputs.reshape(rows_all, model_width).astype(jnp.float32)
    normed_first, first_back = jax.vjp(layer_norm, inputs_flat, gain_first, shift_first)
    normed_low = normed_first.astype(jnp.bfloat16)
    full_bias = jnp.concatenate(
        [qv_full[:model_width], jnp.zeros((model_width,), jnp.float32), qv_full[model_width:]]
    )
    mixed_qkv = (
        jnp.dot(normed_low, gathered[2], preferred_element_type=jnp.float32) + full_bias
    ).astype(jnp.bfloat16)
    queries = mixed_qkv[:, :model_width].reshape(split_shape)
    keys_all = mixed_qkv[:, model_width : 2 * model_width].reshape(split_shape)
    values_all = mixed_qkv[:, 2 * model_width :].reshape(split_shape)
    scores = (
        jnp.einsum("bqhd,bkhd->bhqk", queries, keys_all, preferred_element_type=jnp.float32)
        * head_scale
    )
    scores = jnp.where(key_mask[:, None, None, :], scores, masked_score)
    row_max = jnp.max(scores, axis=-1, keepdims=True)
    exponent = jnp.exp(scores - row_max)
    row_total = jnp.sum(exponent, axis=-1, keepdims=True)
    softmax_probs = exponent / row_total
    log_total = row_max + jnp.log(row_total)
    attended = jnp.einsum(
        "bhqk,bkhd->bqhd",
        softmax_probs.astype(jnp.bfloat16),
        values_all,
        preferred_element_type=jnp.float32,
    )
    attended = attended.reshape(rows_all, model_width).astype(jnp.bfloat16)
    hidden = inputs_flat + (
        jnp.dot(attended, gathered[4], preferred_element_type=jnp.float32) + proj_shift
    )
    normed_second, second_back = jax.vjp(layer_norm, hidden, gain_second, shift_second)
    second_low = normed_second.astype(jnp.bfloat16)
    pre_act = jnp.dot(second_low, gathered[8], preferred_element_type=jnp.float32) + up_shift
    activation, gelu_back = jax.vjp(gelu_exact, pre_act)
    act_low = activation.astype(jnp.bfloat16)
    output_rows = row_mask * (
        hidden + (jnp.dot(act_low, gathered[10], preferred_element_type=jnp.float32) + down_shift)
    )
    result = output_rows.reshape(inputs.shape).astype(jnp.bfloat16)
    grad_rows = cotangent.reshape(rows_all, model_width).astype(jnp.float32) * row_mask
    grad_low = grad_rows.astype(jnp.bfloat16)
    down_grad = contract_rows(act_low, grad_low)
    down_bias_grad = jnp.sum(grad_low.astype(jnp.float32), axis=0)
    grad_pre = gelu_back(contract_cols(grad_low, gathered[10]))[0].astype(jnp.bfloat16)
    up_grad = contract_rows(second_low, grad_pre)
    up_bias_grad = jnp.sum(grad_pre.astype(jnp.float32), axis=0)
    grad_second, gain2_grad, shift2_grad = second_back(contract_cols(grad_pre, gathered[8]))
    grad_hidden = grad_rows + grad_second
    branch_low = grad_hidden.astype(jnp.bfloat16)
    proj_grad = contract_rows(attended, branch_low)
    proj_bias_grad = jnp.sum(branch_low.astype(jnp.float32), axis=0)
    grad_att = contract_cols(branch_low, gathered[4]).astype(jnp.bfloat16).reshape(split_shape)
    scores_again = (
        jnp.einsum("bqhd,bkhd->bhqk", queries, keys_all, preferred_element_type=jnp.float32)
        * head_scale
    )
    scores_again = jnp.where(key_mask[:, None, None, :], scores_again, masked_score)
    probs_again = jnp.exp(scores_again - log_total)
    probs_low = probs_again.astype(jnp.bfloat16)
    grad_probs = jnp.einsum(
        "bqhd,bkhd->bhqk", grad_att, values_all, preferred_element_type=jnp.float32
    )
    grad_values = jnp.einsum(
        "bhqk,bqhd->bkhd", probs_low, grad_att, preferred_element_type=jnp.float32
    )
    inner_sum = jnp.sum(probs_again * grad_probs, axis=-1, keepdims=True)
    grad_scores = (probs_again * (grad_probs - inner_sum)).astype(jnp.bfloat16)
    grad_queries = (
        jnp.einsum("bhqk,bkhd->bqhd", grad_scores, keys_all, preferred_element_type=jnp.float32)
        * head_scale
    )
    grad_keys = (
        jnp.einsum("bhqk,bqhd->bkhd", grad_scores, queries, preferred_element_type=jnp.float32)
        * head_scale
    )
    grad_mixed = jnp.concatenate(
        [
            grad_queries.reshape(rows_all, model_width),
            grad_keys.reshape(rows_all, model_width),
            grad_values.reshape(rows_all, model_width),
        ],
        axis=1,
    ).astype(jnp.bfloat16)
    qkv_grad = contract_rows(normed_low, grad_mixed)
    column_sums = jnp.sum(grad_mixed.astype(jnp.float32), axis=0)
    qv_grad = jnp.concatenate([column_sums[:model_width], column_sums[2 * model_width :]])
    grad_first, gain1_grad, shift1_grad = first_back(contract_cols(grad_mixed, gathered[2]))
    input_grad = (grad_hidden + grad_first).reshape(inputs.shape).astype(jnp.bfloat16)
    all_sums = scatter_all(
        (gain1_grad, shift1_grad, qkv_grad, qv_grad, proj_grad, proj_bias_grad)
        + (gain2_grad, shift2_grad, up_grad, up_bias_grad, down_grad, down_bias_grad)
    )
    attn_sums = all_sums[:6]
    mlp_sums = all_sums[6:]
    return (
        result,
        input_grad,
        attn_sums[0],
        attn_sums[1],
        attn_sums[2],
        attn_sums[3],
        attn_sums[4],
        attn_sums[5],
        mlp_sums[0],
        mlp_sums[1],
        mlp_sums[2],
        mlp_sums[3],
        mlp_sums[4],
        mlp_sums[5],
    )


def solution(mesh):
    placed = (
        P("dp", None, None),
        P(),
        P("dp"),
        P("dp"),
        P("dp"),
        P("dp", None),
        P("dp"),
        P("dp", None),
        P("dp"),
        P("dp"),
        P("dp"),
        P("dp", None),
        P("dp"),
        P("dp", None),
        P("dp"),
        P("dp", None, None),
    )
    return jax.shard_map(
        local,
        mesh=mesh,
        in_specs=placed,
        out_specs=(
            P("dp", None, None),
            P("dp", None, None),
            P("dp"),
            P("dp"),
            P("dp", None),
            P("dp"),
            P("dp", None),
            P("dp"),
            P("dp"),
            P("dp"),
            P("dp", None),
            P("dp"),
            P("dp", None),
            P("dp"),
        ),
        check_vma=False,
    )
```

```python
import jax
import jax.numpy as jnp
from jax import lax
from jax.experimental import pallas as pl
from jax.experimental.pallas import tpu as pltpu
from jax.sharding import PartitionSpec as P

HEADS = 16
HEAD = 64


eps = 1e-06
masked_score = -1000000000.0


def layer_norm(values, norm_gain, norm_shift):
    average = jnp.mean(values, axis=-1, keepdims=True)
    centered = values - average
    variance = jnp.mean(centered * centered, axis=-1, keepdims=True)
    return centered * lax.rsqrt(variance + eps) * norm_gain + norm_shift


def gelu_exact(values):
    return jax.nn.gelu(values, approximate=False)


def contract_rows(left, right):
    return lax.dot_general(
        left, right, (((0,), (0,)), ((), ())), preferred_element_type=jnp.float32
    )


def contract_cols(left, right):
    return lax.dot_general(
        left, right, (((1,), (1,)), ((), ())), preferred_element_type=jnp.float32
    )


BF16 = jnp.bfloat16
F32 = jnp.float32
MESH = pl.DeviceIdType.MESH
SIZES = {"z": 4, "y": 2, "x": 2}
STRIDE = {"z": 8, "y": 4, "x": 2}
ROWS = 32
WIDE = 1024
STREAMS = (("zyx", 0, 384), ("zxy", 384, 384), ("xzy", 768, 128), ("yzx", 896, 128))
CHUNKS = (
    tuple((0, 0, c) for c in (0, 1024, 2048))
    + ((1, 0, 0),)
    + tuple((2, 0, c) for c in (0, 1024, 2048, 3072))
    + tuple((3, r, 0) for r in (0, 32, 64, 96))
)


def coords():
    me = lax.axis_index("dp")
    at = {
        "z": lax.div(me, 8),
        "y": lax.rem(lax.div(me, 4), 2),
        "x": lax.rem(lax.div(me, 2), 2),
        "c": lax.rem(me, 2),
    }
    return me, at


def partners(me, at, dim):
    size = SIZES[dim]
    found = []
    for k in range(1, size):
        there = lax.rem(at[dim] + k, size)
        found.append((there, me + (there - at[dim]) * STRIDE[dim]))
    return found


def sibling(me, at):
    return me + 1 - 2 * at["c"]


def greet(me, at):
    barrier = pltpu.get_barrier_semaphore()
    devices = [sibling(me, at)]
    for dim in "zyx":
        devices += [device for _, device in partners(me, at, dim)]
    for device in devices:
        pl.semaphore_signal(barrier, inc=1, device_id=(device,), device_id_type=MESH)
    pl.semaphore_wait(barrier, len(devices))


def remote(src, dst, sems, slot, number, device):
    return pltpu.make_async_remote_copy(
        src_ref=src,
        dst_ref=dst,
        send_sem=sems[0].at[slot, number],
        recv_sem=sems[1].at[slot, number],
        device_id=(device,),
        device_id_type=MESH,
    )


def held(order, stage, at):
    return tuple(
        slice(None) if dim in order[:stage] else at[dim] for dim in "zyx"
    )


COPIES = 5 * len(STREAMS) + 1


def small_stage(stage, small, smalls, me, at, sems):
    number = {0: 0, 1: 3, 2: 4, 3: 5}[stage]
    if stage == 3:
        block = smalls.at[:, :, :, at["c"]]
        return [remote(block, block, sems, 4, number, sibling(me, at))]
    copies = []
    for _, device in partners(me, at, "zyx"[stage]):
        block = smalls.at[held("zyx", stage, at) + (at["c"],)]
        copies.append(remote(small if stage == 0 else block, block, sems, 4, number, device))
        number += 1
    return copies


def remaining(order, stage):
    return tuple(SIZES[dim] for dim in "zyx" if dim not in order[:stage])


def pick(order, stage, dim, index):
    return tuple(
        index if d == dim else slice(None) for d in "zyx" if d not in order[:stage]
    )


BACK = tuple((order[::-1], first, width) for order, first, width in STREAMS)


def add_up(dst, terms, lead):
    count = 1
    for n in lead:
        count *= n

    def at_index(i):
        index = []
        for n in lead[::-1]:
            index.append(lax.rem(i, n))
            i = lax.div(i, n)
        return tuple(index[::-1])

    def body(i, carry):
        index = at_index(i)
        total = terms[0][index + (slice(None),) * 2].astype(F32)
        for term in terms[1:]:
            total = total + term[index + (slice(None),) * 2].astype(F32)
        dst[index + (slice(None),) * 2] = total.astype(dst.dtype)
        return carry

    if count == 1:
        body(0, 0) if lead else None
        if not lead:
            total = terms[0][...].astype(F32)
            for term in terms[1:]:
                total = total + term[...].astype(F32)
            dst[...] = total.astype(dst.dtype)
    else:
        lax.fori_loop(0, count, body, 0)


class Sum:
    def __init__(self, grad, out, streams, dtype_bufs, slot, sems, me, at):
        self.grad, self.out, self.streams = grad, out, streams
        self.own, self.from_core, self.bufs = dtype_bufs
        self.slot, self.sems, self.me, self.at = slot, sems, me, at

    def start(self):
        there = 1 - self.at["c"]
        self.load = pltpu.make_async_copy(
            self.grad.at[:, :, :, self.at["c"]], self.own, self.sems[2].at[self.slot]
        )
        return [
            self.load,
            remote(
                self.grad.at[:, :, :, there],
                self.from_core,
                self.sems,
                self.slot,
                COPIES - 1,
                sibling(self.me, self.at),
            ),
        ]

    def step(self, stage):
        if stage == 1:
            add_up(self.own, [self.own, self.from_core], (4, 2, 2))
        copies, number = [], 0
        for (order, first, width), bufs in zip(self.streams, self.bufs):
            columns = pl.ds(first, width)
            everything = slice(None)
            for s in range(3):
                dim = order[s]
                if s + 1 == stage:
                    if stage == 1:
                        held_now = lambda index: self.own.at[index + (everything, columns)]
                    else:
                        prior = order[s - 1]
                        if stage == 2:
                            before = self.own.at[
                                pick(order, 0, prior, self.at[prior]) + (everything, columns)
                            ]
                        else:
                            before = bufs[s - 2][1].at[pick(order, s - 1, prior, self.at[prior])]
                        arrived, total = bufs[s - 1]
                        add_up(
                            total,
                            [before] + [arrived.at[i] for i in range(SIZES[prior] - 1)],
                            remaining(order, s),
                        )
                        held_now = lambda index, total=total: total.at[index]
                    for i, (there, device) in enumerate(partners(self.me, self.at, dim)):
                        copies.append(
                            remote(
                                held_now(pick(order, s, dim, there)),
                                bufs[s][0].at[i],
                                self.sems,
                                self.slot,
                                number + i,
                                device,
                            )
                        )
                number += SIZES[dim] - 1
            if stage == 4:
                prior = order[2]
                before = bufs[1][1].at[pick(order, 2, prior, self.at[prior])]
                arrived = bufs[2][0]
                add_up(
                    self.out.at[:, columns],
                    [before] + [arrived.at[i] for i in range(SIZES[prior] - 1)],
                    (),
                )
        return copies


def sum_buffers(streams, rows, width, dtype):
    shapes = [pltpu.VMEM((4, 2, 2, rows, width), dtype)] * 2
    for order, _, columns in streams:
        for s in range(3):
            left = remaining(order, s + 1)
            shapes.append(pltpu.VMEM((SIZES[order[s]] - 1,) + left + (rows, columns), dtype))
            if s < 2:
                shapes.append(pltpu.VMEM(left + (rows, columns), dtype))
    return shapes


def view_buffers(streams, refs, slot=None):
    refs = [r if slot is None else r.at[slot] for r in refs]
    own, from_core, rest = refs[0], refs[1], refs[2:]
    bufs = [(rest[5 * i : 5 * i + 2], rest[5 * i + 2 : 5 * i + 4], rest[5 * i + 4 : 5 * i + 5]) for i in range(len(streams))]
    return own, from_core, bufs


SMALL_STREAM = (("xyz", 0, 128),)


def sum_kernel(*refs):
    grads, small, outs, small_out, refs = refs[:4], refs[4], refs[5:9], refs[9], refs[10:]
    per = 2 + 5 * len(BACK)
    slots = [refs[:per], refs[per : 2 * per]]
    small_refs, refs = refs[2 * per : 2 * per + 7], refs[2 * per + 7 :]
    send, recv, own = refs
    sems = (send, recv, own)
    me, at = coords()
    greet(me, at)
    chunks = len(CHUNKS)
    flows = {}
    for tick in range(chunks + 4):
        copies = []
        if tick == 0:
            tiny = Sum(small, small_out, SMALL_STREAM, view_buffers(SMALL_STREAM, small_refs), 4, sems, me, at)
            copies += tiny.start()
        elif tick <= 4:
            copies += tiny.step(tick)
        for stage in (4, 3, 2, 1, 0):
            k = tick - stage
            if 0 <= k < chunks:
                which, row, col = CHUNKS[k]
                if stage == 0:
                    grad = grads[which].at[:, :, :, :, pl.ds(row, ROWS), pl.ds(col, WIDE)]
                    out = outs[which].at[pl.ds(row, ROWS), pl.ds(col, WIDE)]
                    flows[k] = Sum(grad, out, BACK, view_buffers(BACK, slots[k % 2]), k % 4, sems, me, at)
                    copies += flows[k].start()
                else:
                    copies += flows[k].step(stage)
        for copy in copies:
            copy.start()
        for copy in copies:
            copy.wait()


def sum_up(grads, small):
    anywhere = pl.BlockSpec(memory_space=pl.ANY)
    inside = pl.BlockSpec(memory_space=pltpu.VMEM)
    return pl.pallas_call(
        sum_kernel,
        out_shape=[jax.ShapeDtypeStruct(a.shape[4:], F32) for a in (*grads, small)],
        in_specs=[anywhere] * 5,
        out_specs=[inside] * 5,
        scratch_shapes=sum_buffers(BACK, ROWS, WIDE, BF16) * 2
        + sum_buffers(SMALL_STREAM, 8, 128, F32)
        + [
            pltpu.SemaphoreType.DMA((5, COPIES)),
            pltpu.SemaphoreType.DMA((5, COPIES)),
            pltpu.SemaphoreType.DMA((5,)),
        ],
        compiler_params=pltpu.CompilerParams(
            collective_id=1, has_side_effects=True, vmem_limit_bytes=48 << 20
        ),
        name="sum_gradients",
    )(*grads, small)
EPS = 1e-06
MASKED = -1000000000.0
LEN_PAD = 384


def dot_nn(a, b):
    return jnp.dot(a, b, preferred_element_type=F32)


def dot_nt(a, b):
    return lax.dot_general(a, b, (((1,), (1,)), ((), ())), preferred_element_type=F32)


def dot_tn(a, b):
    return lax.dot_general(a, b, (((0,), (0,)), ((), ())), preferred_element_type=F32)


def block_of(index, size):
    return pl.ds(pl.multiple_of(index * size, size), size)


def spread_vectors(smalls, v4, v2, v1):
    for z in range(4):
        for y in range(2):
            four = None
            for x in range(2):
                two = None
                for c in range(2):
                    one = smalls[z, y, x, c]
                    d = ((z * 2 + y) * 2 + x) * 2 + c
                    v1[:, d * 128 : d * 128 + 128] = one
                    two = one if two is None else two + one
                d = (z * 2 + y) * 2 + x
                v2[:, d * 128 : d * 128 + 128] = two
                four = two if four is None else four + two
            d = z * 2 + y
            v4[:, d * 128 : d * 128 + 128] = four


def norm_rows(src, gain, shift, dst):
    @pl.loop(0, src.shape[0] // 64)
    def _(i):
        rows = block_of(i, 64)
        values = src[rows, :].astype(F32)
        centered = values - jnp.mean(values, axis=-1, keepdims=True)
        variance = jnp.mean(centered * centered, axis=-1, keepdims=True)
        normed = centered * lax.rsqrt(variance + EPS)
        dst[rows, :] = (normed * gain[...] + shift[...]).astype(BF16)


def project(normed, weight, shift, dst, col):
    @pl.loop(0, 2)
    def _(i):
        columns = block_of(i, 512)
        mixed = dot_nn(normed[...], weight[:, :, :, :, :, columns].reshape(1024, 512))
        if shift is not None:
            mixed = mixed + shift[:, columns]
        dst[pl.ds(0, 640), pl.ds(pl.multiple_of(col + i * 512, 512), 512)] = mixed.astype(BF16)


def attend(first, count, mixed, key_mask, attended, probs, probs_out, sems):
    lane = lax.broadcasted_iota(jnp.int32, (1, 128), 1)

    def out_copy(unit, slot):
        return pltpu.make_async_copy(probs.at[slot], probs_out.at[unit], sems.at[slot])

    @pl.loop(0, count // 2)
    def _(i):
        for slot in range(2):
            unit = first + i * 2 + slot
            seq, pair = lax.div(unit, 8), lax.rem(unit, 8)
            start = pl.multiple_of(seq * 320, 64)
            columns = block_of(pair, 128)
            q = mixed[pl.ds(start, 320), columns]
            k = mixed[pl.ds(start, LEN_PAD), block_of(pair + 8, 128)]
            v = mixed[pl.ds(start, LEN_PAD), block_of(pair + 16, 128)]
            kept = key_mask[seq] > 0.0

            @pl.when(i > 0)
            def _():
                out_copy(unit, slot).wait()

            found = []
            for head in range(2):
                scale = jnp.where(lax.div(lane, 64) == head, 0.125, 0.0).astype(BF16)
                scores = jnp.where(kept, dot_nt(q * scale, k), MASKED)
                exponent = jnp.exp(scores - jnp.max(scores, axis=-1, keepdims=True))
                total = jnp.sum(exponent, axis=-1, keepdims=True)
                low = (exponent * (1.0 / total)).astype(BF16)
                probs[slot, head] = low
                found.append(dot_nn(low, v))
            attended[pl.ds(start, 320), columns] = jnp.where(
                lane < 64, found[0], found[1]
            ).astype(BF16)
            out_copy(unit, slot).start()

    for slot in range(2):
        out_copy(0, slot).wait()


def branch_out(attended, weight, shift, x, hidden):
    @pl.loop(0, 2)
    def _(i):
        columns = block_of(i, 512)
        branch = dot_nn(attended[...], weight[:, :, :, :, :, columns].reshape(1024, 512))
        hidden[:, columns] = x[:, columns].astype(F32) + (branch + shift[:, columns])


def feed_up(normed, weight, shift, act, slope, col):
    @pl.loop(0, 4)
    def _(i):
        columns = block_of(i, 256)
        there = pl.ds(pl.multiple_of(col + i * 256, 256), 256)
        pre = dot_nn(normed[...], weight[:, :, :, :, :, columns].reshape(1024, 256))
        pre = pre + shift[:, there]
        below = 0.5 + 0.5 * lax.erf(pre * 0.7071067811865476)
        act[:, there] = (pre * below).astype(BF16)
        density = jnp.exp(pre * pre * -0.5) * 0.3989422804014327
        slope[:, columns] = (below + pre * density).astype(BF16)


def outer(left, right, dst, blocks=4, col=0):
    @pl.loop(0, blocks)
    def _(i):
        columns = pl.ds(pl.multiple_of(col + i * 256, 256), 256)
        dst[block_of(i, 256), :] = dot_tn(left[:, columns], right[...]).astype(BF16)


def feed_down(act, weight, shift, hidden, row_mask, result, j):
    columns = pl.ds(j * 256, 256)
    branch = dot_nn(act[...], weight[:, :, :, :, :, columns].reshape(4096, 256))
    whole = hidden[:, columns] + (branch + shift[:, columns])
    result[:, columns] = (whole * row_mask[...]).astype(BF16)


def forward_kernel(*refs):
    x, cot, key_mask, row_mask = refs[:4]
    shards, small = refs[4:8], refs[8]
    (wa_o, wd_o, v4_o, normed1_o, mixed_o, attended_o, hidden_o, normed2_o, slope_o, probs_o, low_o, down_o, result_o) = refs[9:22]
    (wa, wd, smalls, v4, v2, v1, normed1, mixed, attended, hidden, normed2, act, slope, low, probs, staged, result) = refs[22:39]
    send, recv, own, out_sems, probs_sems, stage_sems = refs[39:]
    sems = (send, recv)
    me, at = coords()
    mine = (at["z"], at["y"], at["x"], at["c"])
    everything = slice(None)

    def place(k, index):
        which, row, col = CHUNKS[k]
        if k < 8:
            base = wa.at[k]
            shard = shards[which].at[:, pl.ds(col, WIDE)]
            parts = [(o, everything, pl.ds(c, w)) for o, c, w in STREAMS]
        else:
            base = wd.at[:, :, :, :, :, pl.ds((k - 8) * 256, 256)]
            shard = shards[3].at[:, pl.ds((k - 8) * 256, 256)]
            parts = [(o, pl.ds(c // 8, w // 8), everything) for o, c, w in STREAMS]
        return base, shard, parts

    def stage_copies(k, stage):
        base, shard, parts = place(k, stage)
        slot, number, copies = k % 4, 0, []
        if stage == 3:
            block = base.at[:, :, :, at["c"]]
            return [remote(block, block, sems, slot, COPIES - 1, sibling(me, at))]
        for order, rows, columns in parts:
            for s in range(3):
                for _, device in partners(me, at, order[s]):
                    if s == stage:
                        block = base.at[held(order, stage, at) + (at["c"], rows, columns)]
                        src = shard.at[rows, columns] if stage == 0 else block
                        copies.append(remote(src, block, sems, slot, number, device))
                    number += 1
        return copies

    local = [pltpu.make_async_copy(small, smalls.at[mine], own.at[12])]
    for k in range(12):
        base, shard, _ = place(k, 0)
        local.append(pltpu.make_async_copy(shard, base.at[mine], own.at[k]))
    for copy in local:
        copy.start()
    greet(me, at)

    going = []

    def put_out(src, dst, number):
        copy = pltpu.make_async_copy(src, dst, out_sems.at[number])
        copy.start()
        going.append(copy)

    def row(vectors, i):
        return vectors.at[pl.ds(i, 1), :]

    def task_low():
        low[...] = (cot[...].astype(F32) * row_mask[...]).astype(BF16)
        put_out(low, low_o, 0)
        mixed[pl.ds(640, 64), :] = jnp.zeros((64, 3072), BF16)

    def task_first():
        spread_vectors(smalls, v4, v2, v1)
        put_out(v4, v4_o, 1)
        norm_rows(x, row(v4, 0), row(v4, 1), normed1)
        put_out(normed1, normed1_o, 2)

    def task_project(j):
        shift = None if j == 1 else v2.at[pl.ds(6, 1), pl.ds(0 if j == 0 else 1024, 1024)]
        project(normed1, wa.at[j], shift, mixed, j * 1024)
        if j == 2:
            put_out(mixed, mixed_o, 3)

    def task_attend(first, count):
        attend(first, count, mixed, key_mask, attended, probs, probs_o, probs_sems)
        if first + count == 16:
            put_out(attended, attended_o, 4)

    def task_hidden():
        branch_out(attended, wa.at[3], row(v4, 2), x, hidden)
        put_out(hidden, hidden_o, 5)
        norm_rows(hidden, row(v4, 3), row(v4, 4), normed2)
        put_out(normed2, normed2_o, 6)

    slope_going, stage_going = {}, {}

    def task_up(j):
        if j >= 2:
            slope_going[j - 2].wait()
        feed_up(normed2, wa.at[4 + j], row(v1, 7), act, slope.at[j % 2], j * 1024)
        slope_going[j] = pltpu.make_async_copy(slope.at[j % 2], slope_o.at[j], stage_sems.at[j % 2])
        slope_going[j].start()

    def task_outer(j):
        if j >= 2:
            stage_going[j - 2].wait()
        outer(act, low, staged.at[j % 2], 4, j * 1024)
        stage_going[j] = pltpu.make_async_copy(
            staged.at[j % 2], down_o.at[pl.ds(j * 1024, 1024), :], stage_sems.at[2 + j % 2]
        )
        stage_going[j].start()

    def task_down(j):
        feed_down(act, wd, row(v4, 5), hidden, row_mask, result, j)

    tasks = {
        3: [(task_low,)],
        4: [(task_first,), (task_project, 0)],
        5: [(task_project, 1)],
        6: [(task_project, 2), (task_attend, 0, 8)],
        7: [(task_attend, 8, 8)],
        8: [(task_hidden,), (task_up, 0)],
        9: [(task_up, 1), (task_outer, 0)],
        10: [(task_up, 2), (task_outer, 1)],
        11: [(task_up, 3), (task_outer, 2)],
        12: [(task_outer, 3), (task_down, 0)],
        13: [(task_down, 1)],
        14: [(task_down, 2)],
    }
    for tick in range(15):
        copies = []
        if tick < 4:
            copies += small_stage(tick, small, smalls, me, at, sems)
        for stage in (3, 2, 1, 0):
            if 0 <= tick - stage < 12:
                copies += stage_copies(tick - stage, stage)
        for copy in copies:
            copy.start()
        if tick == 0:
            for copy in local:
                copy.wait()
        for task, *args in tasks.get(tick, ()):
            task(*args)
        for copy in copies:
            copy.wait()
        k = tick - 3
        if 0 <= k < 8:
            put_out(wa.at[k], wa_o.at[k], 8 + k)
        elif k == 11:
            put_out(wd, wd_o, 16)
    task_down(3)
    put_out(result, result_o, 7)
    for j in (2, 3):
        slope_going[j].wait()
        stage_going[j].wait()
    for copy in going:
        copy.wait()


def forward(x, cot, key_mask, row_mask, shards, small):
    anywhere = pl.BlockSpec(memory_space=pl.ANY)
    inside = pl.BlockSpec(memory_space=pltpu.VMEM)
    box = (4, 2, 2, 2)
    flat = (640, 1024)
    kept = [
        ((8,) + box + (32, 1024), BF16),
        (box + (128, 1024), BF16),
        ((8, 1024), F32),
        (flat, BF16),
        ((704, 3072), BF16),
        (flat, BF16),
        (flat, F32),
        (flat, BF16),
        ((4, 640, 1024), BF16),
        ((16, 2, 320, LEN_PAD), BF16),
        (flat, BF16),
        ((4096, 1024), BF16),
        (flat, BF16),
    ]
    scratch = [
        kept[0],
        kept[1],
        (box + (8, 128), F32),
        ((8, 1024), F32),
        ((8, 2048), F32),
        ((8, 4096), F32),
        (flat, BF16),
        ((704, 3072), BF16),
        (flat, BF16),
        (flat, F32),
        (flat, BF16),
        ((640, 4096), BF16),
        ((2, 640, 1024), BF16),
        (flat, BF16),
        ((2, 2, 320, LEN_PAD), BF16),
        ((2, 1024, 1024), BF16),
        (flat, BF16),
    ]
    dma = pltpu.SemaphoreType.DMA
    return pl.pallas_call(
        forward_kernel,
        out_shape=[jax.ShapeDtypeStruct(s, d) for s, d in kept],
        in_specs=[inside] * 4 + [anywhere] * 5,
        out_specs=[anywhere] * 13,
        scratch_shapes=[pltpu.VMEM(s, d) for s, d in scratch]
        + [dma((5, COPIES)), dma((5, COPIES)), dma((13,)), dma((17,)), dma((2,)), dma((4,))],
        compiler_params=pltpu.CompilerParams(
            collective_id=0, has_side_effects=True, vmem_limit_bytes=63 << 20
        ),
        name="gather_forward",
    )(x, cot, key_mask, row_mask, *shards, small)


NARROW = (0, 1, 5, 6, 7, 11)
WEIGHTS = (2, 4, 8, 10)


def pack_weights(weights):
    me = lax.axis_index("dp")
    lane = jnp.arange(128, dtype=jnp.int32)[None, :]
    narrow = jnp.tile(jnp.stack([weights[i] for i in NARROW]), (1, 4))
    rows = [
        jnp.where(lane // 32 == me % 4, narrow, 0),
        jnp.where(lane // 64 == me % 2, jnp.tile(weights[3][None], (1, 2)), 0),
        weights[9][None],
    ]
    return jnp.concatenate(rows, axis=0).astype(F32)


def scatter_all(grads):
    me = lax.axis_index("dp")
    rows = [jnp.repeat(grads[i].reshape(8, 128), 4, axis=0) for i in NARROW]
    rows += [jnp.repeat(grads[3].reshape(16, 128), 2, axis=0), grads[9].reshape(32, 128)]
    small = jnp.stack(rows, axis=1).reshape(4, 2, 2, 2, 8, 128)
    wide = []
    for i in WEIGHTS:
        g = grads[i].astype(BF16)
        wide.append(g.reshape(4, 2, 2, 2, g.shape[0] // 32, g.shape[1]))
    *sums, total = sum_up(wide, small)
    found = [None] * 12
    for row, i in enumerate(NARROW):
        found[i] = lax.dynamic_slice(total[row], (me % 4 * 32,), (32,))
    found[3] = lax.dynamic_slice(total[6], (me % 2 * 64,), (64,))
    found[9] = total[7]
    for i, s in zip(WEIGHTS, sums):
        found[i] = s
    return found


def on_box(inputs, lengths, assignment, *rest):
    weights, cotangent = rest[:12], rest[12]
    matches = assignment[:, None] == jnp.arange(lengths.shape[0], dtype=jnp.int32)[None, :]
    kept_len = jnp.sum(jnp.where(matches, lengths[None, :], 0), axis=1)
    key_mask = (jnp.arange(LEN_PAD, dtype=jnp.int32)[None, :] < kept_len[:, None]).astype(F32)
    row_mask = key_mask[:, :320].reshape(640, 1)
    x = inputs.reshape(640, 1024)
    cot = cotangent.reshape(640, 1024)
    small = pack_weights(weights)
    (wa, wd, v4, normed_low, mixed_qkv, attended, hidden, second_low, slope, probs, grad_low, down_grad, result) = forward(
        x, cot, key_mask[:, None, :], row_mask, [weights[i] for i in WEIGHTS], small
    )
    wa = wa.reshape(8, 1024, 1024)
    wd = wd.reshape(4096, 1024)
    qkv_w = jnp.concatenate([wa[0], wa[1], wa[2]], axis=1)
    up_w = jnp.concatenate([wa[4], wa[5], wa[6], wa[7]], axis=1)
    slope = jnp.concatenate([slope[i] for i in range(4)], axis=1)
    ln = lambda v, g, b: layer_norm(v, g, b)
    _, first_back = jax.vjp(ln, x.astype(F32), v4[0], v4[1])
    _, second_back = jax.vjp(ln, hidden, v4[3], v4[4])
    grad_rows = grad_low.astype(F32)
    down_bias_grad = jnp.sum(grad_rows, axis=0)
    grad_pre = (contract_cols(grad_low, wd) * slope.astype(F32)).astype(BF16)
    up_grad = contract_rows(second_low, grad_pre)
    up_bias_grad = jnp.sum(grad_pre.astype(F32), axis=0)
    grad_second, gain2_grad, shift2_grad = second_back(contract_cols(grad_pre, up_w))
    grad_hidden = grad_rows + grad_second
    branch_low = grad_hidden.astype(BF16)
    proj_grad = contract_rows(attended, branch_low)
    proj_bias_grad = jnp.sum(branch_low.astype(F32), axis=0)
    grad_att = contract_cols(branch_low, wa[3]).astype(BF16).reshape(2, 320, 16, 64)
    probs = probs.reshape(2, 16, 320, LEN_PAD)[..., :320]
    split = lambda i: mixed_qkv[:640, i * 1024 : i * 1024 + 1024].reshape(2, 320, 16, 64)
    queries, keys_all, values_all = split(0), split(1), split(2)
    grad_probs = jnp.einsum("bqhd,bkhd->bhqk", grad_att, values_all, preferred_element_type=F32)
    grad_values = jnp.einsum("bhqk,bqhd->bkhd", probs, grad_att, preferred_element_type=F32)
    probs = probs.astype(F32)
    inner_sum = jnp.sum(probs * grad_probs, axis=-1, keepdims=True)
    grad_scores = (probs * (grad_probs - inner_sum)).astype(BF16)
    grad_queries = jnp.einsum("bhqk,bkhd->bqhd", grad_scores, keys_all, preferred_element_type=F32) * 0.125
    grad_keys = jnp.einsum("bhqk,bqhd->bkhd", grad_scores, queries, preferred_element_type=F32) * 0.125
    grad_mixed = jnp.concatenate(
        [grad_queries.reshape(640, 1024), grad_keys.reshape(640, 1024), grad_values.reshape(640, 1024)], axis=1
    ).astype(BF16)
    qkv_grad = contract_rows(normed_low, grad_mixed)
    column_sums = jnp.sum(grad_mixed.astype(F32), axis=0)
    qv_grad = jnp.concatenate([column_sums[:1024], column_sums[2048:]])
    grad_first, gain1_grad, shift1_grad = first_back(contract_cols(grad_mixed, qkv_w))
    input_grad = (grad_hidden + grad_first).reshape(inputs.shape).astype(BF16)
    sums = scatter_all(
        (gain1_grad, shift1_grad, qkv_grad, qv_grad, proj_grad, proj_bias_grad)
        + (gain2_grad, shift2_grad, up_grad, up_bias_grad, down_grad, down_bias_grad)
    )
    return (result.reshape(inputs.shape), input_grad, *sums)


def plain(
    inputs,
    lengths,
    assignment,
    norm1_gain,
    norm1_bias,
    qkv_weight,
    qv_bias,
    out_weight,
    out_bias,
    norm2_gain,
    norm2_bias,
    up_weight,
    up_bias,
    down_weight,
    down_bias,
    cotangent,
):
    gathered = (
        lax.all_gather(norm1_gain, "dp", axis=0, tiled=True),
        lax.all_gather(norm1_bias, "dp", axis=0, tiled=True),
        lax.all_gather(qkv_weight, "dp", axis=0, tiled=True),
        lax.all_gather(qv_bias, "dp", axis=0, tiled=True),
        lax.all_gather(out_weight, "dp", axis=0, tiled=True),
        lax.all_gather(out_bias, "dp", axis=0, tiled=True),
        lax.all_gather(norm2_gain, "dp", axis=0, tiled=True),
        lax.all_gather(norm2_bias, "dp", axis=0, tiled=True),
        lax.all_gather(up_weight, "dp", axis=0, tiled=True),
        lax.all_gather(up_bias, "dp", axis=0, tiled=True),
        lax.all_gather(down_weight, "dp", axis=0, tiled=True),
        lax.all_gather(down_bias, "dp", axis=0, tiled=True),
    )
    seq_count, tok_count, model_width = inputs.shape
    rows_all = seq_count * tok_count
    split_shape = (seq_count, tok_count, HEADS, HEAD)
    head_scale = HEAD ** (-0.5)
    matches = assignment[:, None] == jnp.arange(lengths.shape[0], dtype=jnp.int32)[None, :]
    kept_len = jnp.sum(jnp.where(matches, lengths[None, :], 0), axis=1)
    key_mask = jnp.arange(tok_count, dtype=jnp.int32)[None, :] < kept_len[:, None]
    row_mask = key_mask.reshape(rows_all, 1).astype(jnp.float32)
    gain_first = gathered[0].astype(jnp.float32)
    shift_first = gathered[1].astype(jnp.float32)
    qv_full = gathered[3].astype(jnp.float32)
    proj_shift = gathered[5].astype(jnp.float32)
    gain_second = gathered[6].astype(jnp.float32)
    shift_second = gathered[7].astype(jnp.float32)
    up_shift = gathered[9].astype(jnp.float32)
    down_shift = gathered[11].astype(jnp.float32)
    inputs_flat = inputs.reshape(rows_all, model_width).astype(jnp.float32)
    normed_first, first_back = jax.vjp(layer_norm, inputs_flat, gain_first, shift_first)
    normed_low = normed_first.astype(jnp.bfloat16)
    full_bias = jnp.concatenate(
        [qv_full[:model_width], jnp.zeros((model_width,), jnp.float32), qv_full[model_width:]]
    )
    mixed_qkv = (
        jnp.dot(normed_low, gathered[2], preferred_element_type=jnp.float32) + full_bias
    ).astype(jnp.bfloat16)
    queries = mixed_qkv[:, :model_width].reshape(split_shape)
    keys_all = mixed_qkv[:, model_width : 2 * model_width].reshape(split_shape)
    values_all = mixed_qkv[:, 2 * model_width :].reshape(split_shape)
    scores = (
        jnp.einsum("bqhd,bkhd->bhqk", queries, keys_all, preferred_element_type=jnp.float32)
        * head_scale
    )
    scores = jnp.where(key_mask[:, None, None, :], scores, masked_score)
    row_max = jnp.max(scores, axis=-1, keepdims=True)
    exponent = jnp.exp(scores - row_max)
    row_total = jnp.sum(exponent, axis=-1, keepdims=True)
    softmax_probs = exponent / row_total
    log_total = row_max + jnp.log(row_total)
    attended = jnp.einsum(
        "bhqk,bkhd->bqhd",
        softmax_probs.astype(jnp.bfloat16),
        values_all,
        preferred_element_type=jnp.float32,
    )
    attended = attended.reshape(rows_all, model_width).astype(jnp.bfloat16)
    hidden = inputs_flat + (
        jnp.dot(attended, gathered[4], preferred_element_type=jnp.float32) + proj_shift
    )
    normed_second, second_back = jax.vjp(layer_norm, hidden, gain_second, shift_second)
    second_low = normed_second.astype(jnp.bfloat16)
    pre_act = jnp.dot(second_low, gathered[8], preferred_element_type=jnp.float32) + up_shift
    activation, gelu_back = jax.vjp(gelu_exact, pre_act)
    act_low = activation.astype(jnp.bfloat16)
    output_rows = row_mask * (
        hidden + (jnp.dot(act_low, gathered[10], preferred_element_type=jnp.float32) + down_shift)
    )
    result = output_rows.reshape(inputs.shape).astype(jnp.bfloat16)
    grad_rows = cotangent.reshape(rows_all, model_width).astype(jnp.float32) * row_mask
    grad_low = grad_rows.astype(jnp.bfloat16)
    down_grad = contract_rows(act_low, grad_low)
    down_bias_grad = jnp.sum(grad_low.astype(jnp.float32), axis=0)
    grad_pre = gelu_back(contract_cols(grad_low, gathered[10]))[0].astype(jnp.bfloat16)
    up_grad = contract_rows(second_low, grad_pre)
    up_bias_grad = jnp.sum(grad_pre.astype(jnp.float32), axis=0)
    grad_second, gain2_grad, shift2_grad = second_back(contract_cols(grad_pre, gathered[8]))
    grad_hidden = grad_rows + grad_second
    branch_low = grad_hidden.astype(jnp.bfloat16)
    proj_grad = contract_rows(attended, branch_low)
    proj_bias_grad = jnp.sum(branch_low.astype(jnp.float32), axis=0)
    grad_att = contract_cols(branch_low, gathered[4]).astype(jnp.bfloat16).reshape(split_shape)
    scores_again = (
        jnp.einsum("bqhd,bkhd->bhqk", queries, keys_all, preferred_element_type=jnp.float32)
        * head_scale
    )
    scores_again = jnp.where(key_mask[:, None, None, :], scores_again, masked_score)
    probs_again = jnp.exp(scores_again - log_total)
    probs_low = probs_again.astype(jnp.bfloat16)
    grad_probs = jnp.einsum(
        "bqhd,bkhd->bhqk", grad_att, values_all, preferred_element_type=jnp.float32
    )
    grad_values = jnp.einsum(
        "bhqk,bqhd->bkhd", probs_low, grad_att, preferred_element_type=jnp.float32
    )
    inner_sum = jnp.sum(probs_again * grad_probs, axis=-1, keepdims=True)
    grad_scores = (probs_again * (grad_probs - inner_sum)).astype(jnp.bfloat16)
    grad_queries = (
        jnp.einsum("bhqk,bkhd->bqhd", grad_scores, keys_all, preferred_element_type=jnp.float32)
        * head_scale
    )
    grad_keys = (
        jnp.einsum("bhqk,bqhd->bkhd", grad_scores, queries, preferred_element_type=jnp.float32)
        * head_scale
    )
    grad_mixed = jnp.concatenate(
        [
            grad_queries.reshape(rows_all, model_width),
            grad_keys.reshape(rows_all, model_width),
            grad_values.reshape(rows_all, model_width),
        ],
        axis=1,
    ).astype(jnp.bfloat16)
    qkv_grad = contract_rows(normed_low, grad_mixed)
    column_sums = jnp.sum(grad_mixed.astype(jnp.float32), axis=0)
    qv_grad = jnp.concatenate([column_sums[:model_width], column_sums[2 * model_width :]])
    grad_first, gain1_grad, shift1_grad = first_back(contract_cols(grad_mixed, gathered[2]))
    input_grad = (grad_hidden + grad_first).reshape(inputs.shape).astype(jnp.bfloat16)
    all_sums = (
        lax.psum_scatter(gain1_grad, "dp", scatter_dimension=0, tiled=True),
        lax.psum_scatter(shift1_grad, "dp", scatter_dimension=0, tiled=True),
        lax.psum_scatter(qkv_grad, "dp", scatter_dimension=0, tiled=True),
        lax.psum_scatter(qv_grad, "dp", scatter_dimension=0, tiled=True),
        lax.psum_scatter(proj_grad, "dp", scatter_dimension=0, tiled=True),
        lax.psum_scatter(proj_bias_grad, "dp", scatter_dimension=0, tiled=True),
        lax.psum_scatter(gain2_grad, "dp", scatter_dimension=0, tiled=True),
        lax.psum_scatter(shift2_grad, "dp", scatter_dimension=0, tiled=True),
        lax.psum_scatter(up_grad, "dp", scatter_dimension=0, tiled=True),
        lax.psum_scatter(up_bias_grad, "dp", scatter_dimension=0, tiled=True),
        lax.psum_scatter(down_grad, "dp", scatter_dimension=0, tiled=True),
        lax.psum_scatter(down_bias_grad, "dp", scatter_dimension=0, tiled=True),
    )
    attn_sums = all_sums[:6]
    mlp_sums = all_sums[6:]
    return (
        result,
        input_grad,
        attn_sums[0],
        attn_sums[1],
        attn_sums[2],
        attn_sums[3],
        attn_sums[4],
        attn_sums[5],
        mlp_sums[0],
        mlp_sums[1],
        mlp_sums[2],
        mlp_sums[3],
        mlp_sums[4],
        mlp_sums[5],
    )


def local(*args):
    return on_box(*args) if lax.axis_size("dp") == 32 else plain(*args)


def solution(mesh):
    placed = (
        P("dp", None, None),
        P(),
        P("dp"),
        P("dp"),
        P("dp"),
        P("dp", None),
        P("dp"),
        P("dp", None),
        P("dp"),
        P("dp"),
        P("dp"),
        P("dp", None),
        P("dp"),
        P("dp", None),
        P("dp"),
        P("dp", None, None),
    )
    return jax.shard_map(
        local,
        mesh=mesh,
        in_specs=placed,
        out_specs=(
            P("dp", None, None),
            P("dp", None, None),
            P("dp"),
            P("dp"),
            P("dp", None),
            P("dp"),
            P("dp", None),
            P("dp"),
            P("dp"),
            P("dp"),
            P("dp", None),
            P("dp"),
            P("dp", None),
            P("dp"),
        ),
        check_vma=False,
    )
```

```python
import jax
import jax.numpy as jnp
from jax import lax
from jax.experimental import pallas as pl
from jax.experimental.pallas import tpu as pltpu
from jax.sharding import PartitionSpec as P

HEADS = 16
HEAD = 64


eps = 1e-06
masked_score = -1000000000.0


def layer_norm(values, norm_gain, norm_shift):
    average = jnp.mean(values, axis=-1, keepdims=True)
    centered = values - average
    variance = jnp.mean(centered * centered, axis=-1, keepdims=True)
    return centered * lax.rsqrt(variance + eps) * norm_gain + norm_shift


def gelu_exact(values):
    return jax.nn.gelu(values, approximate=False)


def contract_rows(left, right):
    return lax.dot_general(
        left, right, (((0,), (0,)), ((), ())), preferred_element_type=jnp.float32
    )


def contract_cols(left, right):
    return lax.dot_general(
        left, right, (((1,), (1,)), ((), ())), preferred_element_type=jnp.float32
    )


BF16 = jnp.bfloat16
F32 = jnp.float32
MESH = pl.DeviceIdType.MESH
SIZES = {"z": 4, "y": 2, "x": 2}
STRIDE = {"z": 8, "y": 4, "x": 2}
ROWS = 32
WIDE = 1024
STREAMS = (("zyx", 0, 384), ("zxy", 384, 384), ("xzy", 768, 128), ("yzx", 896, 128))
CHUNKS = (
    tuple((0, 0, c) for c in (0, 1024, 2048))
    + ((1, 0, 0),)
    + tuple((2, 0, c) for c in (0, 1024, 2048, 3072))
    + tuple((3, r, 0) for r in (0, 32, 64, 96))
)


def coords():
    me = lax.axis_index("dp")
    at = {
        "z": lax.div(me, 8),
        "y": lax.rem(lax.div(me, 4), 2),
        "x": lax.rem(lax.div(me, 2), 2),
        "c": lax.rem(me, 2),
    }
    return me, at


def partners(me, at, dim):
    size = SIZES[dim]
    found = []
    for k in range(1, size):
        there = lax.rem(at[dim] + k, size)
        found.append((there, me + (there - at[dim]) * STRIDE[dim]))
    return found


def sibling(me, at):
    return me + 1 - 2 * at["c"]


def greet(me, at):
    barrier = pltpu.get_barrier_semaphore()
    devices = [sibling(me, at)]
    for dim in "zyx":
        devices += [device for _, device in partners(me, at, dim)]
    for device in devices:
        pl.semaphore_signal(barrier, inc=1, device_id=(device,), device_id_type=MESH)
    pl.semaphore_wait(barrier, len(devices))


def remote(src, dst, sems, slot, number, device):
    return pltpu.make_async_remote_copy(
        src_ref=src,
        dst_ref=dst,
        send_sem=sems[0].at[slot, number],
        recv_sem=sems[1].at[slot, number],
        device_id=(device,),
        device_id_type=MESH,
    )


def held(order, stage, at):
    return tuple(
        slice(None) if dim in order[:stage] else at[dim] for dim in "zyx"
    )


COPIES = 5 * len(STREAMS) + 1


def small_stage(stage, small, smalls, me, at, sems):
    number = {0: 0, 1: 3, 2: 4, 3: 5}[stage]
    if stage == 3:
        block = smalls.at[:, :, :, at["c"]]
        return [remote(block, block, sems, 4, number, sibling(me, at))]
    copies = []
    for _, device in partners(me, at, "zyx"[stage]):
        block = smalls.at[held("zyx", stage, at) + (at["c"],)]
        copies.append(remote(small if stage == 0 else block, block, sems, 4, number, device))
        number += 1
    return copies


def remaining(order, stage):
    return tuple(SIZES[dim] for dim in "zyx" if dim not in order[:stage])


def pick(order, stage, dim, index):
    return tuple(
        index if d == dim else slice(None) for d in "zyx" if d not in order[:stage]
    )


BACK = tuple((order[::-1], first, width) for order, first, width in STREAMS)


def add_up(dst, terms, lead):
    count = 1
    for n in lead:
        count *= n

    def at_index(i):
        index = []
        for n in lead[::-1]:
            index.append(lax.rem(i, n))
            i = lax.div(i, n)
        return tuple(index[::-1])

    def body(i, carry):
        index = at_index(i)
        total = terms[0][index + (slice(None),) * 2].astype(F32)
        for term in terms[1:]:
            total = total + term[index + (slice(None),) * 2].astype(F32)
        dst[index + (slice(None),) * 2] = total.astype(dst.dtype)
        return carry

    if count == 1:
        body(0, 0) if lead else None
        if not lead:
            total = terms[0][...].astype(F32)
            for term in terms[1:]:
                total = total + term[...].astype(F32)
            dst[...] = total.astype(dst.dtype)
    else:
        lax.fori_loop(0, count, body, 0)


SMALL_STREAM = (("xyz", 0, 128),)


EPS = 1e-06
MASKED = -1000000000.0
LEN_PAD = 384


def dot_nn(a, b):
    return jnp.dot(a, b, preferred_element_type=F32)


def dot_nt(a, b):
    return lax.dot_general(a, b, (((1,), (1,)), ((), ())), preferred_element_type=F32)


def dot_tn(a, b):
    return lax.dot_general(a, b, (((0,), (0,)), ((), ())), preferred_element_type=F32)


def block_of(index, size):
    return pl.ds(pl.multiple_of(index * size, size), size)


def spread_vectors(smalls, v4, v2, v1):
    for z in range(4):
        for y in range(2):
            four = None
            for x in range(2):
                two = None
                for c in range(2):
                    one = smalls[z, y, x, c]
                    d = ((z * 2 + y) * 2 + x) * 2 + c
                    v1[:, d * 128 : d * 128 + 128] = one
                    two = one if two is None else two + one
                d = (z * 2 + y) * 2 + x
                v2[:, d * 128 : d * 128 + 128] = two
                four = two if four is None else four + two
            d = z * 2 + y
            v4[:, d * 128 : d * 128 + 128] = four


def norm_rows(src, gain, shift, dst):
    @pl.loop(0, src.shape[0] // 64)
    def _(i):
        rows = block_of(i, 64)
        values = src[rows, :].astype(F32)
        centered = values - jnp.mean(values, axis=-1, keepdims=True)
        variance = jnp.mean(centered * centered, axis=-1, keepdims=True)
        normed = centered * lax.rsqrt(variance + EPS)
        dst[rows, :] = (normed * gain[...] + shift[...]).astype(BF16)


def project(normed, weight, shift, dst, col):
    @pl.loop(0, 2)
    def _(i):
        columns = block_of(i, 512)
        mixed = dot_nn(normed[...], weight[:, :, :, :, :, columns].reshape(1024, 512))
        if shift is not None:
            mixed = mixed + shift[:, columns]
        dst[pl.ds(0, 640), pl.ds(pl.multiple_of(col + i * 512, 512), 512)] = mixed.astype(BF16)


def attend(first, count, mixed, key_mask, attended, probs, probs_out, sems):
    lane = lax.broadcasted_iota(jnp.int32, (1, 128), 1)

    def out_copy(unit, slot):
        return pltpu.make_async_copy(probs.at[slot], probs_out.at[unit], sems.at[slot])

    @pl.loop(0, count // 2)
    def _(i):
        for slot in range(2):
            unit = first + i * 2 + slot
            seq, pair = lax.div(unit, 8), lax.rem(unit, 8)
            start = pl.multiple_of(seq * 320, 64)
            columns = block_of(pair, 128)
            q = mixed[pl.ds(start, 320), columns]
            k = mixed[pl.ds(start, LEN_PAD), block_of(pair + 8, 128)]
            v = mixed[pl.ds(start, LEN_PAD), block_of(pair + 16, 128)]
            kept = key_mask[seq] > 0.0

            @pl.when(i > 0)
            def _():
                out_copy(unit, slot).wait()

            found = []
            for head in range(2):
                scale = jnp.where(lax.div(lane, 64) == head, 0.125, 0.0).astype(BF16)
                scores = jnp.where(kept, dot_nt(q * scale, k), MASKED)
                exponent = jnp.exp(scores - jnp.max(scores, axis=-1, keepdims=True))
                total = jnp.sum(exponent, axis=-1, keepdims=True)
                low = (exponent * (1.0 / total)).astype(BF16)
                probs[slot, head] = low
                found.append(dot_nn(low, v))
            attended[pl.ds(start, 320), columns] = jnp.where(
                lane < 64, found[0], found[1]
            ).astype(BF16)
            out_copy(unit, slot).start()

    for slot in range(2):
        out_copy(0, slot).wait()


def branch_out(attended, weight, shift, x, hidden):
    @pl.loop(0, 2)
    def _(i):
        columns = block_of(i, 512)
        branch = dot_nn(attended[...], weight[:, :, :, :, :, columns].reshape(1024, 512))
        hidden[:, columns] = x[:, columns].astype(F32) + (branch + shift[:, columns])


def feed_up(normed, weight, shift, act, slope, col):
    @pl.loop(0, 4)
    def _(i):
        columns = block_of(i, 256)
        there = pl.ds(pl.multiple_of(col + i * 256, 256), 256)
        pre = dot_nn(normed[...], weight[:, :, :, :, :, columns].reshape(1024, 256))
        pre = pre + shift[:, there]
        below = 0.5 + 0.5 * lax.erf(pre * 0.7071067811865476)
        act[:, there] = (pre * below).astype(BF16)
        density = jnp.exp(pre * pre * -0.5) * 0.3989422804014327
        slope[:, columns] = (below + pre * density).astype(BF16)


def outer(left, right, dst, blocks=4, col=0):
    @pl.loop(0, blocks)
    def _(i):
        columns = pl.ds(pl.multiple_of(col + i * 256, 256), 256)
        dst[block_of(i, 256), :] = dot_tn(left[:, columns], right[...]).astype(BF16)


def feed_down(act, weight, shift, hidden, row_mask, result, j):
    columns = pl.ds(j * 256, 256)
    branch = dot_nn(act[...], weight[:, :, :, :, :, columns].reshape(4096, 256))
    whole = hidden[:, columns] + (branch + shift[:, columns])
    result[:, columns] = (whole * row_mask[...]).astype(BF16)


def forward_kernel(*refs):
    x, cot, key_mask, row_mask = refs[:4]
    shards, small = refs[4:8], refs[8]
    (wa_o, wd_o, v4_o, normed1_o, mixed_o, attended_o, hidden_o, normed2_o, slope_o, probs_o, low_o, down_o, result_o) = refs[9:22]
    (wa, wd, smalls, v4, v2, v1, normed1, mixed, attended, hidden, normed2, act, slope, low, probs, staged, result) = refs[22:39]
    send, recv, own, out_sems, probs_sems, stage_sems = refs[39:]
    sems = (send, recv)
    me, at = coords()
    mine = (at["z"], at["y"], at["x"], at["c"])
    everything = slice(None)

    def place(k, index):
        which, row, col = CHUNKS[k]
        if k < 8:
            base = wa.at[k]
            shard = shards[which].at[:, pl.ds(col, WIDE)]
            parts = [(o, everything, pl.ds(c, w)) for o, c, w in STREAMS]
        else:
            base = wd.at[:, :, :, :, :, pl.ds((k - 8) * 256, 256)]
            shard = shards[3].at[:, pl.ds((k - 8) * 256, 256)]
            parts = [(o, pl.ds(c // 8, w // 8), everything) for o, c, w in STREAMS]
        return base, shard, parts

    def stage_copies(k, stage):
        base, shard, parts = place(k, stage)
        slot, number, copies = k % 4, 0, []
        if stage == 3:
            block = base.at[:, :, :, at["c"]]
            return [remote(block, block, sems, slot, COPIES - 1, sibling(me, at))]
        for order, rows, columns in parts:
            for s in range(3):
                for _, device in partners(me, at, order[s]):
                    if s == stage:
                        block = base.at[held(order, stage, at) + (at["c"], rows, columns)]
                        src = shard.at[rows, columns] if stage == 0 else block
                        copies.append(remote(src, block, sems, slot, number, device))
                    number += 1
        return copies

    local = [pltpu.make_async_copy(small, smalls.at[mine], own.at[12])]
    for k in range(12):
        base, shard, _ = place(k, 0)
        local.append(pltpu.make_async_copy(shard, base.at[mine], own.at[k]))
    for copy in local:
        copy.start()
    greet(me, at)

    going = []

    def put_out(src, dst, number):
        copy = pltpu.make_async_copy(src, dst, out_sems.at[number])
        copy.start()
        going.append(copy)

    def row(vectors, i):
        return vectors.at[pl.ds(i, 1), :]

    def task_low():
        low[...] = (cot[...].astype(F32) * row_mask[...]).astype(BF16)
        put_out(low, low_o, 0)
        mixed[pl.ds(640, 64), :] = jnp.zeros((64, 3072), BF16)

    def task_first():
        spread_vectors(smalls, v4, v2, v1)
        put_out(v4, v4_o, 1)
        norm_rows(x, row(v4, 0), row(v4, 1), normed1)
        put_out(normed1, normed1_o, 2)

    def task_project(j):
        shift = None if j == 1 else v2.at[pl.ds(6, 1), pl.ds(0 if j == 0 else 1024, 1024)]
        project(normed1, wa.at[j], shift, mixed, j * 1024)
        if j == 2:
            put_out(mixed, mixed_o, 3)

    def task_attend(first, count):
        attend(first, count, mixed, key_mask, attended, probs, probs_o, probs_sems)
        if first + count == 16:
            put_out(attended, attended_o, 4)

    def task_hidden():
        branch_out(attended, wa.at[3], row(v4, 2), x, hidden)
        put_out(hidden, hidden_o, 5)
        norm_rows(hidden, row(v4, 3), row(v4, 4), normed2)
        put_out(normed2, normed2_o, 6)

    slope_going, stage_going = {}, {}

    def task_up(j):
        if j >= 2:
            slope_going[j - 2].wait()
        feed_up(normed2, wa.at[4 + j], row(v1, 7), act, slope.at[j % 2], j * 1024)
        slope_going[j] = pltpu.make_async_copy(slope.at[j % 2], slope_o.at[j], stage_sems.at[j % 2])
        slope_going[j].start()

    def task_outer(j):
        if j >= 2:
            stage_going[j - 2].wait()
        outer(act, low, staged.at[j % 2], 4, j * 1024)
        stage_going[j] = pltpu.make_async_copy(
            staged.at[j % 2], down_o.at[pl.ds(j * 1024, 1024), :], stage_sems.at[2 + j % 2]
        )
        stage_going[j].start()

    def task_down(j):
        feed_down(act, wd, row(v4, 5), hidden, row_mask, result, j)

    tasks = {
        3: [(task_low,)],
        4: [(task_first,), (task_project, 0)],
        5: [(task_project, 1)],
        6: [(task_project, 2), (task_attend, 0, 8)],
        7: [(task_attend, 8, 8)],
        8: [(task_hidden,), (task_up, 0)],
        9: [(task_up, 1), (task_outer, 0)],
        10: [(task_up, 2), (task_outer, 1)],
        11: [(task_up, 3), (task_outer, 2)],
        12: [(task_outer, 3), (task_down, 0)],
        13: [(task_down, 1)],
        14: [(task_down, 2)],
    }
    for tick in range(15):
        copies = []
        if tick < 4:
            copies += small_stage(tick, small, smalls, me, at, sems)
        for stage in (3, 2, 1, 0):
            if 0 <= tick - stage < 12:
                copies += stage_copies(tick - stage, stage)
        for copy in copies:
            copy.start()
        if tick == 0:
            for copy in local:
                copy.wait()
        for task, *args in tasks.get(tick, ()):
            task(*args)
        for copy in copies:
            copy.wait()
        k = tick - 3
        if 0 <= k < 8:
            put_out(wa.at[k], wa_o.at[k], 8 + k)
        elif k == 11:
            put_out(wd, wd_o, 16)
    task_down(3)
    put_out(result, result_o, 7)
    for j in (2, 3):
        slope_going[j].wait()
        stage_going[j].wait()
    for copy in going:
        copy.wait()


def forward(x, cot, key_mask, row_mask, shards, small):
    anywhere = pl.BlockSpec(memory_space=pl.ANY)
    inside = pl.BlockSpec(memory_space=pltpu.VMEM)
    box = (4, 2, 2, 2)
    flat = (640, 1024)
    kept = [
        ((8,) + box + (32, 1024), BF16),
        (box + (128, 1024), BF16),
        ((8, 1024), F32),
        (flat, BF16),
        ((704, 3072), BF16),
        (flat, BF16),
        (flat, F32),
        (flat, BF16),
        ((4, 640, 1024), BF16),
        ((16, 2, 320, LEN_PAD), BF16),
        (flat, BF16),
        ((4096, 1024), BF16),
        (flat, BF16),
    ]
    scratch = [
        kept[0],
        kept[1],
        (box + (8, 128), F32),
        ((8, 1024), F32),
        ((8, 2048), F32),
        ((8, 4096), F32),
        (flat, BF16),
        ((704, 3072), BF16),
        (flat, BF16),
        (flat, F32),
        (flat, BF16),
        ((640, 4096), BF16),
        ((2, 640, 1024), BF16),
        (flat, BF16),
        ((2, 2, 320, LEN_PAD), BF16),
        ((2, 1024, 1024), BF16),
        (flat, BF16),
    ]
    dma = pltpu.SemaphoreType.DMA
    return pl.pallas_call(
        forward_kernel,
        out_shape=[jax.ShapeDtypeStruct(s, d) for s, d in kept],
        in_specs=[inside] * 4 + [anywhere] * 5,
        out_specs=[anywhere] * 13,
        scratch_shapes=[pltpu.VMEM(s, d) for s, d in scratch]
        + [dma((5, COPIES)), dma((5, COPIES)), dma((13,)), dma((17,)), dma((2,)), dma((4,))],
        compiler_params=pltpu.CompilerParams(
            collective_id=0, has_side_effects=True, vmem_limit_bytes=63 << 20
        ),
        name="gather_forward",
    )(x, cot, key_mask, row_mask, *shards, small)


NARROW = (0, 1, 5, 6, 7, 11)
WEIGHTS = (2, 4, 8, 10)


def column_sum(values):
    return jnp.sum(values.reshape(values.shape[0] // 8, 8, values.shape[1]), axis=0)


def norm_back(src, gain, grads, base, dst, dst_low, by_scale, by_shift, by_low):
    for total in (by_scale, by_shift, by_low):
        if total is not None:
            total[...] = jnp.zeros_like(total)

    @pl.loop(0, 640 // 64)
    def _(i):
        rows = block_of(i, 64)
        values = src[rows, :].astype(F32)
        centered = values - jnp.mean(values, axis=-1, keepdims=True)
        inverse = lax.rsqrt(jnp.mean(centered * centered, axis=-1, keepdims=True) + EPS)
        normed = centered * inverse
        g = grads[rows, :]
        scaled = g * gain[...]
        along = jnp.mean(scaled * normed, axis=-1, keepdims=True)
        back = inverse * (scaled - jnp.mean(scaled, axis=-1, keepdims=True) - normed * along)
        whole = base[rows, :].astype(F32) + back
        rounded = whole.astype(BF16)
        if dst is not None:
            dst[rows, :] = whole
        dst_low[rows, :] = rounded
        by_scale[...] += column_sum(g * normed)
        by_shift[...] += column_sum(g)
        if by_low is not None:
            by_low[...] += column_sum(rounded.astype(F32))


def whole_sum(part):
    return jnp.sum(part, axis=0, keepdims=True)


def slope_back(low, weight, slope, grad_pre, col, total):
    @pl.loop(0, 4)
    def _(i):
        rows = block_of(i, 256)
        there = pl.ds(pl.multiple_of(col + i * 256, 256), 256)
        grad = (dot_nt(low[...], weight[rows, :]) * slope[:, rows].astype(F32)).astype(BF16)
        grad_pre[:, there] = grad
        total[pl.ds(7, 1), there] = whole_sum(column_sum(grad.astype(F32)))


def back_through(left, cols, weight, total, first):
    @pl.loop(0, 2)
    def _(i):
        rows = block_of(i, 512)
        part = dot_nt(left[:, cols], weight[rows, :])
        total[:, rows] = part.astype(total.dtype) if first else total[:, rows] + part


def outer_box(left, right, cols, dst):
    @pl.loop(0, 4)
    def _(i):
        part = dot_tn(left[:, block_of(i, 256)], right[:, cols])
        dst[i] = part.astype(BF16).reshape(2, 2, 2, 32, 1024)


def attend_back(first, count, mixed, grad_att, probs, probs_in, sems, grad_mixed):
    lane = lax.broadcasted_iota(jnp.int32, (1, 128), 1)

    def load(unit, slot):
        return pltpu.make_async_copy(probs_in.at[unit], probs.at[slot], sems.at[slot])

    load(first, 0).start()

    @pl.loop(0, count // 2)
    def _(i):
        for slot in range(2):
            unit = first + i * 2 + slot
            seq, pair = lax.div(unit, 8), lax.rem(unit, 8)
            start = pl.multiple_of(seq * 320, 64)
            rows = pl.ds(start, 320)
            col_q, col_k, col_v = (block_of(pair + 8 * n, 128) for n in range(3))
            load(unit, slot).wait()
            if slot == 0:
                load(unit + 1, 1).start()
            else:

                @pl.when(i + 1 < count // 2)
                def _():
                    load(unit + 1, 0).start()

            q = mixed[rows, col_q]
            k = mixed[pl.ds(start, LEN_PAD), col_k]
            v = mixed[pl.ds(start, LEN_PAD), col_v]
            grad_out = grad_att[rows, col_q]
            found = []
            for head in range(2):
                mine = jnp.where(lax.div(lane, 64) == head, 1.0, 0.0).astype(BF16)
                low = probs[slot, head]
                p = low.astype(F32)
                grad_p = dot_nt(grad_out * mine, v)
                inner = jnp.sum(p * grad_p, axis=-1, keepdims=True)
                grad_s = (p * (grad_p - inner)).astype(BF16)
                found.append((dot_nn(grad_s, k), dot_tn(grad_s, q), dot_tn(low, grad_out)))
            grad_q, grad_k, grad_v = (
                jnp.where(lane < 64, a, b) for a, b in zip(found[0], found[1])
            )
            grad_mixed[rows, col_q] = (grad_q * 0.125).astype(BF16)
            grad_mixed[rows, col_k] = (grad_k[:320] * 0.125).astype(BF16)
            grad_mixed[rows, col_v] = grad_v[:320].astype(BF16)


def backward_kernel(*refs):
    (x_i, wa_i, wd_i, v4, normed1_i, mixed_i, attended_i, hidden_i, normed2_i, slope_i, probs_i, low_i, down_i) = refs[:13]
    outs, small_out, input_grad_o = refs[13:17], refs[17], refs[18]
    refs = refs[19:]
    (weights, slope, low, normed2, grad_pre, total, hidden, branch, attended, grad_att, mixed, grad_mixed, probs, normed1, x, input_grad, made, s4, s2, s1, part1, part2, part3) = refs[:23]
    refs = refs[23:]
    per = 1 + 5 * len(BACK)
    slots = [refs[:per], refs[per : 2 * per]]
    small_refs, refs = refs[2 * per : 2 * per + 7], refs[2 * per + 7 :]
    send, recv, own, weight_sems, slope_sems, probs_sems, in_sems, out_sem = refs
    sems = (send, recv, own)
    me, at = coords()

    def get(src, dst, number):
        copy = pltpu.make_async_copy(src, dst, in_sems.at[number])
        copy.start()
        return copy

    wanted = []
    for j in range(4):
        wanted += [wd_i.at[pl.ds(j * 1024, 1024), :], wa_i.at[4 + j]]
    wanted += [wa_i.at[3], wa_i.at[2], wa_i.at[1], wa_i.at[0]]
    weight_going, slope_going = {}, {}

    def get_weight(i):
        if i < len(wanted):
            weight_going[i] = pltpu.make_async_copy(wanted[i], weights.at[i % 3], weight_sems.at[i % 3])
            weight_going[i].start()

    def get_slope(j):
        if j < 4:
            slope_going[j] = pltpu.make_async_copy(slope_i.at[j], slope.at[j % 2], slope_sems.at[j % 2])
            slope_going[j].start()

    low_in = get(low_i, low, 0)
    get_weight(0)
    get_slope(0)
    get_weight(1)
    get_slope(1)
    get_weight(2)
    normed2_in = get(normed2_i, normed2, 1)
    hidden_in = get(hidden_i, hidden, 2)
    attended_in = get(attended_i, attended, 3)
    mixed_in = get(mixed_i, mixed, 4)
    normed1_in = get(normed1_i, normed1, 5)
    x_in = get(x_i, x, 6)
    greet(me, at)

    def row(vectors, i):
        return vectors.at[pl.ds(i, 1), :]

    def weight(i):
        weight_going[i].wait()
        return weights.at[i % 3]

    everything = slice(None)

    def task_start():
        for s in (s4, s2, s1):
            s[...] = jnp.zeros_like(s)
        low_in.wait()
        s4[pl.ds(5, 1), :] = whole_sum(column_sum(low[...].astype(F32)))

    def task_pre(j):
        w = weight(2 * j)
        slope_going[j].wait()
        slope_back(low, w, slope.at[j % 2], grad_pre, j * 1024, s1)
        get_weight(2 * j + 3)
        get_slope(j + 2)

    def task_through(j):
        back_through(grad_pre, pl.ds(j * 1024, 1024), weight(2 * j + 1), total, j == 0)
        get_weight(2 * j + 4)

    def task_up(j):
        if j == 0:
            normed2_in.wait()
        outer_box(normed2, grad_pre, pl.ds(j * 1024, 1024), made.at[(4 + j) % 3])

    def task_second():
        hidden_in.wait()
        norm_back(hidden, row(v4, 3), total, low, hidden, branch, part1, part2, part3)
        for i, part in ((3, part1), (4, part2), (2, part3)):
            s4[pl.ds(i, 1), :] = whole_sum(part[...])

    def task_att():
        back_through(branch, everything, weight(8), grad_att, True)
        get_weight(11)

    def task_out():
        attended_in.wait()
        outer_box(attended, branch, everything, made.at[8 % 3])

    def task_attend(first, count):
        if first == 0:
            mixed_in.wait()
        attend_back(first, count, mixed, grad_att, probs, probs_i, probs_sems, grad_mixed)

    def task_mixed(j, k):
        if j == 2:
            normed1_in.wait()
        columns = pl.ds(j * 1024, 1024)
        outer_box(normed1, grad_mixed, columns, made.at[k % 3])
        if j != 1:
            s2[pl.ds(6, 1), pl.ds(0 if j == 0 else 1024, 1024)] = whole_sum(
                column_sum(grad_mixed[:, columns].astype(F32))
            )

    def task_through_mixed(j):
        back_through(grad_mixed, pl.ds(j * 1024, 1024), weight(11 - j), total, j == 2)

    input_going = []

    def task_first():
        x_in.wait()
        norm_back(x, row(v4, 0), total, hidden, None, input_grad, part1, part2, None)
        for i, part in ((0, part1), (1, part2)):
            s4[pl.ds(i, 1), :] = whole_sum(part[...])
        copy = pltpu.make_async_copy(input_grad, input_grad_o, out_sem.at[0])
        copy.start()
        input_going.append(copy)
        tiny = small_refs[0]
        for z in range(4):
            for y in range(2):
                for x_ in range(2):
                    for c in range(2):
                        d = ((z * 2 + y) * 2 + x_) * 2 + c
                        tiny[z, y, x_, c] = (
                            s4[:, d // 4 * 128 : d // 4 * 128 + 128]
                            + s2[:, d // 2 * 128 : d // 2 * 128 + 128]
                            + s1[:, d * 128 : d * 128 + 128]
                        )

    tasks = {
        0: [(task_start,), (task_pre, 0), (task_through, 0)],
        1: [(task_pre, 1), (task_through, 1)],
        2: [(task_pre, 2), (task_through, 2)],
        3: [(task_pre, 3), (task_through, 3), (task_up, 0)],
        4: [(task_up, 1), (task_second,), (task_att,)],
        5: [(task_up, 2), (task_attend, 0, 4)],
        6: [(task_up, 3), (task_attend, 4, 4)],
        7: [(task_out,), (task_attend, 8, 4)],
        8: [(task_attend, 12, 4), (task_mixed, 2, 9)],
        9: [(task_mixed, 1, 10), (task_through_mixed, 2), (task_through_mixed, 1)],
        10: [(task_mixed, 0, 11), (task_through_mixed, 0), (task_first,)],
    }
    goals = [(3, r, 0) for r in (0, 32, 64, 96)] + [(2, 0, c) for c in (0, 1024, 2048, 3072)]
    goals += [(1, 0, 0), (0, 0, 2048), (0, 0, 1024), (0, 0, 0)]
    flows = {}
    for tick in range(16):
        copies = []
        for stage in (4, 3, 2, 1, 0):
            k = tick - stage
            if 0 <= k < 12:
                if stage == 0:
                    which, r, c = goals[k]
                    out = outs[which].at[pl.ds(r, ROWS), pl.ds(c, WIDE)]
                    source = down_i.at[:, :, :, :, pl.ds(r, ROWS), :] if which == 3 else None
                    flows[k] = Flow(made.at[k % 3], source, out, BACK, slots[k % 2], k % 4, sems, me, at)
                    copies += flows[k].start()
                else:
                    copies += flows[k].step(stage)
        if 11 <= tick <= 15:
            if tick == 11:
                tiny = Flow(small_refs[0], None, small_out, SMALL_STREAM, small_refs[1:], 4, sems, me, at)
                copies += tiny.start()
            else:
                copies += tiny.step(tick - 11)
        for task, *args in tasks.get(tick, ()):
            task(*args)
        for copy in copies:
            copy.wait()
    for copy in input_going:
        copy.wait()


class Flow:
    def __init__(self, made, source, out, streams, refs, slot, sems, me, at):
        self.made, self.source, self.out, self.streams = made, source, out, streams
        self.from_core, rest = refs[0], refs[1:]
        self.bufs = [
            (rest[5 * i : 5 * i + 2], rest[5 * i + 2 : 5 * i + 4], rest[5 * i + 4 : 5 * i + 5])
            for i in range(len(streams))
        ]
        self.slot, self.sems, self.me, self.at = slot, sems, me, at
        self.own = made.at[:, :, :, at["c"]]

    def start(self):
        there = 1 - self.at["c"]
        source = self.made if self.source is None else self.source
        copies = [
            remote(
                source.at[:, :, :, there],
                self.from_core,
                self.sems,
                self.slot,
                COPIES - 1,
                sibling(self.me, self.at),
            )
        ]
        if self.source is not None:
            copies.append(
                pltpu.make_async_copy(source.at[:, :, :, self.at["c"]], self.own, self.sems[2].at[self.slot])
            )
        for copy in copies:
            copy.start()
        return copies

    def step(self, stage):
        if stage == 1:
            add_up(self.own, [self.own, self.from_core], (4, 2, 2))
        copies, number = [], 0
        for (order, first, width), bufs in zip(self.streams, self.bufs):
            columns = pl.ds(first, width)
            rows = slice(None)
            for s in range(3):
                dim = order[s]
                if s + 1 == stage:
                    if stage == 1:
                        held_now = lambda index: self.own.at[index + (rows, columns)]
                    else:
                        prior = order[s - 1]
                        index = pick(order, s - 1, prior, self.at[prior])
                        before = (
                            self.own.at[index + (rows, columns)]
                            if stage == 2
                            else bufs[s - 2][1].at[index]
                        )
                        arrived, total = bufs[s - 1]
                        terms = [arrived.at[i] for i in range(SIZES[prior] - 1)]
                        add_up(total, [before] + terms, remaining(order, s))
                        held_now = lambda index, total=total: total.at[index]
                    for i, (there, device) in enumerate(partners(self.me, self.at, dim)):
                        copy = remote(
                            held_now(pick(order, s, dim, there)),
                            bufs[s][0].at[i],
                            self.sems,
                            self.slot,
                            number + i,
                            device,
                        )
                        copy.start()
                        copies.append(copy)
                number += SIZES[dim] - 1
            if stage == 4:
                prior = order[2]
                before = bufs[1][1].at[pick(order, 2, prior, self.at[prior])]
                arrived = bufs[2][0]
                terms = [arrived.at[i] for i in range(SIZES[prior] - 1)]
                add_up(self.out.at[:, columns], [before] + terms, ())
        return copies


def flow_buffers(streams, rows, width, dtype):
    shapes = [((4, 2, 2, rows, width), dtype)]
    for order, _, columns in streams:
        for s in range(3):
            left = remaining(order, s + 1)
            shapes.append(((SIZES[order[s]] - 1,) + left + (rows, columns), dtype))
            if s < 2:
                shapes.append((left + (rows, columns), dtype))
    return shapes


def backward(*args):
    anywhere = pl.BlockSpec(memory_space=pl.ANY)
    inside = pl.BlockSpec(memory_space=pltpu.VMEM)
    flat = (640, 1024)
    scratch = [
        ((3, 1024, 1024), BF16),
        ((2, 640, 1024), BF16),
        (flat, BF16),
        (flat, BF16),
        ((640, 4096), BF16),
        (flat, F32),
        (flat, F32),
        (flat, BF16),
        (flat, BF16),
        (flat, BF16),
        ((704, 3072), BF16),
        ((640, 3072), BF16),
        ((2, 2, 320, LEN_PAD), BF16),
        (flat, BF16),
        (flat, BF16),
        (flat, BF16),
        ((3, 4, 2, 2, 2, 32, 1024), BF16),
        ((8, 1024), F32),
        ((8, 2048), F32),
        ((8, 4096), F32),
    ] + [((8, 1024), F32)] * 3
    scratch += flow_buffers(BACK, ROWS, WIDE, BF16) * 2
    scratch += [((4, 2, 2, 2, 8, 128), F32)] + flow_buffers(SMALL_STREAM, 8, 128, F32)
    sums = [(32, 3072), (32, 1024), (32, 4096), (128, 1024), (8, 128)]
    dma = pltpu.SemaphoreType.DMA
    return pl.pallas_call(
        backward_kernel,
        out_shape=[jax.ShapeDtypeStruct(s, F32) for s in sums]
        + [jax.ShapeDtypeStruct(flat, BF16)],
        in_specs=[anywhere] * 3 + [inside] + [anywhere] * 9,
        out_specs=[inside] * 5 + [anywhere],
        scratch_shapes=[pltpu.VMEM(s, d) for s, d in scratch]
        + [dma((5, COPIES)), dma((5, COPIES)), dma((5,)), dma((3,)), dma((2,)), dma((2,)), dma((7,)), dma((1,))],
        compiler_params=pltpu.CompilerParams(
            collective_id=1, has_side_effects=True, vmem_limit_bytes=63 << 20
        ),
        name="backward_sum",
    )(*args)


def pack_weights(weights):
    me = lax.axis_index("dp")
    lane = jnp.arange(128, dtype=jnp.int32)[None, :]
    narrow = jnp.tile(jnp.stack([weights[i] for i in NARROW]), (1, 4))
    rows = [
        jnp.where(lane // 32 == me % 4, narrow, 0),
        jnp.where(lane // 64 == me % 2, jnp.tile(weights[3][None], (1, 2)), 0),
        weights[9][None],
    ]
    return jnp.concatenate(rows, axis=0).astype(F32)


def on_box(inputs, lengths, assignment, *rest):
    weights, cotangent = rest[:12], rest[12]
    me = lax.axis_index("dp")
    matches = assignment[:, None] == jnp.arange(lengths.shape[0], dtype=jnp.int32)[None, :]
    kept_len = jnp.sum(jnp.where(matches, lengths[None, :], 0), axis=1)
    key_mask = (jnp.arange(LEN_PAD, dtype=jnp.int32)[None, :] < kept_len[:, None]).astype(F32)
    row_mask = key_mask[:, :320].reshape(640, 1)
    x = inputs.reshape(640, 1024)
    cot = cotangent.reshape(640, 1024)
    small = pack_weights(weights)
    *kept, result = forward(
        x, cot, key_mask[:, None, :], row_mask, [weights[i] for i in WEIGHTS], small
    )
    kept[0] = kept[0].reshape(8, 1024, 1024)
    kept[1] = kept[1].reshape(4096, 1024)
    kept[-1] = kept[-1].reshape(4, 2, 2, 2, 128, 1024)
    *sums, total, input_grad = backward(x, *kept)
    found = [None] * 12
    for row, i in enumerate(NARROW):
        found[i] = lax.dynamic_slice(total[row], (me % 4 * 32,), (32,))
    found[3] = lax.dynamic_slice(total[6], (me % 2 * 64,), (64,))
    found[9] = total[7]
    for i, s in zip(WEIGHTS, sums):
        found[i] = s
    return (result.reshape(inputs.shape), input_grad.reshape(inputs.shape), *found)


def plain(
    inputs,
    lengths,
    assignment,
    norm1_gain,
    norm1_bias,
    qkv_weight,
    qv_bias,
    out_weight,
    out_bias,
    norm2_gain,
    norm2_bias,
    up_weight,
    up_bias,
    down_weight,
    down_bias,
    cotangent,
):
    gathered = (
        lax.all_gather(norm1_gain, "dp", axis=0, tiled=True),
        lax.all_gather(norm1_bias, "dp", axis=0, tiled=True),
        lax.all_gather(qkv_weight, "dp", axis=0, tiled=True),
        lax.all_gather(qv_bias, "dp", axis=0, tiled=True),
        lax.all_gather(out_weight, "dp", axis=0, tiled=True),
        lax.all_gather(out_bias, "dp", axis=0, tiled=True),
        lax.all_gather(norm2_gain, "dp", axis=0, tiled=True),
        lax.all_gather(norm2_bias, "dp", axis=0, tiled=True),
        lax.all_gather(up_weight, "dp", axis=0, tiled=True),
        lax.all_gather(up_bias, "dp", axis=0, tiled=True),
        lax.all_gather(down_weight, "dp", axis=0, tiled=True),
        lax.all_gather(down_bias, "dp", axis=0, tiled=True),
    )
    seq_count, tok_count, model_width = inputs.shape
    rows_all = seq_count * tok_count
    split_shape = (seq_count, tok_count, HEADS, HEAD)
    head_scale = HEAD ** (-0.5)
    matches = assignment[:, None] == jnp.arange(lengths.shape[0], dtype=jnp.int32)[None, :]
    kept_len = jnp.sum(jnp.where(matches, lengths[None, :], 0), axis=1)
    key_mask = jnp.arange(tok_count, dtype=jnp.int32)[None, :] < kept_len[:, None]
    row_mask = key_mask.reshape(rows_all, 1).astype(jnp.float32)
    gain_first = gathered[0].astype(jnp.float32)
    shift_first = gathered[1].astype(jnp.float32)
    qv_full = gathered[3].astype(jnp.float32)
    proj_shift = gathered[5].astype(jnp.float32)
    gain_second = gathered[6].astype(jnp.float32)
    shift_second = gathered[7].astype(jnp.float32)
    up_shift = gathered[9].astype(jnp.float32)
    down_shift = gathered[11].astype(jnp.float32)
    inputs_flat = inputs.reshape(rows_all, model_width).astype(jnp.float32)
    normed_first, first_back = jax.vjp(layer_norm, inputs_flat, gain_first, shift_first)
    normed_low = normed_first.astype(jnp.bfloat16)
    full_bias = jnp.concatenate(
        [qv_full[:model_width], jnp.zeros((model_width,), jnp.float32), qv_full[model_width:]]
    )
    mixed_qkv = (
        jnp.dot(normed_low, gathered[2], preferred_element_type=jnp.float32) + full_bias
    ).astype(jnp.bfloat16)
    queries = mixed_qkv[:, :model_width].reshape(split_shape)
    keys_all = mixed_qkv[:, model_width : 2 * model_width].reshape(split_shape)
    values_all = mixed_qkv[:, 2 * model_width :].reshape(split_shape)
    scores = (
        jnp.einsum("bqhd,bkhd->bhqk", queries, keys_all, preferred_element_type=jnp.float32)
        * head_scale
    )
    scores = jnp.where(key_mask[:, None, None, :], scores, masked_score)
    row_max = jnp.max(scores, axis=-1, keepdims=True)
    exponent = jnp.exp(scores - row_max)
    row_total = jnp.sum(exponent, axis=-1, keepdims=True)
    softmax_probs = exponent / row_total
    log_total = row_max + jnp.log(row_total)
    attended = jnp.einsum(
        "bhqk,bkhd->bqhd",
        softmax_probs.astype(jnp.bfloat16),
        values_all,
        preferred_element_type=jnp.float32,
    )
    attended = attended.reshape(rows_all, model_width).astype(jnp.bfloat16)
    hidden = inputs_flat + (
        jnp.dot(attended, gathered[4], preferred_element_type=jnp.float32) + proj_shift
    )
    normed_second, second_back = jax.vjp(layer_norm, hidden, gain_second, shift_second)
    second_low = normed_second.astype(jnp.bfloat16)
    pre_act = jnp.dot(second_low, gathered[8], preferred_element_type=jnp.float32) + up_shift
    activation, gelu_back = jax.vjp(gelu_exact, pre_act)
    act_low = activation.astype(jnp.bfloat16)
    output_rows = row_mask * (
        hidden + (jnp.dot(act_low, gathered[10], preferred_element_type=jnp.float32) + down_shift)
    )
    result = output_rows.reshape(inputs.shape).astype(jnp.bfloat16)
    grad_rows = cotangent.reshape(rows_all, model_width).astype(jnp.float32) * row_mask
    grad_low = grad_rows.astype(jnp.bfloat16)
    down_grad = contract_rows(act_low, grad_low)
    down_bias_grad = jnp.sum(grad_low.astype(jnp.float32), axis=0)
    grad_pre = gelu_back(contract_cols(grad_low, gathered[10]))[0].astype(jnp.bfloat16)
    up_grad = contract_rows(second_low, grad_pre)
    up_bias_grad = jnp.sum(grad_pre.astype(jnp.float32), axis=0)
    grad_second, gain2_grad, shift2_grad = second_back(contract_cols(grad_pre, gathered[8]))
    grad_hidden = grad_rows + grad_second
    branch_low = grad_hidden.astype(jnp.bfloat16)
    proj_grad = contract_rows(attended, branch_low)
    proj_bias_grad = jnp.sum(branch_low.astype(jnp.float32), axis=0)
    grad_att = contract_cols(branch_low, gathered[4]).astype(jnp.bfloat16).reshape(split_shape)
    scores_again = (
        jnp.einsum("bqhd,bkhd->bhqk", queries, keys_all, preferred_element_type=jnp.float32)
        * head_scale
    )
    scores_again = jnp.where(key_mask[:, None, None, :], scores_again, masked_score)
    probs_again = jnp.exp(scores_again - log_total)
    probs_low = probs_again.astype(jnp.bfloat16)
    grad_probs = jnp.einsum(
        "bqhd,bkhd->bhqk", grad_att, values_all, preferred_element_type=jnp.float32
    )
    grad_values = jnp.einsum(
        "bhqk,bqhd->bkhd", probs_low, grad_att, preferred_element_type=jnp.float32
    )
    inner_sum = jnp.sum(probs_again * grad_probs, axis=-1, keepdims=True)
    grad_scores = (probs_again * (grad_probs - inner_sum)).astype(jnp.bfloat16)
    grad_queries = (
        jnp.einsum("bhqk,bkhd->bqhd", grad_scores, keys_all, preferred_element_type=jnp.float32)
        * head_scale
    )
    grad_keys = (
        jnp.einsum("bhqk,bqhd->bkhd", grad_scores, queries, preferred_element_type=jnp.float32)
        * head_scale
    )
    grad_mixed = jnp.concatenate(
        [
            grad_queries.reshape(rows_all, model_width),
            grad_keys.reshape(rows_all, model_width),
            grad_values.reshape(rows_all, model_width),
        ],
        axis=1,
    ).astype(jnp.bfloat16)
    qkv_grad = contract_rows(normed_low, grad_mixed)
    column_sums = jnp.sum(grad_mixed.astype(jnp.float32), axis=0)
    qv_grad = jnp.concatenate([column_sums[:model_width], column_sums[2 * model_width :]])
    grad_first, gain1_grad, shift1_grad = first_back(contract_cols(grad_mixed, gathered[2]))
    input_grad = (grad_hidden + grad_first).reshape(inputs.shape).astype(jnp.bfloat16)
    all_sums = (
        lax.psum_scatter(gain1_grad, "dp", scatter_dimension=0, tiled=True),
        lax.psum_scatter(shift1_grad, "dp", scatter_dimension=0, tiled=True),
        lax.psum_scatter(qkv_grad, "dp", scatter_dimension=0, tiled=True),
        lax.psum_scatter(qv_grad, "dp", scatter_dimension=0, tiled=True),
        lax.psum_scatter(proj_grad, "dp", scatter_dimension=0, tiled=True),
        lax.psum_scatter(proj_bias_grad, "dp", scatter_dimension=0, tiled=True),
        lax.psum_scatter(gain2_grad, "dp", scatter_dimension=0, tiled=True),
        lax.psum_scatter(shift2_grad, "dp", scatter_dimension=0, tiled=True),
        lax.psum_scatter(up_grad, "dp", scatter_dimension=0, tiled=True),
        lax.psum_scatter(up_bias_grad, "dp", scatter_dimension=0, tiled=True),
        lax.psum_scatter(down_grad, "dp", scatter_dimension=0, tiled=True),
        lax.psum_scatter(down_bias_grad, "dp", scatter_dimension=0, tiled=True),
    )
    attn_sums = all_sums[:6]
    mlp_sums = all_sums[6:]
    return (
        result,
        input_grad,
        attn_sums[0],
        attn_sums[1],
        attn_sums[2],
        attn_sums[3],
        attn_sums[4],
        attn_sums[5],
        mlp_sums[0],
        mlp_sums[1],
        mlp_sums[2],
        mlp_sums[3],
        mlp_sums[4],
        mlp_sums[5],
    )


def local(*args):
    return on_box(*args) if lax.axis_size("dp") == 32 else plain(*args)


def solution(mesh):
    placed = (
        P("dp", None, None),
        P(),
        P("dp"),
        P("dp"),
        P("dp"),
        P("dp", None),
        P("dp"),
        P("dp", None),
        P("dp"),
        P("dp"),
        P("dp"),
        P("dp", None),
        P("dp"),
        P("dp", None),
        P("dp"),
        P("dp", None, None),
    )
    return jax.shard_map(
        local,
        mesh=mesh,
        in_specs=placed,
        out_specs=(
            P("dp", None, None),
            P("dp", None, None),
            P("dp"),
            P("dp"),
            P("dp", None),
            P("dp"),
            P("dp", None),
            P("dp"),
            P("dp"),
            P("dp"),
            P("dp", None),
            P("dp"),
            P("dp", None),
            P("dp"),
        ),
        check_vma=False,
    )
```

```python
import jax
import jax.numpy as jnp
from jax import lax
from jax.experimental import pallas as pl
from jax.experimental.pallas import tpu as pltpu
from jax.sharding import PartitionSpec as P

HEADS = 16
HEAD = 64


eps = 1e-06
masked_score = -1000000000.0


def layer_norm(values, norm_gain, norm_shift):
    average = jnp.mean(values, axis=-1, keepdims=True)
    centered = values - average
    variance = jnp.mean(centered * centered, axis=-1, keepdims=True)
    return centered * lax.rsqrt(variance + eps) * norm_gain + norm_shift


def gelu_exact(values):
    return jax.nn.gelu(values, approximate=False)


def contract_rows(left, right):
    return lax.dot_general(
        left, right, (((0,), (0,)), ((), ())), preferred_element_type=jnp.float32
    )


def contract_cols(left, right):
    return lax.dot_general(
        left, right, (((1,), (1,)), ((), ())), preferred_element_type=jnp.float32
    )


BF16 = jnp.bfloat16
F32 = jnp.float32
MESH = pl.DeviceIdType.MESH
STRIDE = {"z": 8, "y": 4, "x": 2}
ROWS = 32
WIDE = 1024
STAGES = 4
PARTS = (
    ("zZyx", 0, 16, 0, 384),
    ("zZxy", 16, 16, 0, 384),
    ("xzZy", 0, 16, 384, 640),
    ("yzZx", 16, 16, 384, 640),
)
TALL = (
    ("zZyx", 0, 48, 0, 128),
    ("zZxy", 0, 48, 128, 128),
    ("xzZy", 48, 80, 0, 128),
    ("yzZx", 48, 80, 128, 128),
)
COPIES = 6 * len(PARTS) + 1
CHUNKS = (
    tuple((0, 0, c) for c in (0, 1024, 2048))
    + ((1, 0, 0),)
    + tuple((2, 0, c) for c in (0, 1024, 2048, 3072))
)


def coords():
    me = lax.axis_index("dp")
    at = {
        "z": lax.div(me, 8),
        "y": lax.rem(lax.div(me, 4), 2),
        "x": lax.rem(lax.div(me, 2), 2),
        "c": lax.rem(me, 2),
    }
    return me, at


def sibling(me, at):
    return me + 1 - 2 * at["c"]


class Hop:
    def __init__(self, copy, sends=None, hears=None):
        self.copy, self.sends, self.hears = copy, sends, hears

    def start(self):
        if self.sends is None:
            self.copy.start()
        else:
            pl.when(self.sends)(self.copy.start)

    def wait(self):
        if self.sends is None:
            self.copy.wait()
        else:
            pl.when(self.sends)(self.copy.wait_send)
            pl.when(self.hears)(self.copy.wait_recv)


def inner(at):
    return lax.div(at["z"] + 1, 2) == 1


def far(at):
    return 3 * (1 - lax.div(at["z"], 2))


def hops(me, at, dim):
    z = at["z"]
    if dim == "z":
        found = []
        for k in (1, 2, 3):
            there = lax.rem(z + k, 4)
            when = {1: (z < 3, z > 0), 2: (None, None), 3: (z > 0, z < 3)}[k]
            found.append((there, me + (there - z) * 8, *when))
        return found
    if dim == "Z":
        return [(far(at), me + 8 - 16 * lax.rem(z, 2), inner(at), jnp.logical_not(inner(at)))]
    there = 1 - at[dim]
    return [(there, me + (there - at[dim]) * STRIDE[dim], None, None)]


def count_of(dim):
    return 3 if dim == "z" else 1


def greet(me, at):
    barrier = pltpu.get_barrier_semaphore()
    devices = [sibling(me, at)]
    for dim in "yx":
        devices += [hop[1] for hop in hops(me, at, dim)]
    for k in (1, 2, 3):
        devices.append(me + (lax.rem(at["z"] + k, 4) - at["z"]) * 8)
    for device in devices:
        pl.semaphore_signal(barrier, inc=1, device_id=(device,), device_id_type=MESH)
    pl.semaphore_wait(barrier, len(devices))


def remote(src, dst, sems, slot, number, device):
    return pltpu.make_async_remote_copy(
        src_ref=src,
        dst_ref=dst,
        send_sem=sems[0].at[slot, number],
        recv_sem=sems[1].at[slot, number],
        device_id=(device,),
        device_id_type=MESH,
    )


def held(order, stage, at):
    index = []
    for dim in "zyx":
        if dim == "z" and order[stage] == "Z":
            index.append(far(at))
        else:
            done = "Z" if dim == "z" else dim
            index.append(slice(None) if done in order[:stage] else at[dim])
    return tuple(index)


def gather_stage(base, parts, stage, me, at, sems, slot, source=None):
    if stage == STAGES:
        block = base.at[:, :, :, at["c"]]
        return [Hop(remote(block, block, sems, slot, COPIES - 1, sibling(me, at)))]
    number, copies = 0, []
    for order, row, rows, col, columns in parts:
        here = (pl.ds(row, rows), pl.ds(col, columns))
        for s in range(STAGES):
            for _, device, sends, hears in hops(me, at, order[s]):
                if s == stage:
                    block = base.at[held(order, stage, at) + (at["c"],) + here]
                    src = source.at[here] if source is not None and stage == 0 else block
                    copies.append(Hop(remote(src, block, sems, slot, number, device), sends, hears))
                number += 1
    return copies


SMALL = (("zZyx", 0, 8, 0, 128),)


def remaining(order, stage):
    left = [dim for dim in "zyx" if dim not in order[:stage]]
    return tuple({"z": 4, "y": 2, "x": 2}[dim] for dim in left)


def pick(order, stage, dim, index):
    return tuple(index if d == dim.lower() else slice(None) for d in "zyx" if d not in order[:stage])


BACK = tuple((part[0][::-1], *part[1:]) for part in PARTS)
SMALL_BACK = tuple((part[0][::-1], *part[1:]) for part in SMALL)


def add_up(dst, terms, lead):
    loops = lead[: max(len(lead) - 1, 0)] if len(lead) > 1 else ()
    count = 1
    for n in loops:
        count *= n

    def body(i, carry):
        index = []
        for n in loops[::-1]:
            index.append(lax.rem(i, n))
            i = lax.div(i, n)
        index = tuple(index[::-1]) + (slice(None),) * (len(lead) - len(loops) + 2)
        total = terms[0][index].astype(F32)
        for term in terms[1:]:
            total = total + term[index].astype(F32)
        dst[index] = total.astype(dst.dtype)
        return carry

    if count == 1:
        body(0, 0)
    else:
        lax.fori_loop(0, count, body, 0)


class Flow:
    def __init__(self, made, source, out, parts, refs, slot, sems, me, at):
        self.made, self.source, self.out, self.parts = made, source, out, parts
        self.from_core, rest = refs[0], refs[1:]
        self.arrived, self.totals = [], []
        for order, *_ in parts:
            self.arrived.append(rest[:4])
            self.totals.append(dict(zip([s for s in range(3) if order[s] != "Z"], rest[4:6])))
            rest = rest[6:]
        self.slot, self.sems, self.me, self.at = slot, sems, me, at
        self.own = made.at[:, :, :, at["c"]]

    def start(self):
        there = 1 - self.at["c"]
        source = self.made if self.source is None else self.source
        self.going = [
            remote(
                source.at[:, :, :, there],
                self.from_core,
                self.sems,
                self.slot,
                COPIES - 1,
                sibling(self.me, self.at),
            )
        ]
        if self.source is not None:
            self.going.append(
                pltpu.make_async_copy(source.at[:, :, :, self.at["c"]], self.own, self.sems[2].at[self.slot])
            )
        for copy in self.going:
            copy.start()

    def sum_before(self, part, stage):
        order, row, rows, col, columns = self.parts[part]
        done = [s for s in range(stage) if s in self.totals[part]]
        if not done:
            return self.own.at[:, :, :, pl.ds(row, rows), pl.ds(col, columns)]
        return self.totals[part][done[-1]]

    def take(self, part, stage):
        order, row, rows, col, columns = self.parts[part]
        s = stage - 2
        dim, arrived = order[s], self.arrived[part][s]
        before = self.sum_before(part, s)
        if dim == "Z":
            index = pick(order, s, "z", far(self.at))

            @pl.when(inner(self.at))
            def _():
                add_up(before.at[index], [before.at[index], arrived.at[0]], remaining(order, s)[1:])

            return
        if stage == STAGES + 1:
            total = self.out.at[pl.ds(row, rows), pl.ds(col, columns)]
        else:
            total = self.totals[part][s]
        mine = before.at[pick(order, s, dim, self.at[dim])]
        left = remaining(order, s + 1)
        if dim != "z":
            add_up(total, [mine, arrived.at[0]], left)
            return
        z = self.at["z"]
        for when, came in ((z == 0, (1, 2)), (inner(self.at), (0, 1, 2)), (z == 3, (0, 1))):

            @pl.when(when)
            def _(came=came):
                add_up(total, [mine] + [arrived.at[i] for i in came], left)

    def step(self, stage):
        for copy in self.going:
            copy.wait()
        if stage == 1:
            add_up(self.own, [self.own, self.from_core], (4, 2, 2))
        else:
            for part in range(len(self.parts)):
                self.take(part, stage)
        self.going, number = [], 0
        for part, (order, row, rows, col, columns) in enumerate(self.parts):
            for s in range(STAGES):
                if s + 1 == stage:
                    before = self.sum_before(part, s)
                    for i, (there, device, sends, hears) in enumerate(hops(self.me, self.at, order[s])):
                        if order[s] == "Z":
                            sends, hears = hears, sends
                        src = before.at[pick(order, s, order[s], there)]
                        copy = remote(src, self.arrived[part][s].at[i], self.sems, self.slot, number + i, device)
                        self.going.append(Hop(copy, sends, hears))
                number += count_of(order[s])
        for copy in self.going:
            copy.start()


def flow_buffers(parts, rows, width, dtype):
    shapes = [((4, 2, 2, rows, width), dtype)]
    for order, _, high, _, wide in parts:
        totals = []
        for s in range(STAGES):
            if order[s] == "Z":
                left = remaining(order, s)[1:]
            else:
                left = remaining(order, s + 1)
                if s < 3:
                    totals.append((left + (high, wide), dtype))
            shapes.append(((count_of(order[s]),) + left + (high, wide), dtype))
        shapes += totals
    return shapes


EPS = 1e-06
MASKED = -1000000000.0
LEN_PAD = 384


def dot_nn(a, b):
    return jnp.dot(a, b, preferred_element_type=F32)


def dot_nt(a, b):
    return lax.dot_general(a, b, (((1,), (1,)), ((), ())), preferred_element_type=F32)


def dot_tn(a, b):
    return lax.dot_general(a, b, (((0,), (0,)), ((), ())), preferred_element_type=F32)


def block_of(index, size):
    return pl.ds(pl.multiple_of(index * size, size), size)


def spread_vectors(smalls, v4, v2, v1):
    for z in range(4):
        for y in range(2):
            four = None
            for x in range(2):
                two = None
                for c in range(2):
                    one = smalls[z, y, x, c]
                    d = ((z * 2 + y) * 2 + x) * 2 + c
                    v1[:, d * 128 : d * 128 + 128] = one
                    two = one if two is None else two + one
                d = (z * 2 + y) * 2 + x
                v2[:, d * 128 : d * 128 + 128] = two
                four = two if four is None else four + two
            d = z * 2 + y
            v4[:, d * 128 : d * 128 + 128] = four


def norm_rows(src, gain, shift, dst):
    @pl.loop(0, src.shape[0] // 64)
    def _(i):
        rows = block_of(i, 64)
        values = src[rows, :].astype(F32)
        centered = values - jnp.mean(values, axis=-1, keepdims=True)
        variance = jnp.mean(centered * centered, axis=-1, keepdims=True)
        normed = centered * lax.rsqrt(variance + EPS)
        dst[rows, :] = (normed * gain[...] + shift[...]).astype(BF16)


def project(normed, weight, shift, dst, col):
    @pl.loop(0, 2)
    def _(i):
        columns = block_of(i, 512)
        mixed = dot_nn(normed[...], weight[:, :, :, :, :, columns].reshape(1024, 512))
        if shift is not None:
            mixed = mixed + shift[:, columns]
        dst[pl.ds(0, 640), pl.ds(pl.multiple_of(col + i * 512, 512), 512)] = mixed.astype(BF16)


def attend(first, count, mixed, kept_len, attended, probs, probs_out, sems):
    lane = lax.broadcasted_iota(jnp.int32, (1, 128), 1)

    def out_copy(unit, slot):
        return pltpu.make_async_copy(probs.at[slot], probs_out.at[unit], sems.at[slot])

    @pl.loop(0, count // 2)
    def _(i):
        for slot in range(2):
            unit = first + i * 2 + slot
            seq, pair = lax.div(unit, 8), lax.rem(unit, 8)
            start = pl.multiple_of(seq * 320, 64)
            columns = block_of(pair, 128)
            q = mixed[pl.ds(start, 320), columns]
            k = mixed[pl.ds(start, LEN_PAD), block_of(pair + 8, 128)]
            v = mixed[pl.ds(start, LEN_PAD), block_of(pair + 16, 128)]
            kept = lax.broadcasted_iota(jnp.int32, (1, LEN_PAD), 1) < kept_len(seq)

            @pl.when(i > 0)
            def _():
                out_copy(unit, slot).wait()

            found = []
            for head in range(2):
                scale = jnp.where(lax.div(lane, 64) == head, 0.125, 0.0).astype(BF16)
                scores = jnp.where(kept, dot_nt(q * scale, k), MASKED)
                exponent = jnp.exp(scores - jnp.max(scores, axis=-1, keepdims=True))
                total = jnp.sum(exponent, axis=-1, keepdims=True)
                low = (exponent * (1.0 / total)).astype(BF16)
                probs[slot, head] = low
                found.append(dot_nn(low, v))
            attended[pl.ds(start, 320), columns] = jnp.where(
                lane < 64, found[0], found[1]
            ).astype(BF16)
            out_copy(unit, slot).start()

    for slot in range(2):
        out_copy(0, slot).wait()


def branch_out(attended, weight, shift, x, hidden):
    @pl.loop(0, 2)
    def _(i):
        columns = block_of(i, 512)
        branch = dot_nn(attended[...], weight[:, :, :, :, :, columns].reshape(1024, 512))
        hidden[:, columns] = x[:, columns].astype(F32) + (branch + shift[:, columns])


def feed_up(normed, weight, shift, act, slope, col):
    @pl.loop(0, 2)
    def _(i):
        columns = block_of(i, 512)
        there = pl.ds(pl.multiple_of(col + i * 512, 512), 512)
        pre = dot_nn(normed[...], weight[:, :, :, :, :, columns].reshape(1024, 512))
        pre = pre + shift[:, there]
        below = 0.5 + 0.5 * lax.erf(pre * 0.7071067811865476)
        act[:, there] = (pre * below).astype(BF16)
        density = jnp.exp(pre * pre * -0.5) * 0.3989422804014327
        slope[:, columns] = (below + pre * density).astype(BF16)


def outer(left, right, dst, col):
    @pl.loop(0, 2)
    def _(i):
        columns = pl.ds(pl.multiple_of(col + i * 512, 512), 512)
        dst[block_of(i, 512), :] = dot_tn(left[:, columns], right[...]).astype(BF16)


def turn(src, dst):
    @pl.loop(0, 4)
    def _(i):
        rows = block_of(i, 256)
        dst[rows, :] = src[:, rows].T


def feed_down(act, weight, shift, hidden, row_mask, result, j):
    columns = pl.ds(j * 256, 256)
    branch = dot_nn(act[...], weight[:, :, :, :, :, columns].reshape(4096, 256))
    whole = hidden[:, columns] + (branch + shift[:, columns])
    result[:, columns] = (whole * row_mask[...]).astype(BF16)


def forward_kernel(*refs):
    x, cot, lengths, assignment = refs[:4]
    shards, small = refs[4:8], refs[8]
    (wa_o, wd_o, v4_o, normed1_o, mixed_o, attended_o, hidden_o, normed2_o, slope_o, probs_o, low_o, down_o, plain_o, result_o) = refs[9:23]
    (wa, wd, smalls, v4, v2, v1, normed1, mixed, attended, hidden, normed2, act, slope, low, probs, staged, result, row_mask, turned) = refs[23:42]
    send, recv, own, out_sems, probs_sems, stage_sems = refs[42:]
    sems = (send, recv)
    me, at = coords()
    mine = (at["z"], at["y"], at["x"], at["c"])
    everything = slice(None)

    def place(k):
        if k < 8:
            which, row, col = CHUNKS[k]
            return wa.at[k], shards[which].at[:, pl.ds(col, WIDE)], PARTS
        columns = pl.ds((k - 8) * 256, 256)
        return wd.at[:, :, :, :, :, columns], shards[3].at[:, columns], TALL

    def stage_copies(k, stage):
        base, shard, parts = place(k)
        return gather_stage(base, parts, stage, me, at, sems, k % 8, shard)

    local = [pltpu.make_async_copy(small, smalls.at[mine], own.at[12])]
    for k in range(12):
        base, shard, _ = place(k)
        local.append(pltpu.make_async_copy(shard, base.at[mine], own.at[k]))
    for copy in local:
        copy.start()
    greet(me, at)

    going = []

    def put_out(src, dst, number):
        copy = pltpu.make_async_copy(src, dst, out_sems.at[number])
        copy.start()
        going.append(copy)

    def row(vectors, i):
        return vectors.at[pl.ds(i, 1), :]

    def kept_len(seq):
        return lengths[assignment[seq]]

    def task_low():
        for seq in range(2):
            inside = lax.broadcasted_iota(jnp.int32, (320, 1), 0) < kept_len(seq)
            row_mask[pl.ds(seq * 320, 320), :] = jnp.where(inside, 1.0, 0.0)
        low[...] = (cot[...].astype(F32) * row_mask[...]).astype(BF16)
        put_out(low, low_o, 0)
        mixed[pl.ds(640, 64), :] = jnp.zeros((64, 3072), BF16)

    def task_first():
        spread_vectors(smalls, v4, v2, v1)
        put_out(v4, v4_o, 1)
        norm_rows(x, row(v4, 0), row(v4, 1), normed1)

    def task_project(j):
        shift = None if j == 1 else v2.at[pl.ds(6, 1), pl.ds(0 if j == 0 else 1024, 1024)]
        project(normed1, wa.at[j], shift, mixed, j * 1024)
        if j == 2:
            put_out(mixed, mixed_o, 3)

    def task_attend(first, count):
        attend(first, count, mixed, kept_len, attended, probs, probs_o, probs_sems)
        if first + count == 16:
            put_out(attended, plain_o, 20)

    def task_hidden():
        branch_out(attended, wa.at[3], row(v4, 2), x, hidden)
        put_out(hidden, hidden_o, 4)
        norm_rows(hidden, row(v4, 3), row(v4, 4), normed2)

    slope_going, stage_going = {}, {}

    def task_up(j):
        if j >= 2:
            slope_going[j - 2].wait()
        feed_up(normed2, wa.at[4 + j], row(v1, 7), act, slope.at[j % 2], j * 1024)
        slope_going[j] = pltpu.make_async_copy(slope.at[j % 2], slope_o.at[j], stage_sems.at[j % 2])
        slope_going[j].start()

    def task_outer(j):
        if j >= 2:
            stage_going[j - 2].wait()
        outer(act, low, staged.at[j % 2], j * 1024)
        stage_going[j] = pltpu.make_async_copy(
            staged.at[j % 2], down_o.at[pl.ds(j * 1024, 1024), :], stage_sems.at[2 + j % 2]
        )
        stage_going[j].start()

    def task_turn(src, dst, number):
        slot = turned.at[number % 2]
        if number == 6:
            turn_going.pop(2).wait()
        turn(src, slot)
        turn_going[number] = pltpu.make_async_copy(slot, dst, out_sems.at[number])
        turn_going[number].start()

    turn_going = {}

    def task_down(j):
        feed_down(act, wd, row(v4, 5), hidden, row_mask, result, j)

    tasks = {
        3: [(task_low,)],
        5: [(task_first,), (task_project, 0)],
        6: [(task_project, 1), (task_turn, normed1, normed1_o, 2)],
        7: [(task_project, 2), (task_attend, 0, 4)],
        8: [(task_attend, 4, 6)],
        9: [(task_attend, 10, 6)],
        10: [(task_hidden,), (task_up, 0)],
        11: [(task_up, 1), (task_outer, 0)],
        12: [(task_up, 2), (task_outer, 1)],
        13: [(task_up, 3), (task_outer, 2)],
        14: [(task_outer, 3), (task_down, 0)],
        15: [(task_down, 1), (task_turn, attended, attended_o, 5)],
        16: [(task_down, 2), (task_turn, normed2, normed2_o, 6)],
    }
    flying = {}

    def begin(k, stage):
        if stage:
            for copy in flying.pop((k, stage - 1)):
                copy.wait()
        flying[k, stage] = stage_copies(k, stage)
        for copy in flying[k, stage]:
            copy.start()

    def arrive(k):
        for copy in flying.pop((k, STAGES)):
            copy.wait()
        if k < 8:
            put_out(wa.at[k], wa_o.at[k], 8 + k)
        else:
            columns = pl.ds((k - 8) * 256, 256)
            put_out(wd.at[:, :, :, :, :, columns], wd_o.at[:, :, :, :, :, columns], 8 + k)

    small_going = []
    for tick in range(12 + STAGES + 1):
        for stage in range(STAGES + 1):
            if 0 <= tick - stage < 12:
                begin(tick - stage, stage)
            if stage == 0 and tick <= STAGES + 1:
                for copy in small_going:
                    copy.wait()
                small_going = []
                if tick <= STAGES:
                    small_going = gather_stage(smalls, SMALL, tick, me, at, sems, 8, small)
                for copy in small_going:
                    copy.start()
            if tick == 0 and stage == 0:
                for copy in local:
                    copy.wait()
        if 0 <= tick - STAGES - 1 < 12:
            arrive(tick - STAGES - 1)
        for task, *args in tasks.get(tick, ()):
            task(*args)
    task_down(3)
    put_out(result, result_o, 7)
    for j in (2, 3):
        slope_going[j].wait()
        stage_going[j].wait()
    for copy in (*going, *turn_going.values()):
        copy.wait()


def forward(x, cot, lengths, assignment, shards, small):
    anywhere = pl.BlockSpec(memory_space=pl.ANY)
    inside = pl.BlockSpec(memory_space=pltpu.VMEM)
    box = (4, 2, 2, 2)
    flat, turned = (640, 1024), (1024, 640)
    kept = [
        ((8,) + box + (32, 1024), BF16),
        (box + (128, 1024), BF16),
        ((8, 1024), F32),
        (turned, BF16),
        ((704, 3072), BF16),
        (turned, BF16),
        (flat, F32),
        (turned, BF16),
        ((4, 640, 1024), BF16),
        ((16, 2, 320, LEN_PAD), BF16),
        (flat, BF16),
        ((4096, 1024), BF16),
        (flat, BF16),
        (flat, BF16),
    ]
    scratch = [
        kept[0],
        kept[1],
        (box + (8, 128), F32),
        ((8, 1024), F32),
        ((8, 2048), F32),
        ((8, 4096), F32),
        (flat, BF16),
        ((704, 3072), BF16),
        (flat, BF16),
        (flat, F32),
        (flat, BF16),
        ((640, 4096), BF16),
        ((2, 640, 1024), BF16),
        (flat, BF16),
        ((2, 2, 320, LEN_PAD), BF16),
        ((2, 1024, 1024), BF16),
        (flat, BF16),
        ((640, 1), F32),
        ((2, 1024, 640), BF16),
    ]
    dma = pltpu.SemaphoreType.DMA
    return pl.pallas_call(
        forward_kernel,
        out_shape=[jax.ShapeDtypeStruct(s, d) for s, d in kept],
        in_specs=[inside] * 2 + [pl.BlockSpec(memory_space=pltpu.SMEM)] * 2 + [anywhere] * 5,
        out_specs=[anywhere] * 14,
        scratch_shapes=[pltpu.VMEM(s, d) for s, d in scratch]
        + [dma((9, COPIES)), dma((9, COPIES)), dma((13,)), dma((21,)), dma((2,)), dma((4,))],
        compiler_params=pltpu.CompilerParams(
            collective_id=0, has_side_effects=True, vmem_limit_bytes=63 << 20
        ),
        name="gather_forward",
    )(x, cot, lengths, assignment, *shards, small)


NARROW = (0, 1, 5, 6, 7, 11)
WEIGHTS = (2, 4, 8, 10)


def column_sum(values):
    return jnp.sum(values.reshape(values.shape[0] // 8, 8, values.shape[1]), axis=0)


def norm_back(src, gain, grads, base, dst, dst_low, by_scale, by_shift, by_low):
    for total in (by_scale, by_shift, by_low):
        if total is not None:
            total[...] = jnp.zeros_like(total)

    @pl.loop(0, 640 // 64)
    def _(i):
        rows = block_of(i, 64)
        values = src[rows, :].astype(F32)
        centered = values - jnp.mean(values, axis=-1, keepdims=True)
        inverse = lax.rsqrt(jnp.mean(centered * centered, axis=-1, keepdims=True) + EPS)
        normed = centered * inverse
        g = grads[rows, :]
        scaled = g * gain[...]
        along = jnp.mean(scaled * normed, axis=-1, keepdims=True)
        back = inverse * (scaled - jnp.mean(scaled, axis=-1, keepdims=True) - normed * along)
        whole = base[rows, :].astype(F32) + back
        rounded = whole.astype(BF16)
        if dst is not None:
            dst[rows, :] = whole
        dst_low[rows, :] = rounded
        by_scale[...] += column_sum(g * normed)
        by_shift[...] += column_sum(g)
        if by_low is not None:
            by_low[...] += column_sum(rounded.astype(F32))


def whole_sum(part):
    return jnp.sum(part, axis=0, keepdims=True)


def slope_back(low, weight, slope, grad_pre, col, total):
    @pl.loop(0, 2)
    def _(i):
        rows = block_of(i, 512)
        there = pl.ds(pl.multiple_of(col + i * 512, 512), 512)
        grad = (dot_nt(low[...], weight[rows, :]) * slope[:, rows].astype(F32)).astype(BF16)
        grad_pre[:, there] = grad
        total[pl.ds(7, 1), there] = whole_sum(column_sum(grad.astype(F32)))


def back_through(left, cols, weight, total, first):
    @pl.loop(0, 2)
    def _(i):
        rows = block_of(i, 512)
        part = dot_nt(left[:, cols], weight[rows, :])
        total[:, rows] = part.astype(total.dtype) if first else total[:, rows] + part


def outer_box(turned, right, cols, dst):
    @pl.loop(0, 2)
    def _(i):
        part = dot_nn(turned[block_of(i, 512), :], right[:, cols])
        dst[block_of(i, 2)] = part.astype(BF16).reshape(2, 2, 2, 2, 32, 1024)


def attend_back(first, count, mixed, attended, grad_att, probs, probs_in, sems, grad_mixed):
    lane = lax.broadcasted_iota(jnp.int32, (1, 128), 1)

    def load(unit, slot):
        return pltpu.make_async_copy(probs_in.at[unit], probs.at[slot], sems.at[slot])

    load(first, 0).start()

    @pl.loop(0, count // 2)
    def _(i):
        for slot in range(2):
            unit = first + i * 2 + slot
            seq, pair = lax.div(unit, 8), lax.rem(unit, 8)
            start = pl.multiple_of(seq * 320, 64)
            rows = pl.ds(start, 320)
            col_q, col_k, col_v = (block_of(pair + 8 * n, 128) for n in range(3))
            load(unit, slot).wait()
            if slot == 0:
                load(unit + 1, 1).start()
            else:

                @pl.when(i + 1 < count // 2)
                def _():
                    load(unit + 1, 0).start()

            q = mixed[rows, col_q]
            k = mixed[pl.ds(start, LEN_PAD), col_k]
            v = mixed[pl.ds(start, LEN_PAD), col_v]
            grad_out = grad_att[rows, col_q]
            along = grad_out.astype(F32) * attended[rows, col_q].astype(F32)
            found = []
            for head in range(2):
                mine = lax.div(lane, 64) == head
                low = probs[slot, head]
                grad_p = dot_nt(grad_out * jnp.where(mine, 1.0, 0.0).astype(BF16), v)
                inner = jnp.sum(jnp.where(mine, along, 0.0), axis=-1, keepdims=True)
                grad_s = (low.astype(F32) * (grad_p - inner)).astype(BF16)
                found.append((dot_nn(grad_s, k), dot_tn(grad_s, q), dot_tn(low, grad_out)))
            grad_q, grad_k, grad_v = (
                jnp.where(lane < 64, a, b) for a, b in zip(found[0], found[1])
            )
            grad_mixed[rows, col_q] = (grad_q * 0.125).astype(BF16)
            grad_mixed[rows, col_k] = (grad_k[:320] * 0.125).astype(BF16)
            grad_mixed[rows, col_v] = grad_v[:320].astype(BF16)


def backward_kernel(*refs):
    (x_i, wa_i, wd_i, v4, normed1_i, mixed_i, attended_i, hidden_i, normed2_i, slope_i, probs_i, low_i, down_i, plain_i) = refs[:14]
    outs, small_out, input_grad_o = refs[14:18], refs[18], refs[19]
    refs = refs[20:]
    (weights, slope, low, normed2, grad_pre, total, hidden, branch, attended, grad_att, mixed, grad_mixed, probs, normed1, x, made, s4, s2, s1, part1, part2, part3, plain) = refs[:23]
    refs = refs[23:]
    per = 1 + 6 * len(BACK)
    slots = [refs[i * per : i * per + per] for i in range(3)]
    small_refs, refs = refs[3 * per : 3 * per + 8], refs[3 * per + 8 :]
    send, recv, own, weight_sems, slope_sems, probs_sems, in_sems, out_sem = refs
    sems = (send, recv, own)
    me, at = coords()

    def get(src, dst, number):
        copy = pltpu.make_async_copy(src, dst, in_sems.at[number])
        copy.start()
        return copy

    wanted = []
    for j in range(4):
        wanted += [wd_i.at[pl.ds(j * 1024, 1024), :], wa_i.at[4 + j]]
    wanted += [wa_i.at[3], wa_i.at[2], wa_i.at[1], wa_i.at[0]]
    weight_going, slope_going = {}, {}

    def get_weight(i):
        if i < len(wanted):
            weight_going[i] = pltpu.make_async_copy(wanted[i], weights.at[i % 3], weight_sems.at[i % 3])
            weight_going[i].start()

    def get_slope(j):
        if j < 4:
            slope_going[j] = pltpu.make_async_copy(slope_i.at[j], slope.at[j % 2], slope_sems.at[j % 2])
            slope_going[j].start()

    low_in = get(low_i, low, 0)
    get_weight(0)
    get_slope(0)
    get_weight(1)
    get_slope(1)
    get_weight(2)
    normed2_in = get(normed2_i, normed2, 1)
    hidden_in = get(hidden_i, hidden, 2)
    attended_in = get(attended_i, attended, 3)
    mixed_in = get(mixed_i, mixed, 4)
    normed1_in = get(normed1_i, normed1, 5)
    x_in = get(x_i, x, 6)
    plain_in = get(plain_i, plain, 7)
    greet(me, at)

    def row(vectors, i):
        return vectors.at[pl.ds(i, 1), :]

    def weight(i):
        weight_going[i].wait()
        return weights.at[i % 3]

    everything = slice(None)

    def task_start():
        for s in (s4, s2, s1):
            s[...] = jnp.zeros_like(s)
        low_in.wait()
        s4[pl.ds(5, 1), :] = whole_sum(column_sum(low[...].astype(F32)))

    def task_pre(j):
        w = weight(2 * j)
        slope_going[j].wait()
        slope_back(low, w, slope.at[j % 2], grad_pre, j * 1024, s1)
        get_weight(2 * j + 3)
        get_slope(j + 2)

    def task_through(j):
        back_through(grad_pre, pl.ds(j * 1024, 1024), weight(2 * j + 1), total, j == 0)
        get_weight(2 * j + 4)

    def task_up(j):
        if j == 0:
            normed2_in.wait()
        outer_box(normed2, grad_pre, pl.ds(j * 1024, 1024), made.at[(4 + j) % 3])

    def task_second():
        hidden_in.wait()
        norm_back(hidden, row(v4, 3), total, low, hidden, branch, part1, part2, part3)
        for i, part in ((3, part1), (4, part2), (2, part3)):
            s4[pl.ds(i, 1), :] = whole_sum(part[...])

    def task_att():
        back_through(branch, everything, weight(8), grad_att, True)
        get_weight(11)

    def task_out():
        attended_in.wait()
        outer_box(attended, branch, everything, made.at[8 % 3])

    def task_attend(first, count):
        if first == 0:
            mixed_in.wait()
            plain_in.wait()
        attend_back(first, count, mixed, plain, grad_att, probs, probs_i, probs_sems, grad_mixed)

    def task_mixed(j, k):
        if j == 2:
            normed1_in.wait()
        columns = pl.ds(j * 1024, 1024)
        outer_box(normed1, grad_mixed, columns, made.at[k % 3])
        if j != 1:
            s2[pl.ds(6, 1), pl.ds(0 if j == 0 else 1024, 1024)] = whole_sum(
                column_sum(grad_mixed[:, columns].astype(F32))
            )

    def task_through_mixed(j):
        back_through(grad_mixed, pl.ds(j * 1024, 1024), weight(11 - j), total, j == 2)

    input_going = []

    def task_first():
        x_in.wait()
        norm_back(x, row(v4, 0), total, hidden, None, x, part1, part2, None)
        for i, part in ((0, part1), (1, part2)):
            s4[pl.ds(i, 1), :] = whole_sum(part[...])
        copy = pltpu.make_async_copy(x, input_grad_o, out_sem.at[0])
        copy.start()
        input_going.append(copy)
        tiny = small_refs[0]
        for z in range(4):
            for y in range(2):
                for x_ in range(2):
                    for c in range(2):
                        d = ((z * 2 + y) * 2 + x_) * 2 + c
                        tiny[z, y, x_, c] = (
                            s4[:, d // 4 * 128 : d // 4 * 128 + 128]
                            + s2[:, d // 2 * 128 : d // 2 * 128 + 128]
                            + s1[:, d * 128 : d * 128 + 128]
                        )

    tasks = {
        0: [(task_start,), (task_pre, 0), (task_through, 0), (task_pre, 1)],
        1: [(task_through, 1), (task_pre, 2), (task_through, 2)],
        2: [(task_pre, 3), (task_through, 3), (task_second,)],
        3: [(task_up, 0), (task_att,), (task_attend, 0, 2)],
        4: [(task_up, 1), (task_attend, 2, 4)],
        5: [(task_up, 2), (task_attend, 6, 2)],
        6: [(task_up, 3), (task_attend, 8, 4)],
        7: [(task_out,), (task_attend, 12, 2)],
        8: [(task_attend, 14, 2), (task_mixed, 2, 9)],
        9: [(task_mixed, 1, 10), (task_through_mixed, 2)],
        10: [(task_mixed, 0, 11), (task_through_mixed, 1)],
        11: [(task_through_mixed, 0), (task_first,)],
    }
    goals = [(3, r, 0) for r in (0, 32, 64, 96)] + [(2, 0, c) for c in (0, 1024, 2048, 3072)]
    goals += [(1, 0, 0), (0, 0, 2048), (0, 0, 1024), (0, 0, 0)]
    flows = {}
    for tick in range(12 + STAGES + 2):
        for stage in (1, 5, 2, 3, 4, 0):
            k = tick - stage
            if 0 <= k < 12:
                if stage == 0:
                    which, r, c = goals[k]
                    out = outs[which].at[pl.ds(r, ROWS), pl.ds(c, WIDE)]
                    source = down_i.at[:, :, :, :, pl.ds(r, ROWS), :] if which == 3 else None
                    flows[k] = Flow(made.at[k % 3], source, out, BACK, slots[k % 3], k % 8, sems, me, at)
                    flows[k].start()
                else:
                    flows[k].step(stage)
        if 12 <= tick <= 13 + STAGES:
            if tick == 12:
                tiny = Flow(small_refs[0], None, small_out, SMALL_BACK, small_refs[1:], 8, sems, me, at)
                tiny.start()
            else:
                tiny.step(tick - 12)
        for task, *args in tasks.get(tick, ()):
            task(*args)
    for copy in input_going:
        copy.wait()


def backward(*args):
    anywhere = pl.BlockSpec(memory_space=pl.ANY)
    inside = pl.BlockSpec(memory_space=pltpu.VMEM)
    flat, turned = (640, 1024), (1024, 640)
    scratch = [
        ((3, 1024, 1024), BF16),
        ((2, 640, 1024), BF16),
        (flat, BF16),
        (turned, BF16),
        ((640, 4096), BF16),
        (flat, F32),
        (flat, F32),
        (flat, BF16),
        (turned, BF16),
        (flat, BF16),
        ((704, 3072), BF16),
        ((640, 3072), BF16),
        ((2, 2, 320, LEN_PAD), BF16),
        (turned, BF16),
        (flat, BF16),
        ((3, 4, 2, 2, 2, 32, 1024), BF16),
        ((8, 1024), F32),
        ((8, 2048), F32),
        ((8, 4096), F32),
    ] + [((8, 1024), F32)] * 3 + [(flat, BF16)]
    scratch += flow_buffers(BACK, ROWS, WIDE, BF16) * 3
    scratch += [((4, 2, 2, 2, 8, 128), F32)] + flow_buffers(SMALL_BACK, 8, 128, F32)
    sums = [(32, 3072), (32, 1024), (32, 4096), (128, 1024), (8, 128)]
    dma = pltpu.SemaphoreType.DMA
    return pl.pallas_call(
        backward_kernel,
        out_shape=[jax.ShapeDtypeStruct(s, F32) for s in sums]
        + [jax.ShapeDtypeStruct(flat, BF16)],
        in_specs=[anywhere] * 3 + [inside] + [anywhere] * 10,
        out_specs=[inside] * 5 + [anywhere],
        scratch_shapes=[pltpu.VMEM(s, d) for s, d in scratch]
        + [dma((9, COPIES)), dma((9, COPIES)), dma((9,)), dma((3,)), dma((2,)), dma((2,)), dma((8,)), dma((1,))],
        compiler_params=pltpu.CompilerParams(
            collective_id=1, has_side_effects=True, vmem_limit_bytes=63 << 20
        ),
        name="backward_sum",
    )(*args)


def finish_kernel(*refs):
    small, refs = refs[0], refs[1:]
    arrays, narrow, outs, refs = refs[:6], refs[6:14], refs[14:20], refs[20:]
    blocks, refs = refs[:6], refs[6:]
    into = [pltpu.make_async_copy(a, block, refs[0].at[i]) for i, (a, block) in enumerate(zip(arrays, blocks))]
    back = [pltpu.make_async_copy(block, o, refs[1].at[i]) for i, (o, block) in enumerate(zip(outs, blocks))]
    for copy in into:
        copy.start()
    me = lax.axis_index("dp")
    fours = pltpu.roll(small[...], 128 - lax.rem(me, 4) * 32, 1)
    for i in range(6):
        narrow[i][...] = fours[i : i + 1, :32]
    twos = pltpu.roll(small[...], 128 - lax.rem(me, 2) * 64, 1)
    narrow[6][...] = twos[6:7, :64]
    narrow[7][...] = small[7:8, :]
    for first, second in zip(into, back):
        first.wait()
        second.start()
    for copy in back:
        copy.wait()


def finish(total, *arrays):
    anywhere = pl.BlockSpec(memory_space=pl.ANY)
    inside = pl.BlockSpec(memory_space=pltpu.VMEM)
    found = pl.pallas_call(
        lambda *refs: finish_kernel(*refs[:7], *refs[7:15], *refs[15:]),
        out_shape=[jax.ShapeDtypeStruct((1, n), F32) for n in (32,) * 6 + (64, 128)]
        + [jax.ShapeDtypeStruct(a.shape, a.dtype) for a in arrays],
        in_specs=[inside] + [anywhere] * 6,
        out_specs=[inside] * 8 + [anywhere] * 6,
        scratch_shapes=[pltpu.VMEM(a.shape, a.dtype) for a in arrays]
        + [pltpu.SemaphoreType.DMA((len(arrays),))] * 2,
        compiler_params=pltpu.CompilerParams(vmem_limit_bytes=63 << 20),
        name="finish",
    )(total, *arrays)
    return [a.reshape(-1) for a in found[:8]], found[8:]


def pack_weights(weights):
    me = lax.axis_index("dp")
    lane = jnp.arange(128, dtype=jnp.int32)[None, :]
    narrow = jnp.tile(jnp.stack([weights[i] for i in NARROW]), (1, 4))
    rows = [
        jnp.where(lane // 32 == me % 4, narrow, 0),
        jnp.where(lane // 64 == me % 2, jnp.tile(weights[3][None], (1, 2)), 0),
        weights[9][None],
    ]
    return jnp.concatenate(rows, axis=0).astype(F32)


def on_box(inputs, lengths, assignment, *rest):
    weights, cotangent = rest[:12], rest[12]
    me = lax.axis_index("dp")
    x = inputs.reshape(640, 1024)
    cot = cotangent.reshape(640, 1024)
    small = pack_weights(weights)
    *kept, plain_att, result = forward(
        x, cot, lengths, assignment, [weights[i] for i in WEIGHTS], small
    )
    kept[0] = kept[0].reshape(8, 1024, 1024)
    kept[1] = kept[1].reshape(4096, 1024)
    kept[-1] = kept[-1].reshape(4, 2, 2, 2, 128, 1024)
    *sums, total, input_grad = backward(x, *kept, plain_att)
    narrow, (result, input_grad, *sums) = finish(total, result, input_grad, *sums)
    found = [None] * 12
    for row, i in enumerate((*NARROW, 3, 9)):
        found[i] = narrow[row]
    for i, s in zip(WEIGHTS, sums):
        found[i] = s
    return (result.reshape(inputs.shape), input_grad.reshape(inputs.shape), *found)


def plain(
    inputs,
    lengths,
    assignment,
    norm1_gain,
    norm1_bias,
    qkv_weight,
    qv_bias,
    out_weight,
    out_bias,
    norm2_gain,
    norm2_bias,
    up_weight,
    up_bias,
    down_weight,
    down_bias,
    cotangent,
):
    gathered = (
        lax.all_gather(norm1_gain, "dp", axis=0, tiled=True),
        lax.all_gather(norm1_bias, "dp", axis=0, tiled=True),
        lax.all_gather(qkv_weight, "dp", axis=0, tiled=True),
        lax.all_gather(qv_bias, "dp", axis=0, tiled=True),
        lax.all_gather(out_weight, "dp", axis=0, tiled=True),
        lax.all_gather(out_bias, "dp", axis=0, tiled=True),
        lax.all_gather(norm2_gain, "dp", axis=0, tiled=True),
        lax.all_gather(norm2_bias, "dp", axis=0, tiled=True),
        lax.all_gather(up_weight, "dp", axis=0, tiled=True),
        lax.all_gather(up_bias, "dp", axis=0, tiled=True),
        lax.all_gather(down_weight, "dp", axis=0, tiled=True),
        lax.all_gather(down_bias, "dp", axis=0, tiled=True),
    )
    seq_count, tok_count, model_width = inputs.shape
    rows_all = seq_count * tok_count
    split_shape = (seq_count, tok_count, HEADS, HEAD)
    head_scale = HEAD ** (-0.5)
    matches = assignment[:, None] == jnp.arange(lengths.shape[0], dtype=jnp.int32)[None, :]
    kept_len = jnp.sum(jnp.where(matches, lengths[None, :], 0), axis=1)
    key_mask = jnp.arange(tok_count, dtype=jnp.int32)[None, :] < kept_len[:, None]
    row_mask = key_mask.reshape(rows_all, 1).astype(jnp.float32)
    gain_first = gathered[0].astype(jnp.float32)
    shift_first = gathered[1].astype(jnp.float32)
    qv_full = gathered[3].astype(jnp.float32)
    proj_shift = gathered[5].astype(jnp.float32)
    gain_second = gathered[6].astype(jnp.float32)
    shift_second = gathered[7].astype(jnp.float32)
    up_shift = gathered[9].astype(jnp.float32)
    down_shift = gathered[11].astype(jnp.float32)
    inputs_flat = inputs.reshape(rows_all, model_width).astype(jnp.float32)
    normed_first, first_back = jax.vjp(layer_norm, inputs_flat, gain_first, shift_first)
    normed_low = normed_first.astype(jnp.bfloat16)
    full_bias = jnp.concatenate(
        [qv_full[:model_width], jnp.zeros((model_width,), jnp.float32), qv_full[model_width:]]
    )
    mixed_qkv = (
        jnp.dot(normed_low, gathered[2], preferred_element_type=jnp.float32) + full_bias
    ).astype(jnp.bfloat16)
    queries = mixed_qkv[:, :model_width].reshape(split_shape)
    keys_all = mixed_qkv[:, model_width : 2 * model_width].reshape(split_shape)
    values_all = mixed_qkv[:, 2 * model_width :].reshape(split_shape)
    scores = (
        jnp.einsum("bqhd,bkhd->bhqk", queries, keys_all, preferred_element_type=jnp.float32)
        * head_scale
    )
    scores = jnp.where(key_mask[:, None, None, :], scores, masked_score)
    row_max = jnp.max(scores, axis=-1, keepdims=True)
    exponent = jnp.exp(scores - row_max)
    row_total = jnp.sum(exponent, axis=-1, keepdims=True)
    softmax_probs = exponent / row_total
    log_total = row_max + jnp.log(row_total)
    attended = jnp.einsum(
        "bhqk,bkhd->bqhd",
        softmax_probs.astype(jnp.bfloat16),
        values_all,
        preferred_element_type=jnp.float32,
    )
    attended = attended.reshape(rows_all, model_width).astype(jnp.bfloat16)
    hidden = inputs_flat + (
        jnp.dot(attended, gathered[4], preferred_element_type=jnp.float32) + proj_shift
    )
    normed_second, second_back = jax.vjp(layer_norm, hidden, gain_second, shift_second)
    second_low = normed_second.astype(jnp.bfloat16)
    pre_act = jnp.dot(second_low, gathered[8], preferred_element_type=jnp.float32) + up_shift
    activation, gelu_back = jax.vjp(gelu_exact, pre_act)
    act_low = activation.astype(jnp.bfloat16)
    output_rows = row_mask * (
        hidden + (jnp.dot(act_low, gathered[10], preferred_element_type=jnp.float32) + down_shift)
    )
    result = output_rows.reshape(inputs.shape).astype(jnp.bfloat16)
    grad_rows = cotangent.reshape(rows_all, model_width).astype(jnp.float32) * row_mask
    grad_low = grad_rows.astype(jnp.bfloat16)
    down_grad = contract_rows(act_low, grad_low)
    down_bias_grad = jnp.sum(grad_low.astype(jnp.float32), axis=0)
    grad_pre = gelu_back(contract_cols(grad_low, gathered[10]))[0].astype(jnp.bfloat16)
    up_grad = contract_rows(second_low, grad_pre)
    up_bias_grad = jnp.sum(grad_pre.astype(jnp.float32), axis=0)
    grad_second, gain2_grad, shift2_grad = second_back(contract_cols(grad_pre, gathered[8]))
    grad_hidden = grad_rows + grad_second
    branch_low = grad_hidden.astype(jnp.bfloat16)
    proj_grad = contract_rows(attended, branch_low)
    proj_bias_grad = jnp.sum(branch_low.astype(jnp.float32), axis=0)
    grad_att = contract_cols(branch_low, gathered[4]).astype(jnp.bfloat16).reshape(split_shape)
    scores_again = (
        jnp.einsum("bqhd,bkhd->bhqk", queries, keys_all, preferred_element_type=jnp.float32)
        * head_scale
    )
    scores_again = jnp.where(key_mask[:, None, None, :], scores_again, masked_score)
    probs_again = jnp.exp(scores_again - log_total)
    probs_low = probs_again.astype(jnp.bfloat16)
    grad_probs = jnp.einsum(
        "bqhd,bkhd->bhqk", grad_att, values_all, preferred_element_type=jnp.float32
    )
    grad_values = jnp.einsum(
        "bhqk,bqhd->bkhd", probs_low, grad_att, preferred_element_type=jnp.float32
    )
    inner_sum = jnp.sum(probs_again * grad_probs, axis=-1, keepdims=True)
    grad_scores = (probs_again * (grad_probs - inner_sum)).astype(jnp.bfloat16)
    grad_queries = (
        jnp.einsum("bhqk,bkhd->bqhd", grad_scores, keys_all, preferred_element_type=jnp.float32)
        * head_scale
    )
    grad_keys = (
        jnp.einsum("bhqk,bqhd->bkhd", grad_scores, queries, preferred_element_type=jnp.float32)
        * head_scale
    )
    grad_mixed = jnp.concatenate(
        [
            grad_queries.reshape(rows_all, model_width),
            grad_keys.reshape(rows_all, model_width),
            grad_values.reshape(rows_all, model_width),
        ],
        axis=1,
    ).astype(jnp.bfloat16)
    qkv_grad = contract_rows(normed_low, grad_mixed)
    column_sums = jnp.sum(grad_mixed.astype(jnp.float32), axis=0)
    qv_grad = jnp.concatenate([column_sums[:model_width], column_sums[2 * model_width :]])
    grad_first, gain1_grad, shift1_grad = first_back(contract_cols(grad_mixed, gathered[2]))
    input_grad = (grad_hidden + grad_first).reshape(inputs.shape).astype(jnp.bfloat16)
    all_sums = (
        lax.psum_scatter(gain1_grad, "dp", scatter_dimension=0, tiled=True),
        lax.psum_scatter(shift1_grad, "dp", scatter_dimension=0, tiled=True),
        lax.psum_scatter(qkv_grad, "dp", scatter_dimension=0, tiled=True),
        lax.psum_scatter(qv_grad, "dp", scatter_dimension=0, tiled=True),
        lax.psum_scatter(proj_grad, "dp", scatter_dimension=0, tiled=True),
        lax.psum_scatter(proj_bias_grad, "dp", scatter_dimension=0, tiled=True),
        lax.psum_scatter(gain2_grad, "dp", scatter_dimension=0, tiled=True),
        lax.psum_scatter(shift2_grad, "dp", scatter_dimension=0, tiled=True),
        lax.psum_scatter(up_grad, "dp", scatter_dimension=0, tiled=True),
        lax.psum_scatter(up_bias_grad, "dp", scatter_dimension=0, tiled=True),
        lax.psum_scatter(down_grad, "dp", scatter_dimension=0, tiled=True),
        lax.psum_scatter(down_bias_grad, "dp", scatter_dimension=0, tiled=True),
    )
    attn_sums = all_sums[:6]
    mlp_sums = all_sums[6:]
    return (
        result,
        input_grad,
        attn_sums[0],
        attn_sums[1],
        attn_sums[2],
        attn_sums[3],
        attn_sums[4],
        attn_sums[5],
        mlp_sums[0],
        mlp_sums[1],
        mlp_sums[2],
        mlp_sums[3],
        mlp_sums[4],
        mlp_sums[5],
    )


def local(*args):
    return on_box(*args) if lax.axis_size("dp") == 32 else plain(*args)


def solution(mesh):
    placed = (
        P("dp", None, None),
        P(),
        P("dp"),
        P("dp"),
        P("dp"),
        P("dp", None),
        P("dp"),
        P("dp", None),
        P("dp"),
        P("dp"),
        P("dp"),
        P("dp", None),
        P("dp"),
        P("dp", None),
        P("dp"),
        P("dp", None, None),
    )
    return jax.shard_map(
        local,
        mesh=mesh,
        in_specs=placed,
        out_specs=(
            P("dp", None, None),
            P("dp", None, None),
            P("dp"),
            P("dp"),
            P("dp", None),
            P("dp"),
            P("dp", None),
            P("dp"),
            P("dp"),
            P("dp"),
            P("dp", None),
            P("dp"),
            P("dp", None),
            P("dp"),
        ),
        check_vma=False,
    )
```

```python
import jax
import jax.numpy as jnp
from jax import lax
from jax.experimental import pallas as pl
from jax.experimental.pallas import tpu as pltpu
from jax.sharding import PartitionSpec as P

HEADS = 16
HEAD = 64


eps = 1e-06
masked_score = -1000000000.0


def layer_norm(values, norm_gain, norm_shift):
    average = jnp.mean(values, axis=-1, keepdims=True)
    centered = values - average
    variance = jnp.mean(centered * centered, axis=-1, keepdims=True)
    return centered * lax.rsqrt(variance + eps) * norm_gain + norm_shift


def gelu_exact(values):
    return jax.nn.gelu(values, approximate=False)


def contract_rows(left, right):
    return lax.dot_general(
        left, right, (((0,), (0,)), ((), ())), preferred_element_type=jnp.float32
    )


def contract_cols(left, right):
    return lax.dot_general(
        left, right, (((1,), (1,)), ((), ())), preferred_element_type=jnp.float32
    )


BF16 = jnp.bfloat16
F32 = jnp.float32
MESH = pl.DeviceIdType.MESH
STRIDE = {"z": 8, "y": 4, "x": 2}
ROWS = 32
WIDE = 1024
STAGES = 4
PARTS = (
    ("zZyx", 0, 16, 0, 384),
    ("zZxy", 16, 16, 0, 384),
    ("xzZy", 0, 16, 384, 640),
    ("yzZx", 16, 16, 384, 640),
)
TALL = (
    ("zZyx", 0, 48, 0, 128),
    ("zZxy", 0, 48, 128, 128),
    ("xzZy", 48, 80, 0, 128),
    ("yzZx", 48, 80, 128, 128),
)
COPIES = 6 * len(PARTS) + 1
CHUNKS = (
    tuple((0, 0, c) for c in (0, 1024, 2048))
    + ((1, 0, 0),)
    + tuple((2, 0, c) for c in (0, 1024, 2048, 3072))
)


def coords():
    me = lax.axis_index("dp")
    at = {
        "z": lax.div(me, 8),
        "y": lax.rem(lax.div(me, 4), 2),
        "x": lax.rem(lax.div(me, 2), 2),
        "c": lax.rem(me, 2),
    }
    return me, at


def sibling(me, at):
    return me + 1 - 2 * at["c"]


class Hop:
    def __init__(self, copy, sends=None, hears=None):
        self.copy, self.sends, self.hears = copy, sends, hears

    def start(self):
        if self.sends is None:
            self.copy.start()
        else:
            pl.when(self.sends)(self.copy.start)

    def wait(self):
        if self.sends is None:
            self.copy.wait()
        else:
            pl.when(self.sends)(self.copy.wait_send)
            pl.when(self.hears)(self.copy.wait_recv)


def inner(at):
    return lax.div(at["z"] + 1, 2) == 1


def far(at):
    return 3 * (1 - lax.div(at["z"], 2))


def hops(me, at, dim):
    z = at["z"]
    if dim == "z":
        found = []
        for k in (1, 2, 3):
            there = lax.rem(z + k, 4)
            when = {1: (z < 3, z > 0), 2: (None, None), 3: (z > 0, z < 3)}[k]
            found.append((there, me + (there - z) * 8, *when))
        return found
    if dim == "Z":
        return [(far(at), me + 8 - 16 * lax.rem(z, 2), inner(at), jnp.logical_not(inner(at)))]
    there = 1 - at[dim]
    return [(there, me + (there - at[dim]) * STRIDE[dim], None, None)]


def count_of(dim):
    return 3 if dim == "z" else 1


def greet(me, at):
    barrier = pltpu.get_barrier_semaphore()
    devices = [sibling(me, at)]
    for dim in "yx":
        devices += [hop[1] for hop in hops(me, at, dim)]
    for k in (1, 2, 3):
        devices.append(me + (lax.rem(at["z"] + k, 4) - at["z"]) * 8)
    for device in devices:
        pl.semaphore_signal(barrier, inc=1, device_id=(device,), device_id_type=MESH)
    pl.semaphore_wait(barrier, len(devices))


def remote(src, dst, sems, slot, number, device):
    return pltpu.make_async_remote_copy(
        src_ref=src,
        dst_ref=dst,
        send_sem=sems[0].at[slot, number],
        recv_sem=sems[1].at[slot, number],
        device_id=(device,),
        device_id_type=MESH,
    )


def held(order, stage, at):
    index = []
    for dim in "zyx":
        if dim == "z" and order[stage] == "Z":
            index.append(far(at))
        else:
            done = "Z" if dim == "z" else dim
            index.append(slice(None) if done in order[:stage] else at[dim])
    return tuple(index)


def gather_stage(base, parts, stage, me, at, sems, slot, source=None):
    if stage == STAGES:
        block = base.at[:, :, :, at["c"]]
        return [Hop(remote(block, block, sems, slot, COPIES - 1, sibling(me, at)))]
    number, copies = 0, []
    for order, row, rows, col, columns in parts:
        here = (pl.ds(row, rows), pl.ds(col, columns))
        for s in range(STAGES):
            for _, device, sends, hears in hops(me, at, order[s]):
                if s == stage:
                    block = base.at[held(order, stage, at) + (at["c"],) + here]
                    src = source.at[here] if source is not None and stage == 0 else block
                    copies.append(Hop(remote(src, block, sems, slot, number, device), sends, hears))
                number += 1
    return copies


SMALL = (("zZyx", 0, 8, 0, 128),)


def remaining(order, stage):
    left = [dim for dim in "zyx" if dim not in order[:stage]]
    return tuple({"z": 4, "y": 2, "x": 2}[dim] for dim in left)


def pick(order, stage, dim, index):
    return tuple(index if d == dim.lower() else slice(None) for d in "zyx" if d not in order[:stage])


BACK = tuple((part[0][::-1], *part[1:]) for part in PARTS)
SMALL_BACK = tuple((part[0][::-1], *part[1:]) for part in SMALL)


def add_up(dst, terms, lead):
    loops = lead[: max(len(lead) - 1, 0)] if len(lead) > 1 else ()
    count = 1
    for n in loops:
        count *= n

    def body(i, carry):
        index = []
        for n in loops[::-1]:
            index.append(lax.rem(i, n))
            i = lax.div(i, n)
        index = tuple(index[::-1]) + (slice(None),) * (len(lead) - len(loops) + 2)
        total = terms[0][index].astype(F32)
        for term in terms[1:]:
            total = total + term[index].astype(F32)
        dst[index] = total.astype(dst.dtype)
        return carry

    if count == 1:
        body(0, 0)
    else:
        lax.fori_loop(0, count, body, 0)


class Flow:
    def __init__(self, made, source, out, parts, from_core, rest, slot, sems, me, at):
        self.made, self.source, self.out, self.parts = made, source, out, parts
        self.from_core = from_core
        self.arrived, self.totals = [], []
        for order, *_ in parts:
            self.arrived.append(rest[:4])
            self.totals.append(dict(zip([s for s in range(3) if order[s] != "Z"], rest[4:6])))
            rest = rest[6:]
        self.slot, self.sems, self.me, self.at = slot, sems, me, at
        self.own = made.at[:, :, :, at["c"]]

    def start(self):
        there = 1 - self.at["c"]
        source = self.made if self.source is None else self.source
        self.going = [
            remote(
                source.at[:, :, :, there],
                self.from_core,
                self.sems,
                self.slot,
                COPIES - 1,
                sibling(self.me, self.at),
            )
        ]
        if self.source is not None:
            self.going.append(
                pltpu.make_async_copy(source.at[:, :, :, self.at["c"]], self.own, self.sems[2].at[self.slot])
            )
        for copy in self.going:
            copy.start()

    def sum_before(self, part, stage):
        order, row, rows, col, columns = self.parts[part]
        done = [s for s in range(stage) if s in self.totals[part]]
        if not done:
            return self.own.at[:, :, :, pl.ds(row, rows), pl.ds(col, columns)]
        return self.totals[part][done[-1]]

    def take(self, part, stage):
        order, row, rows, col, columns = self.parts[part]
        s = stage - 2
        dim, arrived = order[s], self.arrived[part][s]
        before = self.sum_before(part, s)
        if dim == "Z":
            index = pick(order, s, "z", far(self.at))

            @pl.when(inner(self.at))
            def _():
                add_up(before.at[index], [before.at[index], arrived.at[0]], remaining(order, s)[1:])

            return
        if stage == STAGES + 1:
            total = self.out.at[pl.ds(row, rows), pl.ds(col, columns)]
        else:
            total = self.totals[part][s]
        mine = before.at[pick(order, s, dim, self.at[dim])]
        left = remaining(order, s + 1)
        if dim != "z":
            add_up(total, [mine, arrived.at[0]], left)
            return
        z = self.at["z"]
        for when, came in ((z == 0, (1, 2)), (inner(self.at), (0, 1, 2)), (z == 3, (0, 1))):

            @pl.when(when)
            def _(came=came):
                add_up(total, [mine] + [arrived.at[i] for i in came], left)

    def step(self, stage):
        for copy in self.going:
            copy.wait()
        if stage == 1:
            add_up(self.own, [self.own, self.from_core], (4, 2, 2))
        else:
            for part in range(len(self.parts)):
                self.take(part, stage)
        self.going, number = [], 0
        for part, (order, row, rows, col, columns) in enumerate(self.parts):
            for s in range(STAGES):
                if s + 1 == stage:
                    before = self.sum_before(part, s)
                    for i, (there, device, sends, hears) in enumerate(hops(self.me, self.at, order[s])):
                        if order[s] == "Z":
                            sends, hears = hears, sends
                        src = before.at[pick(order, s, order[s], there)]
                        copy = remote(src, self.arrived[part][s].at[i], self.sems, self.slot, number + i, device)
                        self.going.append(Hop(copy, sends, hears))
                number += count_of(order[s])
        for copy in self.going:
            copy.start()


def flow_buffers(parts, dtype):
    shapes = []
    for order, _, high, _, wide in parts:
        totals = []
        for s in range(STAGES):
            if order[s] == "Z":
                left = remaining(order, s)[1:]
            else:
                left = remaining(order, s + 1)
                if s < 3:
                    totals.append((left + (high, wide), dtype))
            shapes.append(((count_of(order[s]),) + left + (high, wide), dtype))
        shapes += totals
    return shapes


EPS = 1e-06
MASKED = -1000000000.0
LEN_PAD = 384


def dot_nn(a, b):
    return jnp.dot(a, b, preferred_element_type=F32)


def dot_nt(a, b):
    return lax.dot_general(a, b, (((1,), (1,)), ((), ())), preferred_element_type=F32)


def dot_tn(a, b):
    return lax.dot_general(a, b, (((0,), (0,)), ((), ())), preferred_element_type=F32)


def block_of(index, size):
    return pl.ds(pl.multiple_of(index * size, size), size)


def spread_vectors(smalls, v4, v2, v1):
    for z in range(4):
        for y in range(2):
            four = None
            for x in range(2):
                two = None
                for c in range(2):
                    one = smalls[z, y, x, c]
                    d = ((z * 2 + y) * 2 + x) * 2 + c
                    v1[:, d * 128 : d * 128 + 128] = one
                    two = one if two is None else two + one
                d = (z * 2 + y) * 2 + x
                v2[:, d * 128 : d * 128 + 128] = two
                four = two if four is None else four + two
            d = z * 2 + y
            v4[:, d * 128 : d * 128 + 128] = four


def norm_rows(src, gain, shift, dst):
    @pl.loop(0, src.shape[0] // 64)
    def _(i):
        rows = block_of(i, 64)
        values = src[rows, :].astype(F32)
        centered = values - jnp.mean(values, axis=-1, keepdims=True)
        variance = jnp.mean(centered * centered, axis=-1, keepdims=True)
        normed = centered * lax.rsqrt(variance + EPS)
        dst[rows, :] = (normed * gain[...] + shift[...]).astype(BF16)


def project(normed, weight, shift, dst, col):
    @pl.loop(0, 2)
    def _(i):
        columns = block_of(i, 512)
        mixed = dot_nn(normed[...], weight[:, :, :, :, :, columns].reshape(1024, 512))
        if shift is not None:
            mixed = mixed + shift[:, columns]
        dst[pl.ds(0, 640), pl.ds(pl.multiple_of(col + i * 512, 512), 512)] = mixed.astype(BF16)


def attend(first, count, mixed, kept_len, attended, probs, probs_out, sems):
    lane = lax.broadcasted_iota(jnp.int32, (1, 128), 1)

    def out_copy(unit, slot):
        return pltpu.make_async_copy(probs.at[slot], probs_out.at[unit], sems.at[slot])

    @pl.loop(0, count // 2)
    def _(i):
        for slot in range(2):
            unit = first + i * 2 + slot
            seq, pair = lax.div(unit, 8), lax.rem(unit, 8)
            start = pl.multiple_of(seq * 320, 64)
            columns = block_of(pair, 128)
            q = mixed[pl.ds(start, 320), columns]
            k = mixed[pl.ds(start, LEN_PAD), block_of(pair + 8, 128)]
            v = mixed[pl.ds(start, LEN_PAD), block_of(pair + 16, 128)]
            kept = lax.broadcasted_iota(jnp.int32, (1, LEN_PAD), 1) < kept_len(seq)

            @pl.when(i > 0)
            def _():
                out_copy(unit, slot).wait()

            found = []
            for head in range(2):
                scale = jnp.where(lax.div(lane, 64) == head, 0.125, 0.0).astype(BF16)
                scores = jnp.where(kept, dot_nt(q * scale, k), MASKED)
                exponent = jnp.exp(scores - jnp.max(scores, axis=-1, keepdims=True))
                total = jnp.sum(exponent, axis=-1, keepdims=True)
                low = (exponent * (1.0 / total)).astype(BF16)
                probs[slot, head] = low
                found.append(dot_nn(low, v))
            attended[pl.ds(start, 320), columns] = jnp.where(
                lane < 64, found[0], found[1]
            ).astype(BF16)
            out_copy(unit, slot).start()

    for slot in range(2):
        out_copy(0, slot).wait()


def branch_out(attended, weight, shift, x, hidden):
    @pl.loop(0, 2)
    def _(i):
        columns = block_of(i, 512)
        branch = dot_nn(attended[...], weight[:, :, :, :, :, columns].reshape(1024, 512))
        hidden[:, columns] = x[:, columns].astype(F32) + (branch + shift[:, columns])


def feed_up(normed, weight, shift, act, slope, col):
    @pl.loop(0, 2)
    def _(i):
        columns = block_of(i, 512)
        pre = dot_nn(normed[...], weight[:, :, :, :, :, columns].reshape(1024, 512))
        pre = pre + shift[:, pl.ds(pl.multiple_of(col + i * 512, 512), 512)]
        below = 0.5 + 0.5 * lax.erf(pre * 0.7071067811865476)
        act[:, columns] = (pre * below).astype(BF16)
        density = jnp.exp(pre * pre * -0.5) * 0.3989422804014327
        slope[:, columns] = (below + pre * density).astype(BF16)


def outer(left, right, dst):
    @pl.loop(0, 2)
    def _(i):
        part = dot_tn(left[:, block_of(i, 512)], right[...])
        dst[i] = part.astype(BF16).reshape(2, 2, 4, 32, 1024)


def turn(src, dst):
    @pl.loop(0, 4)
    def _(i):
        rows = block_of(i, 256)
        dst[rows, :] = src[:, rows].T


def tall(block):
    parts = [block[..., i * 256 : i * 256 + 256] for i in range(4)]
    rows = jnp.stack(parts, axis=block.ndim - 2)
    return rows.reshape(-1, 256)


def feed_down(acts, page, shift, hidden, row_mask, result, c):
    columns = pl.ds(c * 256, 256)
    branch = dot_nn(acts[0][...], tall(page[0]))
    for z in range(1, 4):
        branch = branch + dot_nn(acts[z][...], tall(page[z]))
    whole = hidden[:, columns] + (branch + shift[:, columns])
    result[:, columns] = (whole * row_mask[...]).astype(BF16)


def column_sum(values):
    return jnp.sum(values.reshape(values.shape[0] // 8, 8, values.shape[1]), axis=0)


def norm_back(src, gain, grads, base, dst, by_scale, by_shift, by_low):
    for total in (by_scale, by_shift, by_low):
        if total is not None:
            total[...] = jnp.zeros_like(total)

    @pl.loop(0, 640 // 64)
    def _(i):
        rows = block_of(i, 64)
        values = src[rows, :].astype(F32)
        centered = values - jnp.mean(values, axis=-1, keepdims=True)
        inverse = lax.rsqrt(jnp.mean(centered * centered, axis=-1, keepdims=True) + EPS)
        normed = centered * inverse
        g = grads[rows, :]
        scaled = g * gain[...]
        along = jnp.mean(scaled * normed, axis=-1, keepdims=True)
        back = inverse * (scaled - jnp.mean(scaled, axis=-1, keepdims=True) - normed * along)
        whole = base[rows, :].astype(F32) + back
        rounded = whole.astype(BF16)
        dst[rows, :] = rounded
        by_scale[...] += column_sum(g * normed)
        by_shift[...] += column_sum(g)
        if by_low is not None:
            by_low[...] += column_sum(rounded.astype(F32))


def whole_sum(part):
    return jnp.sum(part, axis=0, keepdims=True)


def slope_back(low, pages, j, slope, grad_pre, total):
    @pl.loop(0, 2)
    def _(i):
        columns = block_of(i, 512)
        weight = jnp.concatenate([tall(page[j, i]) for page in pages], axis=1)
        grad = (dot_nt(low[...], weight) * slope[:, columns].astype(F32)).astype(BF16)
        grad_pre[:, columns] = grad
        there = pl.ds(pl.multiple_of(j * 1024 + i * 512, 512), 512)
        total[pl.ds(7, 1), there] = whole_sum(column_sum(grad.astype(F32)))


def back_through(left, page, total, first):
    @pl.loop(0, 2)
    def _(i):
        rows = block_of(i, 512)
        part = dot_nt(left[...], page[block_of(i, 2)].reshape(512, 1024))
        total[:, rows] = part.astype(total.dtype) if first else total[:, rows] + part


def outer_box(turned, right, dst):
    @pl.loop(0, 2)
    def _(i):
        part = dot_nn(turned[block_of(i, 512), :], right[...])
        dst[block_of(i, 2)] = part.astype(BF16).reshape(2, 2, 2, 2, 32, 1024)


def attend_back(first, count, mixed, attended, grad_att, probs, probs_in, sems, grads):
    lane = lax.broadcasted_iota(jnp.int32, (1, 128), 1)

    def load(unit, slot):
        return pltpu.make_async_copy(probs_in.at[unit], probs.at[slot], sems.at[slot])

    load(first, 0).start()

    @pl.loop(0, count // 2)
    def _(i):
        for slot in range(2):
            unit = first + i * 2 + slot
            seq, pair = lax.div(unit, 8), lax.rem(unit, 8)
            start = pl.multiple_of(seq * 320, 64)
            rows = pl.ds(start, 320)
            col_q, col_k, col_v = (block_of(pair + 8 * n, 128) for n in range(3))
            load(unit, slot).wait()
            if slot == 0:
                load(unit + 1, 1).start()
            else:

                @pl.when(i + 1 < count // 2)
                def _():
                    load(unit + 1, 0).start()

            q = mixed[rows, col_q]
            k = mixed[pl.ds(start, LEN_PAD), col_k]
            v = mixed[pl.ds(start, LEN_PAD), col_v]
            grad_out = grad_att[rows, col_q]
            along = grad_out.astype(F32) * attended[rows, col_q].astype(F32)
            found = []
            for head in range(2):
                mine = lax.div(lane, 64) == head
                low = probs[slot, head]
                grad_p = dot_nt(grad_out * jnp.where(mine, 1.0, 0.0).astype(BF16), v)
                inner = jnp.sum(jnp.where(mine, along, 0.0), axis=-1, keepdims=True)
                grad_s = (low.astype(F32) * (grad_p - inner)).astype(BF16)
                found.append((dot_nn(grad_s, k), dot_tn(grad_s, q), dot_tn(low, grad_out)))
            grad_q, grad_k, grad_v = (
                jnp.where(lane < 64, a, b) for a, b in zip(found[0], found[1])
            )
            grads[0][rows, col_q] = (grad_q * 0.125).astype(BF16)
            grads[1][rows, col_q] = (grad_k[:320] * 0.125).astype(BF16)
            grads[2][rows, col_q] = grad_v[:320].astype(BF16)


UP = (4, 9, 10, 11)
DOWN = (5, 6, 7, 8)
HOMES = (0, 1, 2, 3, 4, 5, 6, 7, 0, 1, 2, 8)
MADE = (3, 9, 10)
BEGIN = 14
LAST = BEGIN + 12 + STAGES


def layer_kernel(*refs):
    x_i, cot_i, lengths, assignment = refs[:4]
    shards, small = refs[4:8], refs[8]
    outs, small_out, input_grad_o, result_o, spilled, probs_o, down_o, attended_o = refs[9:13], *refs[13:20]
    (pages, staged, smalls, v4, v2, v1, flat, normed1_t, other_t, mixed, hidden, total, probs, row_mask, s4, s2, s1, part1, part2, part3) = refs[20:40]
    refs = refs[40:]
    per = 6 * len(BACK)
    slots = [refs[i * per : i * per + per] for i in range(3)]
    cores, refs = refs[3 * per : 3 * per + 2], refs[3 * per + 2 :]
    small_refs, refs = refs[:8], refs[8:]
    send, recv, back_send, back_recv, back_own, own, single, probs_sems = refs
    sems, back_sems = (send, recv), (back_send, back_recv, back_own)
    me, at = coords()
    mine = (at["z"], at["y"], at["x"], at["c"])
    normed = branch = result = flat.at[0]
    slope = grad_att = flat.at[1]
    grad_pre = flat.at[2]
    x, low, attended = flat.at[4], flat.at[5], flat.at[6]
    acts = [flat.at[7 + j] for j in range(4)]
    grads = (flat.at[2], flat.at[5], flat.at[3])
    downs = [pages.at[HOMES[k]] for k in DOWN]
    going = {}

    def move(src, dst, number):
        going[number] = pltpu.make_async_copy(src, dst, single.at[number])
        going[number].start()

    def done(*numbers):
        for number in numbers:
            going.pop(number).wait()

    def shard_of(k):
        if k < 3:
            return shards[0].at[:, pl.ds(k * 1024, 1024)]
        if k == 3:
            return shards[1]
        return shards[2].at[:, pl.ds(UP.index(k) * 1024, 1024)]

    def page_of(k):
        return pages.at[HOMES[k]]

    def local_copies(k):
        if k in DOWN:
            return [
                pltpu.make_async_copy(
                    shards[3].at[pl.ds(r * 32, 32), pl.ds(DOWN.index(k) * 256, 256)],
                    page_of(k).at[mine + (slice(None), pl.ds(r * 256, 256))],
                    own.at[k * 4 + r],
                )
                for r in range(4)
            ]
        return [pltpu.make_async_copy(shard_of(k), page_of(k).at[mine], own.at[k * 4])]

    local = {k: local_copies(k) for k in range(12)}
    early = [pltpu.make_async_copy(small, smalls.at[mine], own.at[48])]
    for k in (0, 1, 2, 3, 4, 5, 6, 7, 11):
        early += local[k]
    for copy in early:
        copy.start()
    move(cot_i, low, 0)
    move(x_i, x, 1)
    greet(me, at)

    def row(vectors, i):
        return vectors.at[pl.ds(i, 1), :]

    def kept_len(seq):
        return lengths[assignment[seq]]

    def task_low():
        for seq in range(2):
            inside = lax.broadcasted_iota(jnp.int32, (320, 1), 0) < kept_len(seq)
            row_mask[pl.ds(seq * 320, 320), :] = jnp.where(inside, 1.0, 0.0)
        for s in (s4, s2, s1):
            s[...] = jnp.zeros_like(s)
        mixed[pl.ds(640, 64), :] = jnp.zeros((64, 3072), BF16)
        done(0)
        low[...] = (low[...].astype(F32) * row_mask[...]).astype(BF16)
        s4[pl.ds(5, 1), :] = whole_sum(column_sum(low[...].astype(F32)))

    def task_first():
        spread_vectors(smalls, v4, v2, v1)
        done(1)
        norm_rows(x, row(v4, 0), row(v4, 1), normed)

    def task_project(j):
        shift = None if j == 1 else v2.at[pl.ds(6, 1), pl.ds(0 if j == 0 else 1024, 1024)]
        project(normed, page_of(j), shift, mixed, j * 1024)
        if j == 1:
            turn(normed, normed1_t)
        done(8 + j)

    def task_attend(first, count):
        attend(first, count, mixed, kept_len, attended, probs, probs_o, probs_sems)

    def task_hidden():
        branch_out(attended, page_of(3), row(v4, 2), x, hidden)
        norm_rows(hidden, row(v4, 3), row(v4, 4), normed)
        done(11)

    def task_turns():
        turn(attended, other_t)
        move(other_t, attended_o, 5)
        done(5)
        turn(normed, other_t)

    def task_up(j):
        feed_up(normed, page_of(UP[j]), row(v1, 7), acts[j], slope, j * 1024)

    def task_feed(j):
        page = page_of(UP[j])
        slope_back(low, downs, j, slope, grad_pre, s1)
        outer_box(other_t, grad_pre, pages.at[MADE[j % 3]])
        back_through(grad_pre, page, total, j == 0)
        if j == 3:
            move(attended_o, other_t, 5)
        back = (3, 2, 1, 0)[j]
        move(spilled.at[back], page, 12 + back)

    def task_outer(j):
        if j:
            done(2)
        outer(acts[j], low, staged)
        move(staged, down_o.at[j], 2)
        if j == 3:
            done(2)

    def task_second():
        norm_back(hidden, row(v4, 3), total, low, branch, part1, part2, part3)
        for i, part in ((3, part1), (4, part2), (2, part3)):
            s4[pl.ds(i, 1), :] = whole_sum(part[...])

    def task_out():
        done(5)
        outer_box(other_t, branch, pages.at[MADE[4 % 3]])

    def task_att():
        done(12 + 3)
        back_through(branch, page_of(UP[0]), grad_att, True)

    def task_attend_back(first, count):
        attend_back(first, count, mixed, attended, grad_att, probs, probs_o, probs_sems, grads)

    def task_mixed(j, m):
        outer_box(normed1_t, grads[j], pages.at[MADE[m % 3]])
        if j != 1:
            s2[pl.ds(6, 1), pl.ds(0 if j == 0 else 1024, 1024)] = whole_sum(
                column_sum(grads[j][...].astype(F32))
            )

    def task_through(j):
        done(12 + j)
        back_through(grads[j], page_of(UP[3 - j]), total, j == 2)

    def task_down(c):
        feed_down(acts, downs[c], row(v4, 5), hidden, row_mask, result, c)
        if c == 3:
            move(result, result_o, 3)

    def task_end():
        norm_back(x, row(v4, 0), total, branch, x, part1, part2, None)
        for i, part in ((0, part1), (1, part2)):
            s4[pl.ds(i, 1), :] = whole_sum(part[...])
        move(x, input_grad_o, 4)
        tiny = small_refs[0]
        for z in range(4):
            for y in range(2):
                for x_ in range(2):
                    for c in range(2):
                        d = ((z * 2 + y) * 2 + x_) * 2 + c
                        tiny[z, y, x_, c] = (
                            s4[:, d // 4 * 128 : d // 4 * 128 + 128]
                            + s2[:, d // 2 * 128 : d // 2 * 128 + 128]
                            + s1[:, d * 128 : d * 128 + 128]
                        )

    tasks = {
        3: [(task_low,)],
        5: [(task_first,), (task_project, 0)],
        6: [(task_project, 1)],
        7: [(task_project, 2), (task_attend, 0, 4)],
        8: [(task_attend, 4, 6)],
        9: [(task_attend, 10, 6)],
        10: [(task_hidden,)],
        11: [(task_turns,), (task_up, 0)],
        12: [(task_outer, 0)],
        13: [(task_feed, 0)],
        14: [(task_up, 1), (task_feed, 1)],
        15: [(task_up, 2), (task_feed, 2)],
        16: [(task_up, 3), (task_feed, 3)],
        17: [(task_second,), (task_out,)],
        18: [(task_outer, 1), (task_outer, 2), (task_outer, 3)],
        19: [(task_att,), (task_attend_back, 0, 4)],
        20: [(task_attend_back, 4, 4)],
        21: [(task_attend_back, 8, 4)],
        22: [(task_attend_back, 12, 4), (task_mixed, 2, 9)],
        23: [(task_mixed, 1, 10), (task_through, 2)],
        24: [(task_mixed, 0, 11), (task_through, 1), (task_through, 0), (task_end,)],
        25: [(task_down, 0), (task_down, 1)],
        26: [(task_down, 2), (task_down, 3)],
    }
    goals = [(2, 0, c) for c in (0, 1024, 2048, 3072)] + [(1, 0, 0)]
    goals += [(3, r, 0) for r in (0, 32, 64, 96)] + [(0, 0, 2048), (0, 0, 1024), (0, 0, 0)]
    flying, flows = {}, {}

    def begin(k, stage):
        if stage:
            for copy in flying.pop((k, stage - 1)):
                copy.wait()
        source = None if k in DOWN else shard_of(k)
        flying[k, stage] = gather_stage(page_of(k), PARTS, stage, me, at, sems, k % 8, source)
        for copy in flying[k, stage]:
            copy.start()

    small_going = []
    for tick in range(LAST + 1):
        for stage in range(STAGES + 1):
            if 0 <= tick - stage < 12:
                begin(tick - stage, stage)
            if stage == 0 and tick <= STAGES + 1:
                for copy in small_going:
                    copy.wait()
                small_going = []
                if tick <= STAGES:
                    small_going = gather_stage(smalls, SMALL, tick, me, at, sems, 8, small)
                for copy in small_going:
                    copy.start()
            if tick == 0 and stage == 0:
                for copy in early:
                    copy.wait()
            if tick + 1 in (8, 9, 10) and stage == 0:
                for copy in local[tick + 1]:
                    copy.start()
        k = tick - STAGES - 1
        if 0 <= k < 12:
            for copy in flying.pop((k, STAGES)):
                copy.wait()
            if k < 4:
                move(page_of(k), spilled.at[k], 8 + k)
        for stage in (1, 5, 2, 3, 4, 0):
            m = tick - BEGIN - stage
            if 0 <= m < 12:
                if stage == 0:
                    which, r, c = goals[m]
                    out = outs[which].at[pl.ds(r, ROWS), pl.ds(c, WIDE)]
                    source = down_o.at[:, :, :, :, r // 32] if which == 3 else None
                    made = pages.at[MADE[m % 3]]
                    flows[m] = Flow(made, source, out, BACK, cores[m % 2], slots[m % 3], m % 8, back_sems, me, at)
                    flows[m].start()
                else:
                    flows[m].step(stage)
        if tick >= LAST - STAGES - 1:
            if tick == LAST - STAGES - 1:
                flows["small"] = Flow(small_refs[0], None, small_out, SMALL_BACK, small_refs[1], small_refs[2:], 8, back_sems, me, at)
                flows["small"].start()
            else:
                flows["small"].step(tick - LAST + STAGES + 1)
        for task, *args in tasks.get(tick, ()):
            task(*args)
        if tick + 1 in (8, 9, 10):
            for copy in local[tick + 1]:
                copy.wait()
    done(3, 4)


def layer(x, cot, lengths, assignment, shards, small):
    anywhere = pl.BlockSpec(memory_space=pl.ANY)
    inside = pl.BlockSpec(memory_space=pltpu.VMEM)
    box = (4, 2, 2, 2)
    page = box + (32, 1024)
    flat, turned = (640, 1024), (1024, 640)
    made = [((32, 3072), F32), ((32, 1024), F32), ((32, 4096), F32), ((128, 1024), F32), ((8, 128), F32)]
    made += [(flat, BF16), (flat, BF16)]
    made += [((4,) + page, BF16), ((16, 2, 320, LEN_PAD), BF16), (box + (4, 32, 1024), BF16), (turned, BF16)]
    scratch = [
        ((11,) + page, BF16),
        ((2, 2, 2, 4, 32, 1024), BF16),
        (box + (8, 128), F32),
        ((8, 1024), F32),
        ((8, 2048), F32),
        ((8, 4096), F32),
        ((11,) + flat, BF16),
        (turned, BF16),
        (turned, BF16),
        ((704, 3072), BF16),
        (flat, F32),
        (flat, F32),
        ((2, 2, 320, LEN_PAD), BF16),
        ((640, 1), F32),
        ((8, 1024), F32),
        ((8, 2048), F32),
        ((8, 4096), F32),
    ] + [((8, 1024), F32)] * 3
    scratch += flow_buffers(BACK, BF16) * 3 + [((4, 2, 2, 32, 1024), BF16)] * 2
    scratch += [(box + (8, 128), F32), ((4, 2, 2, 8, 128), F32)] + flow_buffers(SMALL_BACK, F32)
    dma = pltpu.SemaphoreType.DMA
    return pl.pallas_call(
        layer_kernel,
        out_shape=[jax.ShapeDtypeStruct(s, d) for s, d in made],
        in_specs=[anywhere] * 2 + [pl.BlockSpec(memory_space=pltpu.SMEM)] * 2 + [anywhere] * 5,
        out_specs=[inside] * 5 + [anywhere] * 6,
        scratch_shapes=[pltpu.VMEM(s, d) for s, d in scratch]
        + [dma((9, COPIES))] * 4
        + [dma((9,)), dma((49,)), dma((16,)), dma((2,))],
        compiler_params=pltpu.CompilerParams(
            collective_id=0, has_side_effects=True, vmem_limit_bytes=64 << 20
        ),
        name="layer",
    )(x, cot, lengths, assignment, *shards, small)


def finish_kernel(*refs):
    small, refs = refs[0], refs[1:]
    arrays, narrow, outs, refs = refs[:6], refs[6:14], refs[14:20], refs[20:]
    blocks, refs = refs[:6], refs[6:]
    into = [pltpu.make_async_copy(a, block, refs[0].at[i]) for i, (a, block) in enumerate(zip(arrays, blocks))]
    back = [pltpu.make_async_copy(block, o, refs[1].at[i]) for i, (o, block) in enumerate(zip(outs, blocks))]
    for copy in into:
        copy.start()
    me = lax.axis_index("dp")
    fours = pltpu.roll(small[...], 128 - lax.rem(me, 4) * 32, 1)
    for i in range(6):
        narrow[i][...] = fours[i : i + 1, :32]
    twos = pltpu.roll(small[...], 128 - lax.rem(me, 2) * 64, 1)
    narrow[6][...] = twos[6:7, :64]
    narrow[7][...] = small[7:8, :]
    for first, second in zip(into, back):
        first.wait()
        second.start()
    for copy in back:
        copy.wait()


def finish(total, *arrays):
    anywhere = pl.BlockSpec(memory_space=pl.ANY)
    inside = pl.BlockSpec(memory_space=pltpu.VMEM)
    found = pl.pallas_call(
        lambda *refs: finish_kernel(*refs[:7], *refs[7:15], *refs[15:]),
        out_shape=[jax.ShapeDtypeStruct((1, n), F32) for n in (32,) * 6 + (64, 128)]
        + [jax.ShapeDtypeStruct(a.shape, a.dtype) for a in arrays],
        in_specs=[inside] + [anywhere] * 6,
        out_specs=[inside] * 8 + [anywhere] * 6,
        scratch_shapes=[pltpu.VMEM(a.shape, a.dtype) for a in arrays]
        + [pltpu.SemaphoreType.DMA((len(arrays),))] * 2,
        compiler_params=pltpu.CompilerParams(vmem_limit_bytes=63 << 20),
        name="finish",
    )(total, *arrays)
    return [a.reshape(-1) for a in found[:8]], found[8:]


NARROW = (0, 1, 5, 6, 7, 11)
WEIGHTS = (2, 4, 8, 10)


def pack_weights(weights):
    me = lax.axis_index("dp")
    lane = jnp.arange(128, dtype=jnp.int32)[None, :]
    narrow = jnp.tile(jnp.stack([weights[i] for i in NARROW]), (1, 4))
    rows = [
        jnp.where(lane // 32 == me % 4, narrow, 0),
        jnp.where(lane // 64 == me % 2, jnp.tile(weights[3][None], (1, 2)), 0),
        weights[9][None],
    ]
    return jnp.concatenate(rows, axis=0).astype(F32)


def on_box(inputs, lengths, assignment, *rest):
    weights, cotangent = rest[:12], rest[12]
    me = lax.axis_index("dp")
    x = inputs.reshape(640, 1024)
    cot = cotangent.reshape(640, 1024)
    small = pack_weights(weights)
    made = layer(
        x, cot, lengths, assignment, [weights[i] for i in WEIGHTS], small
    )
    sums, (total, input_grad, result) = made[:4], made[4:7]
    narrow, (result, input_grad, *sums) = finish(total, result, input_grad, *sums)
    found = [None] * 12
    for row, i in enumerate((*NARROW, 3, 9)):
        found[i] = narrow[row]
    for i, s in zip(WEIGHTS, sums):
        found[i] = s
    return (result.reshape(inputs.shape), input_grad.reshape(inputs.shape), *found)


def plain(
    inputs,
    lengths,
    assignment,
    norm1_gain,
    norm1_bias,
    qkv_weight,
    qv_bias,
    out_weight,
    out_bias,
    norm2_gain,
    norm2_bias,
    up_weight,
    up_bias,
    down_weight,
    down_bias,
    cotangent,
):
    gathered = (
        lax.all_gather(norm1_gain, "dp", axis=0, tiled=True),
        lax.all_gather(norm1_bias, "dp", axis=0, tiled=True),
        lax.all_gather(qkv_weight, "dp", axis=0, tiled=True),
        lax.all_gather(qv_bias, "dp", axis=0, tiled=True),
        lax.all_gather(out_weight, "dp", axis=0, tiled=True),
        lax.all_gather(out_bias, "dp", axis=0, tiled=True),
        lax.all_gather(norm2_gain, "dp", axis=0, tiled=True),
        lax.all_gather(norm2_bias, "dp", axis=0, tiled=True),
        lax.all_gather(up_weight, "dp", axis=0, tiled=True),
        lax.all_gather(up_bias, "dp", axis=0, tiled=True),
        lax.all_gather(down_weight, "dp", axis=0, tiled=True),
        lax.all_gather(down_bias, "dp", axis=0, tiled=True),
    )
    seq_count, tok_count, model_width = inputs.shape
    rows_all = seq_count * tok_count
    split_shape = (seq_count, tok_count, HEADS, HEAD)
    head_scale = HEAD ** (-0.5)
    matches = assignment[:, None] == jnp.arange(lengths.shape[0], dtype=jnp.int32)[None, :]
    kept_len = jnp.sum(jnp.where(matches, lengths[None, :], 0), axis=1)
    key_mask = jnp.arange(tok_count, dtype=jnp.int32)[None, :] < kept_len[:, None]
    row_mask = key_mask.reshape(rows_all, 1).astype(jnp.float32)
    gain_first = gathered[0].astype(jnp.float32)
    shift_first = gathered[1].astype(jnp.float32)
    qv_full = gathered[3].astype(jnp.float32)
    proj_shift = gathered[5].astype(jnp.float32)
    gain_second = gathered[6].astype(jnp.float32)
    shift_second = gathered[7].astype(jnp.float32)
    up_shift = gathered[9].astype(jnp.float32)
    down_shift = gathered[11].astype(jnp.float32)
    inputs_flat = inputs.reshape(rows_all, model_width).astype(jnp.float32)
    normed_first, first_back = jax.vjp(layer_norm, inputs_flat, gain_first, shift_first)
    normed_low = normed_first.astype(jnp.bfloat16)
    full_bias = jnp.concatenate(
        [qv_full[:model_width], jnp.zeros((model_width,), jnp.float32), qv_full[model_width:]]
    )
    mixed_qkv = (
        jnp.dot(normed_low, gathered[2], preferred_element_type=jnp.float32) + full_bias
    ).astype(jnp.bfloat16)
    queries = mixed_qkv[:, :model_width].reshape(split_shape)
    keys_all = mixed_qkv[:, model_width : 2 * model_width].reshape(split_shape)
    values_all = mixed_qkv[:, 2 * model_width :].reshape(split_shape)
    scores = (
        jnp.einsum("bqhd,bkhd->bhqk", queries, keys_all, preferred_element_type=jnp.float32)
        * head_scale
    )
    scores = jnp.where(key_mask[:, None, None, :], scores, masked_score)
    row_max = jnp.max(scores, axis=-1, keepdims=True)
    exponent = jnp.exp(scores - row_max)
    row_total = jnp.sum(exponent, axis=-1, keepdims=True)
    softmax_probs = exponent / row_total
    log_total = row_max + jnp.log(row_total)
    attended = jnp.einsum(
        "bhqk,bkhd->bqhd",
        softmax_probs.astype(jnp.bfloat16),
        values_all,
        preferred_element_type=jnp.float32,
    )
    attended = attended.reshape(rows_all, model_width).astype(jnp.bfloat16)
    hidden = inputs_flat + (
        jnp.dot(attended, gathered[4], preferred_element_type=jnp.float32) + proj_shift
    )
    normed_second, second_back = jax.vjp(layer_norm, hidden, gain_second, shift_second)
    second_low = normed_second.astype(jnp.bfloat16)
    pre_act = jnp.dot(second_low, gathered[8], preferred_element_type=jnp.float32) + up_shift
    activation, gelu_back = jax.vjp(gelu_exact, pre_act)
    act_low = activation.astype(jnp.bfloat16)
    output_rows = row_mask * (
        hidden + (jnp.dot(act_low, gathered[10], preferred_element_type=jnp.float32) + down_shift)
    )
    result = output_rows.reshape(inputs.shape).astype(jnp.bfloat16)
    grad_rows = cotangent.reshape(rows_all, model_width).astype(jnp.float32) * row_mask
    grad_low = grad_rows.astype(jnp.bfloat16)
    down_grad = contract_rows(act_low, grad_low)
    down_bias_grad = jnp.sum(grad_low.astype(jnp.float32), axis=0)
    grad_pre = gelu_back(contract_cols(grad_low, gathered[10]))[0].astype(jnp.bfloat16)
    up_grad = contract_rows(second_low, grad_pre)
    up_bias_grad = jnp.sum(grad_pre.astype(jnp.float32), axis=0)
    grad_second, gain2_grad, shift2_grad = second_back(contract_cols(grad_pre, gathered[8]))
    grad_hidden = grad_rows + grad_second
    branch_low = grad_hidden.astype(jnp.bfloat16)
    proj_grad = contract_rows(attended, branch_low)
    proj_bias_grad = jnp.sum(branch_low.astype(jnp.float32), axis=0)
    grad_att = contract_cols(branch_low, gathered[4]).astype(jnp.bfloat16).reshape(split_shape)
    scores_again = (
        jnp.einsum("bqhd,bkhd->bhqk", queries, keys_all, preferred_element_type=jnp.float32)
        * head_scale
    )
    scores_again = jnp.where(key_mask[:, None, None, :], scores_again, masked_score)
    probs_again = jnp.exp(scores_again - log_total)
    probs_low = probs_again.astype(jnp.bfloat16)
    grad_probs = jnp.einsum(
        "bqhd,bkhd->bhqk", grad_att, values_all, preferred_element_type=jnp.float32
    )
    grad_values = jnp.einsum(
        "bhqk,bqhd->bkhd", probs_low, grad_att, preferred_element_type=jnp.float32
    )
    inner_sum = jnp.sum(probs_again * grad_probs, axis=-1, keepdims=True)
    grad_scores = (probs_again * (grad_probs - inner_sum)).astype(jnp.bfloat16)
    grad_queries = (
        jnp.einsum("bhqk,bkhd->bqhd", grad_scores, keys_all, preferred_element_type=jnp.float32)
        * head_scale
    )
    grad_keys = (
        jnp.einsum("bhqk,bqhd->bkhd", grad_scores, queries, preferred_element_type=jnp.float32)
        * head_scale
    )
    grad_mixed = jnp.concatenate(
        [
            grad_queries.reshape(rows_all, model_width),
            grad_keys.reshape(rows_all, model_width),
            grad_values.reshape(rows_all, model_width),
        ],
        axis=1,
    ).astype(jnp.bfloat16)
    qkv_grad = contract_rows(normed_low, grad_mixed)
    column_sums = jnp.sum(grad_mixed.astype(jnp.float32), axis=0)
    qv_grad = jnp.concatenate([column_sums[:model_width], column_sums[2 * model_width :]])
    grad_first, gain1_grad, shift1_grad = first_back(contract_cols(grad_mixed, gathered[2]))
    input_grad = (grad_hidden + grad_first).reshape(inputs.shape).astype(jnp.bfloat16)
    all_sums = (
        lax.psum_scatter(gain1_grad, "dp", scatter_dimension=0, tiled=True),
        lax.psum_scatter(shift1_grad, "dp", scatter_dimension=0, tiled=True),
        lax.psum_scatter(qkv_grad, "dp", scatter_dimension=0, tiled=True),
        lax.psum_scatter(qv_grad, "dp", scatter_dimension=0, tiled=True),
        lax.psum_scatter(proj_grad, "dp", scatter_dimension=0, tiled=True),
        lax.psum_scatter(proj_bias_grad, "dp", scatter_dimension=0, tiled=True),
        lax.psum_scatter(gain2_grad, "dp", scatter_dimension=0, tiled=True),
        lax.psum_scatter(shift2_grad, "dp", scatter_dimension=0, tiled=True),
        lax.psum_scatter(up_grad, "dp", scatter_dimension=0, tiled=True),
        lax.psum_scatter(up_bias_grad, "dp", scatter_dimension=0, tiled=True),
        lax.psum_scatter(down_grad, "dp", scatter_dimension=0, tiled=True),
        lax.psum_scatter(down_bias_grad, "dp", scatter_dimension=0, tiled=True),
    )
    attn_sums = all_sums[:6]
    mlp_sums = all_sums[6:]
    return (
        result,
        input_grad,
        attn_sums[0],
        attn_sums[1],
        attn_sums[2],
        attn_sums[3],
        attn_sums[4],
        attn_sums[5],
        mlp_sums[0],
        mlp_sums[1],
        mlp_sums[2],
        mlp_sums[3],
        mlp_sums[4],
        mlp_sums[5],
    )


def local(*args):
    return on_box(*args) if lax.axis_size("dp") == 32 else plain(*args)


def solution(mesh):
    placed = (
        P("dp", None, None),
        P(),
        P("dp"),
        P("dp"),
        P("dp"),
        P("dp", None),
        P("dp"),
        P("dp", None),
        P("dp"),
        P("dp"),
        P("dp"),
        P("dp", None),
        P("dp"),
        P("dp", None),
        P("dp"),
        P("dp", None, None),
    )
    return jax.shard_map(
        local,
        mesh=mesh,
        in_specs=placed,
        out_specs=(
            P("dp", None, None),
            P("dp", None, None),
            P("dp"),
            P("dp"),
            P("dp", None),
            P("dp"),
            P("dp", None),
            P("dp"),
            P("dp"),
            P("dp"),
            P("dp", None),
            P("dp"),
            P("dp", None),
            P("dp"),
        ),
        check_vma=False,
    )
```

```python
import jax
import jax.numpy as jnp
from jax import lax
from jax.experimental import pallas as pl
from jax.experimental.pallas import tpu as pltpu
from jax.sharding import PartitionSpec as P

HEADS = 16
HEAD = 64


eps = 1e-06
masked_score = -1000000000.0


def layer_norm(values, norm_gain, norm_shift):
    average = jnp.mean(values, axis=-1, keepdims=True)
    centered = values - average
    variance = jnp.mean(centered * centered, axis=-1, keepdims=True)
    return centered * lax.rsqrt(variance + eps) * norm_gain + norm_shift


def gelu_exact(values):
    return jax.nn.gelu(values, approximate=False)


def contract_rows(left, right):
    return lax.dot_general(
        left, right, (((0,), (0,)), ((), ())), preferred_element_type=jnp.float32
    )


def contract_cols(left, right):
    return lax.dot_general(
        left, right, (((1,), (1,)), ((), ())), preferred_element_type=jnp.float32
    )


BF16 = jnp.bfloat16
F32 = jnp.float32
MESH = pl.DeviceIdType.MESH
STRIDE = {"z": 8, "y": 4, "x": 2}
ROWS = 32
WIDE = 1024
STAGES = 4
PARTS = (
    ("zZyx", 0, 16, 0, 384),
    ("zZxy", 16, 16, 0, 384),
    ("xzZy", 0, 16, 384, 640),
    ("yzZx", 16, 16, 384, 640),
)
FIRST = (("zZyx", 0, 16, 0, 1024), ("zZxy", 16, 16, 0, 1024))
COPIES = 6 * len(PARTS) + 1


def coords():
    me = lax.axis_index("dp")
    at = {
        "z": lax.div(me, 8),
        "y": lax.rem(lax.div(me, 4), 2),
        "x": lax.rem(lax.div(me, 2), 2),
        "c": lax.rem(me, 2),
    }
    return me, at


def sibling(me, at):
    return me + 1 - 2 * at["c"]


class Hop:
    def __init__(self, copy, sends=None, hears=None):
        self.copy, self.sends, self.hears = copy, sends, hears

    def start(self):
        if self.sends is None:
            self.copy.start()
        else:
            pl.when(self.sends)(self.copy.start)

    def wait(self):
        if self.sends is None:
            self.copy.wait()
        else:
            pl.when(self.sends)(self.copy.wait_send)
            pl.when(self.hears)(self.copy.wait_recv)


def inner(at):
    return lax.div(at["z"] + 1, 2) == 1


def far(at):
    return 3 * (1 - lax.div(at["z"], 2))


def hops(me, at, dim):
    z = at["z"]
    if dim == "z":
        found = []
        for k in (1, 2, 3):
            there = lax.rem(z + k, 4)
            when = {1: (z < 3, z > 0), 2: (None, None), 3: (z > 0, z < 3)}[k]
            found.append((there, me + (there - z) * 8, *when))
        return found
    if dim == "Z":
        return [(far(at), me + 8 - 16 * lax.rem(z, 2), inner(at), jnp.logical_not(inner(at)))]
    there = 1 - at[dim]
    return [(there, me + (there - at[dim]) * STRIDE[dim], None, None)]


def count_of(dim):
    return 3 if dim == "z" else 1


def greet(me, at):
    barrier = pltpu.get_barrier_semaphore()
    devices = [sibling(me, at)]
    for dim in "yx":
        devices += [hop[1] for hop in hops(me, at, dim)]
    for k in (1, 2, 3):
        devices.append(me + (lax.rem(at["z"] + k, 4) - at["z"]) * 8)
    for device in devices:
        pl.semaphore_signal(barrier, inc=1, device_id=(device,), device_id_type=MESH)
    pl.semaphore_wait(barrier, len(devices))


def remote(src, dst, sems, slot, number, device):
    return pltpu.make_async_remote_copy(
        src_ref=src,
        dst_ref=dst,
        send_sem=sems[0].at[slot, number],
        recv_sem=sems[1].at[slot, number],
        device_id=(device,),
        device_id_type=MESH,
    )


def held(order, stage, at):
    index = []
    for dim in "zyx":
        if dim == "z" and order[stage] == "Z":
            index.append(far(at))
        else:
            done = "Z" if dim == "z" else dim
            index.append(slice(None) if done in order[:stage] else at[dim])
    return tuple(index)


def gather_stage(base, parts, stage, me, at, sems, slot, source=None):
    if stage == STAGES:
        block = base.at[:, :, :, at["c"]]
        return [Hop(remote(block, block, sems, slot, COPIES - 1, sibling(me, at)))]
    number, copies = 0, []
    for order, row, rows, col, columns in parts:
        here = (pl.ds(row, rows), pl.ds(col, columns))
        for s in range(STAGES):
            for _, device, sends, hears in hops(me, at, order[s]):
                if s == stage:
                    block = base.at[held(order, stage, at) + (at["c"],) + here]
                    src = source.at[here] if source is not None and stage == 0 else block
                    copies.append(Hop(remote(src, block, sems, slot, number, device), sends, hears))
                number += 1
    return copies


SMALL = (("zZyx", 0, 8, 0, 128),)


def remaining(order, stage):
    left = [dim for dim in "zyx" if dim not in order[:stage]]
    return tuple({"z": 4, "y": 2, "x": 2}[dim] for dim in left)


def pick(order, stage, dim, index):
    return tuple(index if d == dim.lower() else slice(None) for d in "zyx" if d not in order[:stage])


BACK = tuple((part[0][::-1], *part[1:]) for part in PARTS)
SMALL_BACK = tuple((part[0][::-1], *part[1:]) for part in SMALL)


def add_up(dst, terms, lead):
    loops = lead[: max(len(lead) - 1, 0)] if len(lead) > 1 else ()
    count = 1
    for n in loops:
        count *= n

    def body(i, carry):
        index = []
        for n in loops[::-1]:
            index.append(lax.rem(i, n))
            i = lax.div(i, n)
        index = tuple(index[::-1]) + (slice(None),) * (len(lead) - len(loops) + 2)
        if len(terms) == 2 and dst.dtype == terms[0].dtype:
            dst[index] = terms[0][index] + terms[1][index]
            return carry
        total = terms[0][index].astype(F32)
        for term in terms[1:]:
            total = total + term[index].astype(F32)
        dst[index] = total.astype(dst.dtype)
        return carry

    if count == 1:
        body(0, 0)
    else:
        lax.fori_loop(0, count, body, 0)


class Flow:
    def __init__(self, made, source, out, parts, from_core, rest, last, slot, sems, me, at):
        self.made, self.source, self.out, self.parts = made, source, out, parts
        self.from_core = from_core
        self.arrived, self.totals = [], []
        for part, (order, *_) in enumerate(parts):
            self.arrived.append((*rest[:3], last[part]))
            self.totals.append(dict(zip([s for s in range(3) if order[s] != "Z"], rest[3:5])))
            rest = rest[5:]
        self.slot, self.sems, self.me, self.at = slot, sems, me, at
        self.own = made.at[:, :, :, at["c"]]

    def start(self):
        there = 1 - self.at["c"]
        source = self.made if self.source is None else self.source
        self.going = [
            remote(
                source.at[:, :, :, there],
                self.from_core,
                self.sems,
                self.slot,
                COPIES - 1,
                sibling(self.me, self.at),
            )
        ]
        if self.source is not None:
            self.going.append(
                pltpu.make_async_copy(source.at[:, :, :, self.at["c"]], self.own, self.sems[2].at[self.slot])
            )
        for copy in self.going:
            copy.start()

    def sum_before(self, part, stage):
        order, row, rows, col, columns = self.parts[part]
        done = [s for s in range(stage) if s in self.totals[part]]
        if not done:
            return self.own.at[:, :, :, pl.ds(row, rows), pl.ds(col, columns)]
        return self.totals[part][done[-1]]

    def take(self, part, stage):
        order, row, rows, col, columns = self.parts[part]
        s = stage - 2
        dim, arrived = order[s], self.arrived[part][s]
        before = self.sum_before(part, s)
        if dim == "Z":
            index = pick(order, s, "z", far(self.at))

            @pl.when(inner(self.at))
            def _():
                add_up(before.at[index], [before.at[index], arrived.at[0]], remaining(order, s)[1:])

            return
        if stage == STAGES + 1:
            total = self.out.at[pl.ds(row, rows), pl.ds(col, columns)]
        else:
            total = self.totals[part][s]
        mine = before.at[pick(order, s, dim, self.at[dim])]
        left = remaining(order, s + 1)
        if dim != "z":
            add_up(total, [mine, arrived.at[0]], left)
            return
        z = self.at["z"]
        for when, came in ((z == 0, (1, 2)), (inner(self.at), (0, 1, 2)), (z == 3, (0, 1))):

            @pl.when(when)
            def _(came=came):
                add_up(total, [mine] + [arrived.at[i] for i in came], left)

    def step(self, stage):
        for copy in self.going:
            copy.wait()
        if stage == 1:
            add_up(self.own, [self.own, self.from_core], (4, 2, 2))
        else:
            for part in range(len(self.parts)):
                self.take(part, stage)
        self.going, number = [], 0
        for part, (order, row, rows, col, columns) in enumerate(self.parts):
            for s in range(STAGES):
                if s + 1 == stage:
                    before = self.sum_before(part, s)
                    for i, (there, device, sends, hears) in enumerate(hops(self.me, self.at, order[s])):
                        if order[s] == "Z":
                            sends, hears = hears, sends
                        src = before.at[pick(order, s, order[s], there)]
                        copy = remote(src, self.arrived[part][s].at[i], self.sems, self.slot, number + i, device)
                        self.going.append(Hop(copy, sends, hears))
                number += count_of(order[s])
        for copy in self.going:
            copy.start()


def flow_buffers(parts, dtype):
    shapes, last = [], []
    for order, _, high, _, wide in parts:
        totals = []
        for s in range(STAGES):
            if order[s] == "Z":
                left = remaining(order, s)[1:]
            else:
                left = remaining(order, s + 1)
                if s < 3:
                    totals.append((left + (high, wide), dtype))
            (shapes if s < 3 else last).append(((count_of(order[s]),) + left + (high, wide), dtype))
        shapes += totals
    return shapes, last


EPS = 1e-06
MASKED = -1000000000.0
LEN_PAD = 384


def dot_nn(a, b):
    return jnp.dot(a, b, preferred_element_type=F32)


def dot_nt(a, b):
    return lax.dot_general(a, b, (((1,), (1,)), ((), ())), preferred_element_type=F32)


def dot_tn(a, b):
    return lax.dot_general(a, b, (((0,), (0,)), ((), ())), preferred_element_type=F32)


def block_of(index, size):
    return pl.ds(pl.multiple_of(index * size, size), size)


def spread_vectors(smalls, v4, v2, v1):
    for z in range(4):
        for y in range(2):
            four = None
            for x in range(2):
                two = None
                for c in range(2):
                    one = smalls[z, y, x, c]
                    d = ((z * 2 + y) * 2 + x) * 2 + c
                    v1[:, d * 128 : d * 128 + 128] = one
                    two = one if two is None else two + one
                d = (z * 2 + y) * 2 + x
                v2[:, d * 128 : d * 128 + 128] = two
                four = two if four is None else four + two
            d = z * 2 + y
            v4[:, d * 128 : d * 128 + 128] = four


def norm_rows(src, gain, shift, dst):
    @pl.loop(0, src.shape[0] // 64)
    def _(i):
        rows = block_of(i, 64)
        values = src[rows, :].astype(F32)
        centered = values - jnp.mean(values, axis=-1, keepdims=True)
        variance = jnp.mean(centered * centered, axis=-1, keepdims=True)
        normed = centered * lax.rsqrt(variance + EPS)
        dst[rows, :] = (normed * gain[...] + shift[...]).astype(BF16)


def project(normed, weight, shift, dst, col):
    @pl.loop(0, 2)
    def _(i):
        columns = block_of(i, 512)
        mixed = dot_nn(normed[...], weight[:, :, :, :, :, columns].reshape(1024, 512))
        if shift is not None:
            mixed = mixed + shift[:, columns]
        dst[pl.ds(0, 640), pl.ds(pl.multiple_of(col + i * 512, 512), 512)] = mixed.astype(BF16)


def attend(first, count, mixed, kept_len, attended, probs, probs_out, sems):
    lane = lax.broadcasted_iota(jnp.int32, (1, 128), 1)

    def out_copy(unit, slot):
        return pltpu.make_async_copy(probs.at[slot], probs_out.at[unit], sems.at[slot])

    @pl.loop(0, count // 2)
    def _(i):
        for slot in range(2):
            unit = first + i * 2 + slot
            seq, pair = lax.div(unit, 8), lax.rem(unit, 8)
            start = pl.multiple_of(seq * 320, 64)
            columns = block_of(pair, 128)
            q = mixed[pl.ds(start, 320), columns]
            k = mixed[pl.ds(start, LEN_PAD), block_of(pair + 8, 128)]
            v = mixed[pl.ds(start, LEN_PAD), block_of(pair + 16, 128)]
            kept = lax.broadcasted_iota(jnp.int32, (1, LEN_PAD), 1) < kept_len(seq)

            @pl.when(i > 0)
            def _():
                out_copy(unit, slot).wait()

            found = []
            for head in range(2):
                scale = jnp.where(lax.div(lane, 64) == head, 0.125, 0.0).astype(BF16)
                scores = jnp.where(kept, dot_nt(q * scale, k), MASKED)
                exponent = jnp.exp(scores - jnp.max(scores, axis=-1, keepdims=True))
                total = jnp.sum(exponent, axis=-1, keepdims=True)
                low = (exponent * (1.0 / total)).astype(BF16)
                probs[slot, head] = low
                found.append(dot_nn(low, v))
            attended[pl.ds(start, 320), columns] = jnp.where(
                lane < 64, found[0], found[1]
            ).astype(BF16)
            out_copy(unit, slot).start()

    for slot in range(2):
        out_copy(0, slot).wait()


def branch_out(attended, weight, shift, x, hidden):
    @pl.loop(0, 2)
    def _(i):
        columns = block_of(i, 512)
        branch = dot_nn(attended[...], weight[:, :, :, :, :, columns].reshape(1024, 512))
        hidden[:, columns] = x[:, columns].astype(F32) + (branch + shift[:, columns])


def feed_up(normed, weight, shift, act, slope, col):
    @pl.loop(0, 2)
    def _(i):
        columns = block_of(i, 512)
        pre = dot_nn(normed[...], weight[:, :, :, :, :, columns].reshape(1024, 512))
        pre = pre + shift[:, pl.ds(pl.multiple_of(col + i * 512, 512), 512)]
        below = 0.5 + 0.5 * lax.erf(pre * 0.7071067811865476)
        act[:, columns] = (pre * below).astype(BF16)
        density = jnp.exp(pre * pre * -0.5) * 0.3989422804014327
        slope[:, columns] = (below + pre * density).astype(BF16)


def outer(left, right, halves):
    for i, half in enumerate(halves):
        half[...] = dot_tn(left[:, i * 512 : i * 512 + 512], right[...]).astype(BF16)


def turn(src, dst):
    @pl.loop(0, 4)
    def _(i):
        rows = block_of(i, 256)
        dst[rows, :] = src[:, rows].T


def tall(block):
    parts = [block[..., i * 256 : i * 256 + 256] for i in range(4)]
    rows = jnp.stack(parts, axis=block.ndim - 2)
    return rows.reshape(-1, 256)


def feed_down(acts, page, shift, hidden, row_mask, result, c):
    columns = pl.ds(c * 256, 256)
    branch = dot_nn(acts[0][...], tall(page[0]))
    for z in range(1, 4):
        branch = branch + dot_nn(acts[z][...], tall(page[z]))
    whole = hidden[:, columns] + (branch + shift[:, columns])
    result[:, columns] = (whole * row_mask[...]).astype(BF16)


def column_sum(values):
    return jnp.sum(values.reshape(values.shape[0] // 8, 8, values.shape[1]), axis=0)


def norm_back(src, gain, grads, base, dst, by_scale, by_shift, by_low):
    for total in (by_scale, by_shift, by_low):
        if total is not None:
            total[...] = jnp.zeros_like(total)

    @pl.loop(0, 640 // 64)
    def _(i):
        rows = block_of(i, 64)
        values = src[rows, :].astype(F32)
        centered = values - jnp.mean(values, axis=-1, keepdims=True)
        inverse = lax.rsqrt(jnp.mean(centered * centered, axis=-1, keepdims=True) + EPS)
        normed = centered * inverse
        g = grads[rows, :]
        scaled = g * gain[...]
        along = jnp.mean(scaled * normed, axis=-1, keepdims=True)
        back = inverse * (scaled - jnp.mean(scaled, axis=-1, keepdims=True) - normed * along)
        whole = base[rows, :].astype(F32) + back
        rounded = whole.astype(BF16)
        dst[rows, :] = rounded
        by_scale[...] += column_sum(g * normed)
        by_shift[...] += column_sum(g)
        if by_low is not None:
            by_low[...] += column_sum(rounded.astype(F32))


def whole_sum(part):
    return jnp.sum(part, axis=0, keepdims=True)


def slope_back(low, pages, j, slope, grad_pre, total):
    @pl.loop(0, 2)
    def _(i):
        columns = block_of(i, 512)
        weight = jnp.concatenate([tall(page[j, i]) for page in pages], axis=1)
        grad = (dot_nt(low[...], weight) * slope[:, columns].astype(F32)).astype(BF16)
        grad_pre[:, columns] = grad
        there = pl.ds(pl.multiple_of(j * 1024 + i * 512, 512), 512)
        total[pl.ds(7, 1), there] = whole_sum(column_sum(grad.astype(F32)))


def back_through(left, page, total, first):
    part = dot_nt(left[...], page[...].reshape(1024, 1024))
    total[...] = part.astype(total.dtype) if first else total[...] + part


def outer_box(turned, right, dst):
    dst[...] = dot_nn(turned[...], right[...]).astype(BF16).reshape(4, 2, 2, 2, 32, 1024)


def attend_back(first, count, mixed, attended, grad_att, probs, probs_in, sems, grads):
    lane = lax.broadcasted_iota(jnp.int32, (1, 128), 1)

    def load(unit, slot):
        return pltpu.make_async_copy(probs_in.at[unit], probs.at[slot], sems.at[slot])

    load(first, 0).start()

    @pl.loop(0, count // 2)
    def _(i):
        for slot in range(2):
            unit = first + i * 2 + slot
            seq, pair = lax.div(unit, 8), lax.rem(unit, 8)
            start = pl.multiple_of(seq * 320, 64)
            rows = pl.ds(start, 320)
            col_q, col_k, col_v = (block_of(pair + 8 * n, 128) for n in range(3))
            load(unit, slot).wait()
            if slot == 0:
                load(unit + 1, 1).start()
            else:

                @pl.when(i + 1 < count // 2)
                def _():
                    load(unit + 1, 0).start()

            q = mixed[rows, col_q]
            k = mixed[pl.ds(start, LEN_PAD), col_k]
            v = mixed[pl.ds(start, LEN_PAD), col_v]
            grad_out = grad_att[rows, col_q]
            along = grad_out.astype(F32) * attended[rows, col_q].astype(F32)
            found = []
            for head in range(2):
                mine = lax.div(lane, 64) == head
                low = probs[slot, head]
                grad_p = dot_nt(grad_out * jnp.where(mine, 1.0, 0.0).astype(BF16), v)
                inner = jnp.sum(jnp.where(mine, along, 0.0), axis=-1, keepdims=True)
                grad_s = (low.astype(F32) * (grad_p - inner)).astype(BF16)
                found.append((dot_nn(grad_s, k), dot_tn(grad_s, q), dot_tn(low, grad_out)))
            grad_q, grad_k, grad_v = (
                jnp.where(lane < 64, a, b) for a, b in zip(found[0], found[1])
            )
            grads[0][rows, col_q] = (grad_q * 0.125).astype(BF16)
            grads[1][rows, col_q] = (grad_k[:320] * 0.125).astype(BF16)
            grads[2][rows, col_q] = grad_v[:320].astype(BF16)


UP = (4, 9, 10, 11)
DOWN = (5, 6, 7, 8)
HOMES = (0, 1, 2, 3, 4, 5, 6, 7, 0, 1, 2, 8)
MADE = (3, 9, 10)
BEGIN = 14
LAST = BEGIN + 12 + STAGES


def layer_kernel(*refs):
    x_i, cot_i, lengths, assignment = refs[:4]
    shards, narrow = refs[4:8], refs[8:16]
    refs = refs[7:]
    outs, small_out, input_grad_o, result_o, spilled, probs_o, down_o, attended_o = refs[9:13], *refs[13:20]
    (pages, smalls, v4, v2, v1, flat, normed1_t, other_t, mixed, hidden, total, probs, row_mask, s4, s2, s1, part1, part2, part3, small) = refs[20:40]
    refs = refs[40:]
    per, parts = 5 * len(BACK), len(BACK)
    slots, refs = [refs[i * per : i * per + per] for i in range(3)], refs[3 * per :]
    lasts, refs = [refs[i * parts : i * parts + parts] for i in range(4)], refs[4 * parts :]
    cores, refs = refs[:2], refs[2:]
    small_refs, refs = refs[:8], refs[8:]
    send, recv, back_send, back_recv, back_own, own, single, probs_sems = refs
    sems, back_sems = (send, recv), (back_send, back_recv, back_own)
    me, at = coords()
    mine = (at["z"], at["y"], at["x"], at["c"])
    normed = branch = result = flat.at[0]
    slope = grad_att = flat.at[1]
    grad_pre = flat.at[2]
    x, low, attended = flat.at[4], flat.at[5], flat.at[6]
    acts = [flat.at[7 + j] for j in range(4)]
    grads = (flat.at[2], flat.at[5], flat.at[3])
    downs = [pages.at[HOMES[k]] for k in DOWN]
    going = {}

    def move(src, dst, number):
        going[number] = pltpu.make_async_copy(src, dst, single.at[number])
        going[number].start()

    def done(*numbers):
        for number in numbers:
            going.pop(number).wait()

    def shard_of(k):
        if k < 3:
            return shards[0].at[:, pl.ds(k * 1024, 1024)]
        if k == 3:
            return shards[1]
        return shards[2].at[:, pl.ds(UP.index(k) * 1024, 1024)]

    def page_of(k):
        return pages.at[HOMES[k]]

    def local_copies(k):
        if k in DOWN:
            return [
                pltpu.make_async_copy(
                    shards[3].at[pl.ds(r * 32, 32), pl.ds(DOWN.index(k) * 256, 256)],
                    page_of(k).at[mine + (slice(None), pl.ds(r * 256, 256))],
                    own.at[k * 4 + r],
                )
                for r in range(4)
            ]
        return [pltpu.make_async_copy(shard_of(k), page_of(k).at[mine], own.at[k * 4])]

    local = {k: local_copies(k) for k in range(12)}
    small[...] = jnp.zeros_like(small)
    for i, entries in enumerate(narrow):
        small[pl.ds(i, 1), pl.ds(0, entries.shape[1])] = entries[...].astype(F32)
    packed = small[...]
    kind = lax.broadcasted_iota(jnp.int32, (8, 128), 0)
    fours = pltpu.roll(packed, lax.rem(me, 4) * 32, 1)
    twos = pltpu.roll(packed, lax.rem(me, 2) * 64, 1)
    small[...] = jnp.where(kind < 6, fours, jnp.where(kind == 6, twos, packed))
    early = [pltpu.make_async_copy(small, smalls.at[mine], own.at[48])]
    for k in (0, 1, 2, 3, 4, 5, 6, 7, 11):
        early += local[k]
    for copy in early:
        copy.start()
    move(cot_i, low, 0)
    move(x_i, x, 1)
    greet(me, at)

    def row(vectors, i):
        return vectors.at[pl.ds(i, 1), :]

    def kept_len(seq):
        return lengths[assignment[seq]]

    def task_low():
        for seq in range(2):
            inside = lax.broadcasted_iota(jnp.int32, (320, 1), 0) < kept_len(seq)
            row_mask[pl.ds(seq * 320, 320), :] = jnp.where(inside, 1.0, 0.0)
        for s in (s4, s2, s1):
            s[...] = jnp.zeros_like(s)
        mixed[pl.ds(640, 64), :] = jnp.zeros((64, 3072), BF16)
        done(0)
        low[...] = (low[...].astype(F32) * row_mask[...]).astype(BF16)
        s4[pl.ds(5, 1), :] = whole_sum(column_sum(low[...].astype(F32)))

    def task_first():
        spread_vectors(smalls, v4, v2, v1)
        done(1)
        norm_rows(x, row(v4, 0), row(v4, 1), normed)

    def task_project(j):
        shift = None if j == 1 else v2.at[pl.ds(6, 1), pl.ds(0 if j == 0 else 1024, 1024)]
        project(normed, page_of(j), shift, mixed, j * 1024)
        if j == 1:
            turn(normed, normed1_t)
        done(8 + j)

    def task_attend(first, count):
        attend(first, count, mixed, kept_len, attended, probs, probs_o, probs_sems)

    def task_hidden():
        branch_out(attended, page_of(3), row(v4, 2), x, hidden)
        norm_rows(hidden, row(v4, 3), row(v4, 4), normed)
        done(11)

    def task_turns():
        turn(attended, other_t)
        move(other_t, attended_o, 5)
        done(5)
        turn(normed, other_t)

    def task_up(j):
        feed_up(normed, page_of(UP[j]), row(v1, 7), acts[j], slope, j * 1024)

    def task_feed(j):
        page = page_of(UP[j])
        slope_back(low, downs, j, slope, grad_pre, s1)
        outer_box(other_t, grad_pre, pages.at[MADE[j % 3]])
        back_through(grad_pre, page, total, j == 0)
        if j == 3:
            move(attended_o, other_t, 5)
        back = (3, 2, 1, 0)[j]
        move(spilled.at[back], page, 12 + back)

    def task_outer(j):
        if j > 1:
            done(2, 6)
        halves = [flat.at[2 + y, pl.ds(0, 512)] for y in range(2)]
        outer(acts[j], low, halves)
        for y, number in ((0, 2), (1, 6)):
            move(halves[y].reshape(2, 2, 4, 32, 1024), down_o.at[j, y], number)
        if j in (0, 3):
            done(2, 6)

    def task_second():
        norm_back(hidden, row(v4, 3), total, low, branch, part1, part2, part3)
        for i, part in ((3, part1), (4, part2), (2, part3)):
            s4[pl.ds(i, 1), :] = whole_sum(part[...])

    def task_out():
        done(5)
        outer_box(other_t, branch, pages.at[MADE[4 % 3]])

    def task_att():
        done(12 + 3)
        back_through(branch, page_of(UP[0]), grad_att, True)

    def task_attend_back(first, count):
        attend_back(first, count, mixed, attended, grad_att, probs, probs_o, probs_sems, grads)

    def task_mixed(j, m):
        outer_box(normed1_t, grads[j], pages.at[MADE[m % 3]])
        if j != 1:
            s2[pl.ds(6, 1), pl.ds(0 if j == 0 else 1024, 1024)] = whole_sum(
                column_sum(grads[j][...].astype(F32))
            )

    def task_through(j):
        done(12 + j)
        back_through(grads[j], page_of(UP[3 - j]), total, j == 2)

    def task_down(c):
        feed_down(acts, downs[c], row(v4, 5), hidden, row_mask, result, c)
        if c == 3:
            move(result, result_o, 3)

    def task_end():
        norm_back(x, row(v4, 0), total, branch, x, part1, part2, None)
        for i, part in ((0, part1), (1, part2)):
            s4[pl.ds(i, 1), :] = whole_sum(part[...])
        move(x, input_grad_o, 4)
        tiny = small_refs[0]
        for z in range(4):
            for y in range(2):
                for x_ in range(2):
                    for c in range(2):
                        d = ((z * 2 + y) * 2 + x_) * 2 + c
                        tiny[z, y, x_, c] = (
                            s4[:, d // 4 * 128 : d // 4 * 128 + 128]
                            + s2[:, d // 2 * 128 : d // 2 * 128 + 128]
                            + s1[:, d * 128 : d * 128 + 128]
                        )

    tasks = {
        3: [(task_low,)],
        5: [(task_first,), (task_project, 0)],
        6: [(task_project, 1)],
        7: [(task_project, 2), (task_attend, 0, 4)],
        8: [(task_attend, 4, 6)],
        9: [(task_attend, 10, 6)],
        10: [(task_hidden,)],
        11: [(task_turns,), (task_up, 0)],
        12: [(task_outer, 0)],
        13: [(task_feed, 0)],
        14: [(task_up, 1), (task_feed, 1)],
        15: [(task_up, 2), (task_feed, 2)],
        16: [(task_up, 3), (task_feed, 3)],
        17: [(task_second,), (task_out,)],
        18: [(task_outer, 1), (task_outer, 2), (task_outer, 3)],
        19: [(task_att,), (task_attend_back, 0, 4)],
        20: [(task_attend_back, 4, 4)],
        21: [(task_attend_back, 8, 4)],
        22: [(task_attend_back, 12, 4), (task_mixed, 2, 9)],
        23: [(task_mixed, 1, 10), (task_through, 2), (task_through, 1)],
        24: [(task_mixed, 0, 11), (task_through, 0), (task_end,)],
        25: [(task_down, 0), (task_down, 1)],
        26: [(task_down, 2), (task_down, 3)],
    }
    goals = [(2, 0, c) for c in (0, 1024, 2048, 3072)] + [(1, 0, 0)]
    goals += [(3, r, 0) for r in (0, 32, 64, 96)] + [(0, 0, 2048), (0, 0, 1024), (0, 0, 0)]
    flying, flows = {}, {}

    def begin(k, stage):
        if stage:
            for copy in flying.pop((k, stage - 1)):
                copy.wait()
        source = None if k in DOWN else shard_of(k)
        flying[k, stage] = gather_stage(page_of(k), PARTS if k else FIRST, stage, me, at, sems, k % 8, source)
        for copy in flying[k, stage]:
            copy.start()

    small_going = []
    for tick in range(LAST + 1):
        for stage in range(STAGES + 1):
            if 0 <= tick - stage < 12:
                begin(tick - stage, stage)
            if stage == 0 and tick <= STAGES + 1:
                for copy in small_going:
                    copy.wait()
                small_going = []
                if tick <= STAGES:
                    small_going = gather_stage(smalls, SMALL, tick, me, at, sems, 8, small)
                for copy in small_going:
                    copy.start()
            if tick == 0 and stage == 0:
                for copy in early:
                    copy.wait()
            if tick + 1 in (8, 9, 10) and stage == 0:
                for copy in local[tick + 1]:
                    copy.start()
        k = tick - STAGES - 1
        if 0 <= k < 12:
            for copy in flying.pop((k, STAGES)):
                copy.wait()
            if k < 4:
                move(page_of(k), spilled.at[k], 8 + k)
        for stage in (1, 2, 3, 4, 5, 0):
            m = tick - BEGIN - stage
            if 0 <= m < 12:
                if stage == 0:
                    which, r, c = goals[m]
                    out = outs[which].at[pl.ds(r, ROWS), pl.ds(c, WIDE)]
                    source = down_o.at[:, :, :, :, r // 32] if which == 3 else None
                    made = pages.at[MADE[m % 3]]
                    flows[m] = Flow(made, source, out, BACK, cores[m % 2], slots[m % 3], lasts[m % 4], m % 8, back_sems, me, at)
                    flows[m].start()
                else:
                    flows[m].step(stage)
        if tick >= LAST - STAGES - 1:
            if tick == LAST - STAGES - 1:
                flows["small"] = Flow(small_refs[0], None, small_out, SMALL_BACK, small_refs[1], small_refs[2:7], small_refs[7:], 8, back_sems, me, at)
                flows["small"].start()
            else:
                flows["small"].step(tick - LAST + STAGES + 1)
        for task, *args in tasks.get(tick, ()):
            task(*args)
        if tick + 1 in (8, 9, 10):
            for copy in local[tick + 1]:
                copy.wait()
    done(3, 4)


def layer(x, cot, lengths, assignment, shards, narrow):
    anywhere = pl.BlockSpec(memory_space=pl.ANY)
    inside = pl.BlockSpec(memory_space=pltpu.VMEM)
    box = (4, 2, 2, 2)
    page = box + (32, 1024)
    flat, turned = (640, 1024), (1024, 640)
    made = [((32, 3072), F32), ((32, 1024), F32), ((32, 4096), F32), ((128, 1024), F32), ((8, 128), F32)]
    made += [(flat, BF16), (flat, BF16)]
    made += [((4,) + page, BF16), ((16, 2, 320, LEN_PAD), BF16), (box + (4, 32, 1024), BF16), (turned, BF16)]
    scratch = [
        ((11,) + page, BF16),
        (box + (8, 128), F32),
        ((8, 1024), F32),
        ((8, 2048), F32),
        ((8, 4096), F32),
        ((11,) + flat, BF16),
        (turned, BF16),
        (turned, BF16),
        ((704, 3072), BF16),
        (flat, F32),
        (flat, F32),
        ((2, 2, 320, LEN_PAD), BF16),
        ((640, 1), F32),
        ((8, 1024), F32),
        ((8, 2048), F32),
        ((8, 4096), F32),
    ] + [((8, 1024), F32)] * 3 + [((8, 128), F32)]
    way, last = flow_buffers(BACK, BF16)
    scratch += way * 3 + last * 4 + [((4, 2, 2, 32, 1024), BF16)] * 2
    way, last = flow_buffers(SMALL_BACK, F32)
    scratch += [(box + (8, 128), F32), ((4, 2, 2, 8, 128), F32)] + way + last
    dma = pltpu.SemaphoreType.DMA
    return pl.pallas_call(
        layer_kernel,
        out_shape=[jax.ShapeDtypeStruct(s, d) for s, d in made],
        in_specs=[anywhere] * 2 + [pl.BlockSpec(memory_space=pltpu.SMEM)] * 2 + [anywhere] * 4 + [inside] * 8,
        out_specs=[inside] * 5 + [anywhere] * 6,
        scratch_shapes=[pltpu.VMEM(s, d) for s, d in scratch]
        + [dma((9, COPIES))] * 4
        + [dma((9,)), dma((49,)), dma((16,)), dma((2,))],
        compiler_params=pltpu.CompilerParams(
            collective_id=0, has_side_effects=True, vmem_limit_bytes=64 << 20
        ),
        name="layer",
    )(x, cot, lengths, assignment, *shards, *narrow)


def finish_kernel(*refs):
    small, refs = refs[0], refs[1:]
    arrays, narrow, outs, refs = refs[:6], refs[6:14], refs[14:20], refs[20:]
    blocks, refs = refs[:6], refs[6:]
    into = [pltpu.make_async_copy(a, block, refs[0].at[i]) for i, (a, block) in enumerate(zip(arrays, blocks))]
    back = [pltpu.make_async_copy(block, o, refs[1].at[i]) for i, (o, block) in enumerate(zip(outs, blocks))]
    for copy in into:
        copy.start()
    me = lax.axis_index("dp")
    fours = pltpu.roll(small[...], 128 - lax.rem(me, 4) * 32, 1)
    for i in range(6):
        narrow[i][...] = fours[i : i + 1, :32]
    twos = pltpu.roll(small[...], 128 - lax.rem(me, 2) * 64, 1)
    narrow[6][...] = twos[6:7, :64]
    narrow[7][...] = small[7:8, :]
    for first, second in zip(into, back):
        first.wait()
        second.start()
    for copy in back:
        copy.wait()


def finish(total, *arrays):
    anywhere = pl.BlockSpec(memory_space=pl.ANY)
    inside = pl.BlockSpec(memory_space=pltpu.VMEM)
    found = pl.pallas_call(
        lambda *refs: finish_kernel(*refs[:7], *refs[7:15], *refs[15:]),
        out_shape=[jax.ShapeDtypeStruct((1, n), F32) for n in (32,) * 6 + (64, 128)]
        + [jax.ShapeDtypeStruct(a.shape, a.dtype) for a in arrays],
        in_specs=[inside] + [anywhere] * 6,
        out_specs=[inside] * 8 + [anywhere] * 6,
        scratch_shapes=[pltpu.VMEM(a.shape, a.dtype) for a in arrays]
        + [pltpu.SemaphoreType.DMA((len(arrays),))] * 2,
        compiler_params=pltpu.CompilerParams(vmem_limit_bytes=63 << 20),
        name="finish",
    )(total, *arrays)
    return [a.reshape(-1) for a in found[:8]], found[8:]


NARROW = (0, 1, 5, 6, 7, 11)
WEIGHTS = (2, 4, 8, 10)


def on_box(inputs, lengths, assignment, *rest):
    weights, cotangent = rest[:12], rest[12]
    x = inputs.reshape(640, 1024)
    cot = cotangent.reshape(640, 1024)
    narrow = [weights[i][None] for i in (*NARROW, 3, 9)]
    made = layer(
        x, cot, lengths, assignment, [weights[i] for i in WEIGHTS], narrow
    )
    sums, (total, input_grad, result) = made[:4], made[4:7]
    narrow, (result, input_grad, *sums) = finish(total, result, input_grad, *sums)
    found = [None] * 12
    for row, i in enumerate((*NARROW, 3, 9)):
        found[i] = narrow[row]
    for i, s in zip(WEIGHTS, sums):
        found[i] = s
    return (result.reshape(inputs.shape), input_grad.reshape(inputs.shape), *found)


def plain(
    inputs,
    lengths,
    assignment,
    norm1_gain,
    norm1_bias,
    qkv_weight,
    qv_bias,
    out_weight,
    out_bias,
    norm2_gain,
    norm2_bias,
    up_weight,
    up_bias,
    down_weight,
    down_bias,
    cotangent,
):
    gathered = (
        lax.all_gather(norm1_gain, "dp", axis=0, tiled=True),
        lax.all_gather(norm1_bias, "dp", axis=0, tiled=True),
        lax.all_gather(qkv_weight, "dp", axis=0, tiled=True),
        lax.all_gather(qv_bias, "dp", axis=0, tiled=True),
        lax.all_gather(out_weight, "dp", axis=0, tiled=True),
        lax.all_gather(out_bias, "dp", axis=0, tiled=True),
        lax.all_gather(norm2_gain, "dp", axis=0, tiled=True),
        lax.all_gather(norm2_bias, "dp", axis=0, tiled=True),
        lax.all_gather(up_weight, "dp", axis=0, tiled=True),
        lax.all_gather(up_bias, "dp", axis=0, tiled=True),
        lax.all_gather(down_weight, "dp", axis=0, tiled=True),
        lax.all_gather(down_bias, "dp", axis=0, tiled=True),
    )
    seq_count, tok_count, model_width = inputs.shape
    rows_all = seq_count * tok_count
    split_shape = (seq_count, tok_count, HEADS, HEAD)
    head_scale = HEAD ** (-0.5)
    matches = assignment[:, None] == jnp.arange(lengths.shape[0], dtype=jnp.int32)[None, :]
    kept_len = jnp.sum(jnp.where(matches, lengths[None, :], 0), axis=1)
    key_mask = jnp.arange(tok_count, dtype=jnp.int32)[None, :] < kept_len[:, None]
    row_mask = key_mask.reshape(rows_all, 1).astype(jnp.float32)
    gain_first = gathered[0].astype(jnp.float32)
    shift_first = gathered[1].astype(jnp.float32)
    qv_full = gathered[3].astype(jnp.float32)
    proj_shift = gathered[5].astype(jnp.float32)
    gain_second = gathered[6].astype(jnp.float32)
    shift_second = gathered[7].astype(jnp.float32)
    up_shift = gathered[9].astype(jnp.float32)
    down_shift = gathered[11].astype(jnp.float32)
    inputs_flat = inputs.reshape(rows_all, model_width).astype(jnp.float32)
    normed_first, first_back = jax.vjp(layer_norm, inputs_flat, gain_first, shift_first)
    normed_low = normed_first.astype(jnp.bfloat16)
    full_bias = jnp.concatenate(
        [qv_full[:model_width], jnp.zeros((model_width,), jnp.float32), qv_full[model_width:]]
    )
    mixed_qkv = (
        jnp.dot(normed_low, gathered[2], preferred_element_type=jnp.float32) + full_bias
    ).astype(jnp.bfloat16)
    queries = mixed_qkv[:, :model_width].reshape(split_shape)
    keys_all = mixed_qkv[:, model_width : 2 * model_width].reshape(split_shape)
    values_all = mixed_qkv[:, 2 * model_width :].reshape(split_shape)
    scores = (
        jnp.einsum("bqhd,bkhd->bhqk", queries, keys_all, preferred_element_type=jnp.float32)
        * head_scale
    )
    scores = jnp.where(key_mask[:, None, None, :], scores, masked_score)
    row_max = jnp.max(scores, axis=-1, keepdims=True)
    exponent = jnp.exp(scores - row_max)
    row_total = jnp.sum(exponent, axis=-1, keepdims=True)
    softmax_probs = exponent / row_total
    log_total = row_max + jnp.log(row_total)
    attended = jnp.einsum(
        "bhqk,bkhd->bqhd",
        softmax_probs.astype(jnp.bfloat16),
        values_all,
        preferred_element_type=jnp.float32,
    )
    attended = attended.reshape(rows_all, model_width).astype(jnp.bfloat16)
    hidden = inputs_flat + (
        jnp.dot(attended, gathered[4], preferred_element_type=jnp.float32) + proj_shift
    )
    normed_second, second_back = jax.vjp(layer_norm, hidden, gain_second, shift_second)
    second_low = normed_second.astype(jnp.bfloat16)
    pre_act = jnp.dot(second_low, gathered[8], preferred_element_type=jnp.float32) + up_shift
    activation, gelu_back = jax.vjp(gelu_exact, pre_act)
    act_low = activation.astype(jnp.bfloat16)
    output_rows = row_mask * (
        hidden + (jnp.dot(act_low, gathered[10], preferred_element_type=jnp.float32) + down_shift)
    )
    result = output_rows.reshape(inputs.shape).astype(jnp.bfloat16)
    grad_rows = cotangent.reshape(rows_all, model_width).astype(jnp.float32) * row_mask
    grad_low = grad_rows.astype(jnp.bfloat16)
    down_grad = contract_rows(act_low, grad_low)
    down_bias_grad = jnp.sum(grad_low.astype(jnp.float32), axis=0)
    grad_pre = gelu_back(contract_cols(grad_low, gathered[10]))[0].astype(jnp.bfloat16)
    up_grad = contract_rows(second_low, grad_pre)
    up_bias_grad = jnp.sum(grad_pre.astype(jnp.float32), axis=0)
    grad_second, gain2_grad, shift2_grad = second_back(contract_cols(grad_pre, gathered[8]))
    grad_hidden = grad_rows + grad_second
    branch_low = grad_hidden.astype(jnp.bfloat16)
    proj_grad = contract_rows(attended, branch_low)
    proj_bias_grad = jnp.sum(branch_low.astype(jnp.float32), axis=0)
    grad_att = contract_cols(branch_low, gathered[4]).astype(jnp.bfloat16).reshape(split_shape)
    scores_again = (
        jnp.einsum("bqhd,bkhd->bhqk", queries, keys_all, preferred_element_type=jnp.float32)
        * head_scale
    )
    scores_again = jnp.where(key_mask[:, None, None, :], scores_again, masked_score)
    probs_again = jnp.exp(scores_again - log_total)
    probs_low = probs_again.astype(jnp.bfloat16)
    grad_probs = jnp.einsum(
        "bqhd,bkhd->bhqk", grad_att, values_all, preferred_element_type=jnp.float32
    )
    grad_values = jnp.einsum(
        "bhqk,bqhd->bkhd", probs_low, grad_att, preferred_element_type=jnp.float32
    )
    inner_sum = jnp.sum(probs_again * grad_probs, axis=-1, keepdims=True)
    grad_scores = (probs_again * (grad_probs - inner_sum)).astype(jnp.bfloat16)
    grad_queries = (
        jnp.einsum("bhqk,bkhd->bqhd", grad_scores, keys_all, preferred_element_type=jnp.float32)
        * head_scale
    )
    grad_keys = (
        jnp.einsum("bhqk,bqhd->bkhd", grad_scores, queries, preferred_element_type=jnp.float32)
        * head_scale
    )
    grad_mixed = jnp.concatenate(
        [
            grad_queries.reshape(rows_all, model_width),
            grad_keys.reshape(rows_all, model_width),
            grad_values.reshape(rows_all, model_width),
        ],
        axis=1,
    ).astype(jnp.bfloat16)
    qkv_grad = contract_rows(normed_low, grad_mixed)
    column_sums = jnp.sum(grad_mixed.astype(jnp.float32), axis=0)
    qv_grad = jnp.concatenate([column_sums[:model_width], column_sums[2 * model_width :]])
    grad_first, gain1_grad, shift1_grad = first_back(contract_cols(grad_mixed, gathered[2]))
    input_grad = (grad_hidden + grad_first).reshape(inputs.shape).astype(jnp.bfloat16)
    all_sums = (
        lax.psum_scatter(gain1_grad, "dp", scatter_dimension=0, tiled=True),
        lax.psum_scatter(shift1_grad, "dp", scatter_dimension=0, tiled=True),
        lax.psum_scatter(qkv_grad, "dp", scatter_dimension=0, tiled=True),
        lax.psum_scatter(qv_grad, "dp", scatter_dimension=0, tiled=True),
        lax.psum_scatter(proj_grad, "dp", scatter_dimension=0, tiled=True),
        lax.psum_scatter(proj_bias_grad, "dp", scatter_dimension=0, tiled=True),
        lax.psum_scatter(gain2_grad, "dp", scatter_dimension=0, tiled=True),
        lax.psum_scatter(shift2_grad, "dp", scatter_dimension=0, tiled=True),
        lax.psum_scatter(up_grad, "dp", scatter_dimension=0, tiled=True),
        lax.psum_scatter(up_bias_grad, "dp", scatter_dimension=0, tiled=True),
        lax.psum_scatter(down_grad, "dp", scatter_dimension=0, tiled=True),
        lax.psum_scatter(down_bias_grad, "dp", scatter_dimension=0, tiled=True),
    )
    attn_sums = all_sums[:6]
    mlp_sums = all_sums[6:]
    return (
        result,
        input_grad,
        attn_sums[0],
        attn_sums[1],
        attn_sums[2],
        attn_sums[3],
        attn_sums[4],
        attn_sums[5],
        mlp_sums[0],
        mlp_sums[1],
        mlp_sums[2],
        mlp_sums[3],
        mlp_sums[4],
        mlp_sums[5],
    )


def local(*args):
    return on_box(*args) if lax.axis_size("dp") == 32 else plain(*args)


def solution(mesh):
    placed = (
        P("dp", None, None),
        P(),
        P("dp"),
        P("dp"),
        P("dp"),
        P("dp", None),
        P("dp"),
        P("dp", None),
        P("dp"),
        P("dp"),
        P("dp"),
        P("dp", None),
        P("dp"),
        P("dp", None),
        P("dp"),
        P("dp", None, None),
    )
    return jax.shard_map(
        local,
        mesh=mesh,
        in_specs=placed,
        out_specs=(
            P("dp", None, None),
            P("dp", None, None),
            P("dp"),
            P("dp"),
            P("dp", None),
            P("dp"),
            P("dp", None),
            P("dp"),
            P("dp"),
            P("dp"),
            P("dp", None),
            P("dp"),
            P("dp", None),
            P("dp"),
        ),
        check_vma=False,
    )
```

```python
import jax
import jax.numpy as jnp
from jax import lax
from jax.experimental import pallas as pl
from jax.experimental.pallas import tpu as pltpu
from jax.sharding import PartitionSpec as P

HEADS = 16
HEAD = 64


eps = 1e-06
masked_score = -1000000000.0


def layer_norm(values, norm_gain, norm_shift):
    average = jnp.mean(values, axis=-1, keepdims=True)
    centered = values - average
    variance = jnp.mean(centered * centered, axis=-1, keepdims=True)
    return centered * lax.rsqrt(variance + eps) * norm_gain + norm_shift


def gelu_exact(values):
    return jax.nn.gelu(values, approximate=False)


def contract_rows(left, right):
    return lax.dot_general(
        left, right, (((0,), (0,)), ((), ())), preferred_element_type=jnp.float32
    )


def contract_cols(left, right):
    return lax.dot_general(
        left, right, (((1,), (1,)), ((), ())), preferred_element_type=jnp.float32
    )


BF16 = jnp.bfloat16
F32 = jnp.float32
MESH = pl.DeviceIdType.MESH
STRIDE = {"z": 8, "y": 4, "x": 2}
ROWS = 32
WIDE = 1024
STAGES = 4
PARTS = (
    ("zZyx", 0, 16, 0, 384),
    ("zZxy", 16, 16, 0, 384),
    ("xzZy", 0, 16, 384, 640),
    ("yzZx", 16, 16, 384, 640),
)
FIRST = (("zZyx", 0, 16, 0, 1024), ("zZxy", 16, 16, 0, 1024))
COPIES = 6 * len(PARTS) + 1


def coords():
    me = lax.axis_index("dp")
    at = {
        "z": lax.div(me, 8),
        "y": lax.rem(lax.div(me, 4), 2),
        "x": lax.rem(lax.div(me, 2), 2),
        "c": lax.rem(me, 2),
    }
    return me, at


def sibling(me, at):
    return me + 1 - 2 * at["c"]


class Hop:
    def __init__(self, copy, sends=None, hears=None):
        self.copy, self.sends, self.hears = copy, sends, hears

    def start(self):
        if self.sends is None:
            self.copy.start()
        else:
            pl.when(self.sends)(self.copy.start)

    def wait(self):
        if self.sends is None:
            self.copy.wait()
        else:
            pl.when(self.sends)(self.copy.wait_send)
            pl.when(self.hears)(self.copy.wait_recv)


def inner(at):
    return lax.div(at["z"] + 1, 2) == 1


def far(at):
    return 3 * (1 - lax.div(at["z"], 2))


def hops(me, at, dim):
    z = at["z"]
    if dim == "z":
        found = []
        for k in (1, 2, 3):
            there = lax.rem(z + k, 4)
            when = {1: (z < 3, z > 0), 2: (None, None), 3: (z > 0, z < 3)}[k]
            found.append((there, me + (there - z) * 8, *when))
        return found
    if dim == "Z":
        return [(far(at), me + 8 - 16 * lax.rem(z, 2), inner(at), jnp.logical_not(inner(at)))]
    there = 1 - at[dim]
    return [(there, me + (there - at[dim]) * STRIDE[dim], None, None)]


def count_of(dim):
    return 3 if dim == "z" else 1


def greet(me, at):
    barrier = pltpu.get_barrier_semaphore()
    devices = [sibling(me, at)]
    for dim in "yx":
        devices += [hop[1] for hop in hops(me, at, dim)]
    for k in (1, 2, 3):
        devices.append(me + (lax.rem(at["z"] + k, 4) - at["z"]) * 8)
    for device in devices:
        pl.semaphore_signal(barrier, inc=1, device_id=(device,), device_id_type=MESH)
    pl.semaphore_wait(barrier, len(devices))


def remote(src, dst, sems, slot, number, device):
    return pltpu.make_async_remote_copy(
        src_ref=src,
        dst_ref=dst,
        send_sem=sems[0].at[slot, number],
        recv_sem=sems[1].at[slot, number],
        device_id=(device,),
        device_id_type=MESH,
    )


def held(order, stage, at):
    index = []
    for dim in "zyx":
        if dim == "z" and order[stage] == "Z":
            index.append(far(at))
        else:
            done = "Z" if dim == "z" else dim
            index.append(slice(None) if done in order[:stage] else at[dim])
    return tuple(index)


def gather_stage(base, parts, stage, me, at, sems, slot, source=None):
    if stage == STAGES:
        block = base.at[:, :, :, at["c"]]
        return [Hop(remote(block, block, sems, slot, COPIES - 1, sibling(me, at)))]
    number, copies = 0, []
    for order, row, rows, col, columns in parts:
        here = (pl.ds(row, rows), pl.ds(col, columns))
        for s in range(STAGES):
            for _, device, sends, hears in hops(me, at, order[s]):
                if s == stage:
                    block = base.at[held(order, stage, at) + (at["c"],) + here]
                    src = source.at[here] if source is not None and stage == 0 else block
                    copies.append(Hop(remote(src, block, sems, slot, number, device), sends, hears))
                number += 1
    return copies


SMALL = (("zZyx", 0, 8, 0, 128),)


def remaining(order, stage):
    left = [dim for dim in "zyx" if dim not in order[:stage]]
    return tuple({"z": 4, "y": 2, "x": 2}[dim] for dim in left)


def pick(order, stage, dim, index):
    return tuple(index if d == dim.lower() else slice(None) for d in "zyx" if d not in order[:stage])


BACK = tuple((part[0][::-1], *part[1:]) for part in PARTS)
SMALL_BACK = tuple((part[0][::-1], *part[1:]) for part in SMALL)


def add_up(dst, terms, lead):
    loops = lead[: max(len(lead) - 1, 0)] if len(lead) > 1 else ()
    count = 1
    for n in loops:
        count *= n

    def body(i, carry):
        index = []
        for n in loops[::-1]:
            index.append(lax.rem(i, n))
            i = lax.div(i, n)
        index = tuple(index[::-1]) + (slice(None),) * (len(lead) - len(loops) + 2)
        if len(terms) == 2 and dst.dtype == terms[0].dtype:
            dst[index] = terms[0][index] + terms[1][index]
            return carry
        total = terms[0][index].astype(F32)
        for term in terms[1:]:
            total = total + term[index].astype(F32)
        dst[index] = total.astype(dst.dtype)
        return carry

    if count == 1:
        body(0, 0)
    else:
        lax.fori_loop(0, count, body, 0)


class Flow:
    def __init__(self, made, source, out, parts, from_core, rest, last, slot, sems, me, at):
        self.made, self.source, self.out, self.parts = made, source, out, parts
        self.from_core = from_core
        self.arrived, self.totals = [], []
        for part, (order, *_) in enumerate(parts):
            self.arrived.append((*rest[:3], last[part]))
            self.totals.append(dict(zip([s for s in range(3) if order[s] != "Z"], rest[3:5])))
            rest = rest[5:]
        self.slot, self.sems, self.me, self.at = slot, sems, me, at
        self.own = made.at[:, :, :, at["c"]]

    def start(self):
        there = 1 - self.at["c"]
        source = self.made if self.source is None else self.source
        self.going = [
            remote(
                source.at[:, :, :, there],
                self.from_core,
                self.sems,
                self.slot,
                COPIES - 1,
                sibling(self.me, self.at),
            )
        ]
        if self.source is not None:
            self.going.append(
                pltpu.make_async_copy(source.at[:, :, :, self.at["c"]], self.own, self.sems[2].at[self.slot])
            )
        for copy in self.going:
            copy.start()

    def sum_before(self, part, stage):
        order, row, rows, col, columns = self.parts[part]
        done = [s for s in range(stage) if s in self.totals[part]]
        if not done:
            return self.own.at[:, :, :, pl.ds(row, rows), pl.ds(col, columns)]
        return self.totals[part][done[-1]]

    def take(self, part, stage):
        order, row, rows, col, columns = self.parts[part]
        s = stage - 2
        dim, arrived = order[s], self.arrived[part][s]
        before = self.sum_before(part, s)
        if dim == "Z":
            index = pick(order, s, "z", far(self.at))

            @pl.when(inner(self.at))
            def _():
                add_up(before.at[index], [before.at[index], arrived.at[0]], remaining(order, s)[1:])

            return
        if stage == STAGES + 1:
            total = self.out.at[pl.ds(row, rows), pl.ds(col, columns)]
        else:
            total = self.totals[part][s]
        mine = before.at[pick(order, s, dim, self.at[dim])]
        left = remaining(order, s + 1)
        if dim != "z":
            add_up(total, [mine, arrived.at[0]], left)
            return
        z = self.at["z"]
        for when, came in ((z == 0, (1, 2)), (inner(self.at), (0, 1, 2)), (z == 3, (0, 1))):

            @pl.when(when)
            def _(came=came):
                add_up(total, [mine] + [arrived.at[i] for i in came], left)

    def step(self, stage):
        for copy in self.going:
            copy.wait()
        if stage == 1:
            add_up(self.own, [self.own, self.from_core], (4, 2, 2))
        else:
            for part in range(len(self.parts)):
                self.take(part, stage)
        self.going, number = [], 0
        for part, (order, row, rows, col, columns) in enumerate(self.parts):
            for s in range(STAGES):
                if s + 1 == stage:
                    before = self.sum_before(part, s)
                    for i, (there, device, sends, hears) in enumerate(hops(self.me, self.at, order[s])):
                        if order[s] == "Z":
                            sends, hears = hears, sends
                        src = before.at[pick(order, s, order[s], there)]
                        copy = remote(src, self.arrived[part][s].at[i], self.sems, self.slot, number + i, device)
                        self.going.append(Hop(copy, sends, hears))
                number += count_of(order[s])
        for copy in self.going:
            copy.start()


def flow_buffers(parts, dtype):
    shapes, last = [], []
    for order, _, high, _, wide in parts:
        totals = []
        for s in range(STAGES):
            if order[s] == "Z":
                left = remaining(order, s)[1:]
            else:
                left = remaining(order, s + 1)
                if s < 3:
                    totals.append((left + (high, wide), dtype))
            (shapes if s < 3 else last).append(((count_of(order[s]),) + left + (high, wide), dtype))
        shapes += totals
    return shapes, last


EPS = 1e-06
MASKED = -1000000000.0
LEN_PAD = 384


def dot_nn(a, b):
    return jnp.dot(a, b, preferred_element_type=F32)


def dot_nt(a, b):
    return lax.dot_general(a, b, (((1,), (1,)), ((), ())), preferred_element_type=F32)


def dot_tn(a, b):
    return lax.dot_general(a, b, (((0,), (0,)), ((), ())), preferred_element_type=F32)


def block_of(index, size):
    return pl.ds(pl.multiple_of(index * size, size), size)


def spread_vectors(smalls, v4, v2, v1):
    for z in range(4):
        for y in range(2):
            four = None
            for x in range(2):
                two = None
                for c in range(2):
                    one = smalls[z, y, x, c]
                    d = ((z * 2 + y) * 2 + x) * 2 + c
                    v1[:, d * 128 : d * 128 + 128] = one
                    two = one if two is None else two + one
                d = (z * 2 + y) * 2 + x
                v2[:, d * 128 : d * 128 + 128] = two
                four = two if four is None else four + two
            d = z * 2 + y
            v4[:, d * 128 : d * 128 + 128] = four


def norm_rows(src, gain, shift, dst):
    @pl.loop(0, src.shape[0] // 64)
    def _(i):
        rows = block_of(i, 64)
        values = src[rows, :].astype(F32)
        centered = values - jnp.mean(values, axis=-1, keepdims=True)
        variance = jnp.mean(centered * centered, axis=-1, keepdims=True)
        normed = centered * lax.rsqrt(variance + EPS)
        dst[rows, :] = (normed * gain[...] + shift[...]).astype(BF16)


def project(normed, weight, shift, dst, col):
    @pl.loop(0, 2)
    def _(i):
        columns = block_of(i, 512)
        mixed = dot_nn(normed[...], weight[:, :, :, :, :, columns].reshape(1024, 512))
        if shift is not None:
            mixed = mixed + shift[:, columns]
        dst[pl.ds(0, 640), pl.ds(pl.multiple_of(col + i * 512, 512), 512)] = mixed.astype(BF16)


def attend(first, count, mixed, kept_len, attended, probs, probs_out, sems):
    lane = lax.broadcasted_iota(jnp.int32, (1, 128), 1)

    def out_copy(unit, slot):
        return pltpu.make_async_copy(probs.at[slot], probs_out.at[unit], sems.at[slot])

    @pl.loop(0, count // 2)
    def _(i):
        for slot in range(2):
            unit = first + i * 2 + slot
            seq, pair = lax.div(unit, 8), lax.rem(unit, 8)
            start = pl.multiple_of(seq * 320, 64)
            columns = block_of(pair, 128)
            q = mixed[pl.ds(start, 320), columns]
            k = mixed[pl.ds(start, LEN_PAD), block_of(pair + 8, 128)]
            v = mixed[pl.ds(start, LEN_PAD), block_of(pair + 16, 128)]
            kept = lax.broadcasted_iota(jnp.int32, (1, LEN_PAD), 1) < kept_len(seq)

            @pl.when(i > 0)
            def _():
                out_copy(unit, slot).wait()

            found = []
            for head in range(2):
                scale = jnp.where(lax.div(lane, 64) == head, 0.125, 0.0).astype(BF16)
                scores = jnp.where(kept, dot_nt(q * scale, k), MASKED)
                exponent = jnp.exp(scores - jnp.max(scores, axis=-1, keepdims=True))
                total = jnp.sum(exponent, axis=-1, keepdims=True)
                low = (exponent * (1.0 / total)).astype(BF16)
                probs[slot, head] = low
                found.append(dot_nn(low, v))
            attended[pl.ds(start, 320), columns] = jnp.where(
                lane < 64, found[0], found[1]
            ).astype(BF16)
            out_copy(unit, slot).start()

    for slot in range(2):
        out_copy(0, slot).wait()


def branch_out(attended, weight, shift, x, hidden):
    @pl.loop(0, 2)
    def _(i):
        columns = block_of(i, 512)
        branch = dot_nn(attended[...], weight[:, :, :, :, :, columns].reshape(1024, 512))
        hidden[:, columns] = x[:, columns].astype(F32) + (branch + shift[:, columns])


def feed_up(normed, weight, shift, act, slope, col):
    @pl.loop(0, 2)
    def _(i):
        columns = block_of(i, 512)
        pre = dot_nn(normed[...], weight[:, :, :, :, :, columns].reshape(1024, 512))
        pre = pre + shift[:, pl.ds(pl.multiple_of(col + i * 512, 512), 512)]
        below = 0.5 + 0.5 * lax.erf(pre * 0.7071067811865476)
        act[:, columns] = (pre * below).astype(BF16)
        density = jnp.exp(pre * pre * -0.5) * 0.3989422804014327
        slope[:, columns] = (below + pre * density).astype(BF16)


def outer(left, right, halves):
    for i, half in enumerate(halves):
        half[...] = dot_tn(left[:, i * 512 : i * 512 + 512], right[...]).astype(BF16)


def turn(src, dst):
    @pl.loop(0, 4)
    def _(i):
        rows = block_of(i, 256)
        dst[rows, :] = src[:, rows].T


def tall(block):
    parts = [block[..., i * 256 : i * 256 + 256] for i in range(4)]
    rows = jnp.stack(parts, axis=block.ndim - 2)
    return rows.reshape(-1, 256)


def feed_down(acts, page, shift, hidden, row_mask, result, c):
    columns = pl.ds(c * 256, 256)
    branch = dot_nn(acts[0][...], tall(page[0]))
    for z in range(1, 4):
        branch = branch + dot_nn(acts[z][...], tall(page[z]))
    whole = hidden[:, columns] + (branch + shift[:, columns])
    result[:, columns] = (whole * row_mask[...]).astype(BF16)


def column_sum(values):
    return jnp.sum(values.reshape(values.shape[0] // 8, 8, values.shape[1]), axis=0)


def norm_back(src, gain, grads, base, dst, by_scale, by_shift, by_low):
    for total in (by_scale, by_shift, by_low):
        if total is not None:
            total[...] = jnp.zeros_like(total)

    @pl.loop(0, 640 // 64)
    def _(i):
        rows = block_of(i, 64)
        values = src[rows, :].astype(F32)
        centered = values - jnp.mean(values, axis=-1, keepdims=True)
        inverse = lax.rsqrt(jnp.mean(centered * centered, axis=-1, keepdims=True) + EPS)
        normed = centered * inverse
        g = grads[rows, :]
        scaled = g * gain[...]
        along = jnp.mean(scaled * normed, axis=-1, keepdims=True)
        back = inverse * (scaled - jnp.mean(scaled, axis=-1, keepdims=True) - normed * along)
        whole = base[rows, :].astype(F32) + back
        rounded = whole.astype(BF16)
        dst[rows, :] = rounded
        by_scale[...] += column_sum(g * normed)
        by_shift[...] += column_sum(g)
        if by_low is not None:
            by_low[...] += column_sum(rounded.astype(F32))


def whole_sum(part):
    return jnp.sum(part, axis=0, keepdims=True)


def slope_back(low, pages, j, slope, grad_pre, total):
    @pl.loop(0, 2)
    def _(i):
        columns = block_of(i, 512)
        weight = jnp.concatenate([tall(page[j, i]) for page in pages], axis=1)
        grad = (dot_nt(low[...], weight) * slope[:, columns].astype(F32)).astype(BF16)
        grad_pre[:, columns] = grad
        there = pl.ds(pl.multiple_of(j * 1024 + i * 512, 512), 512)
        total[pl.ds(7, 1), there] = whole_sum(column_sum(grad.astype(F32)))


def back_through(left, page, total, first):
    part = dot_nt(left[...], page[...].reshape(1024, 1024))
    total[...] = part.astype(total.dtype) if first else total[...] + part


def outer_box(turned, right, dst):
    dst[...] = dot_nn(turned[...], right[...]).astype(BF16).reshape(4, 2, 2, 2, 32, 1024)


def attend_back(first, count, mixed, attended, grad_att, probs, probs_in, sems, grads):
    lane = lax.broadcasted_iota(jnp.int32, (1, 128), 1)

    def load(unit, slot):
        return pltpu.make_async_copy(probs_in.at[unit], probs.at[slot], sems.at[slot])

    load(first, 0).start()

    @pl.loop(0, count // 2)
    def _(i):
        for slot in range(2):
            unit = first + i * 2 + slot
            seq, pair = lax.div(unit, 8), lax.rem(unit, 8)
            start = pl.multiple_of(seq * 320, 64)
            rows = pl.ds(start, 320)
            col_q, col_k, col_v = (block_of(pair + 8 * n, 128) for n in range(3))
            load(unit, slot).wait()
            if slot == 0:
                load(unit + 1, 1).start()
            else:

                @pl.when(i + 1 < count // 2)
                def _():
                    load(unit + 1, 0).start()

            q = mixed[rows, col_q]
            k = mixed[pl.ds(start, LEN_PAD), col_k]
            v = mixed[pl.ds(start, LEN_PAD), col_v]
            grad_out = grad_att[rows, col_q]
            along = grad_out.astype(F32) * attended[rows, col_q].astype(F32)
            turned_q, turned_out = q.T, grad_out.T
            found = []
            for head in range(2):
                mine = lax.div(lane, 64) == head
                low = probs[slot, head]
                grad_p = dot_nt(grad_out * jnp.where(mine, 1.0, 0.0).astype(BF16), v)
                inner = jnp.sum(jnp.where(mine, along, 0.0), axis=-1, keepdims=True)
                grad_s = (low.astype(F32) * (grad_p - inner)).astype(BF16)
                part = slice(head * 64, head * 64 + 64)
                found.append((dot_nn(grad_s, k), dot_nn(turned_q[part], grad_s), dot_nn(turned_out[part], low)))
            grads[0][rows, col_q] = (jnp.where(lane < 64, found[0][0], found[1][0]) * 0.125).astype(BF16)
            for grad, scale, of in ((grads[1], 0.125, 1), (grads[2], 1.0, 2)):
                both = jnp.concatenate([found[0][of], found[1][of]], axis=0)
                grad[rows, col_q] = (both * scale).astype(BF16).T[:320]


UP = (4, 9, 10, 11)
DOWN = (5, 6, 7, 8)
HOMES = (0, 1, 2, 3, 4, 5, 6, 7, 0, 1, 2, 8)
MADE = (3, 9, 10)
BEGIN = 14
LAST = BEGIN + 12 + STAGES


def layer_kernel(*refs):
    x_i, cot_i, lengths, assignment = refs[:4]
    shards, narrow_i = refs[4:8], refs[8:16]
    refs = refs[7:]
    outs_o, small_o, input_grad_o, result_o, spilled, probs_o, down_o, attended_o = refs[9:13], *refs[13:20]
    (pages, smalls, v4, v2, v1, flat, normed1_t, other_t, mixed, hidden, total, probs, row_mask, s4, s2, s1, part1, part2, part3, small) = refs[20:40]
    outs, small_out, entries, refs = refs[40:44], refs[44], refs[45:53], refs[53:]
    per, parts = 5 * len(BACK), len(BACK)
    slots, refs = [refs[i * per : i * per + per] for i in range(3)], refs[3 * per :]
    lasts, refs = [refs[i * parts : i * parts + parts] for i in range(4)], refs[4 * parts :]
    cores, refs = refs[:2], refs[2:]
    small_refs, refs = refs[:8], refs[8:]
    send, recv, back_send, back_recv, back_own, own, single, probs_sems = refs
    sems, back_sems = (send, recv), (back_send, back_recv, back_own)
    me, at = coords()
    mine = (at["z"], at["y"], at["x"], at["c"])
    normed = branch = result = flat.at[0]
    slope = grad_att = flat.at[1]
    grad_pre = flat.at[2]
    x, low, attended = flat.at[4], flat.at[5], flat.at[6]
    acts = [flat.at[7 + j] for j in range(4)]
    grads = (flat.at[2], flat.at[5], flat.at[3])
    downs = [pages.at[HOMES[k]] for k in DOWN]
    going = {}

    def move(src, dst, number):
        going[number] = pltpu.make_async_copy(src, dst, single.at[number])
        going[number].start()

    def done(*numbers):
        for number in numbers:
            going.pop(number).wait()

    def shard_of(k):
        if k < 3:
            return shards[0].at[:, pl.ds(k * 1024, 1024)]
        if k == 3:
            return shards[1]
        return shards[2].at[:, pl.ds(UP.index(k) * 1024, 1024)]

    def page_of(k):
        return pages.at[HOMES[k]]

    def local_copies(k):
        if k in DOWN:
            return [
                pltpu.make_async_copy(
                    shards[3].at[pl.ds(r * 32, 32), pl.ds(DOWN.index(k) * 256, 256)],
                    page_of(k).at[mine + (slice(None), pl.ds(r * 256, 256))],
                    own.at[k * 4 + r],
                )
                for r in range(4)
            ]
        return [pltpu.make_async_copy(shard_of(k), page_of(k).at[mine], own.at[k * 4])]

    local = {k: local_copies(k) for k in range(12)}
    early = []
    for k in (0, 1, 2, 3, 4, 5, 6, 7, 11):
        early += local[k]
    for i, narrow in enumerate(entries):
        move(narrow_i[i], narrow, 29 + i)
    for copy in early:
        copy.start()
    move(cot_i, low, 0)
    move(x_i, x, 1)
    greet(me, at)
    def pack():
        small[...] = jnp.zeros_like(small)
        for i, narrow in enumerate(entries):
            done(29 + i)
            small[pl.ds(i, 1), pl.ds(0, narrow.shape[1])] = narrow[...].astype(F32)
        packed = small[...]
        kind = lax.broadcasted_iota(jnp.int32, (8, 128), 0)
        fours = pltpu.roll(packed, lax.rem(me, 4) * 32, 1)
        twos = pltpu.roll(packed, lax.rem(me, 2) * 64, 1)
        small[...] = jnp.where(kind < 6, fours, jnp.where(kind == 6, twos, packed))
        early.append(pltpu.make_async_copy(small, smalls.at[mine], own.at[48]))
        early[-1].start()

    def row(vectors, i):
        return vectors.at[pl.ds(i, 1), :]

    def kept_len(seq):
        return lengths[assignment[seq]]

    def task_low():
        for seq in range(2):
            inside = lax.broadcasted_iota(jnp.int32, (320, 1), 0) < kept_len(seq)
            row_mask[pl.ds(seq * 320, 320), :] = jnp.where(inside, 1.0, 0.0)
        for s in (s4, s2, s1):
            s[...] = jnp.zeros_like(s)
        mixed[pl.ds(640, 64), :] = jnp.zeros((64, 3072), BF16)
        done(0)
        low[...] = (low[...].astype(F32) * row_mask[...]).astype(BF16)
        s4[pl.ds(5, 1), :] = whole_sum(column_sum(low[...].astype(F32)))

    def task_first():
        spread_vectors(smalls, v4, v2, v1)
        done(1)
        norm_rows(x, row(v4, 0), row(v4, 1), normed)

    def task_project(j):
        shift = None if j == 1 else v2.at[pl.ds(6, 1), pl.ds(0 if j == 0 else 1024, 1024)]
        project(normed, page_of(j), shift, mixed, j * 1024)
        if j == 1:
            turn(normed, normed1_t)
        done(8 + j)

    def task_attend(first, count):
        attend(first, count, mixed, kept_len, attended, probs, probs_o, probs_sems)

    def task_hidden():
        branch_out(attended, page_of(3), row(v4, 2), x, hidden)
        norm_rows(hidden, row(v4, 3), row(v4, 4), normed)
        done(11)

    def task_turns():
        turn(attended, other_t)
        move(other_t, attended_o, 5)
        done(5)
        turn(normed, other_t)

    def task_up(j):
        feed_up(normed, page_of(UP[j]), row(v1, 7), acts[j], slope, j * 1024)

    def task_feed(j):
        page = page_of(UP[j])
        slope_back(low, downs, j, slope, grad_pre, s1)
        outer_box(other_t, grad_pre, pages.at[MADE[j % 3]])
        back_through(grad_pre, page, total, j == 0)
        if j == 3:
            move(attended_o, other_t, 5)
        back = (3, 2, 1, 0)[j]
        move(spilled.at[back], page, 12 + back)

    def task_outer(j):
        if j > 1:
            done(2, 6)
        halves = [flat.at[2 + y, pl.ds(0, 512)] for y in range(2)]
        outer(acts[j], low, halves)
        for y, number in ((0, 2), (1, 6)):
            move(halves[y].reshape(2, 2, 4, 32, 1024), down_o.at[j, y], number)
        if j in (0, 3):
            done(2, 6)

    def task_second():
        norm_back(hidden, row(v4, 3), total, low, branch, part1, part2, part3)
        for i, part in ((3, part1), (4, part2), (2, part3)):
            s4[pl.ds(i, 1), :] = whole_sum(part[...])

    def task_out():
        done(5)
        outer_box(other_t, branch, pages.at[MADE[4 % 3]])

    def task_att():
        done(12 + 3)
        back_through(branch, page_of(UP[0]), grad_att, True)

    def task_attend_back(first, count):
        attend_back(first, count, mixed, attended, grad_att, probs, probs_o, probs_sems, grads)

    def task_mixed(j, m):
        outer_box(normed1_t, grads[j], pages.at[MADE[m % 3]])
        if j != 1:
            s2[pl.ds(6, 1), pl.ds(0 if j == 0 else 1024, 1024)] = whole_sum(
                column_sum(grads[j][...].astype(F32))
            )

    def task_through(j):
        done(12 + j)
        back_through(grads[j], page_of(UP[3 - j]), total, j == 2)

    def task_down(c):
        feed_down(acts, downs[c], row(v4, 5), hidden, row_mask, result, c)
        if c == 3:
            move(result, result_o, 3)

    def task_end():
        norm_back(x, row(v4, 0), total, branch, x, part1, part2, None)
        for i, part in ((0, part1), (1, part2)):
            s4[pl.ds(i, 1), :] = whole_sum(part[...])
        move(x, input_grad_o, 4)
        tiny = small_refs[0]
        for z in range(4):
            for y in range(2):
                for x_ in range(2):
                    for c in range(2):
                        d = ((z * 2 + y) * 2 + x_) * 2 + c
                        tiny[z, y, x_, c] = (
                            s4[:, d // 4 * 128 : d // 4 * 128 + 128]
                            + s2[:, d // 2 * 128 : d // 2 * 128 + 128]
                            + s1[:, d * 128 : d * 128 + 128]
                        )

    tasks = {
        3: [(task_low,)],
        5: [(task_first,), (task_project, 0)],
        6: [(task_project, 1)],
        7: [(task_project, 2), (task_attend, 0, 6)],
        8: [(task_attend, 6, 6)],
        9: [(task_attend, 12, 4), (task_hidden,)],
        10: [(task_turns,)],
        11: [(task_up, 0)],
        12: [(task_outer, 0)],
        13: [(task_feed, 0)],
        14: [(task_up, 1), (task_feed, 1)],
        15: [(task_up, 2), (task_feed, 2)],
        16: [(task_up, 3), (task_feed, 3)],
        17: [(task_second,), (task_out,)],
        18: [(task_outer, 1), (task_outer, 2), (task_outer, 3)],
        19: [(task_att,), (task_attend_back, 0, 4)],
        20: [(task_attend_back, 4, 4)],
        21: [(task_attend_back, 8, 4)],
        22: [(task_attend_back, 12, 4), (task_mixed, 2, 9)],
        23: [(task_mixed, 1, 10), (task_through, 2), (task_through, 1)],
        24: [(task_mixed, 0, 11), (task_through, 0), (task_end,)],
        25: [(task_down, 0), (task_down, 1)],
        26: [(task_down, 2), (task_down, 3)],
    }
    goals = [(2, 0, c) for c in (0, 1024, 2048, 3072)] + [(1, 0, 0)]
    goals += [(3, r, 0) for r in (0, 32, 64, 96)] + [(0, 0, 2048), (0, 0, 1024), (0, 0, 0)]
    flying, flows = {}, {}

    def begin(k, stage):
        if stage:
            for copy in flying.pop((k, stage - 1)):
                copy.wait()
        source = None if k in DOWN else shard_of(k)
        flying[k, stage] = gather_stage(page_of(k), PARTS if k else FIRST, stage, me, at, sems, k % 8, source)
        for copy in flying[k, stage]:
            copy.start()

    small_going = []
    for tick in range(LAST + 1):
        for stage in range(STAGES + 1):
            if 0 <= tick - stage < 12:
                begin(tick - stage, stage)
            if stage == 0 and tick == 0:
                pack()
            if stage == 0 and tick <= STAGES + 1:
                for copy in small_going:
                    copy.wait()
                small_going = []
                if tick <= STAGES:
                    small_going = gather_stage(smalls, SMALL, tick, me, at, sems, 8, small)
                for copy in small_going:
                    copy.start()
            if tick == 0 and stage == 0:
                for copy in early:
                    copy.wait()
            if tick + 1 in (8, 9, 10) and stage == 0:
                for copy in local[tick + 1]:
                    copy.start()
        k = tick - STAGES - 1
        if 0 <= k < 12:
            for copy in flying.pop((k, STAGES)):
                copy.wait()
            if k < 4:
                move(page_of(k), spilled.at[k], 8 + k)
        for stage in (1, 2, 3, 4, 5, 0):
            m = tick - BEGIN - stage
            if 0 <= m < 12:
                if stage == 0:
                    which, r, c = goals[m]
                    out = outs[which].at[pl.ds(r, ROWS), pl.ds(c, WIDE)]
                    source = down_o.at[:, :, :, :, r // 32] if which == 3 else None
                    made = pages.at[MADE[m % 3]]
                    flows[m] = Flow(made, source, out, BACK, cores[m % 2], slots[m % 3], lasts[m % 4], m % 8, back_sems, me, at)
                    flows[m].start()
                else:
                    flows[m].step(stage)
                    if stage == 5:
                        which, r, c = goals[m]
                        here = (pl.ds(r, ROWS), pl.ds(c, WIDE))
                        move(outs[which].at[here], outs_o[which].at[here], 16 + m)
        if tick >= LAST - STAGES - 1:
            if tick == LAST - STAGES - 1:
                flows["small"] = Flow(small_refs[0], None, small_out, SMALL_BACK, small_refs[1], small_refs[2:7], small_refs[7:], 8, back_sems, me, at)
                flows["small"].start()
            else:
                flows["small"].step(tick - LAST + STAGES + 1)
        for task, *args in tasks.get(tick, ()):
            task(*args)
        if tick + 1 in (8, 9, 10):
            for copy in local[tick + 1]:
                copy.wait()
    move(small_out, small_o, 28)
    done(3, 4, *range(16, 29))


def layer(x, cot, lengths, assignment, shards, narrow):
    anywhere = pl.BlockSpec(memory_space=pl.ANY)
    inside = pl.BlockSpec(memory_space=pltpu.VMEM)
    box = (4, 2, 2, 2)
    page = box + (32, 1024)
    flat, turned = (640, 1024), (1024, 640)
    made = [((32, 3072), F32), ((32, 1024), F32), ((32, 4096), F32), ((128, 1024), F32), ((8, 128), F32)]
    made += [(flat, BF16), (flat, BF16)]
    made += [((4,) + page, BF16), ((16, 2, 320, LEN_PAD), BF16), (box + (4, 32, 1024), BF16), (turned, BF16)]
    scratch = [
        ((11,) + page, BF16),
        (box + (8, 128), F32),
        ((8, 1024), F32),
        ((8, 2048), F32),
        ((8, 4096), F32),
        ((11,) + flat, BF16),
        (turned, BF16),
        (turned, BF16),
        ((704, 3072), BF16),
        (flat, F32),
        (flat, F32),
        ((2, 2, 320, LEN_PAD), BF16),
        ((640, 1), F32),
        ((8, 1024), F32),
        ((8, 2048), F32),
        ((8, 4096), F32),
    ] + [((8, 1024), F32)] * 3 + [((8, 128), F32)]
    scratch += made[:5] + [((1, n), BF16) for n in (32,) * 6 + (64, 128)]
    way, last = flow_buffers(BACK, BF16)
    scratch += way * 3 + last * 4 + [((4, 2, 2, 32, 1024), BF16)] * 2
    way, last = flow_buffers(SMALL_BACK, F32)
    scratch += [(box + (8, 128), F32), ((4, 2, 2, 8, 128), F32)] + way + last
    dma = pltpu.SemaphoreType.DMA
    return pl.pallas_call(
        layer_kernel,
        out_shape=[jax.ShapeDtypeStruct(s, d) for s, d in made],
        in_specs=[anywhere] * 2 + [pl.BlockSpec(memory_space=pltpu.SMEM)] * 2 + [anywhere] * 12,
        out_specs=[anywhere] * 11,
        scratch_shapes=[pltpu.VMEM(s, d) for s, d in scratch]
        + [dma((9, COPIES))] * 4
        + [dma((9,)), dma((49,)), dma((37,)), dma((2,))],
        compiler_params=pltpu.CompilerParams(
            collective_id=0, has_side_effects=True, vmem_limit_bytes=64 << 20
        ),
        name="layer",
    )(x, cot, lengths, assignment, *shards, *narrow)


def finish_kernel(*refs):
    arrays, outs, narrow_o, refs = refs[:7], refs[7:13], refs[13:21], refs[21:]
    blocks, narrow, sems, back_sems = refs[:7], refs[7:15], refs[15], refs[16]
    into = [pltpu.make_async_copy(a, block, sems.at[i]) for i, (a, block) in enumerate(zip(arrays, blocks))]
    back = [
        pltpu.make_async_copy(block, o, back_sems.at[i])
        for i, (o, block) in enumerate(zip((*outs, *narrow_o), (*blocks[:6], *narrow)))
    ]
    for copy in (into[6], *into[:6]):
        copy.start()
    into[6].wait()
    me = lax.axis_index("dp")
    total = blocks[6][...]
    fours = pltpu.roll(total, 128 - lax.rem(me, 4) * 32, 1)
    for i in range(6):
        narrow[i][...] = fours[i : i + 1, :32]
    narrow[6][...] = pltpu.roll(total, 128 - lax.rem(me, 2) * 64, 1)[6:7, :64]
    narrow[7][...] = total[7:8, :]
    for copy in back[6:]:
        copy.start()
    for i in range(6):
        into[i].wait()
        back[i].start()
    for copy in back:
        copy.wait()


def finish(*arrays):
    anywhere = pl.BlockSpec(memory_space=pl.ANY)
    narrow = [jax.ShapeDtypeStruct((1, n), F32) for n in (32,) * 6 + (64, 128)]
    found = pl.pallas_call(
        finish_kernel,
        out_shape=[jax.ShapeDtypeStruct(a.shape, a.dtype) for a in arrays[:6]] + narrow,
        in_specs=[anywhere] * 7,
        out_specs=[anywhere] * 14,
        scratch_shapes=[pltpu.VMEM(a.shape, a.dtype) for a in (*arrays, *narrow)]
        + [pltpu.SemaphoreType.DMA((7,)), pltpu.SemaphoreType.DMA((14,))],
        compiler_params=pltpu.CompilerParams(vmem_limit_bytes=63 << 20),
        name="finish",
    )(*arrays)
    return found[:6], [a.reshape(-1) for a in found[6:]]


NARROW = (0, 1, 5, 6, 7, 11)
WEIGHTS = (2, 4, 8, 10)


def on_box(inputs, lengths, assignment, *rest):
    weights, cotangent = rest[:12], rest[12]
    x = inputs.reshape(640, 1024)
    cot = cotangent.reshape(640, 1024)
    narrow = [weights[i][None] for i in (*NARROW, 3, 9)]
    made = layer(
        x, cot, lengths, assignment, [weights[i] for i in WEIGHTS], narrow
    )
    sums, (total, input_grad, result) = made[:4], made[4:7]
    (result, input_grad, *sums), narrow = finish(result, input_grad, *sums, total)
    found = [None] * 12
    for row, i in enumerate((*NARROW, 3, 9)):
        found[i] = narrow[row]
    for i, s in zip(WEIGHTS, sums):
        found[i] = s
    return (result.reshape(inputs.shape), input_grad.reshape(inputs.shape), *found)


def plain(
    inputs,
    lengths,
    assignment,
    norm1_gain,
    norm1_bias,
    qkv_weight,
    qv_bias,
    out_weight,
    out_bias,
    norm2_gain,
    norm2_bias,
    up_weight,
    up_bias,
    down_weight,
    down_bias,
    cotangent,
):
    gathered = (
        lax.all_gather(norm1_gain, "dp", axis=0, tiled=True),
        lax.all_gather(norm1_bias, "dp", axis=0, tiled=True),
        lax.all_gather(qkv_weight, "dp", axis=0, tiled=True),
        lax.all_gather(qv_bias, "dp", axis=0, tiled=True),
        lax.all_gather(out_weight, "dp", axis=0, tiled=True),
        lax.all_gather(out_bias, "dp", axis=0, tiled=True),
        lax.all_gather(norm2_gain, "dp", axis=0, tiled=True),
        lax.all_gather(norm2_bias, "dp", axis=0, tiled=True),
        lax.all_gather(up_weight, "dp", axis=0, tiled=True),
        lax.all_gather(up_bias, "dp", axis=0, tiled=True),
        lax.all_gather(down_weight, "dp", axis=0, tiled=True),
        lax.all_gather(down_bias, "dp", axis=0, tiled=True),
    )
    seq_count, tok_count, model_width = inputs.shape
    rows_all = seq_count * tok_count
    split_shape = (seq_count, tok_count, HEADS, HEAD)
    head_scale = HEAD ** (-0.5)
    matches = assignment[:, None] == jnp.arange(lengths.shape[0], dtype=jnp.int32)[None, :]
    kept_len = jnp.sum(jnp.where(matches, lengths[None, :], 0), axis=1)
    key_mask = jnp.arange(tok_count, dtype=jnp.int32)[None, :] < kept_len[:, None]
    row_mask = key_mask.reshape(rows_all, 1).astype(jnp.float32)
    gain_first = gathered[0].astype(jnp.float32)
    shift_first = gathered[1].astype(jnp.float32)
    qv_full = gathered[3].astype(jnp.float32)
    proj_shift = gathered[5].astype(jnp.float32)
    gain_second = gathered[6].astype(jnp.float32)
    shift_second = gathered[7].astype(jnp.float32)
    up_shift = gathered[9].astype(jnp.float32)
    down_shift = gathered[11].astype(jnp.float32)
    inputs_flat = inputs.reshape(rows_all, model_width).astype(jnp.float32)
    normed_first, first_back = jax.vjp(layer_norm, inputs_flat, gain_first, shift_first)
    normed_low = normed_first.astype(jnp.bfloat16)
    full_bias = jnp.concatenate(
        [qv_full[:model_width], jnp.zeros((model_width,), jnp.float32), qv_full[model_width:]]
    )
    mixed_qkv = (
        jnp.dot(normed_low, gathered[2], preferred_element_type=jnp.float32) + full_bias
    ).astype(jnp.bfloat16)
    queries = mixed_qkv[:, :model_width].reshape(split_shape)
    keys_all = mixed_qkv[:, model_width : 2 * model_width].reshape(split_shape)
    values_all = mixed_qkv[:, 2 * model_width :].reshape(split_shape)
    scores = (
        jnp.einsum("bqhd,bkhd->bhqk", queries, keys_all, preferred_element_type=jnp.float32)
        * head_scale
    )
    scores = jnp.where(key_mask[:, None, None, :], scores, masked_score)
    row_max = jnp.max(scores, axis=-1, keepdims=True)
    exponent = jnp.exp(scores - row_max)
    row_total = jnp.sum(exponent, axis=-1, keepdims=True)
    softmax_probs = exponent / row_total
    log_total = row_max + jnp.log(row_total)
    attended = jnp.einsum(
        "bhqk,bkhd->bqhd",
        softmax_probs.astype(jnp.bfloat16),
        values_all,
        preferred_element_type=jnp.float32,
    )
    attended = attended.reshape(rows_all, model_width).astype(jnp.bfloat16)
    hidden = inputs_flat + (
        jnp.dot(attended, gathered[4], preferred_element_type=jnp.float32) + proj_shift
    )
    normed_second, second_back = jax.vjp(layer_norm, hidden, gain_second, shift_second)
    second_low = normed_second.astype(jnp.bfloat16)
    pre_act = jnp.dot(second_low, gathered[8], preferred_element_type=jnp.float32) + up_shift
    activation, gelu_back = jax.vjp(gelu_exact, pre_act)
    act_low = activation.astype(jnp.bfloat16)
    output_rows = row_mask * (
        hidden + (jnp.dot(act_low, gathered[10], preferred_element_type=jnp.float32) + down_shift)
    )
    result = output_rows.reshape(inputs.shape).astype(jnp.bfloat16)
    grad_rows = cotangent.reshape(rows_all, model_width).astype(jnp.float32) * row_mask
    grad_low = grad_rows.astype(jnp.bfloat16)
    down_grad = contract_rows(act_low, grad_low)
    down_bias_grad = jnp.sum(grad_low.astype(jnp.float32), axis=0)
    grad_pre = gelu_back(contract_cols(grad_low, gathered[10]))[0].astype(jnp.bfloat16)
    up_grad = contract_rows(second_low, grad_pre)
    up_bias_grad = jnp.sum(grad_pre.astype(jnp.float32), axis=0)
    grad_second, gain2_grad, shift2_grad = second_back(contract_cols(grad_pre, gathered[8]))
    grad_hidden = grad_rows + grad_second
    branch_low = grad_hidden.astype(jnp.bfloat16)
    proj_grad = contract_rows(attended, branch_low)
    proj_bias_grad = jnp.sum(branch_low.astype(jnp.float32), axis=0)
    grad_att = contract_cols(branch_low, gathered[4]).astype(jnp.bfloat16).reshape(split_shape)
    scores_again = (
        jnp.einsum("bqhd,bkhd->bhqk", queries, keys_all, preferred_element_type=jnp.float32)
        * head_scale
    )
    scores_again = jnp.where(key_mask[:, None, None, :], scores_again, masked_score)
    probs_again = jnp.exp(scores_again - log_total)
    probs_low = probs_again.astype(jnp.bfloat16)
    grad_probs = jnp.einsum(
        "bqhd,bkhd->bhqk", grad_att, values_all, preferred_element_type=jnp.float32
    )
    grad_values = jnp.einsum(
        "bhqk,bqhd->bkhd", probs_low, grad_att, preferred_element_type=jnp.float32
    )
    inner_sum = jnp.sum(probs_again * grad_probs, axis=-1, keepdims=True)
    grad_scores = (probs_again * (grad_probs - inner_sum)).astype(jnp.bfloat16)
    grad_queries = (
        jnp.einsum("bhqk,bkhd->bqhd", grad_scores, keys_all, preferred_element_type=jnp.float32)
        * head_scale
    )
    grad_keys = (
        jnp.einsum("bhqk,bqhd->bkhd", grad_scores, queries, preferred_element_type=jnp.float32)
        * head_scale
    )
    grad_mixed = jnp.concatenate(
        [
            grad_queries.reshape(rows_all, model_width),
            grad_keys.reshape(rows_all, model_width),
            grad_values.reshape(rows_all, model_width),
        ],
        axis=1,
    ).astype(jnp.bfloat16)
    qkv_grad = contract_rows(normed_low, grad_mixed)
    column_sums = jnp.sum(grad_mixed.astype(jnp.float32), axis=0)
    qv_grad = jnp.concatenate([column_sums[:model_width], column_sums[2 * model_width :]])
    grad_first, gain1_grad, shift1_grad = first_back(contract_cols(grad_mixed, gathered[2]))
    input_grad = (grad_hidden + grad_first).reshape(inputs.shape).astype(jnp.bfloat16)
    all_sums = (
        lax.psum_scatter(gain1_grad, "dp", scatter_dimension=0, tiled=True),
        lax.psum_scatter(shift1_grad, "dp", scatter_dimension=0, tiled=True),
        lax.psum_scatter(qkv_grad, "dp", scatter_dimension=0, tiled=True),
        lax.psum_scatter(qv_grad, "dp", scatter_dimension=0, tiled=True),
        lax.psum_scatter(proj_grad, "dp", scatter_dimension=0, tiled=True),
        lax.psum_scatter(proj_bias_grad, "dp", scatter_dimension=0, tiled=True),
        lax.psum_scatter(gain2_grad, "dp", scatter_dimension=0, tiled=True),
        lax.psum_scatter(shift2_grad, "dp", scatter_dimension=0, tiled=True),
        lax.psum_scatter(up_grad, "dp", scatter_dimension=0, tiled=True),
        lax.psum_scatter(up_bias_grad, "dp", scatter_dimension=0, tiled=True),
        lax.psum_scatter(down_grad, "dp", scatter_dimension=0, tiled=True),
        lax.psum_scatter(down_bias_grad, "dp", scatter_dimension=0, tiled=True),
    )
    attn_sums = all_sums[:6]
    mlp_sums = all_sums[6:]
    return (
        result,
        input_grad,
        attn_sums[0],
        attn_sums[1],
        attn_sums[2],
        attn_sums[3],
        attn_sums[4],
        attn_sums[5],
        mlp_sums[0],
        mlp_sums[1],
        mlp_sums[2],
        mlp_sums[3],
        mlp_sums[4],
        mlp_sums[5],
    )


def local(*args):
    return on_box(*args) if lax.axis_size("dp") == 32 else plain(*args)


def solution(mesh):
    placed = (
        P("dp", None, None),
        P(),
        P("dp"),
        P("dp"),
        P("dp"),
        P("dp", None),
        P("dp"),
        P("dp", None),
        P("dp"),
        P("dp"),
        P("dp"),
        P("dp", None),
        P("dp"),
        P("dp", None),
        P("dp"),
        P("dp", None, None),
    )
    return jax.shard_map(
        local,
        mesh=mesh,
        in_specs=placed,
        out_specs=(
            P("dp", None, None),
            P("dp", None, None),
            P("dp"),
            P("dp"),
            P("dp", None),
            P("dp"),
            P("dp", None),
            P("dp"),
            P("dp"),
            P("dp"),
            P("dp", None),
            P("dp"),
            P("dp", None),
            P("dp"),
        ),
        check_vma=False,
    )
```

```python
import jax
import jax.numpy as jnp
from jax import lax
from jax.experimental import pallas as pl
from jax.experimental.pallas import tpu as pltpu
from jax.sharding import PartitionSpec as P

HEADS = 16
HEAD = 64


eps = 1e-06
masked_score = -1000000000.0


def layer_norm(values, norm_gain, norm_shift):
    average = jnp.mean(values, axis=-1, keepdims=True)
    centered = values - average
    variance = jnp.mean(centered * centered, axis=-1, keepdims=True)
    return centered * lax.rsqrt(variance + eps) * norm_gain + norm_shift


def gelu_exact(values):
    return jax.nn.gelu(values, approximate=False)


def contract_rows(left, right):
    return lax.dot_general(
        left, right, (((0,), (0,)), ((), ())), preferred_element_type=jnp.float32
    )


def contract_cols(left, right):
    return lax.dot_general(
        left, right, (((1,), (1,)), ((), ())), preferred_element_type=jnp.float32
    )


BF16 = jnp.bfloat16
F32 = jnp.float32
MESH = pl.DeviceIdType.MESH
STRIDE = {"z": 8, "y": 4, "x": 2}
ROWS = 32
WIDE = 1024
STAGES = 4
PARTS = (
    ("zZyx", 0, 16, 0, 384),
    ("zZxy", 16, 16, 0, 384),
    ("xzZy", 0, 16, 384, 640),
    ("yzZx", 16, 16, 384, 640),
)
FIRST = (("zZyx", 0, 16, 0, 1024), ("zZxy", 16, 16, 0, 1024))
COPIES = 6 * len(PARTS) + 1


def coords():
    me = lax.axis_index("dp")
    at = {
        "z": lax.div(me, 8),
        "y": lax.rem(lax.div(me, 4), 2),
        "x": lax.rem(lax.div(me, 2), 2),
        "c": lax.rem(me, 2),
    }
    return me, at


def sibling(me, at):
    return me + 1 - 2 * at["c"]


class Hop:
    def __init__(self, copy, sends=None, hears=None):
        self.copy, self.sends, self.hears = copy, sends, hears

    def start(self):
        if self.sends is None:
            self.copy.start()
        else:
            pl.when(self.sends)(self.copy.start)

    def wait(self):
        if self.sends is None:
            self.copy.wait()
        else:
            pl.when(self.sends)(self.copy.wait_send)
            pl.when(self.hears)(self.copy.wait_recv)


def inner(at):
    return lax.div(at["z"] + 1, 2) == 1


def far(at):
    return 3 * (1 - lax.div(at["z"], 2))


def hops(me, at, dim):
    z = at["z"]
    if dim == "z":
        found = []
        for k in (1, 2, 3):
            there = lax.rem(z + k, 4)
            when = {1: (z < 3, z > 0), 2: (None, None), 3: (z > 0, z < 3)}[k]
            found.append((there, me + (there - z) * 8, *when))
        return found
    if dim == "Z":
        return [(far(at), me + 8 - 16 * lax.rem(z, 2), inner(at), jnp.logical_not(inner(at)))]
    there = 1 - at[dim]
    return [(there, me + (there - at[dim]) * STRIDE[dim], None, None)]


def count_of(dim):
    return 3 if dim == "z" else 1


def greet(me, at):
    barrier = pltpu.get_barrier_semaphore()
    devices = [sibling(me, at)]
    for dim in "yx":
        devices += [hop[1] for hop in hops(me, at, dim)]
    for k in (1, 2, 3):
        devices.append(me + (lax.rem(at["z"] + k, 4) - at["z"]) * 8)
    for device in devices:
        pl.semaphore_signal(barrier, inc=1, device_id=(device,), device_id_type=MESH)
    pl.semaphore_wait(barrier, len(devices))


def remote(src, dst, sems, slot, number, device):
    return pltpu.make_async_remote_copy(
        src_ref=src,
        dst_ref=dst,
        send_sem=sems[0].at[slot, number],
        recv_sem=sems[1].at[slot, number],
        device_id=(device,),
        device_id_type=MESH,
    )


def held(order, stage, at):
    index = []
    for dim in "zyx":
        if dim == "z" and order[stage] == "Z":
            index.append(far(at))
        else:
            done = "Z" if dim == "z" else dim
            index.append(slice(None) if done in order[:stage] else at[dim])
    return tuple(index)


def gather_stage(base, parts, stage, me, at, sems, slot, source=None):
    if stage == STAGES:
        block = base.at[:, :, :, at["c"]]
        return [Hop(remote(block, block, sems, slot, COPIES - 1, sibling(me, at)))]
    number, copies = 0, []
    for order, row, rows, col, columns in parts:
        here = (pl.ds(row, rows), pl.ds(col, columns))
        for s in range(STAGES):
            for _, device, sends, hears in hops(me, at, order[s]):
                if s == stage:
                    block = base.at[held(order, stage, at) + (at["c"],) + here]
                    src = source.at[here] if source is not None and stage == 0 else block
                    copies.append(Hop(remote(src, block, sems, slot, number, device), sends, hears))
                number += 1
    return copies


SMALL = (("zZyx", 0, 8, 0, 128),)


def remaining(order, stage):
    left = [dim for dim in "zyx" if dim not in order[:stage]]
    return tuple({"z": 4, "y": 2, "x": 2}[dim] for dim in left)


def pick(order, stage, dim, index):
    return tuple(index if d == dim.lower() else slice(None) for d in "zyx" if d not in order[:stage])


BACK = tuple((part[0][::-1], *part[1:]) for part in PARTS)
SMALL_BACK = tuple((part[0][::-1], *part[1:]) for part in SMALL)


def add_up(dst, terms, lead):
    loops = lead[: max(len(lead) - 1, 0)] if len(lead) > 1 else ()
    count = 1
    for n in loops:
        count *= n

    def body(i, carry):
        index = []
        for n in loops[::-1]:
            index.append(lax.rem(i, n))
            i = lax.div(i, n)
        index = tuple(index[::-1]) + (slice(None),) * (len(lead) - len(loops) + 2)
        if len(terms) == 2 and dst.dtype == terms[0].dtype:
            dst[index] = terms[0][index] + terms[1][index]
            return carry
        total = terms[0][index].astype(F32)
        for term in terms[1:]:
            total = total + term[index].astype(F32)
        dst[index] = total.astype(dst.dtype)
        return carry

    if count == 1:
        body(0, 0)
    else:
        lax.fori_loop(0, count, body, 0)


class Flow:
    def __init__(self, made, source, out, parts, from_core, rest, last, slot, sems, me, at):
        self.made, self.source, self.out, self.parts = made, source, out, parts
        self.from_core = from_core
        self.arrived, self.totals = [], []
        for part, (order, *_) in enumerate(parts):
            self.arrived.append((*rest[:3], last[part]))
            self.totals.append(dict(zip([s for s in range(3) if order[s] != "Z"], rest[3:5])))
            rest = rest[5:]
        self.slot, self.sems, self.me, self.at = slot, sems, me, at
        self.own = made.at[:, :, :, at["c"]]

    def start(self):
        there = 1 - self.at["c"]
        source = self.made if self.source is None else self.source
        self.going = [
            remote(
                source.at[:, :, :, there],
                self.from_core,
                self.sems,
                self.slot,
                COPIES - 1,
                sibling(self.me, self.at),
            )
        ]
        if self.source is not None:
            self.going.append(
                pltpu.make_async_copy(source.at[:, :, :, self.at["c"]], self.own, self.sems[2].at[self.slot])
            )
        for copy in self.going:
            copy.start()

    def sum_before(self, part, stage):
        order, row, rows, col, columns = self.parts[part]
        done = [s for s in range(stage) if s in self.totals[part]]
        if not done:
            return self.own.at[:, :, :, pl.ds(row, rows), pl.ds(col, columns)]
        return self.totals[part][done[-1]]

    def take(self, part, stage):
        order, row, rows, col, columns = self.parts[part]
        s = stage - 2
        dim, arrived = order[s], self.arrived[part][s]
        before = self.sum_before(part, s)
        if dim == "Z":
            index = pick(order, s, "z", far(self.at))

            @pl.when(inner(self.at))
            def _():
                add_up(before.at[index], [before.at[index], arrived.at[0]], remaining(order, s)[1:])

            return
        if stage == STAGES + 1:
            total = self.out.at[pl.ds(row, rows), pl.ds(col, columns)]
        else:
            total = self.totals[part][s]
        mine = before.at[pick(order, s, dim, self.at[dim])]
        left = remaining(order, s + 1)
        if dim != "z":
            add_up(total, [mine, arrived.at[0]], left)
            return
        z = self.at["z"]
        for when, came in ((z == 0, (1, 2)), (inner(self.at), (0, 1, 2)), (z == 3, (0, 1))):

            @pl.when(when)
            def _(came=came):
                add_up(total, [mine] + [arrived.at[i] for i in came], left)

    def step(self, stage):
        for copy in self.going:
            copy.wait()
        if stage == 1:
            add_up(self.own, [self.own, self.from_core], (4, 2, 2))
        else:
            for part in range(len(self.parts)):
                self.take(part, stage)
        self.going, number = [], 0
        for part, (order, row, rows, col, columns) in enumerate(self.parts):
            for s in range(STAGES):
                if s + 1 == stage:
                    before = self.sum_before(part, s)
                    for i, (there, device, sends, hears) in enumerate(hops(self.me, self.at, order[s])):
                        if order[s] == "Z":
                            sends, hears = hears, sends
                        src = before.at[pick(order, s, order[s], there)]
                        copy = remote(src, self.arrived[part][s].at[i], self.sems, self.slot, number + i, device)
                        self.going.append(Hop(copy, sends, hears))
                number += count_of(order[s])
        for copy in self.going:
            copy.start()


def flow_buffers(parts, dtype):
    shapes, last = [], []
    for order, _, high, _, wide in parts:
        totals = []
        for s in range(STAGES):
            if order[s] == "Z":
                left = remaining(order, s)[1:]
            else:
                left = remaining(order, s + 1)
                if s < 3:
                    totals.append((left + (high, wide), dtype))
            (shapes if s < 3 else last).append(((count_of(order[s]),) + left + (high, wide), dtype))
        shapes += totals
    return shapes, last


EPS = 1e-06
MASKED = -1000000000.0
LEN_PAD = 384


def dot_nn(a, b):
    return jnp.dot(a, b, preferred_element_type=F32)


def dot_nt(a, b):
    return lax.dot_general(a, b, (((1,), (1,)), ((), ())), preferred_element_type=F32)


def dot_tn(a, b):
    return lax.dot_general(a, b, (((0,), (0,)), ((), ())), preferred_element_type=F32)


def block_of(index, size):
    return pl.ds(pl.multiple_of(index * size, size), size)


def spread_vectors(smalls, v4, v2, v1):
    for z in range(4):
        for y in range(2):
            four = None
            for x in range(2):
                two = None
                for c in range(2):
                    one = smalls[z, y, x, c]
                    d = ((z * 2 + y) * 2 + x) * 2 + c
                    v1[:, d * 128 : d * 128 + 128] = one
                    two = one if two is None else two + one
                d = (z * 2 + y) * 2 + x
                v2[:, d * 128 : d * 128 + 128] = two
                four = two if four is None else four + two
            d = z * 2 + y
            v4[:, d * 128 : d * 128 + 128] = four


def norm_rows(src, gain, shift, dst):
    @pl.loop(0, src.shape[0] // 64)
    def _(i):
        rows = block_of(i, 64)
        values = src[rows, :].astype(F32)
        centered = values - jnp.mean(values, axis=-1, keepdims=True)
        variance = jnp.mean(centered * centered, axis=-1, keepdims=True)
        normed = centered * lax.rsqrt(variance + EPS)
        dst[rows, :] = (normed * gain[...] + shift[...]).astype(BF16)


def project(normed, weight, shift, dst, col):
    @pl.loop(0, 2)
    def _(i):
        columns = block_of(i, 512)
        mixed = dot_nn(normed[...], weight[:, :, :, :, :, columns].reshape(1024, 512))
        if shift is not None:
            mixed = mixed + shift[:, columns]
        dst[pl.ds(0, 640), pl.ds(pl.multiple_of(col + i * 512, 512), 512)] = mixed.astype(BF16)


def attend(first, count, mixed, kept_len, attended, probs, probs_out, sems):
    lane = lax.broadcasted_iota(jnp.int32, (1, 128), 1)

    def out_copy(unit, slot):
        return pltpu.make_async_copy(probs.at[slot], probs_out.at[unit], sems.at[slot])

    @pl.loop(0, count // 2)
    def _(i):
        for slot in range(2):
            unit = first + i * 2 + slot
            seq, pair = lax.div(unit, 8), lax.rem(unit, 8)
            start = pl.multiple_of(seq * 320, 64)
            columns = block_of(pair, 128)
            q = mixed[pl.ds(start, 320), columns]
            k = mixed[pl.ds(start, LEN_PAD), block_of(pair + 8, 128)]
            v = mixed[pl.ds(start, LEN_PAD), block_of(pair + 16, 128)]
            kept = lax.broadcasted_iota(jnp.int32, (1, LEN_PAD), 1) < kept_len(seq)

            @pl.when(i > 0)
            def _():
                out_copy(unit, slot).wait()

            found = []
            for head in range(2):
                scale = jnp.where(lax.div(lane, 64) == head, 0.125, 0.0).astype(BF16)
                scores = jnp.where(kept, dot_nt(q * scale, k), MASKED)
                exponent = jnp.exp(scores - jnp.max(scores, axis=-1, keepdims=True))
                total = jnp.sum(exponent, axis=-1, keepdims=True)
                low = (exponent * (1.0 / total)).astype(BF16)
                probs[slot, head] = low
                found.append(dot_nn(low, v))
            attended[pl.ds(start, 320), columns] = jnp.where(
                lane < 64, found[0], found[1]
            ).astype(BF16)
            out_copy(unit, slot).start()

    for slot in range(2):
        out_copy(0, slot).wait()


def branch_out(attended, weight, shift, x, hidden):
    @pl.loop(0, 2)
    def _(i):
        columns = block_of(i, 512)
        branch = dot_nn(attended[...], weight[:, :, :, :, :, columns].reshape(1024, 512))
        hidden[:, columns] = x[:, columns].astype(F32) + (branch + shift[:, columns])


def feed_up(normed, weight, shift, act, slope, col):
    pre = dot_nn(normed[...], weight[...].reshape(1024, 1024)) + shift[:, pl.ds(col, 1024)]
    below = 0.5 + 0.5 * lax.erf(pre * 0.7071067811865476)
    act[...] = (pre * below).astype(BF16)
    density = jnp.exp(pre * pre * -0.5) * 0.3989422804014327
    slope[...] = (below + pre * density).astype(BF16)


def outer(left, right, halves):
    for i, half in enumerate(halves):
        half[...] = dot_tn(left[:, i * 512 : i * 512 + 512], right[...]).astype(BF16)


def turn(src, dst):
    @pl.loop(0, 4)
    def _(i):
        rows = block_of(i, 256)
        dst[rows, :] = src[:, rows].T


def tall(block):
    parts = [block[..., i * 256 : i * 256 + 256] for i in range(4)]
    rows = jnp.stack(parts, axis=block.ndim - 2)
    return rows.reshape(-1, 256)


def feed_down(acts, page, shift, hidden, row_mask, result, c):
    columns = pl.ds(c * 256, 256)
    branch = dot_nn(acts[0][...], tall(page[0]))
    for z in range(1, 4):
        branch = branch + dot_nn(acts[z][...], tall(page[z]))
    whole = hidden[:, columns] + (branch + shift[:, columns])
    result[:, columns] = (whole * row_mask[...]).astype(BF16)


def column_sum(values):
    return jnp.sum(values.reshape(values.shape[0] // 8, 8, values.shape[1]), axis=0)


def norm_back(src, gain, grads, base, dst, by_scale, by_shift, by_low):
    for total in (by_scale, by_shift, by_low):
        if total is not None:
            total[...] = jnp.zeros_like(total)

    @pl.loop(0, 640 // 64)
    def _(i):
        rows = block_of(i, 64)
        values = src[rows, :].astype(F32)
        centered = values - jnp.mean(values, axis=-1, keepdims=True)
        inverse = lax.rsqrt(jnp.mean(centered * centered, axis=-1, keepdims=True) + EPS)
        normed = centered * inverse
        g = grads[rows, :]
        scaled = g * gain[...]
        along = jnp.mean(scaled * normed, axis=-1, keepdims=True)
        back = inverse * (scaled - jnp.mean(scaled, axis=-1, keepdims=True) - normed * along)
        whole = base[rows, :].astype(F32) + back
        rounded = whole.astype(BF16)
        dst[rows, :] = rounded
        by_scale[...] += column_sum(g * normed)
        by_shift[...] += column_sum(g)
        if by_low is not None:
            by_low[...] += column_sum(rounded.astype(F32))


def whole_sum(part):
    return jnp.sum(part, axis=0, keepdims=True)


def slope_back(low, pages, j, slope, grad_pre, total):
    weight = jnp.concatenate([tall(page[j]) for page in pages], axis=1)
    grad = (dot_nt(low[...], weight) * slope[...].astype(F32)).astype(BF16)
    grad_pre[...] = grad
    total[pl.ds(7, 1), pl.ds(j * 1024, 1024)] = whole_sum(column_sum(grad.astype(F32)))


def back_through(left, page, total, first):
    part = dot_nt(left[...], page[...].reshape(1024, 1024))
    total[...] = part.astype(total.dtype) if first else total[...] + part


def outer_box(turned, right, dst):
    dst[...] = dot_nn(turned[...], right[...]).astype(BF16).reshape(4, 2, 2, 2, 32, 1024)


def attend_back(first, count, mixed, attended, grad_att, probs, probs_in, sems, grads):
    lane = lax.broadcasted_iota(jnp.int32, (1, 128), 1)

    def load(unit, slot):
        return pltpu.make_async_copy(probs_in.at[unit], probs.at[slot], sems.at[slot])

    load(first, 0).start()

    @pl.loop(0, count // 2)
    def _(i):
        for slot in range(2):
            unit = first + i * 2 + slot
            seq, pair = lax.div(unit, 8), lax.rem(unit, 8)
            start = pl.multiple_of(seq * 320, 64)
            rows = pl.ds(start, 320)
            col_q, col_k, col_v = (block_of(pair + 8 * n, 128) for n in range(3))
            load(unit, slot).wait()
            if slot == 0:
                load(unit + 1, 1).start()
            else:

                @pl.when(i + 1 < count // 2)
                def _():
                    load(unit + 1, 0).start()

            q = mixed[rows, col_q]
            k = mixed[pl.ds(start, LEN_PAD), col_k]
            v = mixed[pl.ds(start, LEN_PAD), col_v]
            grad_out = grad_att[rows, col_q]
            along = grad_out.astype(F32) * attended[rows, col_q].astype(F32)
            turned_q, turned_out = q.T, grad_out.T
            found = []
            for head in range(2):
                mine = lax.div(lane, 64) == head
                low = probs[slot, head]
                grad_p = dot_nt(grad_out * jnp.where(mine, 1.0, 0.0).astype(BF16), v)
                inner = jnp.sum(jnp.where(mine, along, 0.0), axis=-1, keepdims=True)
                grad_s = (low.astype(F32) * (grad_p - inner)).astype(BF16)
                part = slice(head * 64, head * 64 + 64)
                found.append((dot_nn(grad_s, k), dot_nn(turned_q[part], grad_s), dot_nn(turned_out[part], low)))
            grads[0][rows, col_q] = (jnp.where(lane < 64, found[0][0], found[1][0]) * 0.125).astype(BF16)
            for grad, scale, of in ((grads[1], 0.125, 1), (grads[2], 1.0, 2)):
                both = jnp.concatenate([found[0][of], found[1][of]], axis=0)
                grad[rows, col_q] = (both * scale).astype(BF16).T[:320]


UP = (4, 9, 10, 11)
DOWN = (5, 6, 7, 8)
HOMES = (0, 1, 2, 3, 4, 5, 6, 7, 0, 1, 2, 8)
MADE = (3, 9, 10)
BEGIN = 14
LAST = BEGIN + 12 + STAGES


def layer_kernel(*refs):
    x_i, cot_i, lengths, assignment = refs[:4]
    shards, narrow_i = refs[4:8], refs[8:16]
    refs = refs[7:]
    outs_o, small_o, input_grad_o, result_o, spilled, probs_o, down_o, attended_o = refs[9:13], *refs[13:20]
    (pages, smalls, v4, v2, v1, flat, normed1_t, other_t, mixed, hidden, total, probs, row_mask, s4, s2, s1, part1, part2, part3, small) = refs[20:40]
    outs, small_out, entries, refs = refs[40:44], refs[44], refs[45:53], refs[53:]
    per, parts = 5 * len(BACK), len(BACK)
    slots, refs = [refs[i * per : i * per + per] for i in range(3)], refs[3 * per :]
    lasts, refs = [refs[i * parts : i * parts + parts] for i in range(4)], refs[4 * parts :]
    cores, refs = refs[:2], refs[2:]
    small_refs, refs = refs[:8], refs[8:]
    send, recv, back_send, back_recv, back_own, own, single, probs_sems = refs
    sems, back_sems = (send, recv), (back_send, back_recv, back_own)
    me, at = coords()
    mine = (at["z"], at["y"], at["x"], at["c"])
    normed = branch = result = flat.at[0]
    slope = grad_att = flat.at[1]
    grad_pre = flat.at[2]
    x, low, attended = flat.at[4], flat.at[5], flat.at[6]
    acts = [flat.at[7 + j] for j in range(4)]
    grads = (flat.at[2], flat.at[5], flat.at[3])
    downs = [pages.at[HOMES[k]] for k in DOWN]
    going = {}

    def move(src, dst, number):
        going[number] = pltpu.make_async_copy(src, dst, single.at[number])
        going[number].start()

    def done(*numbers):
        for number in numbers:
            going.pop(number).wait()

    def shard_of(k):
        if k < 3:
            return shards[0].at[:, pl.ds(k * 1024, 1024)]
        if k == 3:
            return shards[1]
        return shards[2].at[:, pl.ds(UP.index(k) * 1024, 1024)]

    def page_of(k):
        return pages.at[HOMES[k]]

    def local_copies(k):
        if k in DOWN:
            return [
                pltpu.make_async_copy(
                    shards[3].at[pl.ds(r * 32, 32), pl.ds(DOWN.index(k) * 256, 256)],
                    page_of(k).at[mine + (slice(None), pl.ds(r * 256, 256))],
                    own.at[k * 4 + r],
                )
                for r in range(4)
            ]
        return [pltpu.make_async_copy(shard_of(k), page_of(k).at[mine], own.at[k * 4])]

    local = {k: local_copies(k) for k in range(12)}
    early = []
    for k in (0, 1, 2, 3, 4, 5, 6, 7, 11):
        early += local[k]
    for i, narrow in enumerate(entries):
        move(narrow_i[i], narrow, 29 + i)
    for copy in early:
        copy.start()
    move(cot_i, low, 0)
    move(x_i, x, 1)
    greet(me, at)
    def pack():
        small[...] = jnp.zeros_like(small)
        for i, narrow in enumerate(entries):
            done(29 + i)
            small[pl.ds(i, 1), pl.ds(0, narrow.shape[1])] = narrow[...].astype(F32)
        packed = small[...]
        kind = lax.broadcasted_iota(jnp.int32, (8, 128), 0)
        fours = pltpu.roll(packed, lax.rem(me, 4) * 32, 1)
        twos = pltpu.roll(packed, lax.rem(me, 2) * 64, 1)
        small[...] = jnp.where(kind < 6, fours, jnp.where(kind == 6, twos, packed))
        early.append(pltpu.make_async_copy(small, smalls.at[mine], own.at[48]))
        early[-1].start()

    def row(vectors, i):
        return vectors.at[pl.ds(i, 1), :]

    def kept_len(seq):
        return lengths[assignment[seq]]

    def task_low():
        for seq in range(2):
            inside = lax.broadcasted_iota(jnp.int32, (320, 1), 0) < kept_len(seq)
            row_mask[pl.ds(seq * 320, 320), :] = jnp.where(inside, 1.0, 0.0)
        for s in (s4, s2, s1):
            s[...] = jnp.zeros_like(s)
        mixed[pl.ds(640, 64), :] = jnp.zeros((64, 3072), BF16)
        done(0)
        low[...] = (low[...].astype(F32) * row_mask[...]).astype(BF16)
        s4[pl.ds(5, 1), :] = whole_sum(column_sum(low[...].astype(F32)))

    def task_first():
        spread_vectors(smalls, v4, v2, v1)
        done(1)
        norm_rows(x, row(v4, 0), row(v4, 1), normed)

    def task_project(j):
        shift = None if j == 1 else v2.at[pl.ds(6, 1), pl.ds(0 if j == 0 else 1024, 1024)]
        project(normed, page_of(j), shift, mixed, j * 1024)
        if j == 1:
            turn(normed, normed1_t)
        done(8 + j)

    def task_attend(first, count):
        attend(first, count, mixed, kept_len, attended, probs, probs_o, probs_sems)

    def task_hidden():
        branch_out(attended, page_of(3), row(v4, 2), x, hidden)
        norm_rows(hidden, row(v4, 3), row(v4, 4), normed)
        done(11)

    def task_turns():
        turn(attended, other_t)
        move(other_t, attended_o, 5)
        done(5)
        turn(normed, other_t)

    def task_up(j):
        feed_up(normed, page_of(UP[j]), row(v1, 7), acts[j], slope, j * 1024)

    def task_feed(j):
        page = page_of(UP[j])
        slope_back(low, downs, j, slope, grad_pre, s1)
        outer_box(other_t, grad_pre, pages.at[MADE[j % 3]])
        back_through(grad_pre, page, total, j == 0)
        if j == 3:
            move(attended_o, other_t, 5)
        back = (3, 2, 1, 0)[j]
        move(spilled.at[back], page, 12 + back)

    def task_outer(j):
        if j > 1:
            done(2, 6)
        halves = [flat.at[2 + y, pl.ds(0, 512)] for y in range(2)]
        outer(acts[j], low, halves)
        for y, number in ((0, 2), (1, 6)):
            move(halves[y].reshape(2, 2, 4, 32, 1024), down_o.at[j, y], number)
        if j in (0, 3):
            done(2, 6)

    def task_second():
        norm_back(hidden, row(v4, 3), total, low, branch, part1, part2, part3)
        for i, part in ((3, part1), (4, part2), (2, part3)):
            s4[pl.ds(i, 1), :] = whole_sum(part[...])

    def task_out():
        done(5)
        outer_box(other_t, branch, pages.at[MADE[4 % 3]])

    def task_att():
        done(12 + 3)
        back_through(branch, page_of(UP[0]), grad_att, True)

    def task_attend_back(first, count):
        attend_back(first, count, mixed, attended, grad_att, probs, probs_o, probs_sems, grads)

    def task_mixed(j, m):
        outer_box(normed1_t, grads[j], pages.at[MADE[m % 3]])
        if j != 1:
            s2[pl.ds(6, 1), pl.ds(0 if j == 0 else 1024, 1024)] = whole_sum(
                column_sum(grads[j][...].astype(F32))
            )

    def task_through(j):
        done(12 + j)
        back_through(grads[j], page_of(UP[3 - j]), total, j == 2)

    def task_down(c):
        feed_down(acts, downs[c], row(v4, 5), hidden, row_mask, result, c)
        if c == 3:
            move(result, result_o, 3)

    def task_end():
        norm_back(x, row(v4, 0), total, branch, x, part1, part2, None)
        for i, part in ((0, part1), (1, part2)):
            s4[pl.ds(i, 1), :] = whole_sum(part[...])
        move(x, input_grad_o, 4)
        tiny = small_refs[0]
        for z in range(4):
            for y in range(2):
                for x_ in range(2):
                    for c in range(2):
                        d = ((z * 2 + y) * 2 + x_) * 2 + c
                        tiny[z, y, x_, c] = (
                            s4[:, d // 4 * 128 : d // 4 * 128 + 128]
                            + s2[:, d // 2 * 128 : d // 2 * 128 + 128]
                            + s1[:, d * 128 : d * 128 + 128]
                        )

    tasks = {
        3: [(task_low,)],
        5: [(task_first,), (task_project, 0)],
        6: [(task_project, 1)],
        7: [(task_project, 2), (task_attend, 0, 6)],
        8: [(task_attend, 6, 6)],
        9: [(task_attend, 12, 4), (task_hidden,)],
        10: [(task_turns,)],
        11: [(task_up, 0)],
        12: [(task_outer, 0)],
        13: [(task_feed, 0)],
        14: [(task_up, 1), (task_feed, 1)],
        15: [(task_up, 2), (task_feed, 2)],
        16: [(task_up, 3), (task_feed, 3)],
        17: [(task_second,), (task_out,)],
        18: [(task_outer, 1), (task_outer, 2), (task_outer, 3)],
        19: [(task_att,), (task_attend_back, 0, 4)],
        20: [(task_attend_back, 4, 4)],
        21: [(task_attend_back, 8, 4)],
        22: [(task_attend_back, 12, 4), (task_mixed, 2, 9)],
        23: [(task_mixed, 1, 10), (task_through, 2), (task_through, 1)],
        24: [(task_mixed, 0, 11), (task_through, 0), (task_end,)],
        25: [(task_down, 0), (task_down, 1)],
        26: [(task_down, 2), (task_down, 3)],
    }
    goals = [(2, 0, c) for c in (0, 1024, 2048, 3072)] + [(1, 0, 0)]
    goals += [(3, r, 0) for r in (0, 32, 64, 96)] + [(0, 0, 2048), (0, 0, 1024), (0, 0, 0)]
    flying, flows = {}, {}

    def begin(k, stage):
        if stage:
            for copy in flying.pop((k, stage - 1)):
                copy.wait()
        source = None if k in DOWN else shard_of(k)
        flying[k, stage] = gather_stage(page_of(k), PARTS if k else FIRST, stage, me, at, sems, k % 8, source)
        for copy in flying[k, stage]:
            copy.start()

    small_going = []
    for tick in range(LAST + 1):
        for stage in range(STAGES + 1):
            if 0 <= tick - stage < 12:
                begin(tick - stage, stage)
            if stage == 0 and tick == 0:
                pack()
            if stage == 0 and tick <= STAGES + 1:
                for copy in small_going:
                    copy.wait()
                small_going = []
                if tick <= STAGES:
                    small_going = gather_stage(smalls, SMALL, tick, me, at, sems, 8, small)
                for copy in small_going:
                    copy.start()
            if tick == 0 and stage == 0:
                for copy in early:
                    copy.wait()
            if tick + 1 in (8, 9, 10) and stage == 0:
                for copy in local[tick + 1]:
                    copy.start()
        k = tick - STAGES - 1
        if 0 <= k < 12:
            for copy in flying.pop((k, STAGES)):
                copy.wait()
            if k < 4:
                move(page_of(k), spilled.at[k], 8 + k)
        for stage in (1, 2, 3, 4, 5, 0):
            m = tick - BEGIN - stage
            if 0 <= m < 12:
                if stage == 0:
                    which, r, c = goals[m]
                    out = outs[which].at[pl.ds(r, ROWS), pl.ds(c, WIDE)]
                    source = down_o.at[:, :, :, :, r // 32] if which == 3 else None
                    made = pages.at[MADE[m % 3]]
                    flows[m] = Flow(made, source, out, BACK, cores[m % 2], slots[m % 3], lasts[m % 4], m % 8, back_sems, me, at)
                    flows[m].start()
                else:
                    flows[m].step(stage)
                    if stage == 5:
                        which, r, c = goals[m]
                        here = (pl.ds(r, ROWS), pl.ds(c, WIDE))
                        move(outs[which].at[here], outs_o[which].at[here], 16 + m)
        if tick >= LAST - STAGES - 1:
            if tick == LAST - STAGES - 1:
                flows["small"] = Flow(small_refs[0], None, small_out, SMALL_BACK, small_refs[1], small_refs[2:7], small_refs[7:], 8, back_sems, me, at)
                flows["small"].start()
            else:
                flows["small"].step(tick - LAST + STAGES + 1)
        for task, *args in tasks.get(tick, ()):
            task(*args)
        if tick + 1 in (8, 9, 10):
            for copy in local[tick + 1]:
                copy.wait()
    move(small_out, small_o, 28)
    done(3, 4, *range(16, 29))


def layer(x, cot, lengths, assignment, shards, narrow):
    anywhere = pl.BlockSpec(memory_space=pl.ANY)
    inside = pl.BlockSpec(memory_space=pltpu.VMEM)
    box = (4, 2, 2, 2)
    page = box + (32, 1024)
    flat, turned = (640, 1024), (1024, 640)
    made = [((32, 3072), F32), ((32, 1024), F32), ((32, 4096), F32), ((128, 1024), F32), ((8, 128), F32)]
    made += [(flat, BF16), (flat, BF16)]
    made += [((4,) + page, BF16), ((16, 2, 320, LEN_PAD), BF16), (box + (4, 32, 1024), BF16), (turned, BF16)]
    scratch = [
        ((11,) + page, BF16),
        (box + (8, 128), F32),
        ((8, 1024), F32),
        ((8, 2048), F32),
        ((8, 4096), F32),
        ((11,) + flat, BF16),
        (turned, BF16),
        (turned, BF16),
        ((704, 3072), BF16),
        (flat, F32),
        (flat, F32),
        ((2, 2, 320, LEN_PAD), BF16),
        ((640, 1), F32),
        ((8, 1024), F32),
        ((8, 2048), F32),
        ((8, 4096), F32),
    ] + [((8, 1024), F32)] * 3 + [((8, 128), F32)]
    scratch += made[:5] + [((1, n), BF16) for n in (32,) * 6 + (64, 128)]
    way, last = flow_buffers(BACK, BF16)
    scratch += way * 3 + last * 4 + [((4, 2, 2, 32, 1024), BF16)] * 2
    way, last = flow_buffers(SMALL_BACK, F32)
    scratch += [(box + (8, 128), F32), ((4, 2, 2, 8, 128), F32)] + way + last
    dma = pltpu.SemaphoreType.DMA
    return pl.pallas_call(
        layer_kernel,
        out_shape=[jax.ShapeDtypeStruct(s, d) for s, d in made],
        in_specs=[anywhere] * 2 + [pl.BlockSpec(memory_space=pltpu.SMEM)] * 2 + [anywhere] * 12,
        out_specs=[anywhere] * 11,
        scratch_shapes=[pltpu.VMEM(s, d) for s, d in scratch]
        + [dma((9, COPIES))] * 4
        + [dma((9,)), dma((49,)), dma((37,)), dma((2,))],
        compiler_params=pltpu.CompilerParams(
            collective_id=0, has_side_effects=True, vmem_limit_bytes=64 << 20
        ),
        name="layer",
    )(x, cot, lengths, assignment, *shards, *narrow)


def finish_kernel(*refs):
    arrays, outs, narrow_o, refs = refs[:7], refs[7:13], refs[13:21], refs[21:]
    blocks, narrow, sems, back_sems = refs[:7], refs[7:15], refs[15], refs[16]
    into = [pltpu.make_async_copy(a, block, sems.at[i]) for i, (a, block) in enumerate(zip(arrays, blocks))]
    back = [
        pltpu.make_async_copy(block, o, back_sems.at[i])
        for i, (o, block) in enumerate(zip((*outs, *narrow_o), (*blocks[:6], *narrow)))
    ]
    for copy in (into[6], *into[:6]):
        copy.start()
    into[6].wait()
    me = lax.axis_index("dp")
    total = blocks[6][...]
    fours = pltpu.roll(total, 128 - lax.rem(me, 4) * 32, 1)
    for i in range(6):
        narrow[i][...] = fours[i : i + 1, :32]
    narrow[6][...] = pltpu.roll(total, 128 - lax.rem(me, 2) * 64, 1)[6:7, :64]
    narrow[7][...] = total[7:8, :]
    for copy in back[6:]:
        copy.start()
    for i in range(6):
        into[i].wait()
        back[i].start()
    for copy in back:
        copy.wait()


def finish(*arrays):
    anywhere = pl.BlockSpec(memory_space=pl.ANY)
    narrow = [jax.ShapeDtypeStruct((1, n), F32) for n in (32,) * 6 + (64, 128)]
    found = pl.pallas_call(
        finish_kernel,
        out_shape=[jax.ShapeDtypeStruct(a.shape, a.dtype) for a in arrays[:6]] + narrow,
        in_specs=[anywhere] * 7,
        out_specs=[anywhere] * 14,
        scratch_shapes=[pltpu.VMEM(a.shape, a.dtype) for a in (*arrays, *narrow)]
        + [pltpu.SemaphoreType.DMA((7,)), pltpu.SemaphoreType.DMA((14,))],
        compiler_params=pltpu.CompilerParams(vmem_limit_bytes=63 << 20),
        name="finish",
    )(*arrays)
    return found[:6], [a.reshape(-1) for a in found[6:]]


NARROW = (0, 1, 5, 6, 7, 11)
WEIGHTS = (2, 4, 8, 10)


def on_box(inputs, lengths, assignment, *rest):
    weights, cotangent = rest[:12], rest[12]
    x = inputs.reshape(640, 1024)
    cot = cotangent.reshape(640, 1024)
    narrow = [weights[i][None] for i in (*NARROW, 3, 9)]
    made = layer(
        x, cot, lengths, assignment, [weights[i] for i in WEIGHTS], narrow
    )
    sums, (total, input_grad, result) = made[:4], made[4:7]
    (result, input_grad, *sums), narrow = finish(result, input_grad, *sums, total)
    found = [None] * 12
    for row, i in enumerate((*NARROW, 3, 9)):
        found[i] = narrow[row]
    for i, s in zip(WEIGHTS, sums):
        found[i] = s
    return (result.reshape(inputs.shape), input_grad.reshape(inputs.shape), *found)


def plain(
    inputs,
    lengths,
    assignment,
    norm1_gain,
    norm1_bias,
    qkv_weight,
    qv_bias,
    out_weight,
    out_bias,
    norm2_gain,
    norm2_bias,
    up_weight,
    up_bias,
    down_weight,
    down_bias,
    cotangent,
):
    gathered = (
        lax.all_gather(norm1_gain, "dp", axis=0, tiled=True),
        lax.all_gather(norm1_bias, "dp", axis=0, tiled=True),
        lax.all_gather(qkv_weight, "dp", axis=0, tiled=True),
        lax.all_gather(qv_bias, "dp", axis=0, tiled=True),
        lax.all_gather(out_weight, "dp", axis=0, tiled=True),
        lax.all_gather(out_bias, "dp", axis=0, tiled=True),
        lax.all_gather(norm2_gain, "dp", axis=0, tiled=True),
        lax.all_gather(norm2_bias, "dp", axis=0, tiled=True),
        lax.all_gather(up_weight, "dp", axis=0, tiled=True),
        lax.all_gather(up_bias, "dp", axis=0, tiled=True),
        lax.all_gather(down_weight, "dp", axis=0, tiled=True),
        lax.all_gather(down_bias, "dp", axis=0, tiled=True),
    )
    seq_count, tok_count, model_width = inputs.shape
    rows_all = seq_count * tok_count
    split_shape = (seq_count, tok_count, HEADS, HEAD)
    head_scale = HEAD ** (-0.5)
    matches = assignment[:, None] == jnp.arange(lengths.shape[0], dtype=jnp.int32)[None, :]
    kept_len = jnp.sum(jnp.where(matches, lengths[None, :], 0), axis=1)
    key_mask = jnp.arange(tok_count, dtype=jnp.int32)[None, :] < kept_len[:, None]
    row_mask = key_mask.reshape(rows_all, 1).astype(jnp.float32)
    gain_first = gathered[0].astype(jnp.float32)
    shift_first = gathered[1].astype(jnp.float32)
    qv_full = gathered[3].astype(jnp.float32)
    proj_shift = gathered[5].astype(jnp.float32)
    gain_second = gathered[6].astype(jnp.float32)
    shift_second = gathered[7].astype(jnp.float32)
    up_shift = gathered[9].astype(jnp.float32)
    down_shift = gathered[11].astype(jnp.float32)
    inputs_flat = inputs.reshape(rows_all, model_width).astype(jnp.float32)
    normed_first, first_back = jax.vjp(layer_norm, inputs_flat, gain_first, shift_first)
    normed_low = normed_first.astype(jnp.bfloat16)
    full_bias = jnp.concatenate(
        [qv_full[:model_width], jnp.zeros((model_width,), jnp.float32), qv_full[model_width:]]
    )
    mixed_qkv = (
        jnp.dot(normed_low, gathered[2], preferred_element_type=jnp.float32) + full_bias
    ).astype(jnp.bfloat16)
    queries = mixed_qkv[:, :model_width].reshape(split_shape)
    keys_all = mixed_qkv[:, model_width : 2 * model_width].reshape(split_shape)
    values_all = mixed_qkv[:, 2 * model_width :].reshape(split_shape)
    scores = (
        jnp.einsum("bqhd,bkhd->bhqk", queries, keys_all, preferred_element_type=jnp.float32)
        * head_scale
    )
    scores = jnp.where(key_mask[:, None, None, :], scores, masked_score)
    row_max = jnp.max(scores, axis=-1, keepdims=True)
    exponent = jnp.exp(scores - row_max)
    row_total = jnp.sum(exponent, axis=-1, keepdims=True)
    softmax_probs = exponent / row_total
    log_total = row_max + jnp.log(row_total)
    attended = jnp.einsum(
        "bhqk,bkhd->bqhd",
        softmax_probs.astype(jnp.bfloat16),
        values_all,
        preferred_element_type=jnp.float32,
    )
    attended = attended.reshape(rows_all, model_width).astype(jnp.bfloat16)
    hidden = inputs_flat + (
        jnp.dot(attended, gathered[4], preferred_element_type=jnp.float32) + proj_shift
    )
    normed_second, second_back = jax.vjp(layer_norm, hidden, gain_second, shift_second)
    second_low = normed_second.astype(jnp.bfloat16)
    pre_act = jnp.dot(second_low, gathered[8], preferred_element_type=jnp.float32) + up_shift
    activation, gelu_back = jax.vjp(gelu_exact, pre_act)
    act_low = activation.astype(jnp.bfloat16)
    output_rows = row_mask * (
        hidden + (jnp.dot(act_low, gathered[10], preferred_element_type=jnp.float32) + down_shift)
    )
    result = output_rows.reshape(inputs.shape).astype(jnp.bfloat16)
    grad_rows = cotangent.reshape(rows_all, model_width).astype(jnp.float32) * row_mask
    grad_low = grad_rows.astype(jnp.bfloat16)
    down_grad = contract_rows(act_low, grad_low)
    down_bias_grad = jnp.sum(grad_low.astype(jnp.float32), axis=0)
    grad_pre = gelu_back(contract_cols(grad_low, gathered[10]))[0].astype(jnp.bfloat16)
    up_grad = contract_rows(second_low, grad_pre)
    up_bias_grad = jnp.sum(grad_pre.astype(jnp.float32), axis=0)
    grad_second, gain2_grad, shift2_grad = second_back(contract_cols(grad_pre, gathered[8]))
    grad_hidden = grad_rows + grad_second
    branch_low = grad_hidden.astype(jnp.bfloat16)
    proj_grad = contract_rows(attended, branch_low)
    proj_bias_grad = jnp.sum(branch_low.astype(jnp.float32), axis=0)
    grad_att = contract_cols(branch_low, gathered[4]).astype(jnp.bfloat16).reshape(split_shape)
    scores_again = (
        jnp.einsum("bqhd,bkhd->bhqk", queries, keys_all, preferred_element_type=jnp.float32)
        * head_scale
    )
    scores_again = jnp.where(key_mask[:, None, None, :], scores_again, masked_score)
    probs_again = jnp.exp(scores_again - log_total)
    probs_low = probs_again.astype(jnp.bfloat16)
    grad_probs = jnp.einsum(
        "bqhd,bkhd->bhqk", grad_att, values_all, preferred_element_type=jnp.float32
    )
    grad_values = jnp.einsum(
        "bhqk,bqhd->bkhd", probs_low, grad_att, preferred_element_type=jnp.float32
    )
    inner_sum = jnp.sum(probs_again * grad_probs, axis=-1, keepdims=True)
    grad_scores = (probs_again * (grad_probs - inner_sum)).astype(jnp.bfloat16)
    grad_queries = (
        jnp.einsum("bhqk,bkhd->bqhd", grad_scores, keys_all, preferred_element_type=jnp.float32)
        * head_scale
    )
    grad_keys = (
        jnp.einsum("bhqk,bqhd->bkhd", grad_scores, queries, preferred_element_type=jnp.float32)
        * head_scale
    )
    grad_mixed = jnp.concatenate(
        [
            grad_queries.reshape(rows_all, model_width),
            grad_keys.reshape(rows_all, model_width),
            grad_values.reshape(rows_all, model_width),
        ],
        axis=1,
    ).astype(jnp.bfloat16)
    qkv_grad = contract_rows(normed_low, grad_mixed)
    column_sums = jnp.sum(grad_mixed.astype(jnp.float32), axis=0)
    qv_grad = jnp.concatenate([column_sums[:model_width], column_sums[2 * model_width :]])
    grad_first, gain1_grad, shift1_grad = first_back(contract_cols(grad_mixed, gathered[2]))
    input_grad = (grad_hidden + grad_first).reshape(inputs.shape).astype(jnp.bfloat16)
    all_sums = (
        lax.psum_scatter(gain1_grad, "dp", scatter_dimension=0, tiled=True),
        lax.psum_scatter(shift1_grad, "dp", scatter_dimension=0, tiled=True),
        lax.psum_scatter(qkv_grad, "dp", scatter_dimension=0, tiled=True),
        lax.psum_scatter(qv_grad, "dp", scatter_dimension=0, tiled=True),
        lax.psum_scatter(proj_grad, "dp", scatter_dimension=0, tiled=True),
        lax.psum_scatter(proj_bias_grad, "dp", scatter_dimension=0, tiled=True),
        lax.psum_scatter(gain2_grad, "dp", scatter_dimension=0, tiled=True),
        lax.psum_scatter(shift2_grad, "dp", scatter_dimension=0, tiled=True),
        lax.psum_scatter(up_grad, "dp", scatter_dimension=0, tiled=True),
        lax.psum_scatter(up_bias_grad, "dp", scatter_dimension=0, tiled=True),
        lax.psum_scatter(down_grad, "dp", scatter_dimension=0, tiled=True),
        lax.psum_scatter(down_bias_grad, "dp", scatter_dimension=0, tiled=True),
    )
    attn_sums = all_sums[:6]
    mlp_sums = all_sums[6:]
    return (
        result,
        input_grad,
        attn_sums[0],
        attn_sums[1],
        attn_sums[2],
        attn_sums[3],
        attn_sums[4],
        attn_sums[5],
        mlp_sums[0],
        mlp_sums[1],
        mlp_sums[2],
        mlp_sums[3],
        mlp_sums[4],
        mlp_sums[5],
    )


def local(*args):
    return on_box(*args) if lax.axis_size("dp") == 32 else plain(*args)


def solution(mesh):
    placed = (
        P("dp", None, None),
        P(),
        P("dp"),
        P("dp"),
        P("dp"),
        P("dp", None),
        P("dp"),
        P("dp", None),
        P("dp"),
        P("dp"),
        P("dp"),
        P("dp", None),
        P("dp"),
        P("dp", None),
        P("dp"),
        P("dp", None, None),
    )
    return jax.shard_map(
        local,
        mesh=mesh,
        in_specs=placed,
        out_specs=(
            P("dp", None, None),
            P("dp", None, None),
            P("dp"),
            P("dp"),
            P("dp", None),
            P("dp"),
            P("dp", None),
            P("dp"),
            P("dp"),
            P("dp"),
            P("dp", None),
            P("dp"),
            P("dp", None),
            P("dp"),
        ),
        check_vma=False,
    )
```

```python
import jax
import jax.numpy as jnp
from jax import lax
from jax.experimental import pallas as pl
from jax.experimental.pallas import tpu as pltpu
from jax.sharding import PartitionSpec as P

HEADS = 16
HEAD = 64


eps = 1e-06
masked_score = -1000000000.0


def layer_norm(values, norm_gain, norm_shift):
    average = jnp.mean(values, axis=-1, keepdims=True)
    centered = values - average
    variance = jnp.mean(centered * centered, axis=-1, keepdims=True)
    return centered * lax.rsqrt(variance + eps) * norm_gain + norm_shift


def gelu_exact(values):
    return jax.nn.gelu(values, approximate=False)


def contract_rows(left, right):
    return lax.dot_general(
        left, right, (((0,), (0,)), ((), ())), preferred_element_type=jnp.float32
    )


def contract_cols(left, right):
    return lax.dot_general(
        left, right, (((1,), (1,)), ((), ())), preferred_element_type=jnp.float32
    )


BF16 = jnp.bfloat16
F32 = jnp.float32
MESH = pl.DeviceIdType.MESH
STRIDE = {"z": 8, "y": 4, "x": 2}
ROWS = 32
WIDE = 1024
STAGES = 4
PARTS = (
    ("zZyx", 0, 16, 0, 384),
    ("zZxy", 16, 16, 0, 384),
    ("xzZy", 0, 16, 384, 640),
    ("yzZx", 16, 16, 384, 640),
)
FIRST = (("zZyx", 0, 16, 0, 1024), ("zZxy", 16, 16, 0, 1024))
COPIES = 6 * len(PARTS) + 1


def coords():
    me = lax.axis_index("dp")
    at = {
        "z": lax.div(me, 8),
        "y": lax.rem(lax.div(me, 4), 2),
        "x": lax.rem(lax.div(me, 2), 2),
        "c": lax.rem(me, 2),
    }
    return me, at


def sibling(me, at):
    return me + 1 - 2 * at["c"]


class Hop:
    def __init__(self, copy, sends=None, hears=None):
        self.copy, self.sends, self.hears = copy, sends, hears

    def start(self):
        if self.sends is None:
            self.copy.start()
        else:
            pl.when(self.sends)(self.copy.start)

    def wait(self):
        if self.sends is None:
            self.copy.wait()
        else:
            pl.when(self.sends)(self.copy.wait_send)
            pl.when(self.hears)(self.copy.wait_recv)


def inner(at):
    return lax.div(at["z"] + 1, 2) == 1


def far(at):
    return 3 * (1 - lax.div(at["z"], 2))


def hops(me, at, dim):
    z = at["z"]
    if dim == "z":
        found = []
        for k in (1, 2, 3):
            there = lax.rem(z + k, 4)
            when = {1: (z < 3, z > 0), 2: (None, None), 3: (z > 0, z < 3)}[k]
            found.append((there, me + (there - z) * 8, *when))
        return found
    if dim == "Z":
        return [(far(at), me + 8 - 16 * lax.rem(z, 2), inner(at), jnp.logical_not(inner(at)))]
    there = 1 - at[dim]
    return [(there, me + (there - at[dim]) * STRIDE[dim], None, None)]


def count_of(dim):
    return 3 if dim == "z" else 1


def greet(me, at):
    barrier = pltpu.get_barrier_semaphore()
    devices = [sibling(me, at)]
    for dim in "yx":
        devices += [hop[1] for hop in hops(me, at, dim)]
    for k in (1, 2, 3):
        devices.append(me + (lax.rem(at["z"] + k, 4) - at["z"]) * 8)
    for device in devices:
        pl.semaphore_signal(barrier, inc=1, device_id=(device,), device_id_type=MESH)
    pl.semaphore_wait(barrier, len(devices))


def remote(src, dst, sems, slot, number, device):
    return pltpu.make_async_remote_copy(
        src_ref=src,
        dst_ref=dst,
        send_sem=sems[0].at[slot, number],
        recv_sem=sems[1].at[slot, number],
        device_id=(device,),
        device_id_type=MESH,
    )


def held(order, stage, at):
    index = []
    for dim in "zyx":
        if dim == "z" and order[stage] == "Z":
            index.append(far(at))
        else:
            done = "Z" if dim == "z" else dim
            index.append(slice(None) if done in order[:stage] else at[dim])
    return tuple(index)


def gather_stage(base, parts, stage, me, at, sems, slot, source=None):
    if stage == STAGES:
        block = base.at[:, :, :, at["c"]]
        return [Hop(remote(block, block, sems, slot, COPIES - 1, sibling(me, at)))]
    number, copies = 0, []
    for order, row, rows, col, columns in parts:
        here = (pl.ds(row, rows), pl.ds(col, columns))
        for s in range(STAGES):
            for _, device, sends, hears in hops(me, at, order[s]):
                if s == stage:
                    block = base.at[held(order, stage, at) + (at["c"],) + here]
                    src = source.at[here] if source is not None and stage == 0 else block
                    copies.append(Hop(remote(src, block, sems, slot, number, device), sends, hears))
                number += 1
    return copies


SMALL = (("zZyx", 0, 8, 0, 128),)


def remaining(order, stage):
    left = [dim for dim in "zyx" if dim not in order[:stage]]
    return tuple({"z": 4, "y": 2, "x": 2}[dim] for dim in left)


def pick(order, stage, dim, index):
    return tuple(index if d == dim.lower() else slice(None) for d in "zyx" if d not in order[:stage])


BACK = tuple((part[0][::-1], *part[1:]) for part in PARTS)
SMALL_BACK = tuple((part[0][::-1], *part[1:]) for part in SMALL)


def add_up(dst, terms, lead):
    loops = lead[: max(len(lead) - 1, 0)] if len(lead) > 1 else ()
    count = 1
    for n in loops:
        count *= n

    def body(i, carry):
        index = []
        for n in loops[::-1]:
            index.append(lax.rem(i, n))
            i = lax.div(i, n)
        index = tuple(index[::-1]) + (slice(None),) * (len(lead) - len(loops) + 2)
        if len(terms) == 2 and dst.dtype == terms[0].dtype:
            dst[index] = terms[0][index] + terms[1][index]
            return carry
        total = terms[0][index].astype(F32)
        for term in terms[1:]:
            total = total + term[index].astype(F32)
        dst[index] = total.astype(dst.dtype)
        return carry

    if count == 1:
        body(0, 0)
    else:
        lax.fori_loop(0, count, body, 0)


class Flow:
    def __init__(self, made, source, out, parts, from_core, rest, last, slot, sems, me, at):
        self.made, self.source, self.out, self.parts = made, source, out, parts
        self.from_core = from_core
        self.arrived, self.totals = [], []
        for part, (order, *_) in enumerate(parts):
            self.arrived.append((*rest[:3], last[part]))
            self.totals.append(dict(zip([s for s in range(3) if order[s] != "Z"], rest[3:5])))
            rest = rest[5:]
        self.slot, self.sems, self.me, self.at = slot, sems, me, at
        self.own = made.at[:, :, :, at["c"]]

    def start(self):
        there = 1 - self.at["c"]
        source = self.made if self.source is None else self.source
        self.going = [
            remote(
                source.at[:, :, :, there],
                self.from_core,
                self.sems,
                self.slot,
                COPIES - 1,
                sibling(self.me, self.at),
            )
        ]
        if self.source is not None:
            self.going.append(
                pltpu.make_async_copy(source.at[:, :, :, self.at["c"]], self.own, self.sems[2].at[self.slot])
            )
        for copy in self.going:
            copy.start()

    def sum_before(self, part, stage):
        order, row, rows, col, columns = self.parts[part]
        done = [s for s in range(stage) if s in self.totals[part]]
        if not done:
            return self.own.at[:, :, :, pl.ds(row, rows), pl.ds(col, columns)]
        return self.totals[part][done[-1]]

    def take(self, part, stage):
        order, row, rows, col, columns = self.parts[part]
        s = stage - 2
        dim, arrived = order[s], self.arrived[part][s]
        before = self.sum_before(part, s)
        if dim == "Z":
            index = pick(order, s, "z", far(self.at))

            @pl.when(inner(self.at))
            def _():
                add_up(before.at[index], [before.at[index], arrived.at[0]], remaining(order, s)[1:])

            return
        if stage == STAGES + 1:
            total = self.out.at[pl.ds(row, rows), pl.ds(col, columns)]
        else:
            total = self.totals[part][s]
        mine = before.at[pick(order, s, dim, self.at[dim])]
        left = remaining(order, s + 1)
        if dim != "z":
            add_up(total, [mine, arrived.at[0]], left)
            return
        z = self.at["z"]
        for when, came in ((z == 0, (1, 2)), (inner(self.at), (0, 1, 2)), (z == 3, (0, 1))):

            @pl.when(when)
            def _(came=came):
                add_up(total, [mine] + [arrived.at[i] for i in came], left)

    def step(self, stage):
        for copy in self.going:
            copy.wait()
        if stage == 1:
            add_up(self.own, [self.own, self.from_core], (4, 2, 2))
        else:
            for part in range(len(self.parts)):
                self.take(part, stage)
        self.going, number = [], 0
        for part, (order, row, rows, col, columns) in enumerate(self.parts):
            for s in range(STAGES):
                if s + 1 == stage:
                    before = self.sum_before(part, s)
                    for i, (there, device, sends, hears) in enumerate(hops(self.me, self.at, order[s])):
                        if order[s] == "Z":
                            sends, hears = hears, sends
                        src = before.at[pick(order, s, order[s], there)]
                        copy = remote(src, self.arrived[part][s].at[i], self.sems, self.slot, number + i, device)
                        self.going.append(Hop(copy, sends, hears))
                number += count_of(order[s])
        for copy in self.going:
            copy.start()


def flow_buffers(parts, dtype):
    shapes, last = [], []
    for order, _, high, _, wide in parts:
        totals = []
        for s in range(STAGES):
            if order[s] == "Z":
                left = remaining(order, s)[1:]
            else:
                left = remaining(order, s + 1)
                if s < 3:
                    totals.append((left + (high, wide), dtype))
            (shapes if s < 3 else last).append(((count_of(order[s]),) + left + (high, wide), dtype))
        shapes += totals
    return shapes, last


EPS = 1e-06
MASKED = -1000000000.0
LEN_PAD = 384


def dot_nn(a, b):
    return jnp.dot(a, b, preferred_element_type=F32)


def dot_nt(a, b):
    return lax.dot_general(a, b, (((1,), (1,)), ((), ())), preferred_element_type=F32)


def dot_tn(a, b):
    return lax.dot_general(a, b, (((0,), (0,)), ((), ())), preferred_element_type=F32)


def block_of(index, size):
    return pl.ds(pl.multiple_of(index * size, size), size)


def spread_vectors(smalls, v4, v2, v1):
    for z in range(4):
        for y in range(2):
            four = None
            for x in range(2):
                two = None
                for c in range(2):
                    one = smalls[z, y, x, c]
                    d = ((z * 2 + y) * 2 + x) * 2 + c
                    v1[:, d * 128 : d * 128 + 128] = one
                    two = one if two is None else two + one
                d = (z * 2 + y) * 2 + x
                v2[:, d * 128 : d * 128 + 128] = two
                four = two if four is None else four + two
            d = z * 2 + y
            v4[:, d * 128 : d * 128 + 128] = four


def norm_rows(src, gain, shift, dst):
    @pl.loop(0, src.shape[0] // 64)
    def _(i):
        rows = block_of(i, 64)
        values = src[rows, :].astype(F32)
        centered = values - jnp.mean(values, axis=-1, keepdims=True)
        variance = jnp.mean(centered * centered, axis=-1, keepdims=True)
        normed = centered * lax.rsqrt(variance + EPS)
        dst[rows, :] = (normed * gain[...] + shift[...]).astype(BF16)


def project(normed, weight, shift, dst, col):
    @pl.loop(0, 2)
    def _(i):
        columns = block_of(i, 512)
        mixed = dot_nn(normed[...], weight[:, :, :, :, :, columns].reshape(1024, 512))
        if shift is not None:
            mixed = mixed + shift[:, columns]
        dst[pl.ds(0, 640), pl.ds(pl.multiple_of(col + i * 512, 512), 512)] = mixed.astype(BF16)


def attend(first, count, mixed, kept_len, attended, probs, probs_out, sems):
    lane = lax.broadcasted_iota(jnp.int32, (1, 128), 1)

    def out_copy(unit, slot):
        return pltpu.make_async_copy(probs.at[slot], probs_out.at[unit], sems.at[slot])

    @pl.loop(0, count // 2)
    def _(i):
        for slot in range(2):
            unit = first + i * 2 + slot
            seq, pair = lax.div(unit, 8), lax.rem(unit, 8)
            start = pl.multiple_of(seq * 320, 64)
            columns = block_of(pair, 128)
            q = mixed[pl.ds(start, 320), columns]
            k = mixed[pl.ds(start, LEN_PAD), block_of(pair + 8, 128)]
            v = mixed[pl.ds(start, LEN_PAD), block_of(pair + 16, 128)]
            kept = lax.broadcasted_iota(jnp.int32, (1, LEN_PAD), 1) < kept_len(seq)

            @pl.when(i > 0)
            def _():
                out_copy(unit, slot).wait()

            found = []
            for head in range(2):
                scale = jnp.where(lax.div(lane, 64) == head, 0.125, 0.0).astype(BF16)
                scores = jnp.where(kept, dot_nt(q * scale, k), MASKED)
                exponent = jnp.exp(scores - jnp.max(scores, axis=-1, keepdims=True))
                total = jnp.sum(exponent, axis=-1, keepdims=True)
                low = (exponent * (1.0 / total)).astype(BF16)
                probs[slot, head] = low
                found.append(dot_nn(low, v))
            attended[pl.ds(start, 320), columns] = jnp.where(
                lane < 64, found[0], found[1]
            ).astype(BF16)
            out_copy(unit, slot).start()

    for slot in range(2):
        out_copy(0, slot).wait()


def branch_out(attended, weight, shift, x, hidden):
    @pl.loop(0, 2)
    def _(i):
        columns = block_of(i, 512)
        branch = dot_nn(attended[...], weight[:, :, :, :, :, columns].reshape(1024, 512))
        hidden[:, columns] = x[:, columns].astype(F32) + (branch + shift[:, columns])


def feed_up(normed, weight, shift, act, slope, col):
    pre = dot_nn(normed[...], weight[...].reshape(1024, 1024)) + shift[:, pl.ds(col, 1024)]
    below = 0.5 + 0.5 * lax.erf(pre * 0.7071067811865476)
    act[...] = (pre * below).astype(BF16)
    density = jnp.exp(pre * pre * -0.5) * 0.3989422804014327
    slope[...] = (below + pre * density).astype(BF16)


def outer(left, right, halves):
    part = dot_tn(left[...], right[...]).astype(BF16)
    for i, half in enumerate(halves):
        half[...] = part[i * 512 : i * 512 + 512]


def turn(src, dst):
    @pl.loop(0, 4)
    def _(i):
        rows = block_of(i, 256)
        dst[rows, :] = src[:, rows].T


def tall(block):
    parts = [block[..., i * 256 : i * 256 + 256] for i in range(4)]
    rows = jnp.stack(parts, axis=block.ndim - 2)
    return rows.reshape(-1, 256)


def feed_down(acts, page, shift, hidden, row_mask, result, c):
    columns = pl.ds(c * 256, 256)
    branch = dot_nn(acts[0][...], tall(page[0]))
    for z in range(1, 4):
        branch = branch + dot_nn(acts[z][...], tall(page[z]))
    whole = hidden[:, columns] + (branch + shift[:, columns])
    result[:, columns] = (whole * row_mask[...]).astype(BF16)


def column_sum(values):
    return jnp.sum(values.reshape(values.shape[0] // 8, 8, values.shape[1]), axis=0)


def norm_back(src, gain, grads, base, dst, by_scale, by_shift, by_low):
    for total in (by_scale, by_shift, by_low):
        if total is not None:
            total[...] = jnp.zeros_like(total)

    @pl.loop(0, 640 // 64)
    def _(i):
        rows = block_of(i, 64)
        values = src[rows, :].astype(F32)
        centered = values - jnp.mean(values, axis=-1, keepdims=True)
        inverse = lax.rsqrt(jnp.mean(centered * centered, axis=-1, keepdims=True) + EPS)
        normed = centered * inverse
        g = grads[rows, :]
        scaled = g * gain[...]
        along = jnp.mean(scaled * normed, axis=-1, keepdims=True)
        back = inverse * (scaled - jnp.mean(scaled, axis=-1, keepdims=True) - normed * along)
        whole = base[rows, :].astype(F32) + back
        rounded = whole.astype(BF16)
        dst[rows, :] = rounded
        by_scale[...] += column_sum(g * normed)
        by_shift[...] += column_sum(g)
        if by_low is not None:
            by_low[...] += column_sum(rounded.astype(F32))


def whole_sum(part):
    return jnp.sum(part, axis=0, keepdims=True)


def slope_back(low, pages, j, slope, grad_pre, total):
    weight = jnp.concatenate([tall(page[j]) for page in pages], axis=1)
    grad = (dot_nt(low[...], weight) * slope[...].astype(F32)).astype(BF16)
    grad_pre[...] = grad
    total[pl.ds(7, 1), pl.ds(j * 1024, 1024)] = whole_sum(column_sum(grad.astype(F32)))


def back_through(left, page, total, first):
    part = dot_nt(left[...], page[...].reshape(1024, 1024))
    total[...] = part.astype(total.dtype) if first else total[...] + part


def outer_box(turned, right, dst):
    dst[...] = dot_nn(turned[...], right[...]).astype(BF16).reshape(4, 2, 2, 2, 32, 1024)


def attend_back(first, count, mixed, attended, grad_att, probs, probs_in, sems, grads):
    lane = lax.broadcasted_iota(jnp.int32, (1, 128), 1)

    def load(unit, slot):
        return pltpu.make_async_copy(probs_in.at[unit], probs.at[slot], sems.at[slot])

    load(first, 0).start()

    @pl.loop(0, count // 2)
    def _(i):
        for slot in range(2):
            unit = first + i * 2 + slot
            seq, pair = lax.div(unit, 8), lax.rem(unit, 8)
            start = pl.multiple_of(seq * 320, 64)
            rows = pl.ds(start, 320)
            col_q, col_k, col_v = (block_of(pair + 8 * n, 128) for n in range(3))
            load(unit, slot).wait()
            if slot == 0:
                load(unit + 1, 1).start()
            else:

                @pl.when(i + 1 < count // 2)
                def _():
                    load(unit + 1, 0).start()

            q = mixed[rows, col_q]
            k = mixed[pl.ds(start, LEN_PAD), col_k]
            v = mixed[pl.ds(start, LEN_PAD), col_v]
            grad_out = grad_att[rows, col_q]
            along = grad_out.astype(F32) * attended[rows, col_q].astype(F32)
            turned_q, turned_out = q.T, grad_out.T
            found = []
            for head in range(2):
                mine = lax.div(lane, 64) == head
                low = probs[slot, head]
                grad_p = dot_nt(grad_out * jnp.where(mine, 1.0, 0.0).astype(BF16), v)
                inner = jnp.sum(jnp.where(mine, along, 0.0), axis=-1, keepdims=True)
                grad_s = (low.astype(F32) * (grad_p - inner)).astype(BF16)
                part = slice(head * 64, head * 64 + 64)
                found.append((dot_nn(grad_s, k), dot_nn(turned_q[part], grad_s), dot_nn(turned_out[part], low)))
            grads[0][rows, col_q] = (jnp.where(lane < 64, found[0][0], found[1][0]) * 0.125).astype(BF16)
            for grad, scale, of in ((grads[1], 0.125, 1), (grads[2], 1.0, 2)):
                both = jnp.concatenate([found[0][of], found[1][of]], axis=0)
                grad[rows, col_q] = (both * scale).astype(BF16).T[:320]


UP = (4, 9, 10, 11)
DOWN = (5, 6, 7, 8)
HOMES = (0, 1, 2, 3, 4, 5, 6, 7, 0, 1, 2, 8)
MADE = (3, 9, 10)
BEGIN = 14
LAST = BEGIN + 12 + STAGES


def layer_kernel(*refs):
    x_i, cot_i, lengths, assignment = refs[:4]
    shards, narrow_i = refs[4:8], refs[8:16]
    refs = refs[7:]
    outs_o, small_o, input_grad_o, result_o, spilled, probs_o, down_o, attended_o = refs[9:13], *refs[13:20]
    (pages, smalls, v4, v2, v1, flat, normed1_t, other_t, mixed, hidden, total, probs, row_mask, s4, s2, s1, part1, part2, part3, small) = refs[20:40]
    outs, small_out, entries, refs = refs[40:44], refs[44], refs[45:53], refs[53:]
    per, parts = 5 * len(BACK), len(BACK)
    slots, refs = [refs[i * per : i * per + per] for i in range(3)], refs[3 * per :]
    lasts, refs = [refs[i * parts : i * parts + parts] for i in range(4)], refs[4 * parts :]
    cores, refs = refs[:2], refs[2:]
    small_refs, refs = refs[:8], refs[8:]
    send, recv, back_send, back_recv, back_own, own, single, probs_sems = refs
    sems, back_sems = (send, recv), (back_send, back_recv, back_own)
    me, at = coords()
    mine = (at["z"], at["y"], at["x"], at["c"])
    normed = branch = result = flat.at[0]
    slope = grad_att = flat.at[1]
    grad_pre = flat.at[2]
    x, low, attended = flat.at[4], flat.at[5], flat.at[6]
    acts = [flat.at[7 + j] for j in range(4)]
    grads = (flat.at[2], flat.at[5], flat.at[3])
    downs = [pages.at[HOMES[k]] for k in DOWN]
    going = {}

    def move(src, dst, number):
        going[number] = pltpu.make_async_copy(src, dst, single.at[number])
        going[number].start()

    def done(*numbers):
        for number in numbers:
            going.pop(number).wait()

    def shard_of(k):
        if k < 3:
            return shards[0].at[:, pl.ds(k * 1024, 1024)]
        if k == 3:
            return shards[1]
        return shards[2].at[:, pl.ds(UP.index(k) * 1024, 1024)]

    def page_of(k):
        return pages.at[HOMES[k]]

    def local_copies(k):
        if k in DOWN:
            return [
                pltpu.make_async_copy(
                    shards[3].at[pl.ds(r * 32, 32), pl.ds(DOWN.index(k) * 256, 256)],
                    page_of(k).at[mine + (slice(None), pl.ds(r * 256, 256))],
                    own.at[k * 4 + r],
                )
                for r in range(4)
            ]
        return [pltpu.make_async_copy(shard_of(k), page_of(k).at[mine], own.at[k * 4])]

    local = {k: local_copies(k) for k in range(12)}
    early = []
    for k in (0, 1, 2, 3, 4, 5, 6, 7, 11):
        early += local[k]
    for i, narrow in enumerate(entries):
        move(narrow_i[i], narrow, 29 + i)
    for copy in early:
        copy.start()
    move(cot_i, low, 0)
    move(x_i, x, 1)
    greet(me, at)
    def pack():
        small[...] = jnp.zeros_like(small)
        for i, narrow in enumerate(entries):
            done(29 + i)
            small[pl.ds(i, 1), pl.ds(0, narrow.shape[1])] = narrow[...].astype(F32)
        packed = small[...]
        kind = lax.broadcasted_iota(jnp.int32, (8, 128), 0)
        fours = pltpu.roll(packed, lax.rem(me, 4) * 32, 1)
        twos = pltpu.roll(packed, lax.rem(me, 2) * 64, 1)
        small[...] = jnp.where(kind < 6, fours, jnp.where(kind == 6, twos, packed))
        early.append(pltpu.make_async_copy(small, smalls.at[mine], own.at[48]))
        early[-1].start()

    def row(vectors, i):
        return vectors.at[pl.ds(i, 1), :]

    def kept_len(seq):
        return lengths[assignment[seq]]

    def task_low():
        for seq in range(2):
            inside = lax.broadcasted_iota(jnp.int32, (320, 1), 0) < kept_len(seq)
            row_mask[pl.ds(seq * 320, 320), :] = jnp.where(inside, 1.0, 0.0)
        for s in (s4, s2, s1):
            s[...] = jnp.zeros_like(s)
        mixed[pl.ds(640, 64), :] = jnp.zeros((64, 3072), BF16)
        done(0)
        low[...] = (low[...].astype(F32) * row_mask[...]).astype(BF16)
        s4[pl.ds(5, 1), :] = whole_sum(column_sum(low[...].astype(F32)))

    def task_first():
        spread_vectors(smalls, v4, v2, v1)
        done(1)
        norm_rows(x, row(v4, 0), row(v4, 1), normed)

    def task_project(j):
        shift = None if j == 1 else v2.at[pl.ds(6, 1), pl.ds(0 if j == 0 else 1024, 1024)]
        project(normed, page_of(j), shift, mixed, j * 1024)
        if j == 1:
            turn(normed, normed1_t)
        done(8 + j)

    def task_attend(first, count):
        attend(first, count, mixed, kept_len, attended, probs, probs_o, probs_sems)

    def task_hidden():
        branch_out(attended, page_of(3), row(v4, 2), x, hidden)
        norm_rows(hidden, row(v4, 3), row(v4, 4), normed)
        done(11)

    def task_turns():
        turn(attended, other_t)
        move(other_t, attended_o, 5)
        done(5)
        turn(normed, other_t)

    def task_up(j):
        feed_up(normed, page_of(UP[j]), row(v1, 7), acts[j], slope, j * 1024)

    def task_feed(j):
        page = page_of(UP[j])
        slope_back(low, downs, j, slope, grad_pre, s1)
        outer_box(other_t, grad_pre, pages.at[MADE[j % 3]])
        back_through(grad_pre, page, total, j == 0)
        if j == 3:
            move(attended_o, other_t, 5)
        back = (3, 2, 1, 0)[j]
        move(spilled.at[back], page, 12 + back)

    def task_outer(j):
        if j > 1:
            done(2, 6)
        halves = [flat.at[2 + y, pl.ds(0, 512)] for y in range(2)]
        outer(acts[j], low, halves)
        for y, number in ((0, 2), (1, 6)):
            move(halves[y].reshape(2, 2, 4, 32, 1024), down_o.at[j, y], number)
        if j in (0, 3):
            done(2, 6)

    def task_second():
        norm_back(hidden, row(v4, 3), total, low, branch, part1, part2, part3)
        for i, part in ((3, part1), (4, part2), (2, part3)):
            s4[pl.ds(i, 1), :] = whole_sum(part[...])

    def task_out():
        done(5)
        outer_box(other_t, branch, pages.at[MADE[4 % 3]])

    def task_att():
        done(12 + 3)
        back_through(branch, page_of(UP[0]), grad_att, True)

    def task_attend_back(first, count):
        attend_back(first, count, mixed, attended, grad_att, probs, probs_o, probs_sems, grads)

    def task_mixed(j, m):
        outer_box(normed1_t, grads[j], pages.at[MADE[m % 3]])
        if j != 1:
            s2[pl.ds(6, 1), pl.ds(0 if j == 0 else 1024, 1024)] = whole_sum(
                column_sum(grads[j][...].astype(F32))
            )

    def task_through(j):
        done(12 + j)
        back_through(grads[j], page_of(UP[3 - j]), total, j == 2)

    def task_down(c):
        feed_down(acts, downs[c], row(v4, 5), hidden, row_mask, result, c)
        if c == 3:
            move(result, result_o, 3)

    def task_end():
        norm_back(x, row(v4, 0), total, branch, x, part1, part2, None)
        for i, part in ((0, part1), (1, part2)):
            s4[pl.ds(i, 1), :] = whole_sum(part[...])
        move(x, input_grad_o, 4)
        tiny = small_refs[0]
        for z in range(4):
            for y in range(2):
                for x_ in range(2):
                    for c in range(2):
                        d = ((z * 2 + y) * 2 + x_) * 2 + c
                        tiny[z, y, x_, c] = (
                            s4[:, d // 4 * 128 : d // 4 * 128 + 128]
                            + s2[:, d // 2 * 128 : d // 2 * 128 + 128]
                            + s1[:, d * 128 : d * 128 + 128]
                        )

    tasks = {
        3: [(task_low,)],
        5: [(task_first,), (task_project, 0)],
        6: [(task_project, 1)],
        7: [(task_project, 2), (task_attend, 0, 6)],
        8: [(task_attend, 6, 6)],
        9: [(task_attend, 12, 4), (task_hidden,)],
        10: [(task_turns,)],
        11: [(task_up, 0)],
        12: [(task_outer, 0)],
        13: [(task_feed, 0)],
        14: [(task_up, 1), (task_feed, 1)],
        15: [(task_up, 2), (task_feed, 2)],
        16: [(task_up, 3), (task_feed, 3)],
        17: [(task_second,), (task_out,)],
        18: [(task_outer, 1), (task_outer, 2), (task_outer, 3)],
        19: [(task_att,), (task_attend_back, 0, 4)],
        20: [(task_attend_back, 4, 4)],
        21: [(task_attend_back, 8, 4)],
        22: [(task_attend_back, 12, 4), (task_mixed, 2, 9)],
        23: [(task_mixed, 1, 10), (task_through, 2), (task_through, 1)],
        24: [(task_mixed, 0, 11), (task_through, 0), (task_end,)],
        25: [(task_down, 0), (task_down, 1)],
        26: [(task_down, 2), (task_down, 3)],
    }
    goals = [(2, 0, c) for c in (0, 1024, 2048, 3072)] + [(1, 0, 0)]
    goals += [(3, r, 0) for r in (0, 32, 64, 96)] + [(0, 0, 2048), (0, 0, 1024), (0, 0, 0)]
    flying, flows = {}, {}

    def begin(k, stage):
        if stage:
            for copy in flying.pop((k, stage - 1)):
                copy.wait()
        source = None if k in DOWN else shard_of(k)
        flying[k, stage] = gather_stage(page_of(k), PARTS if k else FIRST, stage, me, at, sems, k % 8, source)
        for copy in flying[k, stage]:
            copy.start()

    small_going = []
    for tick in range(LAST + 1):
        for stage in range(STAGES + 1):
            if 0 <= tick - stage < 12:
                begin(tick - stage, stage)
            if stage == 0 and tick == 0:
                pack()
            if stage == 0 and tick <= STAGES + 1:
                for copy in small_going:
                    copy.wait()
                small_going = []
                if tick <= STAGES:
                    small_going = gather_stage(smalls, SMALL, tick, me, at, sems, 8, small)
                for copy in small_going:
                    copy.start()
            if tick == 0 and stage == 0:
                for copy in early:
                    copy.wait()
            if tick + 1 in (8, 9, 10) and stage == 0:
                for copy in local[tick + 1]:
                    copy.start()
        k = tick - STAGES - 1
        if 0 <= k < 12:
            for copy in flying.pop((k, STAGES)):
                copy.wait()
            if k < 4:
                move(page_of(k), spilled.at[k], 8 + k)
        for stage in (1, 2, 3, 4, 5, 0):
            m = tick - BEGIN - stage
            if 0 <= m < 12:
                if stage == 0:
                    which, r, c = goals[m]
                    out = outs[which].at[pl.ds(r, ROWS), pl.ds(c, WIDE)]
                    source = down_o.at[:, :, :, :, r // 32] if which == 3 else None
                    made = pages.at[MADE[m % 3]]
                    flows[m] = Flow(made, source, out, BACK, cores[m % 2], slots[m % 3], lasts[m % 4], m % 8, back_sems, me, at)
                    flows[m].start()
                else:
                    flows[m].step(stage)
                    if stage == 5:
                        which, r, c = goals[m]
                        here = (pl.ds(r, ROWS), pl.ds(c, WIDE))
                        move(outs[which].at[here], outs_o[which].at[here], 16 + m)
        if tick >= LAST - STAGES - 1:
            if tick == LAST - STAGES - 1:
                flows["small"] = Flow(small_refs[0], None, small_out, SMALL_BACK, small_refs[1], small_refs[2:7], small_refs[7:], 8, back_sems, me, at)
                flows["small"].start()
            else:
                flows["small"].step(tick - LAST + STAGES + 1)
        for task, *args in tasks.get(tick, ()):
            task(*args)
        if tick + 1 in (8, 9, 10):
            for copy in local[tick + 1]:
                copy.wait()
    move(small_out, small_o, 28)
    done(3, 4, *range(16, 29))


def layer(x, cot, lengths, assignment, shards, narrow):
    anywhere = pl.BlockSpec(memory_space=pl.ANY)
    inside = pl.BlockSpec(memory_space=pltpu.VMEM)
    box = (4, 2, 2, 2)
    page = box + (32, 1024)
    flat, turned = (640, 1024), (1024, 640)
    made = [((32, 3072), F32), ((32, 1024), F32), ((32, 4096), F32), ((128, 1024), F32), ((8, 128), F32)]
    made += [(flat, BF16), (flat, BF16)]
    made += [((4,) + page, BF16), ((16, 2, 320, LEN_PAD), BF16), (box + (4, 32, 1024), BF16), (turned, BF16)]
    scratch = [
        ((11,) + page, BF16),
        (box + (8, 128), F32),
        ((8, 1024), F32),
        ((8, 2048), F32),
        ((8, 4096), F32),
        ((11,) + flat, BF16),
        (turned, BF16),
        (turned, BF16),
        ((704, 3072), BF16),
        (flat, F32),
        (flat, F32),
        ((2, 2, 320, LEN_PAD), BF16),
        ((640, 1), F32),
        ((8, 1024), F32),
        ((8, 2048), F32),
        ((8, 4096), F32),
    ] + [((8, 1024), F32)] * 3 + [((8, 128), F32)]
    scratch += made[:5] + [((1, n), BF16) for n in (32,) * 6 + (64, 128)]
    way, last = flow_buffers(BACK, BF16)
    scratch += way * 3 + last * 4 + [((4, 2, 2, 32, 1024), BF16)] * 2
    way, last = flow_buffers(SMALL_BACK, F32)
    scratch += [(box + (8, 128), F32), ((4, 2, 2, 8, 128), F32)] + way + last
    dma = pltpu.SemaphoreType.DMA
    return pl.pallas_call(
        layer_kernel,
        out_shape=[jax.ShapeDtypeStruct(s, d) for s, d in made],
        in_specs=[anywhere] * 2 + [pl.BlockSpec(memory_space=pltpu.SMEM)] * 2 + [anywhere] * 12,
        out_specs=[anywhere] * 11,
        scratch_shapes=[pltpu.VMEM(s, d) for s, d in scratch]
        + [dma((9, COPIES))] * 4
        + [dma((9,)), dma((49,)), dma((37,)), dma((2,))],
        compiler_params=pltpu.CompilerParams(
            collective_id=0, has_side_effects=True, vmem_limit_bytes=64 << 20
        ),
        name="layer",
    )(x, cot, lengths, assignment, *shards, *narrow)


def finish_kernel(*refs):
    arrays, outs, narrow_o, refs = refs[:7], refs[7:13], refs[13:21], refs[21:]
    blocks, narrow, sems, back_sems = refs[:7], refs[7:15], refs[15], refs[16]
    into = [pltpu.make_async_copy(a, block, sems.at[i]) for i, (a, block) in enumerate(zip(arrays, blocks))]
    back = [
        pltpu.make_async_copy(block, o, back_sems.at[i])
        for i, (o, block) in enumerate(zip((*outs, *narrow_o), (*blocks[:6], *narrow)))
    ]
    for copy in (into[6], *into[:6]):
        copy.start()
    into[6].wait()
    me = lax.axis_index("dp")
    total = blocks[6][...]
    fours = pltpu.roll(total, 128 - lax.rem(me, 4) * 32, 1)
    for i in range(6):
        narrow[i][...] = fours[i : i + 1, :32]
    narrow[6][...] = pltpu.roll(total, 128 - lax.rem(me, 2) * 64, 1)[6:7, :64]
    narrow[7][...] = total[7:8, :]
    for copy in back[6:]:
        copy.start()
    for i in range(6):
        into[i].wait()
        back[i].start()
    for copy in back:
        copy.wait()


def finish(*arrays):
    anywhere = pl.BlockSpec(memory_space=pl.ANY)
    narrow = [jax.ShapeDtypeStruct((1, n), F32) for n in (32,) * 6 + (64, 128)]
    found = pl.pallas_call(
        finish_kernel,
        out_shape=[jax.ShapeDtypeStruct(a.shape, a.dtype) for a in arrays[:6]] + narrow,
        in_specs=[anywhere] * 7,
        out_specs=[anywhere] * 14,
        scratch_shapes=[pltpu.VMEM(a.shape, a.dtype) for a in (*arrays, *narrow)]
        + [pltpu.SemaphoreType.DMA((7,)), pltpu.SemaphoreType.DMA((14,))],
        compiler_params=pltpu.CompilerParams(vmem_limit_bytes=63 << 20),
        name="finish",
    )(*arrays)
    return found[:6], [a.reshape(-1) for a in found[6:]]


NARROW = (0, 1, 5, 6, 7, 11)
WEIGHTS = (2, 4, 8, 10)


def on_box(inputs, lengths, assignment, *rest):
    weights, cotangent = rest[:12], rest[12]
    x = inputs.reshape(640, 1024)
    cot = cotangent.reshape(640, 1024)
    narrow = [weights[i][None] for i in (*NARROW, 3, 9)]
    made = layer(
        x, cot, lengths, assignment, [weights[i] for i in WEIGHTS], narrow
    )
    sums, (total, input_grad, result) = made[:4], made[4:7]
    (result, input_grad, *sums), narrow = finish(result, input_grad, *sums, total)
    found = [None] * 12
    for row, i in enumerate((*NARROW, 3, 9)):
        found[i] = narrow[row]
    for i, s in zip(WEIGHTS, sums):
        found[i] = s
    return (result.reshape(inputs.shape), input_grad.reshape(inputs.shape), *found)


def plain(
    inputs,
    lengths,
    assignment,
    norm1_gain,
    norm1_bias,
    qkv_weight,
    qv_bias,
    out_weight,
    out_bias,
    norm2_gain,
    norm2_bias,
    up_weight,
    up_bias,
    down_weight,
    down_bias,
    cotangent,
):
    gathered = (
        lax.all_gather(norm1_gain, "dp", axis=0, tiled=True),
        lax.all_gather(norm1_bias, "dp", axis=0, tiled=True),
        lax.all_gather(qkv_weight, "dp", axis=0, tiled=True),
        lax.all_gather(qv_bias, "dp", axis=0, tiled=True),
        lax.all_gather(out_weight, "dp", axis=0, tiled=True),
        lax.all_gather(out_bias, "dp", axis=0, tiled=True),
        lax.all_gather(norm2_gain, "dp", axis=0, tiled=True),
        lax.all_gather(norm2_bias, "dp", axis=0, tiled=True),
        lax.all_gather(up_weight, "dp", axis=0, tiled=True),
        lax.all_gather(up_bias, "dp", axis=0, tiled=True),
        lax.all_gather(down_weight, "dp", axis=0, tiled=True),
        lax.all_gather(down_bias, "dp", axis=0, tiled=True),
    )
    seq_count, tok_count, model_width = inputs.shape
    rows_all = seq_count * tok_count
    split_shape = (seq_count, tok_count, HEADS, HEAD)
    head_scale = HEAD ** (-0.5)
    matches = assignment[:, None] == jnp.arange(lengths.shape[0], dtype=jnp.int32)[None, :]
    kept_len = jnp.sum(jnp.where(matches, lengths[None, :], 0), axis=1)
    key_mask = jnp.arange(tok_count, dtype=jnp.int32)[None, :] < kept_len[:, None]
    row_mask = key_mask.reshape(rows_all, 1).astype(jnp.float32)
    gain_first = gathered[0].astype(jnp.float32)
    shift_first = gathered[1].astype(jnp.float32)
    qv_full = gathered[3].astype(jnp.float32)
    proj_shift = gathered[5].astype(jnp.float32)
    gain_second = gathered[6].astype(jnp.float32)
    shift_second = gathered[7].astype(jnp.float32)
    up_shift = gathered[9].astype(jnp.float32)
    down_shift = gathered[11].astype(jnp.float32)
    inputs_flat = inputs.reshape(rows_all, model_width).astype(jnp.float32)
    normed_first, first_back = jax.vjp(layer_norm, inputs_flat, gain_first, shift_first)
    normed_low = normed_first.astype(jnp.bfloat16)
    full_bias = jnp.concatenate(
        [qv_full[:model_width], jnp.zeros((model_width,), jnp.float32), qv_full[model_width:]]
    )
    mixed_qkv = (
        jnp.dot(normed_low, gathered[2], preferred_element_type=jnp.float32) + full_bias
    ).astype(jnp.bfloat16)
    queries = mixed_qkv[:, :model_width].reshape(split_shape)
    keys_all = mixed_qkv[:, model_width : 2 * model_width].reshape(split_shape)
    values_all = mixed_qkv[:, 2 * model_width :].reshape(split_shape)
    scores = (
        jnp.einsum("bqhd,bkhd->bhqk", queries, keys_all, preferred_element_type=jnp.float32)
        * head_scale
    )
    scores = jnp.where(key_mask[:, None, None, :], scores, masked_score)
    row_max = jnp.max(scores, axis=-1, keepdims=True)
    exponent = jnp.exp(scores - row_max)
    row_total = jnp.sum(exponent, axis=-1, keepdims=True)
    softmax_probs = exponent / row_total
    log_total = row_max + jnp.log(row_total)
    attended = jnp.einsum(
        "bhqk,bkhd->bqhd",
        softmax_probs.astype(jnp.bfloat16),
        values_all,
        preferred_element_type=jnp.float32,
    )
    attended = attended.reshape(rows_all, model_width).astype(jnp.bfloat16)
    hidden = inputs_flat + (
        jnp.dot(attended, gathered[4], preferred_element_type=jnp.float32) + proj_shift
    )
    normed_second, second_back = jax.vjp(layer_norm, hidden, gain_second, shift_second)
    second_low = normed_second.astype(jnp.bfloat16)
    pre_act = jnp.dot(second_low, gathered[8], preferred_element_type=jnp.float32) + up_shift
    activation, gelu_back = jax.vjp(gelu_exact, pre_act)
    act_low = activation.astype(jnp.bfloat16)
    output_rows = row_mask * (
        hidden + (jnp.dot(act_low, gathered[10], preferred_element_type=jnp.float32) + down_shift)
    )
    result = output_rows.reshape(inputs.shape).astype(jnp.bfloat16)
    grad_rows = cotangent.reshape(rows_all, model_width).astype(jnp.float32) * row_mask
    grad_low = grad_rows.astype(jnp.bfloat16)
    down_grad = contract_rows(act_low, grad_low)
    down_bias_grad = jnp.sum(grad_low.astype(jnp.float32), axis=0)
    grad_pre = gelu_back(contract_cols(grad_low, gathered[10]))[0].astype(jnp.bfloat16)
    up_grad = contract_rows(second_low, grad_pre)
    up_bias_grad = jnp.sum(grad_pre.astype(jnp.float32), axis=0)
    grad_second, gain2_grad, shift2_grad = second_back(contract_cols(grad_pre, gathered[8]))
    grad_hidden = grad_rows + grad_second
    branch_low = grad_hidden.astype(jnp.bfloat16)
    proj_grad = contract_rows(attended, branch_low)
    proj_bias_grad = jnp.sum(branch_low.astype(jnp.float32), axis=0)
    grad_att = contract_cols(branch_low, gathered[4]).astype(jnp.bfloat16).reshape(split_shape)
    scores_again = (
        jnp.einsum("bqhd,bkhd->bhqk", queries, keys_all, preferred_element_type=jnp.float32)
        * head_scale
    )
    scores_again = jnp.where(key_mask[:, None, None, :], scores_again, masked_score)
    probs_again = jnp.exp(scores_again - log_total)
    probs_low = probs_again.astype(jnp.bfloat16)
    grad_probs = jnp.einsum(
        "bqhd,bkhd->bhqk", grad_att, values_all, preferred_element_type=jnp.float32
    )
    grad_values = jnp.einsum(
        "bhqk,bqhd->bkhd", probs_low, grad_att, preferred_element_type=jnp.float32
    )
    inner_sum = jnp.sum(probs_again * grad_probs, axis=-1, keepdims=True)
    grad_scores = (probs_again * (grad_probs - inner_sum)).astype(jnp.bfloat16)
    grad_queries = (
        jnp.einsum("bhqk,bkhd->bqhd", grad_scores, keys_all, preferred_element_type=jnp.float32)
        * head_scale
    )
    grad_keys = (
        jnp.einsum("bhqk,bqhd->bkhd", grad_scores, queries, preferred_element_type=jnp.float32)
        * head_scale
    )
    grad_mixed = jnp.concatenate(
        [
            grad_queries.reshape(rows_all, model_width),
            grad_keys.reshape(rows_all, model_width),
            grad_values.reshape(rows_all, model_width),
        ],
        axis=1,
    ).astype(jnp.bfloat16)
    qkv_grad = contract_rows(normed_low, grad_mixed)
    column_sums = jnp.sum(grad_mixed.astype(jnp.float32), axis=0)
    qv_grad = jnp.concatenate([column_sums[:model_width], column_sums[2 * model_width :]])
    grad_first, gain1_grad, shift1_grad = first_back(contract_cols(grad_mixed, gathered[2]))
    input_grad = (grad_hidden + grad_first).reshape(inputs.shape).astype(jnp.bfloat16)
    all_sums = (
        lax.psum_scatter(gain1_grad, "dp", scatter_dimension=0, tiled=True),
        lax.psum_scatter(shift1_grad, "dp", scatter_dimension=0, tiled=True),
        lax.psum_scatter(qkv_grad, "dp", scatter_dimension=0, tiled=True),
        lax.psum_scatter(qv_grad, "dp", scatter_dimension=0, tiled=True),
        lax.psum_scatter(proj_grad, "dp", scatter_dimension=0, tiled=True),
        lax.psum_scatter(proj_bias_grad, "dp", scatter_dimension=0, tiled=True),
        lax.psum_scatter(gain2_grad, "dp", scatter_dimension=0, tiled=True),
        lax.psum_scatter(shift2_grad, "dp", scatter_dimension=0, tiled=True),
        lax.psum_scatter(up_grad, "dp", scatter_dimension=0, tiled=True),
        lax.psum_scatter(up_bias_grad, "dp", scatter_dimension=0, tiled=True),
        lax.psum_scatter(down_grad, "dp", scatter_dimension=0, tiled=True),
        lax.psum_scatter(down_bias_grad, "dp", scatter_dimension=0, tiled=True),
    )
    attn_sums = all_sums[:6]
    mlp_sums = all_sums[6:]
    return (
        result,
        input_grad,
        attn_sums[0],
        attn_sums[1],
        attn_sums[2],
        attn_sums[3],
        attn_sums[4],
        attn_sums[5],
        mlp_sums[0],
        mlp_sums[1],
        mlp_sums[2],
        mlp_sums[3],
        mlp_sums[4],
        mlp_sums[5],
    )


def local(*args):
    return on_box(*args) if lax.axis_size("dp") == 32 else plain(*args)


def solution(mesh):
    placed = (
        P("dp", None, None),
        P(),
        P("dp"),
        P("dp"),
        P("dp"),
        P("dp", None),
        P("dp"),
        P("dp", None),
        P("dp"),
        P("dp"),
        P("dp"),
        P("dp", None),
        P("dp"),
        P("dp", None),
        P("dp"),
        P("dp", None, None),
    )
    return jax.shard_map(
        local,
        mesh=mesh,
        in_specs=placed,
        out_specs=(
            P("dp", None, None),
            P("dp", None, None),
            P("dp"),
            P("dp"),
            P("dp", None),
            P("dp"),
            P("dp", None),
            P("dp"),
            P("dp"),
            P("dp"),
            P("dp", None),
            P("dp"),
            P("dp", None),
            P("dp"),
        ),
        check_vma=False,
    )
```
